32 devices in a mesh: group: 4 (over y, x), replica: 8 (over z, core).
Axes of the slice: x: 2, y: 2, z: 4, core: 2. Of those that a mesh axis runs over, the one named last changes fastest.
Arguments:
- inputs: bfloat16 [16, 1024, 2560], P('replica', 'group'), may hold values from -6 to 6
- segment_ids: int32 [16, 1024], P('replica'), may hold values from 0 to 4, as said below
- adapter_ids: int32 [16], P('replica'), may hold values from 0 to 7
- gain_mix: float32 [2560], replicated, may hold values from 0.25 to 1.75
- gain_mlp: float32 [2560], replicated, may hold values from 0.25 to 1.75
- w_branch: bfloat16 [2560, 2560], P(None, 'group'), may hold values from -0.125 to 0.125
- w_input: bfloat16 [2560, 2560], P(None, 'group'), may hold values from -0.125 to 0.125
- conv_taps: float32 [4, 2560], replicated, may hold values from -2.5 to 2.5
- decay_heads: bfloat16 [10, 256, 256], replicated, may hold values from -0.375 to 0.375
- admit_heads: bfloat16 [10, 256, 256], replicated, may hold values from -0.375 to 0.375
- decay_param: float32 [2560], replicated, may hold values from -9.5 to -3.5, as said below
- w_mixer: bfloat16 [2560, 2560], P('group'), may hold values from -0.25 to 0.25
- w_gate: bfloat16 [2560, 7680], P(None, 'group'), may hold values from -0.125 to 0.125
- w_upper: bfloat16 [2560, 7680], P(None, 'group'), may hold values from -0.125 to 0.125
- w_down: bfloat16 [7680, 2560], P('group'), may hold values from -0.09375 to 0.09375
- down_branch: bfloat16 [8, 2560, 16], P(None, 'group'), may hold values from -0.125 to 0.125
- lift_branch: bfloat16 [8, 16, 2560], P(None, None, 'group'), may hold values from -0.75 to 0.75
- down_input: bfloat16 [8, 2560, 16], P(None, 'group'), may hold values from -0.125 to 0.125
- lift_input: bfloat16 [8, 16, 2560], P(None, None, 'group'), may hold values from -0.75 to 0.75
- down_decay: bfloat16 [8, 2560, 16], P(None, 'group'), may hold values from -0.125 to 0.125
- lift_decay: bfloat16 [8, 16, 2560], P(None, None, 'group'), may hold values from -0.75 to 0.75
- down_admit: bfloat16 [8, 2560, 16], P(None, 'group'), may hold values from -0.125 to 0.125
- lift_admit: bfloat16 [8, 16, 2560], P(None, None, 'group'), may hold values from -0.75 to 0.75
- down_mixer: bfloat16 [8, 2560, 16], P(None, 'group'), may hold values from -0.125 to 0.125
- lift_mixer: bfloat16 [8, 16, 2560], P(None, None, 'group'), may hold values from -0.75 to 0.75
- down_gate: bfloat16 [8, 2560, 16], P(None, 'group'), may hold values from -0.125 to 0.125
- lift_gate: bfloat16 [8, 16, 7680], P(None, None, 'group'), may hold values from -0.75 to 0.75
- down_upper: bfloat16 [8, 2560, 16], P(None, 'group'), may hold values from -0.125 to 0.125
- lift_upper: bfloat16 [8, 16, 7680], P(None, None, 'group'), may hold values from -0.75 to 0.75
- down_outward: bfloat16 [8, 7680, 16], P(None, 'group'), may hold values from -0.0625 to 0.0625
- lift_outward: bfloat16 [8, 16, 2560], P(None, None, 'group'), may hold values from -0.75 to 0.75
- out_grad: bfloat16 [16, 1024, 2560], P('replica', 'group'), may hold values from -6 to 6
Outputs:
- block_out: bfloat16 [16, 1024, 2560], P('replica', 'group')
- grad_inputs: float32 [16, 1024, 2560], P('replica', 'group')
- grad_down_branch: float32 [8, 2560, 16], P(None, 'group')
- grad_lift_branch: float32 [8, 16, 2560], P(None, None, 'group')
- grad_down_input: float32 [8, 2560, 16], P(None, 'group')
- grad_lift_input: float32 [8, 16, 2560], P(None, None, 'group')
- grad_down_decay: float32 [8, 2560, 16], P(None, 'group')
- grad_lift_decay: float32 [8, 16, 2560], P(None, None, 'group')
- grad_down_admit: float32 [8, 2560, 16], P(None, 'group')
- grad_lift_admit: float32 [8, 16, 2560], P(None, None, 'group')
- grad_down_mixer: float32 [8, 2560, 16], P(None, 'group')
- grad_lift_mixer: float32 [8, 16, 2560], P(None, None, 'group')
- grad_down_gate: float32 [8, 2560, 16], P(None, 'group')
- grad_lift_gate: float32 [8, 16, 7680], P(None, None, 'group')
- grad_down_upper: float32 [8, 2560, 16], P(None, 'group')
- grad_lift_upper: float32 [8, 16, 7680], P(None, None, 'group')
- grad_down_outward: float32 [8, 7680, 16], P(None, 'group')
- grad_lift_outward: float32 [8, 16, 2560], P(None, None, 'group')
The draws below stay inside these ranges and needn't reach their ends.
Inputs may be any that keep to these rules, and one draw needn't show every extreme that they name: `segment_ids`: within each sequence the ids start at 0 and rise by 0 or 1 from one token to the next; a rise marks a new document. In each aligned run of 2 sequences one sequence holds a document that starts before position 64 and runs to the sequence's end. Rates softplus(decay_param) are positive; some channels keep most of their state over a whole sequence.
All inputs are finite; a program needn't handle non-finite values.
Results may differ from the reference program's by a relative error of at most 0.017.
Values may be sent and summed in bfloat16 or wider, within the bound.
A program may use at most 576 MiB of HBM per device.

```python
import math
import jax
import jax.numpy as jnp
from jax import lax

D = 2560
F = 7680
H = 10
HS = 256
R = 16
K = 8
CW = 4
LEN = 1024
SEQ_REP = 2
SEQS = 16


def draw_segment_ids(key, part):
    key = jax.random.fold_in(key, 7)
    flag_key, pick_key = jax.random.split(key)
    most = max(LEN // 256, 1)
    flags = (jax.random.randint(flag_key, (SEQS, LEN), 0, LEN // 4) == 0).astype(jnp.int32)
    positions = jnp.arange(LEN, dtype=jnp.int32)
    flags = flags * (positions > 0).astype(jnp.int32)[None, :]
    picked = jax.random.randint(pick_key, (SEQS // SEQ_REP,), 0, SEQ_REP)
    spanning = jnp.arange(SEQS, dtype=jnp.int32) % SEQ_REP == jnp.repeat(picked, SEQ_REP)
    early = ((positions >= 1) & (positions <= most)).astype(jnp.int32)
    flags = jnp.where(spanning[:, None], early[None, :], flags)
    return jnp.minimum(jnp.cumsum(flags, axis=1), most).astype(jnp.int32)


def draw_decay_param(key, part):
    key = jax.random.fold_in(key, 11)
    head_key, slow_key, fast_key = jax.random.split(key, 3)
    keeping = 0.5
    slow_heads = jax.random.uniform(head_key, (H,)) < keeping
    slow = jax.random.uniform(slow_key, (H, HS), minval=-9.5, maxval=-7.5)
    fast = jax.random.uniform(fast_key, (H, HS), minval=-4.5, maxval=-3.5)
    return jnp.where(slow_heads[:, None], slow, fast).reshape(D).astype(jnp.float32)


def set_ends(values, own_key, low, high):
    extent = values.shape
    place = [jax.random.randint(jax.random.fold_in(own_key, axis), (), 0, extent[axis]) for axis in range(len(extent))]
    values = values.at[tuple(place)].set(low)
    longest = extent.index(max(extent))
    place[longest] = (place[longest] + 1) % extent[longest]
    return values.at[tuple(place)].set(high)


def block_scale(key, extent, cuts, smallest, top_value):
    loudness, own = 1.0, jax.random.fold_in(key, 6)
    for dim, blocks in cuts:
        heights = jnp.exp(jax.random.uniform(jax.random.fold_in(own, dim), (blocks,), jnp.float32, smallest / len(cuts), top_value / len(cuts)))
        loudness = loudness * jnp.repeat(heights, extent[dim] // blocks).reshape([-1 if axis == dim else 1 for axis in range(len(extent))])
    return loudness


def centred(stream_key, shape, scale, reach, cuts=(), kind=jnp.bfloat16):
    level = block_scale(stream_key, shape, cuts, -0.22, 0.18) if cuts else 1.0
    entries = jax.random.normal(stream_key, shape, jnp.float32) * scale * level
    return jnp.minimum(jnp.maximum(entries, -reach), reach).astype(kind)


def setup_inputs(seed: int = 0) -> dict:
    streams_of = jax.random.split(jax.random.key(seed), 33)
    return {
        "inputs": centred(streams_of[0], (SEQS, LEN, D), 1.0, 6.0, ((0, 8), (1, 4))),
        "segment_ids": draw_segment_ids(jax.random.fold_in(streams_of[32], 71), 0),
        "adapter_ids": set_ends(jax.random.randint(streams_of[2], (SEQS,), 0, K), jax.random.fold_in(streams_of[2], 1), 0, K - 1).astype(jnp.int32),
        "gain_mix": jnp.clip(1.0 + 0.15 * jax.random.normal(streams_of[3], (D,), jnp.float32), 0.25, 1.75),
        "gain_mlp": jnp.clip(1.0 + 0.15 * jax.random.normal(streams_of[4], (D,), jnp.float32), 0.25, 1.75),
        "w_branch": centred(streams_of[5], (D, D), D ** -0.5, 0.125, ((1, 4),)),
        "w_input": centred(streams_of[6], (D, D), D ** -0.5, 0.125, ((1, 4),)),
        "conv_taps": centred(streams_of[7], (CW, D), 0.5, 2.5, (), jnp.float32),
        "decay_heads": centred(streams_of[8], (H, HS, HS), HS ** -0.5, 0.375),
        "admit_heads": centred(streams_of[9], (H, HS, HS), HS ** -0.5, 0.375),
        "decay_param": draw_decay_param(jax.random.fold_in(streams_of[32], 71), 0),
        "w_mixer": centred(streams_of[11], (D, D), (D // 4) ** -0.5, 0.25, ((0, 4),)),
        "w_gate": centred(streams_of[12], (D, F), D ** -0.5, 0.125, ((1, 4),)),
        "w_upper": centred(streams_of[13], (D, F), D ** -0.5, 0.125, ((1, 4),)),
        "w_down": centred(streams_of[14], (F, D), (F // 2) ** -0.5, 0.09375, ((0, 4),)),
        "down_branch": centred(streams_of[15], (K, D, R), D ** -0.5, 0.125, ((1, 4),)),
        "lift_branch": centred(streams_of[16], (K, R, D), (4 * R) ** -0.5, 0.75, ((2, 4),)),
        "down_input": centred(streams_of[17], (K, D, R), D ** -0.5, 0.125, ((1, 4),)),
        "lift_input": centred(streams_of[18], (K, R, D), (4 * R) ** -0.5, 0.75, ((2, 4),)),
        "down_decay": centred(streams_of[19], (K, D, R), D ** -0.5, 0.125, ((1, 4),)),
        "lift_decay": centred(streams_of[20], (K, R, D), (4 * R) ** -0.5, 0.75, ((2, 4),)),
        "down_admit": centred(streams_of[21], (K, D, R), D ** -0.5, 0.125, ((1, 4),)),
        "lift_admit": centred(streams_of[22], (K, R, D), (4 * R) ** -0.5, 0.75, ((2, 4),)),
        "down_mixer": centred(streams_of[23], (K, D, R), D ** -0.5, 0.125, ((1, 4),)),
        "lift_mixer": centred(streams_of[24], (K, R, D), (4 * R) ** -0.5, 0.75, ((2, 4),)),
        "down_gate": centred(streams_of[25], (K, D, R), D ** -0.5, 0.125, ((1, 4),)),
        "lift_gate": centred(streams_of[26], (K, R, F), (4 * R) ** -0.5, 0.75, ((2, 4),)),
        "down_upper": centred(streams_of[27], (K, D, R), D ** -0.5, 0.125, ((1, 4),)),
        "lift_upper": centred(streams_of[28], (K, R, F), (4 * R) ** -0.5, 0.75, ((2, 4),)),
        "down_outward": centred(streams_of[29], (K, F, R), F ** -0.5, 0.0625, ((1, 4),)),
        "lift_outward": centred(streams_of[30], (K, R, D), (4 * R) ** -0.5, 0.75, ((2, 4),)),
        "out_grad": centred(streams_of[31], (SEQS, LEN, D), 1.0, 6.0, ((0, 8), (1, 4))),
    }


@jax.custom_vjp
def low(v):
    return lax.optimization_barrier(v.astype(jnp.bfloat16)).astype(jnp.float32)

@jax.custom_vjp
def low_back(v):
    return v

def low_keep(v):
    return (low(v), None)

def low_pass(kept, grad):
    return (grad,)

def back_keep(v):
    return (v, None)

def back_low(kept, grad):
    return (low(grad),)
low.defvjp(low_keep, low_pass)
low_back.defvjp(back_keep, back_low)
HIGH = lax.Precision.HIGHEST
EPS = 1e-06

def matmul(values, weight):
    return jnp.einsum('sti,ij->stj', values, weight, precision=HIGH)

def rank_product(values, first, second):
    inner = jnp.einsum('sti,sir->str', values, first, precision=HIGH)
    return jnp.einsum('str,sro->sto', inner, second, precision=HIGH)

def norm_rows(values, gain):
    return values * lax.rsqrt(lax.optimization_barrier(jnp.mean(values * values, axis=-1, keepdims=True)) + EPS) * gain

def gelu_tanh(values):
    return jax.nn.gelu(values, approximate=True)

def head_mix(values, table):
    shaped = values.reshape(values.shape[:2] + (table.shape[0], table.shape[1]))
    return jnp.einsum('sthi,hij->sthj', shaped, table, precision=HIGH).reshape(values.shape)

def affine_join(earlier, later):
    return (earlier[0] * later[0], later[0] * earlier[1] + later[1])

def agreement(segment_rows, taps):
    padded = jnp.pad(segment_rows, ((0, 0), (taps - 1, 0)), constant_values=-1)
    length = segment_rows.shape[1]
    return [(segment_rows == padded[:, taps - 1 - j:taps - 1 - j + length]).astype(jnp.float32) for j in range(taps)]

def block_forward(x_float, segment_rows, set_rows, adapters, frozen):
    gain_mix, gain_mlp, w_branch, w_input, conv_taps, decay_heads, admit_heads, decay_param, w_mixer, w_gate, w_upper, w_down = frozen
    picked = [table[set_rows] for table in adapters]

    def extra(values, slot):
        return rank_product(values, picked[2 * slot], picked[2 * slot + 1])
    taps = conv_taps.shape[0]
    length = x_float.shape[1]
    normed = low(norm_rows(x_float, gain_mix))
    branch = gelu_tanh(low_back(matmul(normed, w_branch) + extra(normed, 0)))
    fed = low_back(low(matmul(normed, w_input) + extra(normed, 1)))
    agree = agreement(segment_rows, taps)
    padded = jnp.pad(fed, ((0, 0), (taps - 1, 0), (0, 0)))
    convolved = sum((conv_taps[j] * agree[j][..., None] * padded[:, taps - 1 - j:taps - 1 - j + length] for j in range(taps)))
    rounded = low(convolved)
    decay_gate = jax.nn.sigmoid(head_mix(rounded, decay_heads) + extra(rounded, 2))
    admit_gate = jax.nn.sigmoid(head_mix(rounded, admit_heads) + extra(rounded, 3))
    log_decay = -8.0 * decay_gate * jax.nn.softplus(decay_param)
    restart = (agree[1] < 0.5)[..., None]
    safe_log = jnp.where(restart, -1.0, log_decay)
    decays = jnp.where(restart, 0.0, jnp.exp(safe_log))
    scale_in = jnp.where(restart, 1.0, jnp.sqrt(-jnp.expm1(2.0 * safe_log)))
    drive = convolved * admit_gate * scale_in
    state = lax.associative_scan(affine_join, (decays, drive), axis=1)[1]
    merged = low(state * branch)
    mixed = low_back(matmul(merged, w_mixer) + extra(merged, 4))
    resid = x_float + mixed
    normed_two = low(norm_rows(resid, gain_mlp))
    gate_pre = low_back(matmul(normed_two, w_gate) + extra(normed_two, 5))
    upper_pre = low_back(matmul(normed_two, w_upper) + extra(normed_two, 6))
    hidden = low(gelu_tanh(gate_pre) * upper_pre)
    outward = low_back(matmul(hidden, w_down) + extra(hidden, 7))
    return resid + outward

def reference(inputs, segment_ids, adapter_ids, gain_mix, gain_mlp, w_branch, w_input, conv_taps, decay_heads, admit_heads, decay_param, w_mixer, w_gate, w_upper, w_down, down_branch, lift_branch, down_input, lift_input, down_decay, lift_decay, down_admit, lift_admit, down_mixer, lift_mixer, down_gate, lift_gate, down_upper, lift_upper, down_outward, lift_outward, out_grad):
    frozen = tuple((table.astype(jnp.float32) for table in (gain_mix, gain_mlp, w_branch, w_input, conv_taps, decay_heads, admit_heads, decay_param, w_mixer, w_gate, w_upper, w_down)))
    tables = tuple((table.astype(jnp.float32) for table in (down_branch, lift_branch, down_input, lift_input, down_decay, lift_decay, down_admit, lift_admit, down_mixer, lift_mixer, down_gate, lift_gate, down_upper, lift_upper, down_outward, lift_outward)))
    block = math.gcd(SEQS, 4)
    count = SEQS // block

    def regroup(values):
        return values.reshape((count, block) + values.shape[1:])

    def step(totals, pieces):
        rows, segment_rows, set_rows, cotangent = pieces

        def forward(x_float, adapters):
            return block_forward(x_float, segment_rows, set_rows, adapters, frozen)
        result, pullback = jax.vjp(forward, rows.astype(jnp.float32), tables)
        grad_rows, grad_tables = pullback(cotangent.astype(jnp.float32))
        summed = tuple((total + piece for total, piece in zip(totals, grad_tables)))
        return (summed, (result.astype(jnp.bfloat16), grad_rows))
    start = tuple((jnp.zeros_like(table) for table in tables))
    totals, (outputs, grads) = lax.scan(step, start, (regroup(inputs), regroup(segment_ids), regroup(adapter_ids), regroup(out_grad)))
    return (outputs.reshape(SEQS, LEN, D), grads.reshape(SEQS, LEN, D), totals[0], totals[1], totals[2], totals[3], totals[4], totals[5], totals[6], totals[7], totals[8], totals[9], totals[10], totals[11], totals[12], totals[13], totals[14], totals[15])
```

```python
import functools

import jax
import jax.numpy as jnp
from jax import lax
from jax.experimental import pallas as pl
from jax.experimental.pallas import tpu as pltpu
from jax.sharding import PartitionSpec as P

EPS = 1e-06
F32 = jnp.float32
BF16 = jnp.bfloat16
GELU_C = 0.7978845608028654
GELU_A = 0.044715
NT = (((1,), (1,)), ((), ()))
NN = (((1,), (0,)), ((), ()))
TN = (((0,), (0,)), ((), ()))


def dot(a, b, dims=NN):
    return lax.dot_general(a, b, dims, preferred_element_type=F32)


def gelu(v):
    return 0.5 * v * (1.0 + jnp.tanh(GELU_C * (v + GELU_A * v * v * v)))


def gelu_both(v):
    th = jnp.tanh(GELU_C * (v + GELU_A * v * v * v))
    value = 0.5 * v * (1.0 + th)
    slope = 0.5 * (1.0 + th) + 0.5 * v * (1.0 - th * th) * GELU_C * (1.0 + 3.0 * GELU_A * v * v)
    return value, slope


def norm_rows(values, gain):
    rate = lax.rsqrt(jnp.mean(values * values, axis=-1, keepdims=True) + EPS)
    return values * rate * gain, rate


def norm_back(values, gain, rate, grads):
    scaled = grads * gain
    along = jnp.mean(scaled * values, axis=-1, keepdims=True)
    return rate * scaled - values * (rate * rate * rate * along)


def rows_shifted(values, by, fill):
    rows, width = values.shape
    if by % 8 == 0:
        return jnp.concatenate([jnp.full((by, width), fill, values.dtype), values[: rows - by]], 0)
    place = lax.broadcasted_iota(jnp.int32, values.shape, 0)
    return jnp.where(place >= by, pltpu.roll(values, by, 0), fill)


def rows_advanced(values, by, fill):
    rows, width = values.shape
    if by % 8 == 0:
        return jnp.concatenate([values[by:], jnp.full((by, width), fill, values.dtype)], 0)
    place = lax.broadcasted_iota(jnp.int32, values.shape, 0)
    return jnp.where(place < rows - by, pltpu.roll(values, rows - by, 0), fill)


def scan_rows(a, b, moved):
    by = 1
    while by < a.shape[0]:
        b = a * moved(b, by, 0.0) + b
        a = a * moved(a, by, 1.0)
        by *= 2
    return a, b


def gate_values(conv, inner, lift, table_d, table_a, softrate, restart):
    rounded = conv.astype(BF16)
    half = lift.shape[0] // 2
    pre_d = dot(rounded, table_d) + dot(inner[:, :half], lift[:half])
    pre_a = dot(rounded, table_a) + dot(inner[:, half:], lift[half:])
    decay_gate = 1.0 / (1.0 + jnp.exp(-pre_d))
    admit_gate = 1.0 / (1.0 + jnp.exp(-pre_a))
    safe = jnp.where(restart, -1.0, -8.0 * decay_gate * softrate)
    grown = jnp.exp(safe)
    scale = jnp.sqrt(jnp.tanh(-safe) * (1.0 + grown * grown))
    return decay_gate, admit_gate, grown, scale


def forward_gates_kernel(seqs, conv_ref, inner_ref, lift_ref, table_d_ref, table_a_ref, soft_ref, restart_ref,
                         cum_ref, local_ref):
    stretch = conv_ref.shape[0] // seqs
    for s in range(seqs):
        rows = pl.ds(s * stretch, stretch)
        conv = conv_ref[rows, :]
        restart = restart_ref[rows, :] > 0.5
        _, admit, grown, scale = gate_values(
            conv, inner_ref[rows, :], lift_ref[...], table_d_ref[0], table_a_ref[0], soft_ref[...], restart)
        decays = jnp.where(restart, 0.0, grown)
        drive = conv * admit * jnp.where(restart, 1.0, scale)
        cum, local = scan_rows(decays, drive, rows_shifted)
        cum_ref[rows, :] = cum
        local_ref[rows, :] = local


def forward_gates(seqs, conv, inner, lift, table_d, table_a, softrate, restart):
    rows, width = conv.shape
    heads, size = table_d.shape[:2]
    tile = pl.BlockSpec((rows, size), lambda h: (0, h))
    table = pl.BlockSpec((1, size, size), lambda h: (h, 0, 0))
    out = jax.ShapeDtypeStruct((rows, width), F32)
    return pl.pallas_call(
        functools.partial(forward_gates_kernel, seqs),
        out_shape=(out, out),
        grid=(heads,),
        in_specs=[
            tile,
            pl.BlockSpec(inner.shape, lambda h: (0, 0)),
            pl.BlockSpec((lift.shape[0], size), lambda h: (0, h)),
            table,
            table,
            pl.BlockSpec((1, size), lambda h: (0, h)),
            pl.BlockSpec(restart.shape, lambda h: (0, 0)),
        ],
        out_specs=(tile, tile),
        compiler_params=pltpu.CompilerParams(vmem_limit_bytes=40 * 2**20),
        cost_estimate=pl.CostEstimate(
            flops=4 * rows * width * size + 60 * rows * width,
            bytes_accessed=12 * rows * width,
            transcendentals=6 * rows * width),
    )(conv, inner, lift, table_d, table_a, softrate, restart)


def backward_scan_kernel(seqs, conv_ref, inner_ref, lift_ref, table_d_ref, soft_ref, restart_ref, cum_ref, local_ref,
                         carried_ref, pre_ref, grad_ref, span_ref, total_ref, first_ref, branch_grad_ref):
    stretch = conv_ref.shape[0] // seqs
    half = lift_ref.shape[0] // 2
    for s in range(seqs):
        rows = pl.ds(s * stretch, stretch)
        restart = restart_ref[rows, :] > 0.5
        rounded = conv_ref[rows, :].astype(BF16)
        pre_d = dot(rounded, table_d_ref[0]) + dot(inner_ref[rows, :half], lift_ref[:half, :])
        grown = jnp.exp(-8.0 * soft_ref[...] / (1.0 + jnp.exp(-pre_d)))
        decays = jnp.where(restart, 0.0, grown)
        state = local_ref[rows, :] + cum_ref[rows, :] * carried_ref[s : s + 1, :]
        value, slope = gelu_both(pre_ref[rows, :])
        grads = grad_ref[rows, :]
        branch_grad_ref[rows, :] = (grads * state * slope).astype(BF16)
        span, total = scan_rows(rows_advanced(decays, 1, 1.0), grads * value, rows_advanced)
        span_ref[rows, :] = span
        total_ref[rows, :] = total
        first_ref[s : s + 1, :] = decays[:1] * span[:1]
        first_ref[seqs + s : seqs + s + 1, :] = decays[:1] * total[:1]


def backward_scan(seqs, conv, inner, lift, table_d, softrate, restart, cum, local, carried, pre, grads):
    rows, width = conv.shape
    heads, size = table_d.shape[:2]
    tile = pl.BlockSpec((rows, size), lambda h: (0, h))
    table = pl.BlockSpec((1, size, size), lambda h: (h, 0, 0))
    out = jax.ShapeDtypeStruct((rows, width), F32)
    return pl.pallas_call(
        functools.partial(backward_scan_kernel, seqs),
        out_shape=(out, out, jax.ShapeDtypeStruct((2 * seqs, width), F32), jax.ShapeDtypeStruct((rows, width), BF16)),
        grid=(heads,),
        in_specs=[
            tile,
            pl.BlockSpec(inner.shape, lambda h: (0, 0)),
            pl.BlockSpec((lift.shape[0], size), lambda h: (0, h)),
            table,
            pl.BlockSpec((1, size), lambda h: (0, h)),
            pl.BlockSpec(restart.shape, lambda h: (0, 0)),
            tile,
            tile,
            pl.BlockSpec((seqs, size), lambda h: (0, h)),
            tile,
            tile,
        ],
        out_specs=(tile, tile, pl.BlockSpec((2 * seqs, size), lambda h: (0, h)), tile),
        compiler_params=pltpu.CompilerParams(vmem_limit_bytes=48 * 2**20),
        cost_estimate=pl.CostEstimate(
            flops=2 * rows * width * size + 80 * rows * width,
            bytes_accessed=30 * rows * width,
            transcendentals=4 * rows * width),
    )(conv, inner, lift, table_d, softrate, restart, cum, local, carried, pre, grads)


def backward_gates_kernel(seqs, conv_ref, inner_ref, lift_ref, table_d_ref, table_a_ref, soft_ref, restart_ref,
                          cum_ref, local_ref, carried_ref, span_ref, total_ref, incoming_ref,
                          conv_grad_ref, through_ref, lift_grad_ref):
    stretch = conv_ref.shape[0] // seqs
    half = lift_ref.shape[0] // 2

    @pl.when(pl.program_id(0) == 0)
    def _():
        through_ref[...] = jnp.zeros_like(through_ref)

    for s in range(seqs):
        rows = pl.ds(s * stretch, stretch)
        conv = conv_ref[rows, :]
        inner = inner_ref[rows, :]
        restart = restart_ref[rows, :] > 0.5
        softrate = soft_ref[...]
        decay_gate, admit, grown, scale = gate_values(
            conv, inner, lift_ref[...], table_d_ref[0], table_a_ref[0], softrate, restart)
        carried = carried_ref[s : s + 1, :]
        state = local_ref[rows, :] + cum_ref[rows, :] * carried
        place = lax.broadcasted_iota(jnp.int32, state.shape, 0)
        before = jnp.where(place >= 1, pltpu.roll(state, 1, 0), carried)
        grads = total_ref[rows, :] + span_ref[rows, :] * incoming_ref[s : s + 1, :]
        driven = grads * jnp.where(restart, 1.0, scale)
        grad_log = jnp.where(
            restart, 0.0, grads * (before * grown - conv * admit * grown * grown / scale))
        grad_d = (-8.0 * softrate) * grad_log * decay_gate * (1.0 - decay_gate)
        grad_a = driven * conv * admit * (1.0 - admit)
        low_d, low_a = grad_d.astype(BF16), grad_a.astype(BF16)
        conv_grad_ref[rows, :] = driven * admit + dot(low_d, table_d_ref[0], NT) + dot(low_a, table_a_ref[0], NT)
        through_ref[rows, :half] += dot(low_d, lift_ref[:half, :], NT)
        through_ref[rows, half:] += dot(low_a, lift_ref[half:, :], NT)
        first = dot(inner[:, :half], low_d, TN)
        second = dot(inner[:, half:], low_a, TN)
        if s == 0:
            lift_grad_ref[:half, :] = first
            lift_grad_ref[half:, :] = second
        else:
            lift_grad_ref[:half, :] += first
            lift_grad_ref[half:, :] += second


def backward_gates(seqs, conv, inner, lift, table_d, table_a, softrate, restart, cum, local, carried, span, total,
                   incoming):
    rows, width = conv.shape
    heads, size = table_d.shape[:2]
    tile = pl.BlockSpec((rows, size), lambda h: (0, h))
    table = pl.BlockSpec((1, size, size), lambda h: (h, 0, 0))
    edge = pl.BlockSpec((seqs, size), lambda h: (0, h))
    ranks = pl.BlockSpec((lift.shape[0], size), lambda h: (0, h))
    return pl.pallas_call(
        functools.partial(backward_gates_kernel, seqs),
        out_shape=(
            jax.ShapeDtypeStruct((rows, width), F32),
            jax.ShapeDtypeStruct(inner.shape, F32),
            jax.ShapeDtypeStruct(lift.shape, F32),
        ),
        grid=(heads,),
        in_specs=[
            tile,
            pl.BlockSpec(inner.shape, lambda h: (0, 0)),
            ranks,
            table,
            table,
            pl.BlockSpec((1, size), lambda h: (0, h)),
            pl.BlockSpec(restart.shape, lambda h: (0, 0)),
            tile,
            tile,
            edge,
            tile,
            tile,
            edge,
        ],
        out_specs=(tile, pl.BlockSpec(inner.shape, lambda h: (0, 0)), ranks),
        compiler_params=pltpu.CompilerParams(vmem_limit_bytes=48 * 2**20),
        cost_estimate=pl.CostEstimate(
            flops=8 * rows * width * size + 80 * rows * width,
            bytes_accessed=24 * rows * width,
            transcendentals=6 * rows * width),
    )(conv, inner, lift, table_d, table_a, softrate, restart, cum, local, carried, span, total, incoming)


def spread_kernel(tables, ids_ref, got_ref, *out_refs):
    replicas, seqs, ranks = got_ref.shape[0], ids_ref.shape[0] // got_ref.shape[0], out_refs[0].shape[1]
    for table in range(tables):
        out_refs[table][...] = jnp.zeros_like(out_refs[table])
    for replica in range(replicas):
        for s in range(seqs):
            place = ids_ref[replica * seqs + s]
            for table in range(tables):
                rows = pl.ds((table * seqs + s) * ranks, ranks)
                out_refs[table][place] += got_ref[replica, rows, :].astype(F32)


def spread(ids, got, tables, sets, seqs):
    replicas, rows, width = got.shape
    ranks = rows // (tables * seqs)
    return pl.pallas_call(
        functools.partial(spread_kernel, tables),
        out_shape=[jax.ShapeDtypeStruct((sets, ranks, width), F32)] * tables,
        in_specs=[pl.BlockSpec(memory_space=pltpu.SMEM), pl.BlockSpec(memory_space=pltpu.VMEM)],
        out_specs=[pl.BlockSpec(memory_space=pltpu.VMEM)] * tables,
        compiler_params=pltpu.CompilerParams(vmem_limit_bytes=56 * 2**20),
        cost_estimate=pl.CostEstimate(
            flops=replicas * rows * width,
            bytes_accessed=2 * replicas * rows * width + 4 * tables * sets * ranks * width, transcendentals=0),
    )(ids, got)


def passed_along(block, axis, distance):
    devices = range(lax.axis_size(axis))
    route = [(i - distance, i) for i in devices if i - distance in devices]
    return lax.ppermute(block, axis, route)


def gathered_halves(weight, split, join):
    count = weight.shape[split] // 2
    parity = lax.axis_index("replica") % 2
    part = lax.dynamic_slice_in_dim(weight, parity * count, count, split)
    mine = lax.all_gather(part, "group", axis=join, tiled=True)
    swap = [(i, i ^ 1) for i in range(lax.axis_size("replica"))]
    return mine, lax.ppermute(mine, "replica", swap)


def by_parity(mine, other, axis):
    parity = lax.axis_index("replica") % 2
    return lax.cond(
        parity == 0,
        lambda: jnp.concatenate([mine, other], axis),
        lambda: jnp.concatenate([other, mine], axis),
    )


def body(
    inputs, segment_ids, adapter_ids, gain_mix, gain_mlp, w_branch, w_input, conv_taps, decay_heads, admit_heads,
    decay_param, w_mixer, w_gate, w_upper, w_down, down_branch, lift_branch, down_input, lift_input, down_decay,
    lift_decay, down_admit, lift_admit, down_mixer, lift_mixer, down_gate, lift_gate, down_upper, lift_upper,
    down_outward, lift_outward, out_grad,
):
    seqs, stretch, width = inputs.shape
    rows = seqs * stretch
    taps = conv_taps.shape[0]
    sets, _, ranks = down_branch.shape
    group, place = lax.axis_size("group"), lax.axis_index("group")
    mask_cols = seqs * ranks

    def chosen(table, down):
        table = jnp.swapaxes(table, 1, 2) if down else table
        return jnp.concatenate(
            [lax.dynamic_index_in_dim(table, adapter_ids[s], 0, False) for s in range(seqs)], 0)

    full_names = [down_branch, down_input, down_decay, down_admit, down_mixer, down_gate, down_upper,
                  lift_branch, lift_input, lift_decay, lift_admit, lift_mixer, lift_outward]
    stack = jnp.concatenate([chosen(t, i < 7) for i, t in enumerate(full_names)], 0)
    stack = lax.all_gather(stack, "group", axis=1, tiled=True)
    pick = [stack[i * mask_cols : (i + 1) * mask_cols] for i in range(13)]
    (p_down_branch, p_down_input, p_down_decay, p_down_admit, p_down_mixer, p_down_gate, p_down_upper,
     p_lift_branch, p_lift_input, p_lift_decay, p_lift_admit, p_lift_mixer, p_lift_outward) = pick
    own_lift_gate, own_lift_upper, own_down_outward = (
        chosen(lift_gate, False), chosen(lift_upper, False), chosen(down_outward, True))
    all_ids = lax.all_gather(adapter_ids, "replica", axis=0, tiled=True)

    branch_mine, branch_other = gathered_halves(w_branch, 0, 1)
    input_mine, input_other = gathered_halves(w_input, 0, 1)
    mixer_mine, mixer_other = gathered_halves(w_mixer, 1, 0)
    half = width // 2

    row_seq = lax.broadcasted_iota(jnp.int32, (rows, mask_cols), 0) // stretch
    col_seq = lax.broadcasted_iota(jnp.int32, (rows, mask_cols), 1) // ranks
    own = (row_seq == col_seq).astype(F32)
    own_two = jnp.concatenate([own, own], 1)

    begin = place * stretch
    padded_ids = jnp.pad(segment_ids, ((0, 0), (taps - 1, taps - 1)), constant_values=-1)
    window = lax.dynamic_slice_in_dim(padded_ids, begin, stretch + 2 * (taps - 1), 1)
    current = window[:, taps - 1 : taps - 1 + stretch + taps - 1]
    agree = [
        ((current == window[:, taps - 1 - j : taps - 1 - j + stretch + taps - 1]) & (current >= 0)).astype(F32)
        for j in range(taps)
    ]
    restart = (1.0 - agree[1][:, :stretch]).reshape(rows, 1)

    x_float = inputs.reshape(rows, width).astype(F32)
    normed_f, rate_one = norm_rows(x_float, gain_mix)
    normed = normed_f.astype(BF16)
    parity = lax.axis_index("replica") % 2
    normed_mine = lax.dynamic_slice_in_dim(normed, parity * half, half, 1)
    normed_other = lax.dynamic_slice_in_dim(normed, (1 - parity) * half, half, 1)
    inner_one = (dot(normed, stack[: 2 * mask_cols], NT) * own_two).astype(BF16)
    inner_branch, inner_input = inner_one[:, :mask_cols], inner_one[:, mask_cols:]
    branch_pre = dot(normed_mine, branch_mine) + dot(normed_other, branch_other) + dot(inner_branch, p_lift_branch)
    fed = (dot(normed_mine, input_mine) + dot(normed_other, input_other) + dot(inner_input, p_lift_input)).astype(BF16)
    fed = fed.reshape(seqs, stretch, width)
    halo = passed_along(fed[:, stretch - (taps - 1) :], "group", 1)
    extended = jnp.concatenate([halo, fed], axis=1).astype(F32)
    convolved = sum(
        conv_taps[j] * agree[j][:, :stretch, None] * extended[:, taps - 1 - j : taps - 1 - j + stretch]
        for j in range(taps)
    ).reshape(rows, width)
    rounded = convolved.astype(BF16)
    softrate = jax.nn.softplus(decay_param).reshape(1, width)
    inner_gates = (dot(rounded, stack[2 * mask_cols : 4 * mask_cols], NT) * own_two).astype(BF16)
    lift_gates = stack[9 * mask_cols : 11 * mask_cols]
    cum, local = forward_gates(seqs, convolved, inner_gates, lift_gates, decay_heads, admit_heads, softrate, restart)
    ends = jnp.concatenate(
        [cum.reshape(seqs, stretch, width)[:, -1], local.reshape(seqs, stretch, width)[:, -1]], 0)
    all_ends = lax.all_gather(ends, "group")
    carried = jnp.zeros((seqs, width), F32)
    for g in range(group - 1):
        longer = all_ends[g, :seqs] * carried + all_ends[g, seqs:]
        carried = jnp.where(g < place, longer, carried)
    carried_rows = jnp.repeat(carried, stretch, axis=0)
    state = local + cum * carried_rows
    merged = (state * gelu(branch_pre)).astype(BF16)
    inner_mixer = (dot(merged, p_down_mixer, NT) * own).astype(BF16)
    mixed = by_parity(dot(merged, mixer_mine), dot(merged, mixer_other), 1) + dot(inner_mixer, p_lift_mixer)
    resid = x_float + mixed
    normed_two_f, rate_two = norm_rows(resid, gain_mlp)
    normed_two = normed_two_f.astype(BF16).reshape(seqs, stretch, width)

    outs, backs, down_parts, lift_parts = [], [], [], []
    grad_own_lift_gate, grad_own_lift_upper, grad_own_down_outward = [], [], []
    grad_down_gate, grad_down_upper, grad_lift_outward = [], [], []
    for s in range(seqs):
        at = slice(s * ranks, (s + 1) * ranks)
        cotangent = lax.all_gather(out_grad[s], "group", axis=0, tiled=True)
        tokens = lax.all_gather(normed_two[s], "group", axis=0, tiled=True)
        inner_gate = dot(tokens, p_down_gate[at], NT).astype(BF16)
        inner_upper = dot(tokens, p_down_upper[at], NT).astype(BF16)
        through_out = dot(cotangent, p_lift_outward[at], NT).astype(BF16)
        gate_pre = dot(tokens, w_gate) + dot(inner_gate, own_lift_gate[at])
        upper_pre = dot(tokens, w_upper) + dot(inner_upper, own_lift_upper[at])
        grad_hidden = dot(cotangent, w_down, NT) + dot(through_out, own_down_outward[at])
        value, slope = gelu_both(gate_pre)
        hidden = (value * upper_pre).astype(BF16)
        grad_gate = (grad_hidden * upper_pre * slope).astype(BF16)
        grad_upper = (grad_hidden * value).astype(BF16)
        inner_out = dot(hidden, own_down_outward[at], NT).astype(BF16)
        outward = dot(hidden, w_down) + dot(inner_out, p_lift_outward[at])
        through_gate = dot(grad_gate, own_lift_gate[at], NT).astype(BF16)
        through_upper = dot(grad_upper, own_lift_upper[at], NT).astype(BF16)
        back = (dot(grad_gate, w_gate, NT) + dot(grad_upper, w_upper, NT)
                + dot(through_gate, p_down_gate[at]) + dot(through_upper, p_down_upper[at]))
        backs.append(lax.psum_scatter(back.astype(BF16), "group", scatter_dimension=0, tiled=True))
        outs.append(lax.psum_scatter(outward.astype(BF16), "group", scatter_dimension=0, tiled=True))
        grad_own_lift_gate.append(dot(inner_gate, grad_gate, TN))
        grad_own_lift_upper.append(dot(inner_upper, grad_upper, TN))
        grad_own_down_outward.append(dot(through_out, hidden, TN))
        grad_down_gate.append(dot(through_gate, tokens, TN))
        grad_down_upper.append(dot(through_upper, tokens, TN))
        grad_lift_outward.append(dot(inner_out, cotangent, TN))
    outward = jnp.concatenate(outs, 0).astype(F32)
    grad_normed_two = jnp.concatenate(backs, 0).astype(F32)
    block_out = (resid + outward).astype(BF16).reshape(seqs, stretch, width)
    grad_resid = out_grad.reshape(rows, width).astype(F32) + norm_back(resid, gain_mlp, rate_two, grad_normed_two)

    grad_mixed = grad_resid.astype(BF16)
    grad_mixed_mine = lax.dynamic_slice_in_dim(grad_mixed, parity * half, half, 1)
    grad_mixed_other = lax.dynamic_slice_in_dim(grad_mixed, (1 - parity) * half, half, 1)
    through_mixer = (dot(grad_mixed, p_lift_mixer, NT) * own).astype(BF16)
    grad_merged = (dot(grad_mixed_mine, mixer_mine, NT) + dot(grad_mixed_other, mixer_other, NT)
                   + dot(through_mixer, p_down_mixer))
    span, total, firsts, grad_branch_pre = backward_scan(
        seqs, convolved, inner_gates, lift_gates, decay_heads, softrate, restart, cum, local, carried, branch_pre,
        grad_merged)
    all_firsts = lax.all_gather(firsts, "group")
    incoming = jnp.zeros((seqs, width), F32)
    for lap in range(group - 1):
        g = group - 1 - lap
        longer = all_firsts[g, :seqs] * incoming + all_firsts[g, seqs:]
        incoming = jnp.where(g > place, longer, incoming)
    grad_direct, through_gates, grad_lift_gates = backward_gates(
        seqs, convolved, inner_gates, lift_gates, decay_heads, admit_heads, softrate, restart, cum, local, carried,
        span, total, incoming)
    through_gates = (through_gates * own_two).astype(BF16)
    grad_convolved = grad_direct + dot(through_gates, stack[2 * mask_cols : 4 * mask_cols])
    grad_convolved = grad_convolved.reshape(seqs, stretch, width)
    below = passed_along(grad_convolved[:, : taps - 1].astype(BF16), "group", -1).astype(F32)
    grad_extended = jnp.concatenate([grad_convolved, below], axis=1)
    grad_fed = sum(
        conv_taps[j] * agree[j][:, j : j + stretch, None] * grad_extended[:, j : j + stretch] for j in range(taps)
    ).astype(BF16).reshape(rows, width)
    through_branch = (dot(grad_branch_pre, p_lift_branch, NT) * own).astype(BF16)
    through_input = (dot(grad_fed, p_lift_input, NT) * own).astype(BF16)
    through_one = jnp.concatenate([through_branch, through_input], 1)
    grad_normed = (
        by_parity(
            dot(grad_branch_pre, branch_mine, NT) + dot(grad_fed, input_mine, NT),
            dot(grad_branch_pre, branch_other, NT) + dot(grad_fed, input_other, NT), 1)
        + dot(through_one, stack[: 2 * mask_cols]))
    grad_inputs = grad_resid + norm_back(x_float, gain_mix, rate_one, grad_normed)

    partial = jnp.concatenate(
        [dot(through_one, normed, TN), dot(through_gates, rounded, TN), dot(through_mixer, merged, TN)]
        + grad_down_gate + grad_down_upper
        + [dot(inner_branch, grad_branch_pre, TN), dot(inner_input, grad_fed, TN), grad_lift_gates,
           dot(inner_mixer, grad_mixed, TN)]
        + grad_lift_outward, 0).astype(BF16)
    owned = lax.psum_scatter(partial, "group", scatter_dimension=1, tiled=True)
    wide = jnp.concatenate(grad_own_lift_gate + grad_own_lift_upper + grad_own_down_outward, 0).astype(BF16)
    totals = spread(all_ids, lax.all_gather(owned, "replica"), 13, sets, seqs)
    wides = spread(all_ids, lax.all_gather(wide, "replica"), 3, sets, seqs)
    turned = lambda table: jnp.swapaxes(table, 1, 2)
    return (
        block_out, grad_inputs.reshape(seqs, stretch, width),
        turned(totals[0]), totals[7], turned(totals[1]), totals[8], turned(totals[2]), totals[9],
        turned(totals[3]), totals[10], turned(totals[4]), totals[11], turned(totals[5]), wides[0],
        turned(totals[6]), wides[1], turned(wides[2]), totals[12],
    )


def solution(mesh):
    tokens = P("replica", "group", None)
    down, lift = P(None, "group", None), P(None, None, "group")
    cols, split = P(None, "group"), P("group", None)
    in_specs = (
        tokens, P("replica", None), P("replica"), P(), P(), cols, cols, P(), P(), P(), P(), split, cols, cols, split,
    ) + (down, lift) * 8 + (tokens,)
    out_specs = (tokens, tokens) + (down, lift) * 8
    return jax.shard_map(body, mesh=mesh, in_specs=in_specs, out_specs=out_specs, check_vma=False)
```

```python
import functools

import jax
import jax.numpy as jnp
from jax import lax
from jax.experimental import pallas as pl
from jax.experimental.pallas import tpu as pltpu
from jax.sharding import PartitionSpec as P

EPS = 1e-06
F32 = jnp.float32
BF16 = jnp.bfloat16
GELU_C = 0.7978845608028654
GELU_A = 0.044715
NT = (((1,), (1,)), ((), ()))
NN = (((1,), (0,)), ((), ()))
TN = (((0,), (0,)), ((), ()))


def dot(a, b, dims=NN):
    return lax.dot_general(a, b, dims, preferred_element_type=F32)


def gelu(v):
    return 0.5 * v * (1.0 + jnp.tanh(GELU_C * (v + GELU_A * v * v * v)))


def gelu_both(v):
    th = jnp.tanh(GELU_C * (v + GELU_A * v * v * v))
    value = 0.5 * v * (1.0 + th)
    slope = 0.5 * (1.0 + th) + 0.5 * v * (1.0 - th * th) * GELU_C * (1.0 + 3.0 * GELU_A * v * v)
    return value, slope


def norm_rows(values, gain):
    rate = lax.rsqrt(jnp.mean(values * values, axis=-1, keepdims=True) + EPS)
    return values * rate * gain, rate


def norm_back(values, gain, rate, grads):
    scaled = grads * gain
    along = jnp.mean(scaled * values, axis=-1, keepdims=True)
    return rate * scaled - values * (rate * rate * rate * along)


def rows_shifted(values, by, fill):
    rows, width = values.shape
    if by % 8 == 0:
        return jnp.concatenate([jnp.full((by, width), fill, values.dtype), values[: rows - by]], 0)
    place = lax.broadcasted_iota(jnp.int32, values.shape, 0)
    return jnp.where(place >= by, pltpu.roll(values, by, 0), fill)


def rows_advanced(values, by, fill):
    rows, width = values.shape
    if by % 8 == 0:
        return jnp.concatenate([values[by:], jnp.full((by, width), fill, values.dtype)], 0)
    place = lax.broadcasted_iota(jnp.int32, values.shape, 0)
    return jnp.where(place < rows - by, pltpu.roll(values, rows - by, 0), fill)


def scan_rows(a, b, moved):
    by = 1
    while by < a.shape[0]:
        b = a * moved(b, by, 0.0) + b
        a = a * moved(a, by, 1.0)
        by *= 2
    return a, b


def gate_values(conv, inner, lift, table_d, table_a, softrate, restart):
    rounded = conv.astype(BF16)
    half = lift.shape[0] // 2
    pre_d = dot(rounded, table_d) + dot(inner[:, :half], lift[:half])
    pre_a = dot(rounded, table_a) + dot(inner[:, half:], lift[half:])
    decay_gate = 1.0 / (1.0 + jnp.exp(-pre_d))
    admit_gate = 1.0 / (1.0 + jnp.exp(-pre_a))
    safe = jnp.where(restart, -1.0, -8.0 * decay_gate * softrate)
    grown = jnp.exp(safe)
    scale = jnp.sqrt(jnp.tanh(-safe) * (1.0 + grown * grown))
    return decay_gate, admit_gate, grown, scale


def forward_gates_kernel(seqs, conv_ref, inner_ref, lift_ref, table_d_ref, table_a_ref, soft_ref, restart_ref,
                         cum_ref, local_ref):
    stretch = conv_ref.shape[0] // seqs
    for s in range(seqs):
        rows = pl.ds(s * stretch, stretch)
        conv = conv_ref[rows, :]
        restart = restart_ref[rows, :] > 0.5
        _, admit, grown, scale = gate_values(
            conv, inner_ref[rows, :], lift_ref[...], table_d_ref[0], table_a_ref[0], soft_ref[...], restart)
        decays = jnp.where(restart, 0.0, grown)
        drive = conv * admit * jnp.where(restart, 1.0, scale)
        cum, local = scan_rows(decays, drive, rows_shifted)
        cum_ref[rows, :] = cum
        local_ref[rows, :] = local


def forward_gates(seqs, conv, inner, lift, table_d, table_a, softrate, restart):
    rows, width = conv.shape
    heads, size = table_d.shape[:2]
    tile = pl.BlockSpec((rows, size), lambda h: (0, h))
    table = pl.BlockSpec((1, size, size), lambda h: (h, 0, 0))
    out = jax.ShapeDtypeStruct((rows, width), F32)
    return pl.pallas_call(
        functools.partial(forward_gates_kernel, seqs),
        out_shape=(out, out),
        grid=(heads,),
        in_specs=[
            tile,
            pl.BlockSpec(inner.shape, lambda h: (0, 0)),
            pl.BlockSpec((lift.shape[0], size), lambda h: (0, h)),
            table,
            table,
            pl.BlockSpec((1, size), lambda h: (0, h)),
            pl.BlockSpec(restart.shape, lambda h: (0, 0)),
        ],
        out_specs=(tile, tile),
        compiler_params=pltpu.CompilerParams(vmem_limit_bytes=40 * 2**20),
        cost_estimate=pl.CostEstimate(
            flops=4 * rows * width * size + 60 * rows * width,
            bytes_accessed=12 * rows * width,
            transcendentals=6 * rows * width),
    )(conv, inner, lift, table_d, table_a, softrate, restart)


def backward_scan_kernel(seqs, conv_ref, inner_ref, lift_ref, table_d_ref, soft_ref, restart_ref, cum_ref, local_ref,
                         carried_ref, pre_ref, grad_ref, span_ref, total_ref, first_ref, branch_grad_ref):
    stretch = conv_ref.shape[0] // seqs
    half = lift_ref.shape[0] // 2
    for s in range(seqs):
        rows = pl.ds(s * stretch, stretch)
        restart = restart_ref[rows, :] > 0.5
        rounded = conv_ref[rows, :].astype(BF16)
        pre_d = dot(rounded, table_d_ref[0]) + dot(inner_ref[rows, :half], lift_ref[:half, :])
        grown = jnp.exp(-8.0 * soft_ref[...] / (1.0 + jnp.exp(-pre_d)))
        decays = jnp.where(restart, 0.0, grown)
        state = local_ref[rows, :] + cum_ref[rows, :] * carried_ref[s : s + 1, :]
        value, slope = gelu_both(pre_ref[rows, :])
        grads = grad_ref[rows, :]
        branch_grad_ref[rows, :] = (grads * state * slope).astype(BF16)
        span, total = scan_rows(rows_advanced(decays, 1, 1.0), grads * value, rows_advanced)
        span_ref[rows, :] = span
        total_ref[rows, :] = total
        first_ref[s : s + 1, :] = decays[:1] * span[:1]
        first_ref[seqs + s : seqs + s + 1, :] = decays[:1] * total[:1]


def backward_scan(seqs, conv, inner, lift, table_d, softrate, restart, cum, local, carried, pre, grads):
    rows, width = conv.shape
    heads, size = table_d.shape[:2]
    tile = pl.BlockSpec((rows, size), lambda h: (0, h))
    table = pl.BlockSpec((1, size, size), lambda h: (h, 0, 0))
    out = jax.ShapeDtypeStruct((rows, width), F32)
    return pl.pallas_call(
        functools.partial(backward_scan_kernel, seqs),
        out_shape=(out, out, jax.ShapeDtypeStruct((2 * seqs, width), F32), jax.ShapeDtypeStruct((rows, width), BF16)),
        grid=(heads,),
        in_specs=[
            tile,
            pl.BlockSpec(inner.shape, lambda h: (0, 0)),
            pl.BlockSpec((lift.shape[0], size), lambda h: (0, h)),
            table,
            pl.BlockSpec((1, size), lambda h: (0, h)),
            pl.BlockSpec(restart.shape, lambda h: (0, 0)),
            tile,
            tile,
            pl.BlockSpec((seqs, size), lambda h: (0, h)),
            tile,
            tile,
        ],
        out_specs=(tile, tile, pl.BlockSpec((2 * seqs, size), lambda h: (0, h)), tile),
        compiler_params=pltpu.CompilerParams(vmem_limit_bytes=48 * 2**20),
        cost_estimate=pl.CostEstimate(
            flops=2 * rows * width * size + 80 * rows * width,
            bytes_accessed=30 * rows * width,
            transcendentals=4 * rows * width),
    )(conv, inner, lift, table_d, softrate, restart, cum, local, carried, pre, grads)


def backward_gates_kernel(seqs, conv_ref, inner_ref, lift_ref, table_d_ref, table_a_ref, soft_ref, restart_ref,
                          cum_ref, local_ref, carried_ref, span_ref, total_ref, incoming_ref,
                          conv_grad_ref, through_ref, lift_grad_ref):
    stretch = conv_ref.shape[0] // seqs
    half = lift_ref.shape[0] // 2

    @pl.when(pl.program_id(0) == 0)
    def _():
        through_ref[...] = jnp.zeros_like(through_ref)

    for s in range(seqs):
        rows = pl.ds(s * stretch, stretch)
        conv = conv_ref[rows, :]
        inner = inner_ref[rows, :]
        restart = restart_ref[rows, :] > 0.5
        softrate = soft_ref[...]
        decay_gate, admit, grown, scale = gate_values(
            conv, inner, lift_ref[...], table_d_ref[0], table_a_ref[0], softrate, restart)
        carried = carried_ref[s : s + 1, :]
        state = local_ref[rows, :] + cum_ref[rows, :] * carried
        place = lax.broadcasted_iota(jnp.int32, state.shape, 0)
        before = jnp.where(place >= 1, pltpu.roll(state, 1, 0), carried)
        grads = total_ref[rows, :] + span_ref[rows, :] * incoming_ref[s : s + 1, :]
        driven = grads * jnp.where(restart, 1.0, scale)
        grad_log = jnp.where(
            restart, 0.0, grads * (before * grown - conv * admit * grown * grown / scale))
        grad_d = (-8.0 * softrate) * grad_log * decay_gate * (1.0 - decay_gate)
        grad_a = driven * conv * admit * (1.0 - admit)
        low_d, low_a = grad_d.astype(BF16), grad_a.astype(BF16)
        conv_grad_ref[rows, :] = driven * admit + dot(low_d, table_d_ref[0], NT) + dot(low_a, table_a_ref[0], NT)
        through_ref[rows, :half] += dot(low_d, lift_ref[:half, :], NT)
        through_ref[rows, half:] += dot(low_a, lift_ref[half:, :], NT)
        first = dot(inner[:, :half], low_d, TN)
        second = dot(inner[:, half:], low_a, TN)
        if s == 0:
            lift_grad_ref[:half, :] = first
            lift_grad_ref[half:, :] = second
        else:
            lift_grad_ref[:half, :] += first
            lift_grad_ref[half:, :] += second


def backward_gates(seqs, conv, inner, lift, table_d, table_a, softrate, restart, cum, local, carried, span, total,
                   incoming):
    rows, width = conv.shape
    heads, size = table_d.shape[:2]
    tile = pl.BlockSpec((rows, size), lambda h: (0, h))
    table = pl.BlockSpec((1, size, size), lambda h: (h, 0, 0))
    edge = pl.BlockSpec((seqs, size), lambda h: (0, h))
    ranks = pl.BlockSpec((lift.shape[0], size), lambda h: (0, h))
    return pl.pallas_call(
        functools.partial(backward_gates_kernel, seqs),
        out_shape=(
            jax.ShapeDtypeStruct((rows, width), F32),
            jax.ShapeDtypeStruct(inner.shape, F32),
            jax.ShapeDtypeStruct(lift.shape, F32),
        ),
        grid=(heads,),
        in_specs=[
            tile,
            pl.BlockSpec(inner.shape, lambda h: (0, 0)),
            ranks,
            table,
            table,
            pl.BlockSpec((1, size), lambda h: (0, h)),
            pl.BlockSpec(restart.shape, lambda h: (0, 0)),
            tile,
            tile,
            edge,
            tile,
            tile,
            edge,
        ],
        out_specs=(tile, pl.BlockSpec(inner.shape, lambda h: (0, 0)), ranks),
        compiler_params=pltpu.CompilerParams(vmem_limit_bytes=48 * 2**20),
        cost_estimate=pl.CostEstimate(
            flops=8 * rows * width * size + 80 * rows * width,
            bytes_accessed=24 * rows * width,
            transcendentals=6 * rows * width),
    )(conv, inner, lift, table_d, table_a, softrate, restart, cum, local, carried, span, total, incoming)


def resident(array):
    return pl.BlockSpec(array.shape, lambda i: (0, 0), pipeline_mode=pl.Buffered(1))


def tile_of(count, tile):
    return tile if count % 128 == 0 and count > tile else count


def grad_hidden_kernel(cot_ref, wd_ref, lift_out_ref, do_ref, out_ref, through_ref):
    @pl.when(pl.program_id(0) == 0)
    def _():
        through_ref[...] = dot(cot_ref[...], lift_out_ref[...], NT).astype(BF16)

    out_ref[...] = (dot(cot_ref[...], wd_ref[...], NT) + dot(through_ref[...], do_ref[...])).astype(BF16)


def grad_hidden_call(cot, wd, lift_out, do):
    rows, width = cot.shape
    units, ranks = wd.shape[0], do.shape[0]
    tile = tile_of(units, 512)
    return pl.pallas_call(
        grad_hidden_kernel,
        grid=(pl.cdiv(units, tile),),
        out_shape=[jax.ShapeDtypeStruct((rows, units), BF16), jax.ShapeDtypeStruct((rows, ranks), BF16)],
        in_specs=[resident(cot), pl.BlockSpec((tile, width), lambda i: (i, 0)), resident(lift_out),
                  pl.BlockSpec((ranks, tile), lambda i: (0, i))],
        out_specs=[pl.BlockSpec((rows, tile), lambda i: (0, i)), pl.BlockSpec((rows, ranks), lambda i: (0, 0))],
        compiler_params=pltpu.CompilerParams(vmem_limit_bytes=60 * 2**20),
        cost_estimate=pl.CostEstimate(
            flops=2 * rows * width * units, bytes_accessed=2 * width * units + 2 * rows * (units + width),
            transcendentals=0),
    )(cot, wd, lift_out, do)


def hidden_kernel(tok_ref, gh_ref, wg_ref, wu_ref, down_ref, lg_ref, lu_ref, hidden_ref, gg_ref, gu_ref, inner_ref):
    ranks = lg_ref.shape[0]

    @pl.when(pl.program_id(0) == 0)
    def _():
        inner_ref[...] = dot(tok_ref[...], down_ref[...], NT).astype(BF16)

    tokens, inner = tok_ref[...], inner_ref[...]
    gate = dot(tokens, wg_ref[...]) + dot(inner[:, :ranks], lg_ref[...])
    upper = dot(tokens, wu_ref[...]) + dot(inner[:, ranks:], lu_ref[...])
    grad_hidden = gh_ref[...].astype(F32)
    value, slope = gelu_both(gate)
    hidden_ref[...] = (value * upper).astype(BF16)
    gg_ref[...] = (grad_hidden * upper * slope).astype(BF16)
    gu_ref[...] = (grad_hidden * value).astype(BF16)


def hidden_call(tok, gh, wg, wu, down, lg, lu):
    rows, width = tok.shape
    units, ranks = wg.shape[1], lg.shape[0]
    tile = tile_of(units, 512)
    cols = pl.BlockSpec((width, tile), lambda i: (0, i))
    rank = pl.BlockSpec((ranks, tile), lambda i: (0, i))
    out = pl.BlockSpec((rows, tile), lambda i: (0, i))
    wide = jax.ShapeDtypeStruct((rows, units), BF16)
    return pl.pallas_call(
        hidden_kernel,
        grid=(pl.cdiv(units, tile),),
        out_shape=[wide, wide, wide, jax.ShapeDtypeStruct((rows, 2 * ranks), BF16)],
        in_specs=[resident(tok), out, cols, cols, resident(down), rank, rank],
        out_specs=[out, out, out, pl.BlockSpec((rows, 2 * ranks), lambda i: (0, 0))],
        compiler_params=pltpu.CompilerParams(vmem_limit_bytes=60 * 2**20),
        cost_estimate=pl.CostEstimate(
            flops=4 * rows * width * units, bytes_accessed=4 * width * units + 10 * rows * units,
            transcendentals=rows * units),
    )(tok, gh, wg, wu, down, lg, lu)


def back_kernel(gg_ref, gu_ref, wg_ref, wu_ref, lg_ref, lu_ref, down_ref, back_ref, through_ref):
    ranks = lg_ref.shape[0]

    @pl.when(pl.program_id(0) == 0)
    def _():
        through_ref[:, :ranks] = dot(gg_ref[...], lg_ref[...], NT).astype(BF16)
        through_ref[:, ranks:] = dot(gu_ref[...], lu_ref[...], NT).astype(BF16)

    back_ref[...] = (dot(gg_ref[...], wg_ref[...], NT) + dot(gu_ref[...], wu_ref[...], NT)
                     + dot(through_ref[...], down_ref[...])).astype(BF16)


def back_call(gg, gu, wg, wu, lg, lu, down):
    rows, units = gg.shape
    width, ranks = wg.shape[0], lg.shape[0]
    tile = tile_of(width, 512)
    weight = pl.BlockSpec((tile, units), lambda i: (i, 0))
    return pl.pallas_call(
        back_kernel,
        grid=(pl.cdiv(width, tile),),
        out_shape=[jax.ShapeDtypeStruct((rows, width), BF16), jax.ShapeDtypeStruct((rows, 2 * ranks), BF16)],
        in_specs=[resident(gg), resident(gu), weight, weight, resident(lg), resident(lu),
                  pl.BlockSpec((2 * ranks, tile), lambda i: (0, i))],
        out_specs=[pl.BlockSpec((rows, tile), lambda i: (0, i)),
                   pl.BlockSpec((rows, 2 * ranks), lambda i: (0, 0))],
        compiler_params=pltpu.CompilerParams(vmem_limit_bytes=60 * 2**20),
        cost_estimate=pl.CostEstimate(
            flops=4 * rows * width * units, bytes_accessed=4 * width * units + 4 * rows * units + 2 * rows * width,
            transcendentals=0),
    )(gg, gu, wg, wu, lg, lu, down)


def outward_kernel(seqs, *refs):
    hiddens, (wd_ref, do_ref, lift_out_ref, _, out_ref, inner_ref) = refs[:seqs], refs[seqs:]
    ranks = do_ref.shape[0] // seqs

    @pl.when(pl.program_id(0) == 0)
    def _():
        for s, hidden_ref in enumerate(hiddens):
            inner_ref[s] = dot(hidden_ref[...], do_ref[s * ranks : (s + 1) * ranks, :], NT).astype(BF16)

    for s, hidden_ref in enumerate(hiddens):
        out_ref[s] = (dot(hidden_ref[...], wd_ref[...])
                      + dot(inner_ref[s], lift_out_ref[s * ranks : (s + 1) * ranks, :])).astype(BF16)


def outward_call(hiddens, wd, do, lift_out, earlier):
    rows, units = hiddens[0].shape
    seqs = len(hiddens)
    width, ranks = wd.shape[1], do.shape[0] // seqs
    tile = tile_of(width, 512)
    return pl.pallas_call(
        functools.partial(outward_kernel, seqs),
        grid=(pl.cdiv(width, tile),),
        out_shape=[jax.ShapeDtypeStruct((seqs, rows, width), BF16), jax.ShapeDtypeStruct((seqs, rows, ranks), BF16)],
        in_specs=[resident(hidden) for hidden in hiddens]
        + [pl.BlockSpec((units, tile), lambda i: (0, i)), resident(do),
           pl.BlockSpec((seqs * ranks, tile), lambda i: (0, i)), pl.BlockSpec(memory_space=pl.ANY)],
        out_specs=[pl.BlockSpec((seqs, rows, tile), lambda i: (0, 0, i)),
                   pl.BlockSpec((seqs, rows, ranks), lambda i: (0, 0, 0))],
        compiler_params=pltpu.CompilerParams(vmem_limit_bytes=60 * 2**20),
        cost_estimate=pl.CostEstimate(
            flops=2 * seqs * rows * width * units,
            bytes_accessed=2 * width * units + 2 * seqs * rows * (units + width), transcendentals=0),
    )(*hiddens, wd, do, lift_out, earlier)


def pick_kernel(counts, ids_ref, *refs):
    tables, (stack_ref, wide_ref) = refs[: sum(counts)], refs[sum(counts) :]
    for i, table in enumerate(tables):
        if i < counts[0]:
            stack_ref[i, 0] = table[0]
        else:
            wide_ref[i - counts[0], 0] = table[0]


def pick(ids, narrow, wide):
    seqs, ranks = ids.shape[0], narrow[0].shape[1]
    counts = (len(narrow), len(wide))
    widths = (narrow[0].shape[2], wide[0].shape[2])
    tables = [pl.BlockSpec((1, ranks, table.shape[2]), lambda s, ids: (ids[s], 0, 0)) for table in narrow + wide]
    picked = pl.pallas_call(
        functools.partial(pick_kernel, counts),
        out_shape=[jax.ShapeDtypeStruct((count, seqs, ranks, width), BF16) for count, width in zip(counts, widths)],
        grid_spec=pltpu.PrefetchScalarGridSpec(
            num_scalar_prefetch=1,
            grid=(seqs,),
            in_specs=tables,
            out_specs=[pl.BlockSpec((count, 1, ranks, width), lambda s, ids: (0, s, 0, 0))
                       for count, width in zip(counts, widths)],
        ),
    )(ids, *narrow, *wide)
    return [part.reshape(-1, part.shape[-1]) for part in picked]


def gather_kernel(units, *refs):
    weights, wholes, staged, (send, recv, local) = refs[:4], refs[4:8], refs[8:12], refs[12:]
    group, replica = lax.axis_index("group"), lax.axis_index("replica")
    beside, above, across = group + 1 - 2 * (group % 2), (group + 2) % 4, 3 - group
    core, level = replica % 2, (replica // 2) % 2
    at_beside, at_above = (beside, replica), (above, replica)
    at_core, at_level = (group, replica + 1 - 2 * core), (group, replica + 2 - 4 * level)
    partners = (at_beside, at_above, at_core, at_level)
    mine, other = 2 * core + level, 2 * core + 1 - level

    barrier = pltpu.get_barrier_semaphore()
    for partner in partners:
        pl.semaphore_signal(barrier, inc=1, device_id=partner, device_id_type=pl.DeviceIdType.MESH)
    pl.semaphore_wait(barrier, 4)

    kept = [pltpu.make_async_copy(weight, stage, local.at[m])
            for m, (weight, stage) in enumerate(zip(weights, staged))]
    for one in kept:
        one.start()

    def keep(m):
        whole = wholes[m]
        rows, cols = weights[m].shape
        if m == 2:
            into = whole.at[pl.ds(pl.multiple_of(group * rows, rows), rows), :]
        else:
            into = whole.at[:, pl.ds(pl.multiple_of(group * cols, cols), cols)]
        kept[m].wait()
        kept[m] = pltpu.make_async_copy(staged[m], into, local.at[m])
        kept[m].start()

    def own(m, part, quarter):
        weight = weights[m]
        size = wholes[m].shape[0] // 4
        step = size // units
        if m < 2:
            return weight.at[pl.ds(pl.multiple_of(quarter * size + part * step, step), step), :]
        return weight.at[pl.ds(part * step, step), pl.ds(pl.multiple_of(quarter * size, size), size)]

    def piece(m, part, shard, quarter):
        whole = wholes[m]
        size = whole.shape[0] // 4
        step = size // units
        down, along = (quarter, shard) if m < 2 else (shard, quarter)
        return whole.at[pl.ds(pl.multiple_of(down * size + part * step, step), step),
                        pl.ds(pl.multiple_of(along * size, size), size)]

    def copy(src, dst, k, slot, partner):
        made = pltpu.make_async_remote_copy(
            src_ref=src, dst_ref=dst, send_sem=send.at[k, slot], recv_sem=recv.at[k, slot], device_id=partner,
            device_id_type=pl.DeviceIdType.MESH)
        made.start()
        return made

    def forward(m, part, shard, quarter, k, slot, partner):
        where = piece(m, part, shard, quarter)
        return copy(where, where, k, slot, partner)

    ranks, cols = weights[3].shape
    last = 3 * units

    def stack_piece(first, count, shard):
        return wholes[3].at[pl.ds(first, count), pl.ds(pl.multiple_of(shard * cols, cols), cols)]

    stack_beside = copy(weights[3], stack_piece(0, ranks, group), last, 0, at_beside)
    stack_above = copy(weights[3], stack_piece(0, ranks, group), last, 1, at_above)

    steps = [(m, part) for m in range(3) for part in range(units)]
    made = {}

    def begin(k):
        m, part = steps[k]
        made[k, 0] = copy(own(m, part, mine), piece(m, part, group, mine), k, 0, at_above)
        made[k, 2] = copy(own(m, part, mine), piece(m, part, group, mine), k, 2, at_beside)
        made[k, 1] = copy(own(m, part, other), piece(m, part, group, other), k, 1, at_above)

    begin(0)
    begin(1)
    for m in range(4):
        keep(m)
    stack_beside.wait_recv()
    stack_above.wait_recv()
    half = ranks // 2
    lower = stack_piece(0, half, above)
    upper = stack_piece(half, half, beside)
    stack_lower = copy(lower, lower, last, 2, at_beside)
    stack_upper = copy(upper, upper, last, 3, at_above)
    for t in range(len(steps) + 2):
        if t < len(steps):
            m, part = steps[t]
            made[t, 0].wait_recv()
            made[t, 4] = forward(m, part, above, mine, t, 4, at_beside)
            made[t, 6] = forward(m, part, above, mine, t, 6, at_core)
            made[t, 2].wait_recv()
            made[t, 3] = forward(m, part, beside, mine, t, 3, at_level)
            made[t, 8] = forward(m, part, beside, mine, t, 8, at_core)
            if t + 2 < len(steps):
                begin(t + 2)
            made[t, 1].wait_recv()
            made[t, 7] = forward(m, part, above, other, t, 7, at_core)
        if 1 <= t <= len(steps):
            m, part = steps[t - 1]
            made[t - 1, 4].wait_recv()
            made[t - 1, 5] = forward(m, part, across, mine, t - 1, 5, at_level)
            made[t - 1, 10] = forward(m, part, across, mine, t - 1, 10, at_core)
            made[t - 1, 3].wait_recv()
            made[t - 1, 9] = forward(m, part, beside, other, t - 1, 9, at_core)
        if 2 <= t:
            m, part = steps[t - 2]
            made[t - 2, 5].wait_recv()
            made[t - 2, 11] = forward(m, part, across, other, t - 2, 11, at_core)
    for k in range(len(steps)):
        for slot in range(6, 12):
            made[k, slot].wait_recv()
    for k in range(len(steps)):
        for slot in range(12):
            made[k, slot].wait_send()
    for one in (stack_lower, stack_upper):
        one.wait_recv()
    for one in (stack_beside, stack_above, stack_lower, stack_upper):
        one.wait_send()
    for one in kept:
        one.wait()


def gather_weights(w_branch, w_input, w_mixer, stack):
    width = w_branch.shape[0]
    if lax.axis_size("group") != 4 or lax.axis_size("replica") % 4 != 0:
        return (lax.all_gather(w_branch, "group", axis=1, tiled=True),
                lax.all_gather(w_input, "group", axis=1, tiled=True),
                lax.all_gather(w_mixer, "group", axis=0, tiled=True),
                lax.all_gather(stack, "group", axis=1, tiled=True))
    units = 4
    anywhere = pl.BlockSpec(memory_space=pl.ANY)
    operands = (w_branch, w_input, w_mixer, stack)
    return pl.pallas_call(
        functools.partial(gather_kernel, units),
        out_shape=[jax.ShapeDtypeStruct((width, width), BF16)] * 3
        + [jax.ShapeDtypeStruct((stack.shape[0], width), BF16)],
        in_specs=[anywhere] * 4,
        out_specs=[anywhere] * 4,
        scratch_shapes=[pltpu.VMEM(operand.shape, BF16) for operand in operands]
        + [pltpu.SemaphoreType.DMA((3 * units + 1, 12)), pltpu.SemaphoreType.DMA((3 * units + 1, 12)),
           pltpu.SemaphoreType.DMA((4,))],
        compiler_params=pltpu.CompilerParams(
            collective_id=0, has_side_effects=True, vmem_limit_bytes=32 * 2**20),
        cost_estimate=pl.CostEstimate(flops=0, bytes_accessed=400 * 2**20, transcendentals=0),
    )(*operands)


def ordered_kernel(value_ref, *refs):
    refs[-1][...] = value_ref[...]


def ordered(value, *earlier):
    flat = value.reshape(-1, value.shape[-1])
    tile = pl.BlockSpec((flat.shape[0] // 2, flat.shape[1]), lambda i: (i, 0))
    return pl.pallas_call(
        ordered_kernel,
        grid=(2,),
        out_shape=jax.ShapeDtypeStruct(flat.shape, flat.dtype),
        in_specs=[tile] + [pl.BlockSpec(memory_space=pl.ANY)] * len(earlier),
        out_specs=tile,
    )(flat, *earlier).reshape(value.shape)


def finish_kernel(resid_ref, outward_ref, grad_resid_ref, inputs_ref, gain_ref, grads_ref, block_ref, out_ref):
    block_ref[...] = (resid_ref[...] + outward_ref[...].astype(F32)).astype(BF16)
    values = inputs_ref[...].astype(F32)
    rate = lax.rsqrt(jnp.mean(values * values, axis=-1, keepdims=True) + EPS)
    out_ref[...] = grad_resid_ref[...] + norm_back(values, gain_ref[...], rate, grads_ref[...])


def finish(resid, outward, grad_resid, inputs, gain, grads):
    rows, width = resid.shape
    step = min(rows, 128)
    tile = pl.BlockSpec((step, width), lambda i: (i, 0))
    return pl.pallas_call(
        finish_kernel,
        grid=(rows // step,),
        out_shape=[jax.ShapeDtypeStruct((rows, width), BF16), jax.ShapeDtypeStruct((rows, width), F32)],
        in_specs=[tile, tile, tile, tile, pl.BlockSpec((1, width), lambda i: (0, 0)), tile],
        out_specs=[tile, tile],
        compiler_params=pltpu.CompilerParams(vmem_limit_bytes=40 * 2**20),
        cost_estimate=pl.CostEstimate(
            flops=20 * rows * width, bytes_accessed=22 * rows * width, transcendentals=rows),
    )(resid, outward, grad_resid, inputs, gain, grads)


def spread_kernel(tables, ids_ref, got_ref, *out_refs):
    replicas, seqs, ranks = got_ref.shape[0], ids_ref.shape[0] // got_ref.shape[0], out_refs[0].shape[1]
    for table in range(tables):
        out_refs[table][...] = jnp.zeros_like(out_refs[table])
    for replica in range(replicas):
        for s in range(seqs):
            place = ids_ref[replica * seqs + s]
            for table in range(tables):
                rows = pl.ds((table * seqs + s) * ranks, ranks)
                out_refs[table][place] += got_ref[replica, rows, :].astype(F32)


def spread(ids, got, tables, sets, seqs):
    replicas, rows, width = got.shape
    ranks = rows // (tables * seqs)
    return pl.pallas_call(
        functools.partial(spread_kernel, tables),
        out_shape=[jax.ShapeDtypeStruct((sets, ranks, width), F32)] * tables,
        in_specs=[pl.BlockSpec(memory_space=pltpu.SMEM), pl.BlockSpec(memory_space=pltpu.VMEM)],
        out_specs=[pl.BlockSpec(memory_space=pltpu.VMEM)] * tables,
        compiler_params=pltpu.CompilerParams(vmem_limit_bytes=56 * 2**20),
        cost_estimate=pl.CostEstimate(
            flops=replicas * rows * width,
            bytes_accessed=2 * replicas * rows * width + 4 * tables * sets * ranks * width, transcendentals=0),
    )(ids, got)


def passed_along(block, axis, distance):
    devices = range(lax.axis_size(axis))
    route = [(i - distance, i) for i in devices if i - distance in devices]
    return lax.ppermute(block, axis, route)


def over_replicas(value):
    count = lax.axis_size("replica")
    if count % 2:
        return lax.all_gather(value, "replica")
    got = lax.all_gather(value, "replica", axis_index_groups=[list(range(p, count, 2)) for p in range(2)])
    return jnp.concatenate([got, lax.ppermute(got, "replica", [(i, i ^ 1) for i in range(count)])], 0)


def body(
    inputs, segment_ids, adapter_ids, gain_mix, gain_mlp, w_branch, w_input, conv_taps, decay_heads, admit_heads,
    decay_param, w_mixer, w_gate, w_upper, w_down, down_branch, lift_branch, down_input, lift_input, down_decay,
    lift_decay, down_admit, lift_admit, down_mixer, lift_mixer, down_gate, lift_gate, down_upper, lift_upper,
    down_outward, lift_outward, out_grad,
):
    seqs, stretch, width = inputs.shape
    rows = seqs * stretch
    taps = conv_taps.shape[0]
    sets, _, ranks = down_branch.shape
    group, place = lax.axis_size("group"), lax.axis_index("group")
    mask_cols = seqs * ranks

    turned = lambda table: jnp.swapaxes(table, 1, 2)
    stack, own_tables = pick(
        adapter_ids,
        [turned(down_branch), turned(down_input), turned(down_decay), turned(down_admit), turned(down_mixer),
         turned(down_gate), turned(down_upper), lift_branch, lift_input, lift_decay, lift_admit, lift_mixer,
         lift_outward],
        [lift_gate, lift_upper, turned(down_outward)])
    full_branch, full_input, full_mixer, stack = gather_weights(w_branch, w_input, w_mixer, stack)
    (p_down_branch, p_down_input, p_down_decay, p_down_admit, p_down_mixer, p_down_gate, p_down_upper,
     p_lift_branch, p_lift_input, p_lift_decay, p_lift_admit, p_lift_mixer, p_lift_outward) = [
        stack[i * mask_cols : (i + 1) * mask_cols] for i in range(13)]
    own_lift_gate, own_lift_upper, own_down_outward = [
        own_tables[i * mask_cols : (i + 1) * mask_cols] for i in range(3)]
    all_ids = over_replicas(adapter_ids).reshape(-1)
    cotangents = lax.all_gather(ordered(out_grad, stack), "group", axis=1, tiled=True)

    row_seq = lax.broadcasted_iota(jnp.int32, (rows, mask_cols), 0) // stretch
    col_seq = lax.broadcasted_iota(jnp.int32, (rows, mask_cols), 1) // ranks
    own = (row_seq == col_seq).astype(F32)
    own_two = jnp.concatenate([own, own], 1)

    begin = place * stretch
    padded_ids = jnp.pad(segment_ids, ((0, 0), (taps - 1, taps - 1)), constant_values=-1)
    window = lax.dynamic_slice_in_dim(padded_ids, begin, stretch + 2 * (taps - 1), 1)
    current = window[:, taps - 1 : taps - 1 + stretch + taps - 1]
    agree = [
        ((current == window[:, taps - 1 - j : taps - 1 - j + stretch + taps - 1]) & (current >= 0)).astype(F32)
        for j in range(taps)
    ]
    restart = (1.0 - agree[1][:, :stretch]).reshape(rows, 1)

    x_float = inputs.reshape(rows, width).astype(F32)
    normed_f, _ = norm_rows(x_float, gain_mix)
    normed = normed_f.astype(BF16)
    inner_one = (dot(normed, stack[: 2 * mask_cols], NT) * own_two).astype(BF16)
    inner_branch, inner_input = inner_one[:, :mask_cols], inner_one[:, mask_cols:]
    branch_pre = dot(normed, full_branch) + dot(inner_branch, p_lift_branch)
    fed = (dot(normed, full_input) + dot(inner_input, p_lift_input)).astype(BF16)
    fed = fed.reshape(seqs, stretch, width)
    halo = passed_along(fed[:, stretch - (taps - 1) :], "group", 1)
    extended = jnp.concatenate([halo, fed], axis=1).astype(F32)
    convolved = sum(
        conv_taps[j] * agree[j][:, :stretch, None] * extended[:, taps - 1 - j : taps - 1 - j + stretch]
        for j in range(taps)
    ).reshape(rows, width)
    rounded = convolved.astype(BF16)
    softrate = jax.nn.softplus(decay_param).reshape(1, width)
    inner_gates = (dot(rounded, stack[2 * mask_cols : 4 * mask_cols], NT) * own_two).astype(BF16)
    lift_gates = stack[9 * mask_cols : 11 * mask_cols]
    cum, local = forward_gates(seqs, convolved, inner_gates, lift_gates, decay_heads, admit_heads, softrate, restart)
    ends = jnp.concatenate(
        [cum.reshape(seqs, stretch, width)[:, -1], local.reshape(seqs, stretch, width)[:, -1]], 0)
    all_ends = lax.all_gather(ends, "group")
    carried = jnp.zeros((seqs, width), F32)
    for g in range(group - 1):
        longer = all_ends[g, :seqs] * carried + all_ends[g, seqs:]
        carried = jnp.where(g < place, longer, carried)
    carried_rows = jnp.repeat(carried, stretch, axis=0)
    state = local + cum * carried_rows
    merged = (state * gelu(branch_pre)).astype(BF16)
    inner_mixer = (dot(merged, p_down_mixer, NT) * own).astype(BF16)
    mixed = dot(merged, full_mixer) + dot(inner_mixer, p_lift_mixer)
    resid = x_float + mixed
    normed_two_f, rate_two = norm_rows(resid, gain_mlp)
    normed_two = normed_two_f.astype(BF16).reshape(seqs, stretch, width)

    all_tokens, backs, hiddens, throughs = [], [], [], []
    grad_own_lift_gate, grad_own_lift_upper, grad_own_down_outward = [], [], []
    grad_down_gate, grad_down_upper, grad_lift_outward = [], [], []
    spans = [slice(s * ranks, (s + 1) * ranks) for s in range(seqs)]
    grad_hiddens = [
        grad_hidden_call(cotangents[s], w_down, p_lift_outward[at], own_down_outward[at])
        for s, at in enumerate(spans)]
    all_tokens = [lax.all_gather(normed_two[s], "group", axis=0, tiled=True) for s in range(seqs)]
    for s, at in enumerate(spans):
        tokens = all_tokens[s]
        grad_hidden, through_out = grad_hiddens[s]
        two_downs = jnp.concatenate([p_down_gate[at], p_down_upper[at]], 0)
        hidden, grad_gate, grad_upper, inner = hidden_call(
            tokens, grad_hidden, w_gate, w_upper, two_downs, own_lift_gate[at], own_lift_upper[at])
        back, through = back_call(
            grad_gate, grad_upper, w_gate, w_upper, own_lift_gate[at], own_lift_upper[at], two_downs)
        backs.append(lax.psum_scatter(back, "group", scatter_dimension=0, tiled=True))
        hiddens.append(hidden)
        grad_own_lift_gate.append(dot(inner[:, :ranks], grad_gate, TN))
        grad_own_lift_upper.append(dot(inner[:, ranks:], grad_upper, TN))
        grad_own_down_outward.append(dot(through_out, hidden, TN))
        grad_down_gate.append(dot(through[:, :ranks], tokens, TN))
        grad_down_upper.append(dot(through[:, ranks:], tokens, TN))
    outward, inner_out = outward_call(hiddens, w_down, own_down_outward, p_lift_outward, back)
    for s in range(seqs):
        grad_lift_outward.append(dot(inner_out[s], cotangents[s], TN))
    outward = lax.psum_scatter(outward, "group", scatter_dimension=1, tiled=True).reshape(rows, width)
    grad_normed_two = jnp.concatenate(backs, 0).astype(F32)
    grad_resid = out_grad.reshape(rows, width).astype(F32) + norm_back(resid, gain_mlp, rate_two, grad_normed_two)

    grad_mixed = grad_resid.astype(BF16)
    through_mixer = (dot(grad_mixed, p_lift_mixer, NT) * own).astype(BF16)
    grad_merged = dot(grad_mixed, full_mixer, NT) + dot(through_mixer, p_down_mixer)
    span, total, firsts, grad_branch_pre = backward_scan(
        seqs, convolved, inner_gates, lift_gates, decay_heads, softrate, restart, cum, local, carried, branch_pre,
        grad_merged)
    all_firsts = lax.all_gather(firsts, "group")
    incoming = jnp.zeros((seqs, width), F32)
    for lap in range(group - 1):
        g = group - 1 - lap
        longer = all_firsts[g, :seqs] * incoming + all_firsts[g, seqs:]
        incoming = jnp.where(g > place, longer, incoming)
    grad_direct, through_gates, grad_lift_gates = backward_gates(
        seqs, convolved, inner_gates, lift_gates, decay_heads, admit_heads, softrate, restart, cum, local, carried,
        span, total, incoming)
    through_gates = (through_gates * own_two).astype(BF16)
    grad_convolved = grad_direct + dot(through_gates, stack[2 * mask_cols : 4 * mask_cols])
    grad_convolved = grad_convolved.reshape(seqs, stretch, width)
    below = passed_along(grad_convolved[:, : taps - 1].astype(BF16), "group", -1).astype(F32)
    grad_extended = jnp.concatenate([grad_convolved, below], axis=1)
    grad_fed = sum(
        conv_taps[j] * agree[j][:, j : j + stretch, None] * grad_extended[:, j : j + stretch] for j in range(taps)
    ).astype(BF16).reshape(rows, width)
    through_branch = (dot(grad_branch_pre, p_lift_branch, NT) * own).astype(BF16)
    through_input = (dot(grad_fed, p_lift_input, NT) * own).astype(BF16)
    through_one = jnp.concatenate([through_branch, through_input], 1)
    grad_normed = (dot(grad_branch_pre, full_branch, NT) + dot(grad_fed, full_input, NT)
                   + dot(through_one, stack[: 2 * mask_cols]))
    block_out, grad_inputs = finish(
        resid, outward, grad_resid, inputs.reshape(rows, width), gain_mix.reshape(1, width), grad_normed)

    partial = jnp.concatenate(
        [dot(through_one, normed, TN), dot(through_gates, rounded, TN), dot(through_mixer, merged, TN),
         dot(inner_branch, grad_branch_pre, TN), dot(inner_input, grad_fed, TN), grad_lift_gates,
         dot(inner_mixer, grad_mixed, TN)] + grad_down_gate + grad_down_upper + grad_lift_outward, 0).astype(BF16)
    owned = lax.psum_scatter(partial, "group", scatter_dimension=1, tiled=True)
    wide = jnp.concatenate(grad_own_lift_gate + grad_own_lift_upper + grad_own_down_outward, 0).astype(BF16)
    wides = spread(all_ids, over_replicas(wide), 3, sets, seqs)
    totals = spread(all_ids, over_replicas(owned), 13, sets, seqs)
    (t_down_branch, t_down_input, t_down_decay, t_down_admit, t_down_mixer, t_lift_branch, t_lift_input, t_lift_decay,
     t_lift_admit, t_lift_mixer, t_down_gate, t_down_upper, t_lift_outward) = totals
    return (
        block_out.reshape(seqs, stretch, width), grad_inputs.reshape(seqs, stretch, width),
        turned(t_down_branch), t_lift_branch, turned(t_down_input), t_lift_input, turned(t_down_decay), t_lift_decay,
        turned(t_down_admit), t_lift_admit, turned(t_down_mixer), t_lift_mixer, turned(t_down_gate), wides[0],
        turned(t_down_upper), wides[1], turned(wides[2]), t_lift_outward,
    )


def solution(mesh):
    tokens = P("replica", "group", None)
    down, lift = P(None, "group", None), P(None, None, "group")
    cols, split = P(None, "group"), P("group", None)
    in_specs = (
        tokens, P("replica", None), P("replica"), P(), P(), cols, cols, P(), P(), P(), P(), split, cols, cols, split,
    ) + (down, lift) * 8 + (tokens,)
    out_specs = (tokens, tokens) + (down, lift) * 8
    return jax.shard_map(body, mesh=mesh, in_specs=in_specs, out_specs=out_specs, check_vma=False)
```

```python
import functools

import jax
import jax.numpy as jnp
from jax import lax
from jax.experimental import pallas as pl
from jax.experimental.pallas import tpu as pltpu
from jax.sharding import PartitionSpec as P

EPS = 1e-06
F32 = jnp.float32
BF16 = jnp.bfloat16
GELU_C = 0.7978845608028654
GELU_A = 0.044715
NT = (((1,), (1,)), ((), ()))
NN = (((1,), (0,)), ((), ()))
TN = (((0,), (0,)), ((), ()))
ANYWHERE = pl.BlockSpec(memory_space=pl.ANY)


def dot(a, b, dims=NN):
    return lax.dot_general(a, b, dims, preferred_element_type=F32)


def gelu(v):
    return 0.5 * v * (1.0 + jnp.tanh(GELU_C * (v + GELU_A * v * v * v)))


def gelu_both(v):
    th = jnp.tanh(GELU_C * (v + GELU_A * v * v * v))
    value = 0.5 * v * (1.0 + th)
    slope = 0.5 * (1.0 + th) + 0.5 * v * (1.0 - th * th) * GELU_C * (1.0 + 3.0 * GELU_A * v * v)
    return value, slope


def norm_rows(values, gain):
    rate = lax.rsqrt(jnp.mean(values * values, axis=-1, keepdims=True) + EPS)
    return values * rate * gain, rate


def norm_back(values, gain, rate, grads):
    scaled = grads * gain
    along = jnp.mean(scaled * values, axis=-1, keepdims=True)
    return rate * scaled - values * (rate * rate * rate * along)


def rows_shifted(values, by, fill):
    rows, width = values.shape
    if by % 8 == 0:
        return jnp.concatenate([jnp.full((by, width), fill, values.dtype), values[: rows - by]], 0)
    place = lax.broadcasted_iota(jnp.int32, values.shape, 0)
    return jnp.where(place >= by, pltpu.roll(values, by, 0), fill)


def rows_advanced(values, by, fill):
    rows, width = values.shape
    if by % 8 == 0:
        return jnp.concatenate([values[by:], jnp.full((by, width), fill, values.dtype)], 0)
    place = lax.broadcasted_iota(jnp.int32, values.shape, 0)
    return jnp.where(place < rows - by, pltpu.roll(values, rows - by, 0), fill)


def scan_rows(a, b, moved):
    by = 1
    while by < a.shape[0]:
        b = a * moved(b, by, 0.0) + b
        a = a * moved(a, by, 1.0)
        by *= 2
    return a, b


def gate_values(conv, inner, lift, table_d, table_a, softrate, restart):
    rounded = conv.astype(BF16)
    half = lift.shape[0] // 2
    pre_d = dot(rounded, table_d) + dot(inner[:, :half], lift[:half])
    pre_a = dot(rounded, table_a) + dot(inner[:, half:], lift[half:])
    decay_gate = 1.0 / (1.0 + jnp.exp(-pre_d))
    admit_gate = 1.0 / (1.0 + jnp.exp(-pre_a))
    safe = jnp.where(restart, -1.0, -8.0 * decay_gate * softrate)
    grown = jnp.exp(safe)
    scale = jnp.sqrt(jnp.tanh(-safe) * (1.0 + grown * grown))
    return decay_gate, admit_gate, grown, scale


def forward_gates_kernel(seqs, conv_ref, inner_ref, lift_ref, table_d_ref, table_a_ref, soft_ref, restart_ref,
                         cum_ref, local_ref):
    stretch = conv_ref.shape[0] // seqs
    for s in range(seqs):
        rows = pl.ds(s * stretch, stretch)
        conv = conv_ref[rows, :]
        restart = restart_ref[rows, :] > 0.5
        _, admit, grown, scale = gate_values(
            conv, inner_ref[rows, :], lift_ref[...], table_d_ref[0], table_a_ref[0], soft_ref[...], restart)
        decays = jnp.where(restart, 0.0, grown)
        drive = conv * admit * jnp.where(restart, 1.0, scale)
        cum, local = scan_rows(decays, drive, rows_shifted)
        cum_ref[rows, :] = cum
        local_ref[rows, :] = local


def forward_gates(seqs, conv, inner, lift, table_d, table_a, softrate, restart):
    rows, width = conv.shape
    heads, size = table_d.shape[:2]
    tile = pl.BlockSpec((rows, size), lambda h: (0, h))
    table = pl.BlockSpec((1, size, size), lambda h: (h, 0, 0))
    out = jax.ShapeDtypeStruct((rows, width), F32)
    return pl.pallas_call(
        functools.partial(forward_gates_kernel, seqs),
        out_shape=(out, out),
        grid=(heads,),
        in_specs=[
            tile,
            pl.BlockSpec(inner.shape, lambda h: (0, 0)),
            pl.BlockSpec((lift.shape[0], size), lambda h: (0, h)),
            table,
            table,
            pl.BlockSpec((1, size), lambda h: (0, h)),
            pl.BlockSpec(restart.shape, lambda h: (0, 0)),
        ],
        out_specs=(tile, tile),
        compiler_params=pltpu.CompilerParams(vmem_limit_bytes=40 * 2**20),
        cost_estimate=pl.CostEstimate(
            flops=4 * rows * width * size + 60 * rows * width,
            bytes_accessed=12 * rows * width,
            transcendentals=6 * rows * width),
    )(conv, inner, lift, table_d, table_a, softrate, restart)


def backward_scan_kernel(seqs, conv_ref, inner_ref, lift_ref, table_d_ref, soft_ref, restart_ref, cum_ref, local_ref,
                         carried_ref, pre_ref, grad_ref, span_ref, total_ref, first_ref, branch_grad_ref):
    stretch = conv_ref.shape[0] // seqs
    half = lift_ref.shape[0] // 2
    for s in range(seqs):
        rows = pl.ds(s * stretch, stretch)
        restart = restart_ref[rows, :] > 0.5
        rounded = conv_ref[rows, :].astype(BF16)
        pre_d = dot(rounded, table_d_ref[0]) + dot(inner_ref[rows, :half], lift_ref[:half, :])
        grown = jnp.exp(-8.0 * soft_ref[...] / (1.0 + jnp.exp(-pre_d)))
        decays = jnp.where(restart, 0.0, grown)
        state = local_ref[rows, :] + cum_ref[rows, :] * carried_ref[s : s + 1, :]
        value, slope = gelu_both(pre_ref[rows, :])
        grads = grad_ref[rows, :]
        branch_grad_ref[rows, :] = (grads * state * slope).astype(BF16)
        span, total = scan_rows(rows_advanced(decays, 1, 1.0), grads * value, rows_advanced)
        span_ref[rows, :] = span
        total_ref[rows, :] = total
        first_ref[s : s + 1, :] = decays[:1] * span[:1]
        first_ref[seqs + s : seqs + s + 1, :] = decays[:1] * total[:1]


def backward_scan(seqs, conv, inner, lift, table_d, softrate, restart, cum, local, carried, pre, grads):
    rows, width = conv.shape
    heads, size = table_d.shape[:2]
    tile = pl.BlockSpec((rows, size), lambda h: (0, h))
    table = pl.BlockSpec((1, size, size), lambda h: (h, 0, 0))
    out = jax.ShapeDtypeStruct((rows, width), F32)
    return pl.pallas_call(
        functools.partial(backward_scan_kernel, seqs),
        out_shape=(out, out, jax.ShapeDtypeStruct((2 * seqs, width), F32), jax.ShapeDtypeStruct((rows, width), BF16)),
        grid=(heads,),
        in_specs=[
            tile,
            pl.BlockSpec(inner.shape, lambda h: (0, 0)),
            pl.BlockSpec((lift.shape[0], size), lambda h: (0, h)),
            table,
            pl.BlockSpec((1, size), lambda h: (0, h)),
            pl.BlockSpec(restart.shape, lambda h: (0, 0)),
            tile,
            tile,
            pl.BlockSpec((seqs, size), lambda h: (0, h)),
            tile,
            tile,
        ],
        out_specs=(tile, tile, pl.BlockSpec((2 * seqs, size), lambda h: (0, h)), tile),
        compiler_params=pltpu.CompilerParams(vmem_limit_bytes=48 * 2**20),
        cost_estimate=pl.CostEstimate(
            flops=2 * rows * width * size + 80 * rows * width,
            bytes_accessed=30 * rows * width,
            transcendentals=4 * rows * width),
    )(conv, inner, lift, table_d, softrate, restart, cum, local, carried, pre, grads)


def backward_gates_kernel(seqs, conv_ref, inner_ref, lift_ref, table_d_ref, table_a_ref, soft_ref, restart_ref,
                          cum_ref, local_ref, carried_ref, span_ref, total_ref, incoming_ref,
                          conv_grad_ref, through_ref, lift_grad_ref):
    stretch = conv_ref.shape[0] // seqs
    half = lift_ref.shape[0] // 2

    @pl.when(pl.program_id(0) == 0)
    def _():
        through_ref[...] = jnp.zeros_like(through_ref)

    for s in range(seqs):
        rows = pl.ds(s * stretch, stretch)
        conv = conv_ref[rows, :]
        inner = inner_ref[rows, :]
        restart = restart_ref[rows, :] > 0.5
        softrate = soft_ref[...]
        decay_gate, admit, grown, scale = gate_values(
            conv, inner, lift_ref[...], table_d_ref[0], table_a_ref[0], softrate, restart)
        carried = carried_ref[s : s + 1, :]
        state = local_ref[rows, :] + cum_ref[rows, :] * carried
        place = lax.broadcasted_iota(jnp.int32, state.shape, 0)
        before = jnp.where(place >= 1, pltpu.roll(state, 1, 0), carried)
        grads = total_ref[rows, :] + span_ref[rows, :] * incoming_ref[s : s + 1, :]
        driven = grads * jnp.where(restart, 1.0, scale)
        grad_log = jnp.where(
            restart, 0.0, grads * (before * grown - conv * admit * grown * grown / scale))
        grad_d = (-8.0 * softrate) * grad_log * decay_gate * (1.0 - decay_gate)
        grad_a = driven * conv * admit * (1.0 - admit)
        low_d, low_a = grad_d.astype(BF16), grad_a.astype(BF16)
        conv_grad_ref[rows, :] = driven * admit + dot(low_d, table_d_ref[0], NT) + dot(low_a, table_a_ref[0], NT)
        through_ref[rows, :half] += dot(low_d, lift_ref[:half, :], NT)
        through_ref[rows, half:] += dot(low_a, lift_ref[half:, :], NT)
        first = dot(inner[:, :half], low_d, TN)
        second = dot(inner[:, half:], low_a, TN)
        if s == 0:
            lift_grad_ref[:half, :] = first
            lift_grad_ref[half:, :] = second
        else:
            lift_grad_ref[:half, :] += first
            lift_grad_ref[half:, :] += second


def backward_gates(seqs, conv, inner, lift, table_d, table_a, softrate, restart, cum, local, carried, span, total,
                   incoming):
    rows, width = conv.shape
    heads, size = table_d.shape[:2]
    tile = pl.BlockSpec((rows, size), lambda h: (0, h))
    table = pl.BlockSpec((1, size, size), lambda h: (h, 0, 0))
    edge = pl.BlockSpec((seqs, size), lambda h: (0, h))
    ranks = pl.BlockSpec((lift.shape[0], size), lambda h: (0, h))
    return pl.pallas_call(
        functools.partial(backward_gates_kernel, seqs),
        out_shape=(
            jax.ShapeDtypeStruct((rows, width), F32),
            jax.ShapeDtypeStruct(inner.shape, F32),
            jax.ShapeDtypeStruct(lift.shape, F32),
        ),
        grid=(heads,),
        in_specs=[
            tile,
            pl.BlockSpec(inner.shape, lambda h: (0, 0)),
            ranks,
            table,
            table,
            pl.BlockSpec((1, size), lambda h: (0, h)),
            pl.BlockSpec(restart.shape, lambda h: (0, 0)),
            tile,
            tile,
            edge,
            tile,
            tile,
            edge,
        ],
        out_specs=(tile, pl.BlockSpec(inner.shape, lambda h: (0, 0)), ranks),
        compiler_params=pltpu.CompilerParams(vmem_limit_bytes=48 * 2**20),
        cost_estimate=pl.CostEstimate(
            flops=8 * rows * width * size + 80 * rows * width,
            bytes_accessed=24 * rows * width,
            transcendentals=6 * rows * width),
    )(conv, inner, lift, table_d, table_a, softrate, restart, cum, local, carried, span, total, incoming)


def resident(array):
    return pl.BlockSpec(array.shape, lambda i: (0, 0), pipeline_mode=pl.Buffered(1))


def tile_of(count, tile):
    return tile if count % 128 == 0 and count > tile else count


def grad_hidden_kernel(cot_ref, wd_ref, lift_out_ref, do_ref, out_ref, through_ref):
    @pl.when(pl.program_id(0) == 0)
    def _():
        through_ref[...] = dot(cot_ref[...], lift_out_ref[...], NT).astype(BF16)

    out_ref[...] = (dot(cot_ref[...], wd_ref[...], NT) + dot(through_ref[...], do_ref[...])).astype(BF16)


def grad_hidden_call(cot, s, wd, lift_out, do):
    rows, width = cot.shape[1:]
    units, ranks = wd.shape[0], do.shape[0]
    tile = tile_of(units, 512)
    return pl.pallas_call(
        grad_hidden_kernel,
        grid=(pl.cdiv(units, tile),),
        out_shape=[jax.ShapeDtypeStruct((rows, units), BF16), jax.ShapeDtypeStruct((rows, ranks), BF16)],
        in_specs=[pl.BlockSpec((None, rows, width), lambda i: (s, 0, 0), pipeline_mode=pl.Buffered(1)),
                  pl.BlockSpec((tile, width), lambda i: (i, 0)), resident(lift_out),
                  pl.BlockSpec((ranks, tile), lambda i: (0, i))],
        out_specs=[pl.BlockSpec((rows, tile), lambda i: (0, i)), pl.BlockSpec((rows, ranks), lambda i: (0, 0))],
        compiler_params=pltpu.CompilerParams(vmem_limit_bytes=60 * 2**20),
        cost_estimate=pl.CostEstimate(
            flops=2 * rows * width * units, bytes_accessed=2 * width * units + 2 * rows * (units + width),
            transcendentals=0),
    )(cot, wd, lift_out, do)


def hidden_kernel(tok_ref, gh_ref, wg_ref, wu_ref, down_ref, lg_ref, lu_ref, *refs):
    hidden_ref, gg_ref, gu_ref, inner_ref = refs[-4:]
    ranks = lg_ref.shape[0]

    @pl.when(pl.program_id(0) == 0)
    def _():
        inner_ref[...] = dot(tok_ref[...], down_ref[...], NT).astype(BF16)

    tokens, inner = tok_ref[...], inner_ref[...]
    gate = dot(tokens, wg_ref[...]) + dot(inner[:, :ranks], lg_ref[...])
    upper = dot(tokens, wu_ref[...]) + dot(inner[:, ranks:], lu_ref[...])
    grad_hidden = gh_ref[...].astype(F32)
    value, slope = gelu_both(gate)
    hidden_ref[...] = (value * upper).astype(BF16)
    gg_ref[...] = (grad_hidden * upper * slope).astype(BF16)
    gu_ref[...] = (grad_hidden * value).astype(BF16)


def hidden_call(tok, gh, wg, wu, down, lg, lu, earlier):
    rows, width = tok.shape
    units, ranks = wg.shape[1], lg.shape[0]
    tile = tile_of(units, 512)
    cols = pl.BlockSpec((width, tile), lambda i: (0, i))
    rank = pl.BlockSpec((ranks, tile), lambda i: (0, i))
    out = pl.BlockSpec((rows, tile), lambda i: (0, i))
    wide = jax.ShapeDtypeStruct((rows, units), BF16)
    return pl.pallas_call(
        hidden_kernel,
        grid=(pl.cdiv(units, tile),),
        out_shape=[wide, wide, wide, jax.ShapeDtypeStruct((rows, 2 * ranks), BF16)],
        in_specs=[resident(tok), out, cols, cols, resident(down), rank, rank] + [ANYWHERE] * len(earlier),
        out_specs=[out, out, out, pl.BlockSpec((rows, 2 * ranks), lambda i: (0, 0))],
        compiler_params=pltpu.CompilerParams(vmem_limit_bytes=60 * 2**20),
        cost_estimate=pl.CostEstimate(
            flops=4 * rows * width * units, bytes_accessed=4 * width * units + 10 * rows * units,
            transcendentals=rows * units),
    )(tok, gh, wg, wu, down, lg, lu, *earlier)


def back_kernel(gg_ref, gu_ref, wg_ref, wu_ref, lg_ref, lu_ref, down_ref, back_ref, through_ref):
    ranks = lg_ref.shape[0]

    @pl.when(pl.program_id(0) == 0)
    def _():
        through_ref[:, :ranks] = dot(gg_ref[...], lg_ref[...], NT).astype(BF16)
        through_ref[:, ranks:] = dot(gu_ref[...], lu_ref[...], NT).astype(BF16)

    back_ref[...] = (dot(gg_ref[...], wg_ref[...], NT) + dot(gu_ref[...], wu_ref[...], NT)
                     + dot(through_ref[...], down_ref[...])).astype(BF16)


def back_call(gg, gu, wg, wu, lg, lu, down):
    rows, units = gg.shape
    width, ranks = wg.shape[0], lg.shape[0]
    tile = tile_of(width, 512)
    weight = pl.BlockSpec((tile, units), lambda i: (i, 0))
    return pl.pallas_call(
        back_kernel,
        grid=(pl.cdiv(width, tile),),
        out_shape=[jax.ShapeDtypeStruct((rows, width), BF16), jax.ShapeDtypeStruct((rows, 2 * ranks), BF16)],
        in_specs=[resident(gg), resident(gu), weight, weight, resident(lg), resident(lu),
                  pl.BlockSpec((2 * ranks, tile), lambda i: (0, i))],
        out_specs=[pl.BlockSpec((rows, tile), lambda i: (0, i)),
                   pl.BlockSpec((rows, 2 * ranks), lambda i: (0, 0))],
        compiler_params=pltpu.CompilerParams(vmem_limit_bytes=60 * 2**20),
        cost_estimate=pl.CostEstimate(
            flops=4 * rows * width * units, bytes_accessed=4 * width * units + 4 * rows * units + 2 * rows * width,
            transcendentals=0),
    )(gg, gu, wg, wu, lg, lu, down)


def outward_kernel(seqs, *refs):
    hiddens, (wd_ref, do_ref, lift_out_ref, _, out_ref, inner_ref) = refs[:seqs], refs[seqs:]
    ranks = do_ref.shape[0] // seqs

    @pl.when(pl.program_id(0) == 0)
    def _():
        for s, hidden_ref in enumerate(hiddens):
            inner_ref[s] = dot(hidden_ref[...], do_ref[s * ranks : (s + 1) * ranks, :], NT).astype(BF16)

    for s, hidden_ref in enumerate(hiddens):
        out_ref[s] = (dot(hidden_ref[...], wd_ref[...])
                      + dot(inner_ref[s], lift_out_ref[s * ranks : (s + 1) * ranks, :])).astype(BF16)


def outward_call(hiddens, wd, do, lift_out, earlier):
    rows, units = hiddens[0].shape
    seqs = len(hiddens)
    width, ranks = wd.shape[1], do.shape[0] // seqs
    tile = tile_of(width, 512)
    return pl.pallas_call(
        functools.partial(outward_kernel, seqs),
        grid=(pl.cdiv(width, tile),),
        out_shape=[jax.ShapeDtypeStruct((seqs, rows, width), BF16), jax.ShapeDtypeStruct((seqs, rows, ranks), BF16)],
        in_specs=[resident(hidden) for hidden in hiddens]
        + [pl.BlockSpec((units, tile), lambda i: (0, i)), resident(do),
           pl.BlockSpec((seqs * ranks, tile), lambda i: (0, i)), pl.BlockSpec(memory_space=pl.ANY)],
        out_specs=[pl.BlockSpec((seqs, rows, tile), lambda i: (0, 0, i)),
                   pl.BlockSpec((seqs, rows, ranks), lambda i: (0, 0, 0))],
        compiler_params=pltpu.CompilerParams(vmem_limit_bytes=60 * 2**20),
        cost_estimate=pl.CostEstimate(
            flops=2 * seqs * rows * width * units,
            bytes_accessed=2 * width * units + 2 * seqs * rows * (units + width), transcendentals=0),
    )(*hiddens, wd, do, lift_out, earlier)


def pick_kernel(counts, ids_ref, *refs):
    tables, (stack_ref, wide_ref) = refs[: sum(counts)], refs[sum(counts) :]
    for i, table in enumerate(tables):
        if i < counts[0]:
            stack_ref[i, 0] = table[0]
        else:
            wide_ref[i - counts[0], 0] = table[0]


def pick(ids, narrow, wide):
    seqs, ranks = ids.shape[0], narrow[0].shape[1]
    counts = (len(narrow), len(wide))
    widths = (narrow[0].shape[2], wide[0].shape[2])
    tables = [pl.BlockSpec((1, ranks, table.shape[2]), lambda s, ids: (ids[s], 0, 0)) for table in narrow + wide]
    picked = pl.pallas_call(
        functools.partial(pick_kernel, counts),
        out_shape=[jax.ShapeDtypeStruct((count, seqs, ranks, width), BF16) for count, width in zip(counts, widths)],
        grid_spec=pltpu.PrefetchScalarGridSpec(
            num_scalar_prefetch=1,
            grid=(seqs,),
            in_specs=tables,
            out_specs=[pl.BlockSpec((count, 1, ranks, width), lambda s, ids: (0, s, 0, 0))
                       for count, width in zip(counts, widths)],
        ),
    )(ids, *narrow, *wide)
    return [part.reshape(-1, part.shape[-1]) for part in picked]


def gather_kernel(units, *refs):
    weights, wholes, staged, (send, recv, local) = refs[:4], refs[4:8], refs[8:12], refs[12:]
    group, replica = lax.axis_index("group"), lax.axis_index("replica")
    beside, above, across = group + 1 - 2 * (group % 2), (group + 2) % 4, 3 - group
    core, level = replica % 2, (replica // 2) % 2
    at_beside, at_above = (beside, replica), (above, replica)
    at_core, at_level = (group, replica + 1 - 2 * core), (group, replica + 2 - 4 * level)
    partners = (at_beside, at_above, at_core, at_level)
    mine, other = 2 * core + level, 2 * core + 1 - level

    barrier = pltpu.get_barrier_semaphore()
    for partner in partners:
        pl.semaphore_signal(barrier, inc=1, device_id=partner, device_id_type=pl.DeviceIdType.MESH)
    pl.semaphore_wait(barrier, 4)

    kept = [pltpu.make_async_copy(weight, stage, local.at[m])
            for m, (weight, stage) in enumerate(zip(weights, staged))]
    for one in kept:
        one.start()

    def keep(m):
        whole = wholes[m]
        rows, cols = weights[m].shape
        if m == 2:
            into = whole.at[pl.ds(pl.multiple_of(group * rows, rows), rows), :]
        else:
            into = whole.at[:, pl.ds(pl.multiple_of(group * cols, cols), cols)]
        kept[m].wait()
        kept[m] = pltpu.make_async_copy(staged[m], into, local.at[m])
        kept[m].start()

    def own(m, part, quarter):
        weight = weights[m]
        size = wholes[m].shape[0] // 4
        step = size // units
        if m < 2:
            return weight.at[pl.ds(pl.multiple_of(quarter * size + part * step, step), step), :]
        return weight.at[pl.ds(part * step, step), pl.ds(pl.multiple_of(quarter * size, size), size)]

    def piece(m, part, shard, quarter):
        whole = wholes[m]
        size = whole.shape[0] // 4
        step = size // units
        down, along = (quarter, shard) if m < 2 else (shard, quarter)
        return whole.at[pl.ds(pl.multiple_of(down * size + part * step, step), step),
                        pl.ds(pl.multiple_of(along * size, size), size)]

    def copy(src, dst, k, slot, partner):
        made = pltpu.make_async_remote_copy(
            src_ref=src, dst_ref=dst, send_sem=send.at[k, slot], recv_sem=recv.at[k, slot], device_id=partner,
            device_id_type=pl.DeviceIdType.MESH)
        made.start()
        return made

    def forward(m, part, shard, quarter, k, slot, partner):
        where = piece(m, part, shard, quarter)
        return copy(where, where, k, slot, partner)

    ranks, cols = weights[3].shape
    last = 3 * units

    def stack_piece(first, count, shard):
        return wholes[3].at[pl.ds(first, count), pl.ds(pl.multiple_of(shard * cols, cols), cols)]

    stack_beside = copy(weights[3], stack_piece(0, ranks, group), last, 0, at_beside)
    stack_above = copy(weights[3], stack_piece(0, ranks, group), last, 1, at_above)

    steps = [(m, part) for m in range(3) for part in range(units)]
    made = {}

    def begin(k):
        m, part = steps[k]
        made[k, 0] = copy(own(m, part, mine), piece(m, part, group, mine), k, 0, at_above)
        made[k, 2] = copy(own(m, part, mine), piece(m, part, group, mine), k, 2, at_beside)
        made[k, 1] = copy(own(m, part, other), piece(m, part, group, other), k, 1, at_above)

    begin(0)
    begin(1)
    for m in range(4):
        keep(m)
    stack_beside.wait_recv()
    stack_above.wait_recv()
    half = ranks // 2
    lower = stack_piece(0, half, above)
    upper = stack_piece(half, half, beside)
    stack_lower = copy(lower, lower, last, 2, at_beside)
    stack_upper = copy(upper, upper, last, 3, at_above)
    for t in range(len(steps) + 2):
        if t < len(steps):
            m, part = steps[t]
            made[t, 0].wait_recv()
            made[t, 4] = forward(m, part, above, mine, t, 4, at_beside)
            made[t, 6] = forward(m, part, above, mine, t, 6, at_core)
            made[t, 2].wait_recv()
            made[t, 3] = forward(m, part, beside, mine, t, 3, at_level)
            made[t, 8] = forward(m, part, beside, mine, t, 8, at_core)
            if t + 2 < len(steps):
                begin(t + 2)
            made[t, 1].wait_recv()
            made[t, 7] = forward(m, part, above, other, t, 7, at_core)
        if 1 <= t <= len(steps):
            m, part = steps[t - 1]
            made[t - 1, 4].wait_recv()
            made[t - 1, 5] = forward(m, part, across, mine, t - 1, 5, at_level)
            made[t - 1, 10] = forward(m, part, across, mine, t - 1, 10, at_core)
            made[t - 1, 3].wait_recv()
            made[t - 1, 9] = forward(m, part, beside, other, t - 1, 9, at_core)
        if 2 <= t:
            m, part = steps[t - 2]
            made[t - 2, 5].wait_recv()
            made[t - 2, 11] = forward(m, part, across, other, t - 2, 11, at_core)
    for k in range(len(steps)):
        for slot in range(6, 12):
            made[k, slot].wait_recv()
    for k in range(len(steps)):
        for slot in range(12):
            made[k, slot].wait_send()
    for one in (stack_lower, stack_upper):
        one.wait_recv()
    for one in (stack_beside, stack_above, stack_lower, stack_upper):
        one.wait_send()
    for one in kept:
        one.wait()


def gather_weights(w_branch, w_input, w_mixer, stack):
    width = w_branch.shape[0]
    if lax.axis_size("group") != 4 or lax.axis_size("replica") % 4 != 0:
        return (lax.all_gather(w_branch, "group", axis=1, tiled=True),
                lax.all_gather(w_input, "group", axis=1, tiled=True),
                lax.all_gather(w_mixer, "group", axis=0, tiled=True),
                lax.all_gather(stack, "group", axis=1, tiled=True))
    units = 4
    anywhere = pl.BlockSpec(memory_space=pl.ANY)
    operands = (w_branch, w_input, w_mixer, stack)
    return pl.pallas_call(
        functools.partial(gather_kernel, units),
        out_shape=[jax.ShapeDtypeStruct((width, width), BF16)] * 3
        + [jax.ShapeDtypeStruct((stack.shape[0], width), BF16)],
        in_specs=[anywhere] * 4,
        out_specs=[anywhere] * 4,
        scratch_shapes=[pltpu.VMEM(operand.shape, BF16) for operand in operands]
        + [pltpu.SemaphoreType.DMA((3 * units + 1, 12)), pltpu.SemaphoreType.DMA((3 * units + 1, 12)),
           pltpu.SemaphoreType.DMA((4,))],
        compiler_params=pltpu.CompilerParams(
            collective_id=0, has_side_effects=True, vmem_limit_bytes=60 * 2**20),
        cost_estimate=pl.CostEstimate(flops=0, bytes_accessed=400 * 2**20, transcendentals=0),
    )(*operands)


def ordered_kernel(value_ref, *refs):
    refs[-1][...] = value_ref[...]


def ordered(value, *earlier):
    flat = value.reshape(-1, value.shape[-1])
    tile = pl.BlockSpec((flat.shape[0] // 2, flat.shape[1]), lambda i: (i, 0))
    return pl.pallas_call(
        ordered_kernel,
        grid=(2,),
        out_shape=jax.ShapeDtypeStruct(flat.shape, flat.dtype),
        in_specs=[tile] + [pl.BlockSpec(memory_space=pl.ANY)] * len(earlier),
        out_specs=tile,
    )(flat, *earlier).reshape(value.shape)


def row_tiles(rows, width, count):
    step = min(rows, 128)
    return (rows // step,), [pl.BlockSpec((step, width), lambda i: (i, 0))] * count


def block_kernel(resid_ref, outward_ref, block_ref):
    block_ref[...] = (resid_ref[...] + outward_ref[...].astype(F32)).astype(BF16)


def block_call(resid, outward):
    rows, width = resid.shape
    grid, tiles = row_tiles(rows, width, 3)
    return pl.pallas_call(
        block_kernel,
        grid=grid,
        out_shape=jax.ShapeDtypeStruct((rows, width), BF16),
        in_specs=tiles[:2],
        out_specs=tiles[2],
        cost_estimate=pl.CostEstimate(flops=rows * width, bytes_accessed=8 * rows * width, transcendentals=0),
    )(resid, outward)


def resid_grad_kernel(resid_ref, cot_ref, gain_ref, grads_ref, *refs):
    full_ref, low_ref = refs[-2:]
    values = resid_ref[...]
    rate = lax.rsqrt(jnp.mean(values * values, axis=-1, keepdims=True) + EPS)
    grads = cot_ref[...].astype(F32) + norm_back(values, gain_ref[...], rate, grads_ref[...].astype(F32))
    full_ref[...] = grads
    low_ref[...] = grads.astype(BF16)


def resid_grad(resid, cot, gain, grads, earlier):
    rows, width = resid.shape
    grid, tiles = row_tiles(rows, width, 5)
    return pl.pallas_call(
        resid_grad_kernel,
        grid=grid,
        out_shape=[jax.ShapeDtypeStruct((rows, width), F32), jax.ShapeDtypeStruct((rows, width), BF16)],
        in_specs=[tiles[0], tiles[0], pl.BlockSpec((1, width), lambda i: (0, 0)), tiles[0]]
        + [ANYWHERE] * len(earlier),
        out_specs=tiles[:2],
        compiler_params=pltpu.CompilerParams(vmem_limit_bytes=40 * 2**20),
        cost_estimate=pl.CostEstimate(
            flops=20 * rows * width, bytes_accessed=14 * rows * width, transcendentals=rows),
    )(resid, cot, gain, grads, *earlier)


def finish_kernel(grad_resid_ref, inputs_ref, gain_ref, grads_ref, out_ref):
    values = inputs_ref[...].astype(F32)
    rate = lax.rsqrt(jnp.mean(values * values, axis=-1, keepdims=True) + EPS)
    out_ref[...] = grad_resid_ref[...] + norm_back(values, gain_ref[...], rate, grads_ref[...])


def finish(grad_resid, inputs, gain, grads):
    rows, width = inputs.shape
    grid, tiles = row_tiles(rows, width, 3)
    return pl.pallas_call(
        finish_kernel,
        grid=grid,
        out_shape=jax.ShapeDtypeStruct((rows, width), F32),
        in_specs=[tiles[0], tiles[0], pl.BlockSpec((1, width), lambda i: (0, 0)), tiles[0]],
        out_specs=tiles[0],
        compiler_params=pltpu.CompilerParams(vmem_limit_bytes=40 * 2**20),
        cost_estimate=pl.CostEstimate(
            flops=20 * rows * width, bytes_accessed=14 * rows * width, transcendentals=rows),
    )(grad_resid, inputs, gain, grads)


def spread_kernel(tables, pieces, ids_ref, from_ref, *refs):
    gots, out_refs = refs[:pieces], refs[-tables:]
    ranks = out_refs[0].shape[1]
    replicas = from_ref.shape[0]
    seqs = ids_ref.shape[0] // replicas
    for table in range(tables):
        out_refs[table][...] = jnp.zeros_like(out_refs[table])
    replica = 0
    for got_ref in gots:
        for at in range(got_ref.shape[0]):
            for s in range(seqs):
                place = ids_ref[from_ref[replica] * seqs + s]
                for table in range(tables):
                    rows = pl.ds((table * seqs + s) * ranks, ranks)
                    out_refs[table][place] += got_ref[at, rows, :].astype(F32)
            replica += 1


def spread(ids, source, gots, tables, sets, seqs, earlier=()):
    rows, width = gots[0].shape[1:]
    replicas = source.shape[0]
    ranks = rows // (tables * seqs)
    scalars = pl.BlockSpec(memory_space=pltpu.SMEM)
    return pl.pallas_call(
        functools.partial(spread_kernel, tables, len(gots)),
        out_shape=[jax.ShapeDtypeStruct((sets, ranks, width), F32)] * tables,
        in_specs=[scalars, scalars] + [pl.BlockSpec(memory_space=pltpu.VMEM)] * len(gots)
        + [ANYWHERE] * len(earlier),
        out_specs=[pl.BlockSpec(memory_space=pltpu.VMEM)] * tables,
        compiler_params=pltpu.CompilerParams(vmem_limit_bytes=56 * 2**20),
        cost_estimate=pl.CostEstimate(
            flops=replicas * rows * width,
            bytes_accessed=2 * replicas * rows * width + 4 * tables * sets * ranks * width, transcendentals=0),
    )(ids, source, *gots, *earlier)


def products_kernel(plan, *refs):
    out_ref, row = refs[-1], 0
    for place, (kind, first, last) in plan:
        if kind == "product":
            result = dot(refs[place][:, first:last], refs[place + 1][...], TN)
        else:
            result = refs[place][...]
        count = last - first
        out_ref[row : row + count, :] = result.astype(BF16)
        row += count


def products(items, earlier=(), blocks=1):
    operands, specs, plan, total = [], [], [], 0
    width = items[0][3].shape[-1]
    tile = width // blocks if blocks > 1 and width % (128 * blocks) == 0 else tile_of(width, 512)
    for item in items:
        if len(item) == 1:
            plan.append((len(operands), ("rows", 0, item[0].shape[0])))
            operands.append(item[0])
            specs.append(pl.BlockSpec((item[0].shape[0], tile), lambda i: (0, i)))
        else:
            lhs, first, last, rhs = item
            plan.append((len(operands), ("product", first, last)))
            if isinstance(rhs, tuple):
                rhs, s = rhs
                block = pl.BlockSpec((None, rhs.shape[1], tile), lambda i, s=s: (s, 0, i))
            else:
                block = pl.BlockSpec((rhs.shape[0], tile), lambda i: (0, i))
            operands += [lhs, rhs]
            specs += [resident(lhs), block]
        total += plan[-1][1][2] - plan[-1][1][1]
    cells = sum(operand.size for operand in operands)
    direct = blocks > 1 and tile * blocks == width
    result = pl.pallas_call(
        functools.partial(products_kernel, plan),
        grid=(pl.cdiv(width, tile),),
        out_shape=jax.ShapeDtypeStruct((blocks, total, tile) if direct else (total, width), BF16),
        in_specs=specs + [ANYWHERE] * len(earlier),
        out_specs=(pl.BlockSpec((None, total, tile), lambda i: (i, 0, 0)) if direct
                   else pl.BlockSpec((total, tile), lambda i: (0, i))),
        compiler_params=pltpu.CompilerParams(vmem_limit_bytes=60 * 2**20),
        cost_estimate=pl.CostEstimate(flops=64 * cells, bytes_accessed=2 * cells, transcendentals=0),
    )(*operands, *earlier)
    if blocks > 1 and not direct:
        result = jnp.swapaxes(result.reshape(total, blocks, width // blocks), 0, 1)
    return result


def passed_along(block, axis, distance):
    devices = range(lax.axis_size(axis))
    route = [(i - distance, i) for i in devices if i - distance in devices]
    return lax.ppermute(block, axis, route)


def over_replicas(value, direct):
    count, here = lax.axis_size("replica"), lax.axis_index("replica")
    if count % 2:
        return [lax.all_gather(value, "replica")], jnp.arange(count, dtype=jnp.int32)
    steps = jnp.arange(count // 2, dtype=jnp.int32)
    if direct:
        got = [value[None]] + [
            lax.ppermute(value, "replica", [(i, (i + 2 * step) % count) for i in range(count)])[None]
            for step in range(1, count // 2)]
        source = (here + count - 2 * steps) % count
    else:
        got = [lax.all_gather(value, "replica", axis_index_groups=[list(range(p, count, 2)) for p in range(2)])]
        source = here % 2 + 2 * steps
    swapped = [lax.ppermute(part, "replica", [(i, i ^ 1) for i in range(count)]) for part in got]
    return got + swapped, jnp.concatenate([source, source + 1 - 2 * (here % 2)], 0)


def body(
    inputs, segment_ids, adapter_ids, gain_mix, gain_mlp, w_branch, w_input, conv_taps, decay_heads, admit_heads,
    decay_param, w_mixer, w_gate, w_upper, w_down, down_branch, lift_branch, down_input, lift_input, down_decay,
    lift_decay, down_admit, lift_admit, down_mixer, lift_mixer, down_gate, lift_gate, down_upper, lift_upper,
    down_outward, lift_outward, out_grad,
):
    seqs, stretch, width = inputs.shape
    rows = seqs * stretch
    taps = conv_taps.shape[0]
    sets, _, ranks = down_branch.shape
    group, place = lax.axis_size("group"), lax.axis_index("group")
    mask_cols = seqs * ranks

    turned = lambda table: jnp.swapaxes(table, 1, 2)
    stack, own_tables = pick(
        adapter_ids,
        [turned(down_branch), turned(down_input), turned(down_decay), turned(down_admit), turned(down_mixer),
         turned(down_gate), turned(down_upper), lift_branch, lift_input, lift_decay, lift_admit, lift_mixer,
         lift_outward],
        [lift_gate, lift_upper, turned(down_outward)])
    full_branch, full_input, full_mixer, stack = gather_weights(w_branch, w_input, w_mixer, stack)
    (p_down_branch, p_down_input, p_down_decay, p_down_admit, p_down_mixer, p_down_gate, p_down_upper,
     p_lift_branch, p_lift_input, p_lift_decay, p_lift_admit, p_lift_mixer, p_lift_outward) = [
        stack[i * mask_cols : (i + 1) * mask_cols] for i in range(13)]
    own_lift_gate, own_lift_upper, own_down_outward = [
        own_tables[i * mask_cols : (i + 1) * mask_cols] for i in range(3)]
    all_ids = lax.all_gather(adapter_ids, "replica", axis=0, tiled=True)
    cotangents = lax.all_gather(ordered(out_grad, stack), "group", axis=1, tiled=True)

    row_seq = lax.broadcasted_iota(jnp.int32, (rows, mask_cols), 0) // stretch
    col_seq = lax.broadcasted_iota(jnp.int32, (rows, mask_cols), 1) // ranks
    own = (row_seq == col_seq).astype(F32)
    own_two = jnp.concatenate([own, own], 1)

    begin = place * stretch
    padded_ids = jnp.pad(segment_ids, ((0, 0), (taps - 1, taps - 1)), constant_values=-1)
    window = lax.dynamic_slice_in_dim(padded_ids, begin, stretch + 2 * (taps - 1), 1)
    current = window[:, taps - 1 : taps - 1 + stretch + taps - 1]
    agree = [
        ((current == window[:, taps - 1 - j : taps - 1 - j + stretch + taps - 1]) & (current >= 0)).astype(F32)
        for j in range(taps)
    ]
    restart = (1.0 - agree[1][:, :stretch]).reshape(rows, 1)

    x_float = inputs.reshape(rows, width).astype(F32)
    normed_f, _ = norm_rows(x_float, gain_mix)
    normed = normed_f.astype(BF16)
    inner_one = (dot(normed, stack[: 2 * mask_cols], NT) * own_two).astype(BF16)
    inner_branch, inner_input = inner_one[:, :mask_cols], inner_one[:, mask_cols:]
    branch_pre = dot(normed, full_branch) + dot(inner_branch, p_lift_branch)
    fed = (dot(normed, full_input) + dot(inner_input, p_lift_input)).astype(BF16)
    fed = fed.reshape(seqs, stretch, width)
    halo = passed_along(fed[:, stretch - (taps - 1) :], "group", 1)
    extended = jnp.concatenate([halo, fed], axis=1).astype(F32)
    convolved = sum(
        conv_taps[j] * agree[j][:, :stretch, None] * extended[:, taps - 1 - j : taps - 1 - j + stretch]
        for j in range(taps)
    ).reshape(rows, width)
    rounded = convolved.astype(BF16)
    softrate = jax.nn.softplus(decay_param).reshape(1, width)
    inner_gates = (dot(rounded, stack[2 * mask_cols : 4 * mask_cols], NT) * own_two).astype(BF16)
    lift_gates = stack[9 * mask_cols : 11 * mask_cols]
    cum, local = forward_gates(seqs, convolved, inner_gates, lift_gates, decay_heads, admit_heads, softrate, restart)
    ends = jnp.concatenate(
        [cum.reshape(seqs, stretch, width)[:, -1], local.reshape(seqs, stretch, width)[:, -1]], 0)
    all_ends = lax.all_gather(ends, "group")
    carried = jnp.zeros((seqs, width), F32)
    for g in range(group - 1):
        longer = all_ends[g, :seqs] * carried + all_ends[g, seqs:]
        carried = jnp.where(g < place, longer, carried)
    carried_rows = jnp.repeat(carried, stretch, axis=0)
    state = local + cum * carried_rows
    merged = (state * gelu(branch_pre)).astype(BF16)
    inner_mixer = (dot(merged, p_down_mixer, NT) * own).astype(BF16)
    mixed = dot(merged, full_mixer) + dot(inner_mixer, p_lift_mixer)
    resid = x_float + mixed
    normed_two_f, _ = norm_rows(resid, gain_mlp)
    normed_two = normed_two_f.astype(BF16).reshape(seqs, stretch, width)

    spans = [slice(s * ranks, (s + 1) * ranks) for s in range(seqs)]
    grad_hiddens = [
        grad_hidden_call(cotangents, s, w_down, p_lift_outward[at], own_down_outward[at])
        for s, at in enumerate(spans)]
    all_tokens = [lax.all_gather(normed_two[s], "group", axis=0, tiled=True) for s in range(seqs)]
    backs, hiddens, throughs, inners, gates, uppers = [], [], [], [], [], []
    for s, at in enumerate(spans):
        two_downs = jnp.concatenate([p_down_gate[at], p_down_upper[at]], 0)
        earlier = (all_ids,) + tuple(grad_hidden for grad_hidden, _ in grad_hiddens) if s == 0 else ()
        hidden, grad_gate, grad_upper, inner = hidden_call(
            all_tokens[s], grad_hiddens[s][0], w_gate, w_upper, two_downs, own_lift_gate[at], own_lift_upper[at],
            earlier)
        back, through = back_call(
            grad_gate, grad_upper, w_gate, w_upper, own_lift_gate[at], own_lift_upper[at], two_downs)
        backs.append(lax.psum_scatter(back, "group", scatter_dimension=0, tiled=True))
        for kept, value in zip((hiddens, throughs, inners, gates, uppers),
                               (hidden, through, inner, grad_gate, grad_upper)):
            kept.append(value)
    outward, inner_out = outward_call(hiddens, w_down, own_down_outward, p_lift_outward, back)
    early = products(
        [(throughs[s], 0, ranks, all_tokens[s]) for s in range(seqs)]
        + [(throughs[s], ranks, 2 * ranks, all_tokens[s]) for s in range(seqs)]
        + [(inner_out[s], 0, ranks, (cotangents, s)) for s in range(seqs)], (outward,))
    wide = products(
        [(inners[s], 0, ranks, gates[s]) for s in range(seqs)]
        + [(inners[s], ranks, 2 * ranks, uppers[s]) for s in range(seqs)]
        + [(grad_hiddens[s][1], 0, ranks, hiddens[s]) for s in range(seqs)], (outward,))
    grad_normed_two = jnp.concatenate(backs, 0)
    grad_resid, grad_mixed = resid_grad(
        resid, out_grad.reshape(rows, width), gain_mlp.reshape(1, width), grad_normed_two, (early, wide))
    outward = lax.psum_scatter(outward, "group", scatter_dimension=1, tiled=True).reshape(rows, width)
    block_out = block_call(resid, outward)
    all_wide, wide_source = over_replicas(wide, True)

    through_mixer = (dot(grad_mixed, p_lift_mixer, NT) * own).astype(BF16)
    grad_merged = dot(grad_mixed, full_mixer, NT) + dot(through_mixer, p_down_mixer)
    span, total, firsts, grad_branch_pre = backward_scan(
        seqs, convolved, inner_gates, lift_gates, decay_heads, softrate, restart, cum, local, carried, branch_pre,
        grad_merged)
    all_firsts = lax.all_gather(firsts, "group")
    incoming = jnp.zeros((seqs, width), F32)
    for lap in range(group - 1):
        g = group - 1 - lap
        longer = all_firsts[g, :seqs] * incoming + all_firsts[g, seqs:]
        incoming = jnp.where(g > place, longer, incoming)
    grad_direct, through_gates, grad_lift_gates = backward_gates(
        seqs, convolved, inner_gates, lift_gates, decay_heads, admit_heads, softrate, restart, cum, local, carried,
        span, total, incoming)
    through_gates = (through_gates * own_two).astype(BF16)
    grad_convolved = grad_direct + dot(through_gates, stack[2 * mask_cols : 4 * mask_cols])
    grad_convolved = grad_convolved.reshape(seqs, stretch, width)
    below = passed_along(grad_convolved[:, : taps - 1].astype(BF16), "group", -1).astype(F32)
    grad_extended = jnp.concatenate([grad_convolved, below], axis=1)
    grad_fed = sum(
        conv_taps[j] * agree[j][:, j : j + stretch, None] * grad_extended[:, j : j + stretch] for j in range(taps)
    ).astype(BF16).reshape(rows, width)
    through_branch = (dot(grad_branch_pre, p_lift_branch, NT) * own).astype(BF16)
    through_input = (dot(grad_fed, p_lift_input, NT) * own).astype(BF16)
    through_one = jnp.concatenate([through_branch, through_input], 1)
    grad_normed = (dot(grad_branch_pre, full_branch, NT) + dot(grad_fed, full_input, NT)
                   + dot(through_one, stack[: 2 * mask_cols]))
    grad_inputs = finish(grad_resid, inputs.reshape(rows, width), gain_mix.reshape(1, width), grad_normed)

    both = 2 * mask_cols
    partial = products(
        [(through_one, 0, both, normed), (through_gates, 0, both, rounded), (through_mixer, 0, mask_cols, merged),
         (inner_branch, 0, mask_cols, grad_branch_pre), (inner_input, 0, mask_cols, grad_fed), (grad_lift_gates,),
         (inner_mixer, 0, mask_cols, grad_mixed), (early,)], (block_out, *all_wide), group)
    owned = lax.psum_scatter(partial, "group", scatter_dimension=0, tiled=False)
    wides = spread(all_ids, wide_source, all_wide, 3, sets, seqs, (partial,))
    all_owned, owned_source = over_replicas(ordered(owned, grad_inputs, wides[0]), False)
    totals = spread(all_ids, owned_source, all_owned, 13, sets, seqs)
    (t_down_branch, t_down_input, t_down_decay, t_down_admit, t_down_mixer, t_lift_branch, t_lift_input, t_lift_decay,
     t_lift_admit, t_lift_mixer, t_down_gate, t_down_upper, t_lift_outward) = totals
    return (
        block_out.reshape(seqs, stretch, width), grad_inputs.reshape(seqs, stretch, width),
        turned(t_down_branch), t_lift_branch, turned(t_down_input), t_lift_input, turned(t_down_decay), t_lift_decay,
        turned(t_down_admit), t_lift_admit, turned(t_down_mixer), t_lift_mixer, turned(t_down_gate), wides[0],
        turned(t_down_upper), wides[1], turned(wides[2]), t_lift_outward,
    )


def solution(mesh):
    tokens = P("replica", "group", None)
    down, lift = P(None, "group", None), P(None, None, "group")
    cols, split = P(None, "group"), P("group", None)
    in_specs = (
        tokens, P("replica", None), P("replica"), P(), P(), cols, cols, P(), P(), P(), P(), split, cols, cols, split,
    ) + (down, lift) * 8 + (tokens,)
    out_specs = (tokens, tokens) + (down, lift) * 8
    return jax.shard_map(body, mesh=mesh, in_specs=in_specs, out_specs=out_specs, check_vma=False)
```

```python
import functools

import jax
import jax.numpy as jnp
from jax import lax
from jax.experimental import pallas as pl
from jax.experimental.pallas import tpu as pltpu
from jax.sharding import PartitionSpec as P

EPS = 1e-06
F32 = jnp.float32
BF16 = jnp.bfloat16
GELU_C = 0.7978845608028654
GELU_A = 0.044715
NT = (((1,), (1,)), ((), ()))
NN = (((1,), (0,)), ((), ()))
TN = (((0,), (0,)), ((), ()))
ANYWHERE = pl.BlockSpec(memory_space=pl.ANY)


def dot(a, b, dims=NN):
    return lax.dot_general(a, b, dims, preferred_element_type=F32)


def gelu(v):
    return 0.5 * v * (1.0 + jnp.tanh(GELU_C * (v + GELU_A * v * v * v)))


def gelu_both(v):
    square = v * v
    half = 0.5 + 0.5 * jnp.tanh(v * (GELU_C + GELU_C * GELU_A * square))
    value = v * half
    return value, half + (value - value * half) * (2.0 * GELU_C + 6.0 * GELU_C * GELU_A * square)


def norm_rows(values, gain):
    rate = lax.rsqrt(jnp.mean(values * values, axis=-1, keepdims=True) + EPS)
    return values * rate * gain, rate


def norm_back(values, gain, rate, grads):
    scaled = grads * gain
    along = jnp.mean(scaled * values, axis=-1, keepdims=True)
    return rate * scaled - values * (rate * rate * rate * along)


def rows_shifted(values, by, fill):
    rows, width = values.shape
    if by % 8 == 0:
        return jnp.concatenate([jnp.full((by, width), fill, values.dtype), values[: rows - by]], 0)
    place = lax.broadcasted_iota(jnp.int32, values.shape, 0)
    return jnp.where(place >= by, pltpu.roll(values, by, 0), fill)


def rows_advanced(values, by, fill):
    rows, width = values.shape
    if by % 8 == 0:
        return jnp.concatenate([values[by:], jnp.full((by, width), fill, values.dtype)], 0)
    place = lax.broadcasted_iota(jnp.int32, values.shape, 0)
    return jnp.where(place < rows - by, pltpu.roll(values, rows - by, 0), fill)


def scan_rows(a, b, moved):
    by = 1
    while by < a.shape[0]:
        b = a * moved(b, by, 0.0) + b
        a = a * moved(a, by, 1.0)
        by *= 2
    return a, b


def gate_values(conv, inner, lift, table_d, table_a, softrate, restart):
    rounded = conv.astype(BF16)
    half = lift.shape[0] // 2
    pre_d = dot(rounded, table_d) + dot(inner[:, :half], lift[:half])
    pre_a = dot(rounded, table_a) + dot(inner[:, half:], lift[half:])
    decay_gate = 1.0 / (1.0 + jnp.exp(-pre_d))
    admit_gate = 1.0 / (1.0 + jnp.exp(-pre_a))
    safe = jnp.where(restart, -1.0, -8.0 * decay_gate * softrate)
    grown = jnp.exp(safe)
    scale = jnp.sqrt(jnp.tanh(-safe) * (1.0 + grown * grown))
    return decay_gate, admit_gate, grown, scale


def forward_gates_kernel(seqs, conv_ref, inner_ref, lift_ref, table_d_ref, table_a_ref, soft_ref, restart_ref,
                         cum_ref, local_ref):
    stretch = conv_ref.shape[0] // seqs
    for s in range(seqs):
        rows = pl.ds(s * stretch, stretch)
        conv = conv_ref[rows, :]
        restart = restart_ref[rows, :] > 0.5
        _, admit, grown, scale = gate_values(
            conv, inner_ref[rows, :], lift_ref[...], table_d_ref[0], table_a_ref[0], soft_ref[...], restart)
        decays = jnp.where(restart, 0.0, grown)
        drive = conv * admit * jnp.where(restart, 1.0, scale)
        cum, local = scan_rows(decays, drive, rows_shifted)
        cum_ref[rows, :] = cum
        local_ref[rows, :] = local


def forward_gates(seqs, conv, inner, lift, table_d, table_a, softrate, restart):
    rows, width = conv.shape
    heads, size = table_d.shape[:2]
    tile = pl.BlockSpec((rows, size), lambda h: (0, h))
    table = pl.BlockSpec((1, size, size), lambda h: (h, 0, 0))
    out = jax.ShapeDtypeStruct((rows, width), F32)
    return pl.pallas_call(
        functools.partial(forward_gates_kernel, seqs),
        out_shape=(out, out),
        grid=(heads,),
        in_specs=[
            tile,
            pl.BlockSpec(inner.shape, lambda h: (0, 0)),
            pl.BlockSpec((lift.shape[0], size), lambda h: (0, h)),
            table,
            table,
            pl.BlockSpec((1, size), lambda h: (0, h)),
            pl.BlockSpec(restart.shape, lambda h: (0, 0)),
        ],
        out_specs=(tile, tile),
        compiler_params=pltpu.CompilerParams(vmem_limit_bytes=40 * 2**20),
        cost_estimate=pl.CostEstimate(
            flops=4 * rows * width * size + 60 * rows * width,
            bytes_accessed=12 * rows * width,
            transcendentals=6 * rows * width),
    )(conv, inner, lift, table_d, table_a, softrate, restart)


def backward_scan_kernel(seqs, conv_ref, inner_ref, lift_ref, table_d_ref, soft_ref, restart_ref, cum_ref, local_ref,
                         carried_ref, pre_ref, grad_ref, span_ref, total_ref, first_ref, branch_grad_ref):
    stretch = conv_ref.shape[0] // seqs
    half = lift_ref.shape[0] // 2
    for s in range(seqs):
        rows = pl.ds(s * stretch, stretch)
        restart = restart_ref[rows, :] > 0.5
        rounded = conv_ref[rows, :].astype(BF16)
        pre_d = dot(rounded, table_d_ref[0]) + dot(inner_ref[rows, :half], lift_ref[:half, :])
        grown = jnp.exp(-8.0 * soft_ref[...] / (1.0 + jnp.exp(-pre_d)))
        decays = jnp.where(restart, 0.0, grown)
        state = local_ref[rows, :] + cum_ref[rows, :] * carried_ref[s : s + 1, :]
        value, slope = gelu_both(pre_ref[rows, :])
        grads = grad_ref[rows, :]
        branch_grad_ref[rows, :] = (grads * state * slope).astype(BF16)
        span, total = scan_rows(rows_advanced(decays, 1, 1.0), grads * value, rows_advanced)
        span_ref[rows, :] = span
        total_ref[rows, :] = total
        first_ref[s : s + 1, :] = decays[:1] * span[:1]
        first_ref[seqs + s : seqs + s + 1, :] = decays[:1] * total[:1]


def backward_scan(seqs, conv, inner, lift, table_d, softrate, restart, cum, local, carried, pre, grads):
    rows, width = conv.shape
    heads, size = table_d.shape[:2]
    tile = pl.BlockSpec((rows, size), lambda h: (0, h))
    table = pl.BlockSpec((1, size, size), lambda h: (h, 0, 0))
    out = jax.ShapeDtypeStruct((rows, width), F32)
    return pl.pallas_call(
        functools.partial(backward_scan_kernel, seqs),
        out_shape=(out, out, jax.ShapeDtypeStruct((2 * seqs, width), F32), jax.ShapeDtypeStruct((rows, width), BF16)),
        grid=(heads,),
        in_specs=[
            tile,
            pl.BlockSpec(inner.shape, lambda h: (0, 0)),
            pl.BlockSpec((lift.shape[0], size), lambda h: (0, h)),
            table,
            pl.BlockSpec((1, size), lambda h: (0, h)),
            pl.BlockSpec(restart.shape, lambda h: (0, 0)),
            tile,
            tile,
            pl.BlockSpec((seqs, size), lambda h: (0, h)),
            tile,
            tile,
        ],
        out_specs=(tile, tile, pl.BlockSpec((2 * seqs, size), lambda h: (0, h)), tile),
        compiler_params=pltpu.CompilerParams(vmem_limit_bytes=48 * 2**20),
        cost_estimate=pl.CostEstimate(
            flops=2 * rows * width * size + 80 * rows * width,
            bytes_accessed=30 * rows * width,
            transcendentals=4 * rows * width),
    )(conv, inner, lift, table_d, softrate, restart, cum, local, carried, pre, grads)


def backward_gates_kernel(seqs, conv_ref, inner_ref, lift_ref, table_d_ref, table_a_ref, soft_ref, restart_ref,
                          cum_ref, local_ref, carried_ref, span_ref, total_ref, incoming_ref,
                          conv_grad_ref, through_ref, lift_grad_ref):
    stretch = conv_ref.shape[0] // seqs
    half = lift_ref.shape[0] // 2

    @pl.when(pl.program_id(0) == 0)
    def _():
        through_ref[...] = jnp.zeros_like(through_ref)

    for s in range(seqs):
        rows = pl.ds(s * stretch, stretch)
        conv = conv_ref[rows, :]
        inner = inner_ref[rows, :]
        restart = restart_ref[rows, :] > 0.5
        softrate = soft_ref[...]
        decay_gate, admit, grown, scale = gate_values(
            conv, inner, lift_ref[...], table_d_ref[0], table_a_ref[0], softrate, restart)
        carried = carried_ref[s : s + 1, :]
        state = local_ref[rows, :] + cum_ref[rows, :] * carried
        place = lax.broadcasted_iota(jnp.int32, state.shape, 0)
        before = jnp.where(place >= 1, pltpu.roll(state, 1, 0), carried)
        grads = total_ref[rows, :] + span_ref[rows, :] * incoming_ref[s : s + 1, :]
        driven = grads * jnp.where(restart, 1.0, scale)
        grad_log = jnp.where(
            restart, 0.0, grads * (before * grown - conv * admit * grown * grown / scale))
        grad_d = (-8.0 * softrate) * grad_log * decay_gate * (1.0 - decay_gate)
        grad_a = driven * conv * admit * (1.0 - admit)
        low_d, low_a = grad_d.astype(BF16), grad_a.astype(BF16)
        conv_grad_ref[rows, :] = driven * admit + dot(low_d, table_d_ref[0], NT) + dot(low_a, table_a_ref[0], NT)
        through_ref[rows, :half] += dot(low_d, lift_ref[:half, :], NT)
        through_ref[rows, half:] += dot(low_a, lift_ref[half:, :], NT)
        first = dot(inner[:, :half], low_d, TN)
        second = dot(inner[:, half:], low_a, TN)
        if s == 0:
            lift_grad_ref[:half, :] = first
            lift_grad_ref[half:, :] = second
        else:
            lift_grad_ref[:half, :] += first
            lift_grad_ref[half:, :] += second


def backward_gates(seqs, conv, inner, lift, table_d, table_a, softrate, restart, cum, local, carried, span, total,
                   incoming):
    rows, width = conv.shape
    heads, size = table_d.shape[:2]
    tile = pl.BlockSpec((rows, size), lambda h: (0, h))
    table = pl.BlockSpec((1, size, size), lambda h: (h, 0, 0))
    edge = pl.BlockSpec((seqs, size), lambda h: (0, h))
    ranks = pl.BlockSpec((lift.shape[0], size), lambda h: (0, h))
    return pl.pallas_call(
        functools.partial(backward_gates_kernel, seqs),
        out_shape=(
            jax.ShapeDtypeStruct((rows, width), F32),
            jax.ShapeDtypeStruct(inner.shape, F32),
            jax.ShapeDtypeStruct(lift.shape, F32),
        ),
        grid=(heads,),
        in_specs=[
            tile,
            pl.BlockSpec(inner.shape, lambda h: (0, 0)),
            ranks,
            table,
            table,
            pl.BlockSpec((1, size), lambda h: (0, h)),
            pl.BlockSpec(restart.shape, lambda h: (0, 0)),
            tile,
            tile,
            edge,
            tile,
            tile,
            edge,
        ],
        out_specs=(tile, pl.BlockSpec(inner.shape, lambda h: (0, 0)), ranks),
        compiler_params=pltpu.CompilerParams(vmem_limit_bytes=48 * 2**20),
        cost_estimate=pl.CostEstimate(
            flops=8 * rows * width * size + 80 * rows * width,
            bytes_accessed=24 * rows * width,
            transcendentals=6 * rows * width),
    )(conv, inner, lift, table_d, table_a, softrate, restart, cum, local, carried, span, total, incoming)


def sequence_mask(rows, cols, seqs):
    row = lax.broadcasted_iota(jnp.int32, (rows, cols), 0) // (rows // seqs)
    col = lax.broadcasted_iota(jnp.int32, (rows, cols), 1) % (cols // 2) // (cols // 2 // seqs)
    return (row == col).astype(F32)


def mixer_back_kernel(
    seqs, heads, mixed_ref, w_ref, thr_mixer_ref, down_mixer_ref, conv_ref, inner_ref, lift_ref, table_d_ref,
    table_a_ref, soft_ref, restart_ref, cum_ref, local_ref, carried_ref, pre_ref, lift_branch_ref, lift_input_ref,
    down_gates_ref, taps_ref, agree_ref,
    branch_grad_ref, through_one_ref, through_gates_ref, lift_grad_ref, fed_grad_ref,
    span_ref, total_ref, ends_ref, all_ends_ref, incoming_ref, halo_ref, below_ref, one_ref, gates_ref, send, recv,
):
    rows, size = conv_ref.shape
    stretch = rows // seqs
    half = lift_ref.shape[0] // 2
    ranks = lift_branch_ref.shape[0]
    step = pl.program_id(0)
    group, replica = lax.axis_index("group"), lax.axis_index("replica")
    partners = [(group + 1 - 2 * (group % 2), replica), ((group + 2) % 4, replica), (3 - group, replica)]

    def copy(src, dst, slot, partner):
        return pltpu.make_async_remote_copy(
            src_ref=src, dst_ref=dst, send_sem=send.at[slot], recv_sem=recv.at[slot], device_id=partner,
            device_id_type=pl.DeviceIdType.MESH)

    exchange = [copy(ends_ref, all_ends_ref.at[group], slot, partner) for slot, partner in enumerate(partners)]
    downward = copy(halo_ref, below_ref, 3, ((group + 3) % 4, replica))

    @pl.when(step == 0)
    def _():
        barrier = pltpu.get_barrier_semaphore()
        for partner in partners:
            pl.semaphore_signal(barrier, inc=1, device_id=partner, device_id_type=pl.DeviceIdType.MESH)
        pl.semaphore_wait(barrier, 3)
        one_ref[...] = jnp.zeros_like(one_ref)
        gates_ref[...] = jnp.zeros_like(gates_ref)
        ends_ref[...] = jnp.zeros_like(ends_ref)

    @pl.when(step < heads)
    def _():
        cols = pl.ds(pl.multiple_of(step * size, size), size)
        merged = dot(mixed_ref[...], w_ref[...], NT) + dot(thr_mixer_ref[...], down_mixer_ref[...])
        for s in range(seqs):
            at = slice(s * stretch, (s + 1) * stretch)
            restart = restart_ref[at, :] > 0.5
            rounded = conv_ref[at, :].astype(BF16)
            pre_d = dot(rounded, table_d_ref[0]) + dot(inner_ref[at, :half], lift_ref[:half, :])
            grown = jnp.exp(-8.0 * soft_ref[...] / (1.0 + jnp.exp(-pre_d)))
            decays = jnp.where(restart, 0.0, grown)
            state = local_ref[at, :] + cum_ref[at, :] * carried_ref[s : s + 1, :]
            value, slope = gelu_both(pre_ref[at, :])
            grads = merged[at, :]
            low = (grads * state * slope).astype(BF16)
            branch_grad_ref[at, :] = low
            one_ref[at, :ranks] += dot(low, lift_branch_ref[...], NT)
            span, total = scan_rows(rows_advanced(decays, 1, 1.0), grads * value, rows_advanced)
            span_ref[step, at, :] = span
            total_ref[step, at, :] = total
            ends_ref[s : s + 1, cols] = decays[:1] * span[:1]
            ends_ref[seqs + s : seqs + s + 1, cols] = decays[:1] * total[:1]

    @pl.when(step == heads - 1)
    def _():
        for one in exchange:
            one.start()

    @pl.when(step == heads)
    def _():
        for one in exchange:
            one.wait_recv()
        incoming = jnp.zeros(incoming_ref.shape, F32)
        for g in (3, 2, 1):
            longer = all_ends_ref[g, :seqs, :] * incoming + all_ends_ref[g, seqs : 2 * seqs, :]
            incoming = jnp.where(group < g, longer, incoming)
        incoming_ref[...] = incoming

    @pl.when((step >= heads) & (step < 2 * heads))
    def _():
        head = step - heads
        cols = pl.ds(pl.multiple_of(head * size, size), size)
        softrate = soft_ref[...]
        for s in range(seqs):
            at = slice(s * stretch, (s + 1) * stretch)
            conv, inner = conv_ref[at, :], inner_ref[at, :]
            restart = restart_ref[at, :] > 0.5
            decay_gate, admit, grown, scale = gate_values(
                conv, inner, lift_ref[...], table_d_ref[0], table_a_ref[0], softrate, restart)
            carried = carried_ref[s : s + 1, :]
            state = local_ref[at, :] + cum_ref[at, :] * carried
            place = lax.broadcasted_iota(jnp.int32, state.shape, 0)
            before = jnp.where(place >= 1, pltpu.roll(state, 1, 0), carried)
            grads = total_ref[head, at, :] + span_ref[head, at, :] * incoming_ref[s : s + 1, cols]
            driven = grads * jnp.where(restart, 1.0, scale)
            grad_log = jnp.where(
                restart, 0.0, grads * (before * grown - conv * admit * grown * grown / scale))
            grad_d = (-8.0 * softrate) * grad_log * decay_gate * (1.0 - decay_gate)
            grad_a = driven * conv * admit * (1.0 - admit)
            low_d, low_a = grad_d.astype(BF16), grad_a.astype(BF16)
            total_ref[head, at, :] = (
                driven * admit + dot(low_d, table_d_ref[0], NT) + dot(low_a, table_a_ref[0], NT))
            gates_ref[at, :half] += dot(low_d, lift_ref[:half, :], NT)
            gates_ref[at, half:] += dot(low_a, lift_ref[half:, :], NT)
            first = dot(inner[:, :half], low_d, TN)
            second = dot(inner[:, half:], low_a, TN)
            if s == 0:
                lift_grad_ref[:half, :] = first
                lift_grad_ref[half:, :] = second
            else:
                lift_grad_ref[:half, :] += first
                lift_grad_ref[half:, :] += second

    @pl.when(step == 2 * heads)
    def _():
        through_gates_ref[...] = (gates_ref[...] * sequence_mask(rows, 2 * half, seqs)).astype(BF16)
        tops = []
        for s in range(seqs):
            top = slice(s * stretch, s * stretch + 8)
            direct = jnp.concatenate([total_ref[h, top, :] for h in range(heads)], 1)
            tops.append(direct + dot(through_gates_ref[top, :], down_gates_ref[...]))
        halo_ref[...] = jnp.concatenate(tops, 0).astype(BF16)
        downward.start()
        downward.wait_recv()

    @pl.when(step >= 2 * heads)
    def _():
        head = step - 2 * heads
        cols = pl.ds(pl.multiple_of(head * size, size), size)
        grads = total_ref[head] + dot(through_gates_ref[...], down_gates_ref[:, cols])
        for s in range(seqs):
            at = slice(s * stretch, (s + 1) * stretch)
            longer = jnp.concatenate([grads[at, :], below_ref[s * 8 : (s + 1) * 8, cols].astype(F32)], 0)
            total = taps_ref[0:1, :] * agree_ref[at, 0:1] * grads[at, :]
            for j in range(1, taps_ref.shape[0]):
                moved = pltpu.roll(longer, stretch + 8 - j, 0)[:stretch]
                total += taps_ref[j : j + 1, :] * agree_ref[at, j : j + 1] * moved
            low = total.astype(BF16)
            fed_grad_ref[at, :] = low
            one_ref[at, ranks:] += dot(low, lift_input_ref[...], NT)

    @pl.when(step == 3 * heads - 1)
    def _():
        through_one_ref[...] = (one_ref[...] * sequence_mask(rows, 2 * ranks, seqs)).astype(BF16)
        for one in exchange:
            one.wait_send()
        downward.wait_send()


def mixer_back(seqs, mixed, w_mixer, thr_mixer, down_mixer, conv, inner, lift, table_d, table_a, softrate, restart,
               cum, local, carried, pre, lift_branch, lift_input, down_gates, taps, agree):
    rows, width = conv.shape
    heads, size = table_d.shape[:2]
    first = lambda i: jnp.minimum(i, heads - 1)
    second = lambda i: jnp.clip(i - heads, 0, heads - 1)
    third = lambda i: jnp.maximum(i - 2 * heads, 0)
    either = lambda i: jnp.minimum(i, 2 * heads - 1) % heads
    full = lambda array: pl.BlockSpec(array.shape, lambda i: (0, 0), pipeline_mode=pl.Buffered(1))
    cols = lambda array, at: pl.BlockSpec((array.shape[0], size), lambda i: (0, at(i)))
    table = pl.BlockSpec((1, size, size), lambda i: (either(i), 0, 0))
    middle = inner.shape[1]
    tile = lambda at: pl.BlockSpec((rows, size), lambda i: (0, at(i)))
    whole = lambda count: pl.BlockSpec((rows, count), lambda i: (0, 0))
    return pl.pallas_call(
        functools.partial(mixer_back_kernel, seqs, heads),
        grid=(3 * heads,),
        out_shape=[
            jax.ShapeDtypeStruct((rows, width), BF16),
            jax.ShapeDtypeStruct((rows, 2 * lift_branch.shape[0]), BF16),
            jax.ShapeDtypeStruct((rows, middle), BF16),
            jax.ShapeDtypeStruct(lift.shape, F32),
            jax.ShapeDtypeStruct((rows, width), BF16),
        ],
        in_specs=[
            full(mixed), pl.BlockSpec((size, width), lambda i: (first(i), 0)), full(thr_mixer), cols(down_mixer, first),
            cols(conv, either), full(inner), cols(lift, either), table, table, cols(softrate, either), full(restart),
            cols(cum, either), cols(local, either), cols(carried, either), cols(pre, first), cols(lift_branch, first),
            cols(lift_input, third), full(down_gates), cols(taps, third), full(agree),
        ],
        out_specs=[tile(first), whole(2 * lift_branch.shape[0]), whole(middle),
                   pl.BlockSpec((lift.shape[0], size), lambda i: (0, second(i))), tile(third)],
        scratch_shapes=[
            pltpu.VMEM((heads, rows, size), F32), pltpu.VMEM((heads, rows, size), F32), pltpu.VMEM((8, width), F32),
            pltpu.VMEM((4, 8, width), F32), pltpu.VMEM((seqs, width), F32), pltpu.VMEM((8 * seqs, width), BF16),
            pltpu.VMEM((8 * seqs, width), BF16), pltpu.VMEM((rows, 2 * lift_branch.shape[0]), F32),
            pltpu.VMEM((rows, middle), F32), pltpu.SemaphoreType.DMA((4,)), pltpu.SemaphoreType.DMA((4,))],
        compiler_params=pltpu.CompilerParams(
            vmem_limit_bytes=60 * 2**20, collective_id=3, has_side_effects=True),
        cost_estimate=pl.CostEstimate(
            flops=2 * rows * width * width + 20 * rows * width * size + 200 * rows * width,
            bytes_accessed=40 * rows * width + 2 * width * width, transcendentals=12 * rows * width),
    )(mixed, w_mixer, thr_mixer, down_mixer, conv, inner, lift, table_d, table_a, softrate, restart, cum, local,
      carried, pre, lift_branch, lift_input, down_gates, taps, agree)


def resident(array):
    return pl.BlockSpec(array.shape, lambda i: (0, 0), pipeline_mode=pl.Buffered(1))


def tile_of(count, tile):
    return tile if count % 128 == 0 and count > tile else count


def grad_hidden_kernel(seqs, gather, steps, *refs):
    if gather:
        cot_ref, wd_ref, lift_out_ref, do_ref, block_ref, out_ref, through_ref, all_ref = refs[:8]
        staged_ref, send, recv, local = refs[8:]
    else:
        cot_ref, wd_ref, lift_out_ref, do_ref, out_ref, through_ref = refs
    ranks = do_ref.shape[0] // seqs
    step = pl.program_id(0)

    if gather:
        group, replica = lax.axis_index("group"), lax.axis_index("replica")
        beside, above = group + 1 - 2 * (group % 2), (group + 2) % 4
        at_beside, at_above = (beside, replica), (above, replica)
        rows = block_ref.shape[0]
        half = rows // 2

        def place(owner, part):
            return all_ref.at[pl.ds(pl.multiple_of(owner * rows + part * half, half), half), :]

        def own(part):
            return block_ref.at[pl.ds(part * half, half), :]

        def copy(src, dst, slot, partner):
            return pltpu.make_async_remote_copy(
                src_ref=src, dst_ref=dst, send_sem=send.at[slot], recv_sem=recv.at[slot], device_id=partner,
                device_id_type=pl.DeviceIdType.MESH)

        firsts = [copy(own(1), place(group, 1), 0, at_beside), copy(own(0), place(group, 0), 1, at_above),
                  copy(own(0), place(group, 0), 2, at_beside), copy(own(1), place(group, 1), 3, at_above)]
        seconds = [copy(place(beside, 1), place(beside, 1), 4, at_above),
                   copy(place(above, 0), place(above, 0), 5, at_beside)]
        stage = pltpu.make_async_copy(block_ref, staged_ref, local.at[0])
        keep = pltpu.make_async_copy(
            staged_ref, all_ref.at[pl.ds(pl.multiple_of(group * rows, rows), rows), :], local.at[1])

        @pl.when(step == 0)
        def _():
            barrier = pltpu.get_barrier_semaphore()
            for partner in (at_beside, at_above):
                pl.semaphore_signal(barrier, inc=1, device_id=partner, device_id_type=pl.DeviceIdType.MESH)
            pl.semaphore_wait(barrier, 2)
            for one in firsts[:2]:
                one.start()
            stage.start()

    @pl.when(step == 0)
    def _():
        for s in range(seqs):
            through_ref[s] = dot(cot_ref[s], lift_out_ref[s * ranks : (s + 1) * ranks, :], NT).astype(BF16)

    for s in range(seqs):
        out_ref[s] = (dot(cot_ref[s], wd_ref[...], NT)
                      + dot(through_ref[s], do_ref[s * ranks : (s + 1) * ranks, :])).astype(BF16)

    if gather:
        @pl.when(step == 0)
        def _():
            stage.wait()
            keep.start()
            for one in firsts[2:]:
                one.start()

        @pl.when(step == min(1, steps - 1))
        def _():
            for one, then in zip(firsts[:2], seconds):
                one.wait_recv()
                then.start()

        @pl.when(step == steps - 1)
        def _():
            for one in firsts[2:] + seconds:
                one.wait_recv()
            for one in firsts + seconds:
                one.wait_send()
            keep.wait()


def grad_hidden_call(cot, wd, lift_out, do, block):
    seqs, rows, width = cot.shape
    units, ranks = wd.shape[0], do.shape[0] // seqs
    tile = tile_of(units, 512)
    gather = lax.axis_size("group") == 4
    got = pl.pallas_call(
        functools.partial(grad_hidden_kernel, seqs, gather, pl.cdiv(units, tile)),
        grid=(pl.cdiv(units, tile),),
        out_shape=[jax.ShapeDtypeStruct((seqs, rows, units), BF16), jax.ShapeDtypeStruct((seqs, rows, ranks), BF16)]
        + [jax.ShapeDtypeStruct((rows, width), BF16)] * gather,
        in_specs=[pl.BlockSpec(cot.shape, lambda i: (0, 0, 0), pipeline_mode=pl.Buffered(1)),
                  pl.BlockSpec((tile, width), lambda i: (i, 0)), resident(lift_out),
                  pl.BlockSpec((seqs * ranks, tile), lambda i: (0, i))] + [ANYWHERE] * gather,
        out_specs=[pl.BlockSpec((seqs, rows, tile), lambda i: (0, 0, i)),
                   pl.BlockSpec((seqs, rows, ranks), lambda i: (0, 0, 0))] + [ANYWHERE] * gather,
        scratch_shapes=[pltpu.VMEM(block.shape, BF16), pltpu.SemaphoreType.DMA((6,)), pltpu.SemaphoreType.DMA((6,)),
                        pltpu.SemaphoreType.DMA((2,))] if gather else [],
        compiler_params=pltpu.CompilerParams(
            vmem_limit_bytes=60 * 2**20, **(dict(collective_id=1, has_side_effects=True) if gather else {})),
        cost_estimate=pl.CostEstimate(
            flops=2 * seqs * rows * width * units,
            bytes_accessed=2 * width * units + 2 * seqs * rows * (units + width), transcendentals=0),
    )(cot, wd, lift_out, do, *([block] if gather else []))
    return got if gather else list(got) + [lax.all_gather(block, "group", axis=0, tiled=True)]


def feed_kernel(steps, tile, units, tok_ref, gh_ref, wg_ref, wu_ref, wg_rows_ref, wu_rows_ref, down_ref, lg_ref,
                lu_ref, through_out_ref, lg_full_ref, lu_full_ref, down_cols_ref, *refs):
    hidden_ref, back_ref, wide_ref, through_ref, inner_ref, gg_ref, gu_ref = refs[-7:]
    ranks = lg_ref.shape[0]
    step = pl.program_id(0)

    @pl.when(step == 0)
    def _():
        inner_ref[...] = dot(tok_ref[...], down_ref[...], NT).astype(BF16)

    @pl.when(step < steps)
    def _():
        tokens, inner = tok_ref[...], inner_ref[...]
        gate = dot(tokens, wg_ref[...]) + dot(inner[:, :ranks], lg_ref[...])
        upper = dot(tokens, wu_ref[...]) + dot(inner[:, ranks:], lu_ref[...])
        grad_hidden = gh_ref[...].astype(F32)
        value, slope = gelu_both(gate)
        hidden = (value * upper).astype(BF16)
        grad_gate = (grad_hidden * upper * slope).astype(BF16)
        grad_upper = (grad_hidden * value).astype(BF16)
        hidden_ref[...] = hidden
        cols = pl.ds(pl.multiple_of(step * tile, tile), tile) if steps > 1 else slice(0, tile)
        gg_ref[:, cols] = grad_gate
        gu_ref[:, cols] = grad_upper
        wide_ref[:ranks, :] = dot(inner[:, :ranks], grad_gate, TN).astype(BF16)
        wide_ref[ranks : 2 * ranks, :] = dot(inner[:, ranks:], grad_upper, TN).astype(BF16)
        wide_ref[2 * ranks :, :] = dot(through_out_ref[...], hidden, TN).astype(BF16)

    @pl.when(step == steps)
    def _():
        through_ref[:, :ranks] = dot(gg_ref[:, :units], lg_full_ref[...], NT).astype(BF16)
        through_ref[:, ranks:] = dot(gu_ref[:, :units], lu_full_ref[...], NT).astype(BF16)

    @pl.when(step >= steps)
    def _():
        back_ref[...] = (dot(gg_ref[:, :units], wg_rows_ref[...], NT) + dot(gu_ref[:, :units], wu_rows_ref[...], NT)
                         + dot(through_ref[...], down_cols_ref[...])).astype(BF16)


def feed_call(s, tok, gh, wg, wu, down, lg, lu, through_out):
    rows, width = tok.shape
    units, ranks = wg.shape[1], lg.shape[0]
    tile, span = tile_of(units, 512), tile_of(width, 512)
    steps, laps = pl.cdiv(units, tile), pl.cdiv(width, span)
    first = lambda i: jnp.minimum(i, steps - 1)
    second = lambda i: jnp.maximum(i - steps, 0)
    cols = pl.BlockSpec((width, tile), lambda i: (0, first(i)))
    across = pl.BlockSpec((span, units), lambda i: (second(i), 0))
    rank = pl.BlockSpec((ranks, tile), lambda i: (0, first(i)))
    out = pl.BlockSpec((rows, tile), lambda i: (0, first(i)))
    return pl.pallas_call(
        functools.partial(feed_kernel, steps, tile, units),
        grid=(steps + laps,),
        out_shape=[jax.ShapeDtypeStruct((rows, units), BF16), jax.ShapeDtypeStruct((rows, width), BF16),
                   jax.ShapeDtypeStruct((3 * ranks, units), BF16), jax.ShapeDtypeStruct((rows, 2 * ranks), BF16)],
        in_specs=[resident(tok), pl.BlockSpec((None, rows, tile), lambda i: (s, 0, first(i))), cols, cols, across,
                  across, resident(down), rank, rank, pl.BlockSpec((None, rows, ranks), lambda i: (s, 0, 0)),
                  resident(lg), resident(lu), pl.BlockSpec((2 * ranks, span), lambda i: (0, second(i)))],
        out_specs=[out, pl.BlockSpec((rows, span), lambda i: (0, second(i))),
                   pl.BlockSpec((3 * ranks, tile), lambda i: (0, first(i))),
                   pl.BlockSpec((rows, 2 * ranks), lambda i: (0, 0))],
        scratch_shapes=[pltpu.VMEM((rows, 2 * ranks), BF16), pltpu.VMEM((rows, steps * tile), BF16),
                        pltpu.VMEM((rows, steps * tile), BF16)],
        compiler_params=pltpu.CompilerParams(vmem_limit_bytes=62 * 2**20),
        cost_estimate=pl.CostEstimate(
            flops=8 * rows * width * units, bytes_accessed=8 * width * units + 6 * rows * units,
            transcendentals=rows * units),
    )(tok, gh, wg, wu, wg, wu, down, lg, lu, through_out, lg, lu, down)


def outward_kernel(seqs, reduce, steps, *refs):
    hiddens, tokens, throughs, cot_ref, refs = (
        refs[:seqs], refs[seqs : 2 * seqs], refs[2 * seqs : 3 * seqs], refs[3 * seqs], refs[3 * seqs + 1 :])
    if reduce:
        wd_ref, do_ref, lift_out_ref, back_ref, out_ref, inner_ref, early_ref, sum_ref = refs[:8]
        first_a, first_b, second_a, second_b, pass_a, pass_b, own_ref, send, recv, local = refs[8:]
    else:
        wd_ref, do_ref, lift_out_ref, out_ref, inner_ref, early_ref = refs
    ranks = do_ref.shape[0] // seqs
    step = pl.program_id(0)

    if reduce:
        group, replica = lax.axis_index("group"), lax.axis_index("replica")
        beside, above, across = group + 1 - 2 * (group % 2), (group + 2) % 4, 3 - group
        at_beside, at_above = (beside, replica), (above, replica)
        rows, width = own_ref.shape
        half = width // 2

        def part(owner, side):
            return back_ref.at[pl.ds(pl.multiple_of(owner * rows, rows), rows), pl.ds(side * half, half)]

        def copy(src, dst, slot, partner):
            return pltpu.make_async_remote_copy(
                src_ref=src, dst_ref=dst, send_sem=send.at[slot], recv_sem=recv.at[slot], device_id=partner,
                device_id_type=pl.DeviceIdType.MESH)

        firsts = [copy(part(across, 0), first_a.at[1], 0, at_beside), copy(part(across, 1), first_b.at[1], 1, at_above),
                  copy(part(beside, 0), first_a.at[0], 2, at_beside), copy(part(above, 1), first_b.at[0], 3, at_above)]
        seconds = [copy(pass_a, second_a, 4, at_above), copy(pass_b, second_b, 5, at_beside)]
        loads = [pltpu.make_async_copy(part(above, 0), pass_a, local.at[0]),
                 pltpu.make_async_copy(part(beside, 1), pass_b, local.at[1]),
                 pltpu.make_async_copy(
                     back_ref.at[pl.ds(pl.multiple_of(group * rows, rows), rows), :], own_ref, local.at[2])]

        @pl.when(step == 0)
        def _():
            barrier = pltpu.get_barrier_semaphore()
            for partner in (at_beside, at_above):
                pl.semaphore_signal(barrier, inc=1, device_id=partner, device_id_type=pl.DeviceIdType.MESH)
            pl.semaphore_wait(barrier, 2)
            for one in firsts:
                one.start()
            for one in loads:
                one.start()

    @pl.when(step == 0)
    def _():
        for s, hidden_ref in enumerate(hiddens):
            inner_ref[s] = dot(hidden_ref[...], do_ref[s * ranks : (s + 1) * ranks, :], NT).astype(BF16)

    for s, hidden_ref in enumerate(hiddens):
        out_ref[s] = (dot(hidden_ref[...], wd_ref[...])
                      + dot(inner_ref[s], lift_out_ref[s * ranks : (s + 1) * ranks, :])).astype(BF16)
        both = dot(throughs[s][...], tokens[s][...], TN).astype(BF16)
        for kind, rows_of in enumerate((both[:ranks], both[ranks:], dot(inner_ref[s], cot_ref[s], TN).astype(BF16))):
            row = (kind * seqs + s) * ranks
            early_ref[row : row + ranks, :] = rows_of

    if reduce:
        @pl.when(step == max(steps - 2, 0))
        def _():
            for one in loads:
                one.wait()
            for one in firsts:
                one.wait_recv()
            pass_a[...] = (pass_a[...].astype(F32) + first_a[1].astype(F32)).astype(BF16)
            pass_b[...] = (pass_b[...].astype(F32) + first_b[1].astype(F32)).astype(BF16)
            for one in seconds:
                one.start()

        @pl.when(step == steps - 1)
        def _():
            for one in seconds:
                one.wait_recv()
            sum_ref[:, :half] = (own_ref[:, :half].astype(F32) + first_a[0].astype(F32)
                                 + second_a[...].astype(F32)).astype(BF16)
            sum_ref[:, half:] = (own_ref[:, half:].astype(F32) + first_b[0].astype(F32)
                                 + second_b[...].astype(F32)).astype(BF16)
            for one in firsts + seconds:
                one.wait_send()


def outward_call(hiddens, tokens, throughs, cot, wd, do, lift_out, back):
    rows, units = hiddens[0].shape
    seqs = len(hiddens)
    width, ranks = wd.shape[1], do.shape[0] // seqs
    tile = tile_of(width, 512)
    steps = pl.cdiv(width, tile)
    group = lax.axis_size("group")
    reduce = group == 4 and width % 256 == 0
    own, half = rows // group, width // 2
    scratch = [pltpu.VMEM((2, own, half), BF16)] * 2 + [pltpu.VMEM((own, half), BF16)] * 4 + [
        pltpu.VMEM((own, width), BF16), pltpu.SemaphoreType.DMA((6,)), pltpu.SemaphoreType.DMA((6,)),
        pltpu.SemaphoreType.DMA((3,))]
    got = pl.pallas_call(
        functools.partial(outward_kernel, seqs, reduce, steps),
        grid=(steps,),
        out_shape=[jax.ShapeDtypeStruct((seqs, rows, width), BF16), jax.ShapeDtypeStruct((seqs, rows, ranks), BF16),
                   jax.ShapeDtypeStruct((3 * seqs * ranks, width), BF16)]
        + [jax.ShapeDtypeStruct((own, width), BF16)] * reduce,
        in_specs=[resident(hidden) for hidden in hiddens] + [pl.BlockSpec((rows, tile), lambda i: (0, i))] * seqs
        + [resident(through) for through in throughs] + [pl.BlockSpec((seqs, rows, tile), lambda i: (0, 0, i))]
        + [pl.BlockSpec((units, tile), lambda i: (0, i)), resident(do),
           pl.BlockSpec((seqs * ranks, tile), lambda i: (0, i))] + [ANYWHERE] * reduce,
        out_specs=[pl.BlockSpec((seqs, rows, tile), lambda i: (0, 0, i)),
                   pl.BlockSpec((seqs, rows, ranks), lambda i: (0, 0, 0)),
                   pl.BlockSpec((3 * seqs * ranks, tile), lambda i: (0, i))]
        + [pl.BlockSpec((own, width), lambda i: (0, 0))] * reduce,
        scratch_shapes=scratch if reduce else [],
        compiler_params=pltpu.CompilerParams(
            vmem_limit_bytes=60 * 2**20, **(dict(collective_id=2, has_side_effects=True) if reduce else {})),
        cost_estimate=pl.CostEstimate(
            flops=2 * seqs * rows * width * units,
            bytes_accessed=2 * width * units + 2 * seqs * rows * (units + width), transcendentals=0),
    )(*hiddens, *tokens, *throughs, cot, wd, do, lift_out, *([back] if reduce else []))
    return got if reduce else list(got) + [lax.psum_scatter(back, "group", scatter_dimension=0, tiled=True)]


def pick_kernel(counts, ids_ref, *refs):
    tables, (stack_ref, wide_ref) = refs[: sum(counts)], refs[sum(counts) :]
    for i, table in enumerate(tables):
        if i < counts[0]:
            stack_ref[i, 0] = table[0]
        else:
            wide_ref[i - counts[0], 0] = table[0]


def pick(ids, narrow, wide):
    seqs, ranks = ids.shape[0], narrow[0].shape[1]
    counts = (len(narrow), len(wide))
    widths = (narrow[0].shape[2], wide[0].shape[2])
    tables = [pl.BlockSpec((1, ranks, table.shape[2]), lambda s, ids: (ids[s], 0, 0)) for table in narrow + wide]
    picked = pl.pallas_call(
        functools.partial(pick_kernel, counts),
        out_shape=[jax.ShapeDtypeStruct((count, seqs, ranks, width), BF16) for count, width in zip(counts, widths)],
        grid_spec=pltpu.PrefetchScalarGridSpec(
            num_scalar_prefetch=1,
            grid=(seqs,),
            in_specs=tables,
            out_specs=[pl.BlockSpec((count, 1, ranks, width), lambda s, ids: (0, s, 0, 0))
                       for count, width in zip(counts, widths)],
        ),
    )(ids, *narrow, *wide)
    return [part.reshape(-1, part.shape[-1]) for part in picked]


def gather_kernel(units, *refs):
    weights, wholes, staged, (send, recv, local) = refs[:4], refs[4:8], refs[8:12], refs[12:]
    group, replica = lax.axis_index("group"), lax.axis_index("replica")
    beside, above, across = group + 1 - 2 * (group % 2), (group + 2) % 4, 3 - group
    core, level = replica % 2, (replica // 2) % 2
    at_beside, at_above = (beside, replica), (above, replica)
    at_core, at_level = (group, replica + 1 - 2 * core), (group, replica + 2 - 4 * level)
    partners = (at_beside, at_above, at_core, at_level)
    mine, other = 2 * core + level, 2 * core + 1 - level

    barrier = pltpu.get_barrier_semaphore()
    for partner in partners:
        pl.semaphore_signal(barrier, inc=1, device_id=partner, device_id_type=pl.DeviceIdType.MESH)
    pl.semaphore_wait(barrier, 4)

    kept = [pltpu.make_async_copy(weight, stage, local.at[m])
            for m, (weight, stage) in enumerate(zip(weights, staged))]
    for one in kept:
        one.start()

    def keep(m):
        whole = wholes[m]
        rows, cols = weights[m].shape
        if m == 2:
            into = whole.at[pl.ds(pl.multiple_of(group * rows, rows), rows), :]
        else:
            into = whole.at[:, pl.ds(pl.multiple_of(group * cols, cols), cols)]
        kept[m].wait()
        kept[m] = pltpu.make_async_copy(staged[m], into, local.at[m])
        kept[m].start()

    def own(m, part, quarter):
        weight = weights[m]
        size = wholes[m].shape[0] // 4
        step = size // units
        if m < 2:
            return weight.at[pl.ds(pl.multiple_of(quarter * size + part * step, step), step), :]
        return weight.at[pl.ds(part * step, step), pl.ds(pl.multiple_of(quarter * size, size), size)]

    def piece(m, part, shard, quarter):
        whole = wholes[m]
        size = whole.shape[0] // 4
        step = size // units
        down, along = (quarter, shard) if m < 2 else (shard, quarter)
        return whole.at[pl.ds(pl.multiple_of(down * size + part * step, step), step),
                        pl.ds(pl.multiple_of(along * size, size), size)]

    def copy(src, dst, k, slot, partner):
        made = pltpu.make_async_remote_copy(
            src_ref=src, dst_ref=dst, send_sem=send.at[k, slot], recv_sem=recv.at[k, slot], device_id=partner,
            device_id_type=pl.DeviceIdType.MESH)
        made.start()
        return made

    def forward(m, part, shard, quarter, k, slot, partner):
        where = piece(m, part, shard, quarter)
        return copy(where, where, k, slot, partner)

    ranks, cols = weights[3].shape
    last = 3 * units

    def stack_piece(first, count, shard):
        return wholes[3].at[pl.ds(first, count), pl.ds(pl.multiple_of(shard * cols, cols), cols)]

    stack_beside = copy(weights[3], stack_piece(0, ranks, group), last, 0, at_beside)
    stack_above = copy(weights[3], stack_piece(0, ranks, group), last, 1, at_above)

    steps = [(m, part) for m in range(3) for part in range(units)]
    made = {}

    def begin(k):
        m, part = steps[k]
        made[k, 0] = copy(own(m, part, mine), piece(m, part, group, mine), k, 0, at_above)
        made[k, 2] = copy(own(m, part, mine), piece(m, part, group, mine), k, 2, at_beside)
        made[k, 1] = copy(own(m, part, other), piece(m, part, group, other), k, 1, at_above)

    begin(0)
    begin(1)
    for m in range(4):
        keep(m)
    stack_beside.wait_recv()
    stack_above.wait_recv()
    half = ranks // 2
    lower = stack_piece(0, half, above)
    upper = stack_piece(half, half, beside)
    stack_lower = copy(lower, lower, last, 2, at_beside)
    stack_upper = copy(upper, upper, last, 3, at_above)
    for t in range(len(steps) + 2):
        if t < len(steps):
            m, part = steps[t]
            made[t, 0].wait_recv()
            made[t, 4] = forward(m, part, above, mine, t, 4, at_beside)
            made[t, 6] = forward(m, part, above, mine, t, 6, at_core)
            made[t, 2].wait_recv()
            made[t, 3] = forward(m, part, beside, mine, t, 3, at_level)
            made[t, 8] = forward(m, part, beside, mine, t, 8, at_core)
            if t + 2 < len(steps):
                begin(t + 2)
            made[t, 1].wait_recv()
            made[t, 7] = forward(m, part, above, other, t, 7, at_core)
        if 1 <= t <= len(steps):
            m, part = steps[t - 1]
            made[t - 1, 4].wait_recv()
            made[t - 1, 5] = forward(m, part, across, mine, t - 1, 5, at_level)
            made[t - 1, 10] = forward(m, part, across, mine, t - 1, 10, at_core)
            made[t - 1, 3].wait_recv()
            made[t - 1, 9] = forward(m, part, beside, other, t - 1, 9, at_core)
        if 2 <= t:
            m, part = steps[t - 2]
            made[t - 2, 5].wait_recv()
            made[t - 2, 11] = forward(m, part, across, other, t - 2, 11, at_core)
    for k in range(len(steps)):
        for slot in range(6, 12):
            made[k, slot].wait_recv()
    for k in range(len(steps)):
        for slot in range(12):
            made[k, slot].wait_send()
    for one in (stack_lower, stack_upper):
        one.wait_recv()
    for one in (stack_beside, stack_above, stack_lower, stack_upper):
        one.wait_send()
    for one in kept:
        one.wait()


def gather_weights(w_branch, w_input, w_mixer, stack):
    width = w_branch.shape[0]
    if lax.axis_size("group") != 4 or lax.axis_size("replica") % 4 != 0:
        return (lax.all_gather(w_branch, "group", axis=1, tiled=True),
                lax.all_gather(w_input, "group", axis=1, tiled=True),
                lax.all_gather(w_mixer, "group", axis=0, tiled=True),
                lax.all_gather(stack, "group", axis=1, tiled=True))
    units = 4
    anywhere = pl.BlockSpec(memory_space=pl.ANY)
    operands = (w_branch, w_input, w_mixer, stack)
    return pl.pallas_call(
        functools.partial(gather_kernel, units),
        out_shape=[jax.ShapeDtypeStruct((width, width), BF16)] * 3
        + [jax.ShapeDtypeStruct((stack.shape[0], width), BF16)],
        in_specs=[anywhere] * 4,
        out_specs=[anywhere] * 4,
        scratch_shapes=[pltpu.VMEM(operand.shape, BF16) for operand in operands]
        + [pltpu.SemaphoreType.DMA((3 * units + 1, 12)), pltpu.SemaphoreType.DMA((3 * units + 1, 12)),
           pltpu.SemaphoreType.DMA((4,))],
        compiler_params=pltpu.CompilerParams(
            collective_id=0, has_side_effects=True, vmem_limit_bytes=60 * 2**20),
        cost_estimate=pl.CostEstimate(flops=0, bytes_accessed=400 * 2**20, transcendentals=0),
    )(*operands)


def ordered_kernel(*refs):
    del refs


def ordered(value, *earlier):
    return pl.pallas_call(
        ordered_kernel,
        out_shape=jax.ShapeDtypeStruct(value.shape, value.dtype),
        in_specs=[ANYWHERE] * (1 + len(earlier)),
        out_specs=ANYWHERE,
        input_output_aliases={0: 0},
    )(value, *earlier)


def ordered_stack_kernel(count, *refs):
    for i in range(count):
        refs[-1][i] = refs[i][...]


def ordered_stack(values, *earlier):
    vmem = pl.BlockSpec(memory_space=pltpu.VMEM)
    return pl.pallas_call(
        functools.partial(ordered_stack_kernel, len(values)),
        out_shape=jax.ShapeDtypeStruct((len(values),) + values[0].shape, values[0].dtype),
        in_specs=[vmem] * len(values) + [ANYWHERE] * len(earlier),
        out_specs=vmem,
    )(*values, *earlier)


def row_tiles(rows, width, count):
    step = min(rows, 128)
    return (rows // step,), [pl.BlockSpec((step, width), lambda i: (i, 0))] * count


def block_kernel(resid_ref, outward_ref, block_ref):
    block_ref[...] = (resid_ref[...] + outward_ref[...].astype(F32)).astype(BF16)


def block_call(resid, outward):
    rows, width = resid.shape
    grid, tiles = row_tiles(rows, width, 3)
    return pl.pallas_call(
        block_kernel,
        grid=grid,
        out_shape=jax.ShapeDtypeStruct((rows, width), BF16),
        in_specs=tiles[:2],
        out_specs=tiles[2],
        cost_estimate=pl.CostEstimate(flops=rows * width, bytes_accessed=8 * rows * width, transcendentals=0),
    )(resid, outward)


def resid_grad_kernel(resid_ref, cot_ref, gain_ref, grads_ref, *refs):
    full_ref, low_ref = refs[-2:]
    values = resid_ref[...]
    rate = lax.rsqrt(jnp.mean(values * values, axis=-1, keepdims=True) + EPS)
    grads = cot_ref[...].astype(F32) + norm_back(values, gain_ref[...], rate, grads_ref[...].astype(F32))
    full_ref[...] = grads
    low_ref[...] = grads.astype(BF16)


def resid_grad(resid, cot, gain, grads, earlier):
    rows, width = resid.shape
    grid, tiles = row_tiles(rows, width, 5)
    return pl.pallas_call(
        resid_grad_kernel,
        grid=grid,
        out_shape=[jax.ShapeDtypeStruct((rows, width), F32), jax.ShapeDtypeStruct((rows, width), BF16)],
        in_specs=[tiles[0], tiles[0], pl.BlockSpec((1, width), lambda i: (0, 0)), tiles[0]]
        + [ANYWHERE] * len(earlier),
        out_specs=tiles[:2],
        compiler_params=pltpu.CompilerParams(vmem_limit_bytes=40 * 2**20),
        cost_estimate=pl.CostEstimate(
            flops=20 * rows * width, bytes_accessed=14 * rows * width, transcendentals=rows),
    )(resid, cot, gain, grads, *earlier)


def finish_kernel(grad_resid_ref, inputs_ref, gain_ref, grads_ref, out_ref):
    values = inputs_ref[...].astype(F32)
    rate = lax.rsqrt(jnp.mean(values * values, axis=-1, keepdims=True) + EPS)
    out_ref[...] = grad_resid_ref[...] + norm_back(values, gain_ref[...], rate, grads_ref[...])


def finish(grad_resid, inputs, gain, grads):
    rows, width = inputs.shape
    grid, tiles = row_tiles(rows, width, 3)
    return pl.pallas_call(
        finish_kernel,
        grid=grid,
        out_shape=jax.ShapeDtypeStruct((rows, width), F32),
        in_specs=[tiles[0], tiles[0], pl.BlockSpec((1, width), lambda i: (0, 0)), tiles[0]],
        out_specs=tiles[0],
        compiler_params=pltpu.CompilerParams(vmem_limit_bytes=40 * 2**20),
        cost_estimate=pl.CostEstimate(
            flops=20 * rows * width, bytes_accessed=14 * rows * width, transcendentals=rows),
    )(grad_resid, inputs, gain, grads)


def spread_kernel(tables, pieces, ids_ref, from_ref, *refs):
    gots, out_refs = refs[:pieces], refs[-tables:]
    ranks = out_refs[0].shape[1]
    replicas = from_ref.shape[0]
    seqs = ids_ref.shape[0] // replicas
    for table in range(tables):
        out_refs[table][...] = jnp.zeros_like(out_refs[table])
    replica = 0
    for got_ref in gots:
        for at in range(got_ref.shape[0]):
            for s in range(seqs):
                place = ids_ref[from_ref[replica] * seqs + s]
                for table in range(tables):
                    rows = pl.ds((table * seqs + s) * ranks, ranks)
                    out_refs[table][place] += got_ref[at, rows, :].astype(F32)
            replica += 1


def spread(ids, source, gots, tables, sets, seqs, ranks, earlier=()):
    rows, width = gots[0].shape[1:]
    replicas = source.shape[0]
    scalars = pl.BlockSpec(memory_space=pltpu.SMEM)
    return pl.pallas_call(
        functools.partial(spread_kernel, tables, len(gots)),
        out_shape=[jax.ShapeDtypeStruct((sets, ranks, width), F32)] * tables,
        in_specs=[scalars, scalars] + [pl.BlockSpec(memory_space=pltpu.VMEM)] * len(gots)
        + [ANYWHERE] * len(earlier),
        out_specs=[pl.BlockSpec(memory_space=pltpu.VMEM)] * tables,
        compiler_params=pltpu.CompilerParams(vmem_limit_bytes=56 * 2**20),
        cost_estimate=pl.CostEstimate(
            flops=replicas * rows * width,
            bytes_accessed=2 * replicas * rows * width + 4 * tables * sets * ranks * width, transcendentals=0),
    )(ids, source, *gots, *earlier)


def products_kernel(plan, *refs):
    out_ref, row = refs[-1], 0
    for place, (kind, first, last) in plan:
        if kind == "product":
            result = dot(refs[place][:, first:last], refs[place + 1][...], TN)
        else:
            result = refs[place][...]
        count = last - first
        out_ref[row : row + count, :] = result.astype(BF16)
        row += count


def products(items, earlier=(), blocks=1):
    operands, specs, plan, total = [], [], [], 0
    width = items[0][3].shape[-1]
    tile = width // blocks if blocks > 1 and width % (128 * blocks) == 0 else tile_of(width, 512)
    for item in items:
        if len(item) == 1:
            plan.append((len(operands), ("rows", 0, item[0].shape[0])))
            operands.append(item[0])
            specs.append(pl.BlockSpec((item[0].shape[0], tile), lambda i: (0, i)))
        else:
            lhs, first, last, rhs = item
            plan.append((len(operands), ("product", first, last)))
            if isinstance(rhs, tuple):
                rhs, s = rhs
                block = pl.BlockSpec((None, rhs.shape[1], tile), lambda i, s=s: (s, 0, i))
            else:
                block = pl.BlockSpec((rhs.shape[0], tile), lambda i: (0, i))
            operands += [lhs, rhs]
            specs += [resident(lhs), block]
        total += plan[-1][1][2] - plan[-1][1][1]
    cells = sum(operand.size for operand in operands)
    direct = blocks > 1 and tile * blocks == width
    result = pl.pallas_call(
        functools.partial(products_kernel, plan),
        grid=(pl.cdiv(width, tile),),
        out_shape=jax.ShapeDtypeStruct((blocks, total, tile) if direct else (total, width), BF16),
        in_specs=specs + [ANYWHERE] * len(earlier),
        out_specs=(pl.BlockSpec((None, total, tile), lambda i: (i, 0, 0)) if direct
                   else pl.BlockSpec((total, tile), lambda i: (0, i))),
        compiler_params=pltpu.CompilerParams(vmem_limit_bytes=60 * 2**20),
        cost_estimate=pl.CostEstimate(flops=64 * cells, bytes_accessed=2 * cells, transcendentals=0),
    )(*operands, *earlier)
    if blocks > 1 and not direct:
        result = jnp.swapaxes(result.reshape(total, blocks, width // blocks), 0, 1)
    return result


def passed_along(block, axis, distance):
    devices = range(lax.axis_size(axis))
    route = [(i - distance, i) for i in devices if i - distance in devices]
    return lax.ppermute(block, axis, route)


def over_replicas(value, direct, *earlier):
    count, here = lax.axis_size("replica"), lax.axis_index("replica")
    if count % 2:
        return [lax.all_gather(value, "replica")], jnp.arange(count, dtype=jnp.int32)
    steps = jnp.arange(count // 2, dtype=jnp.int32)
    if direct:
        got = ordered_stack([value] + [
            lax.ppermute(value, "replica", [(i, (i + 2 * step) % count) for i in range(count)])
            for step in range(1, count // 2)], *earlier)
        source = (here + count - 2 * steps) % count
    else:
        got = lax.all_gather(value, "replica", axis_index_groups=[list(range(p, count, 2)) for p in range(2)])
        source = here % 2 + 2 * steps
    swapped = lax.ppermute(got, "replica", [(i, i ^ 1) for i in range(count)])
    return [got, swapped], jnp.concatenate([source, source + 1 - 2 * (here % 2)], 0)


def body(
    inputs, segment_ids, adapter_ids, gain_mix, gain_mlp, w_branch, w_input, conv_taps, decay_heads, admit_heads,
    decay_param, w_mixer, w_gate, w_upper, w_down, down_branch, lift_branch, down_input, lift_input, down_decay,
    lift_decay, down_admit, lift_admit, down_mixer, lift_mixer, down_gate, lift_gate, down_upper, lift_upper,
    down_outward, lift_outward, out_grad,
):
    seqs, stretch, width = inputs.shape
    rows = seqs * stretch
    taps = conv_taps.shape[0]
    sets, _, ranks = down_branch.shape
    group, place = lax.axis_size("group"), lax.axis_index("group")
    mask_cols = seqs * ranks

    turned = lambda table: jnp.swapaxes(table, 1, 2)
    stack, own_tables = pick(
        adapter_ids,
        [turned(down_branch), turned(down_input), turned(down_decay), turned(down_admit), turned(down_mixer),
         turned(down_gate), turned(down_upper), lift_branch, lift_input, lift_decay, lift_admit, lift_mixer,
         lift_outward],
        [lift_gate, lift_upper, turned(down_outward)])
    full_branch, full_input, full_mixer, stack = gather_weights(w_branch, w_input, w_mixer, stack)
    (p_down_branch, p_down_input, p_down_decay, p_down_admit, p_down_mixer, p_down_gate, p_down_upper,
     p_lift_branch, p_lift_input, p_lift_decay, p_lift_admit, p_lift_mixer, p_lift_outward) = [
        stack[i * mask_cols : (i + 1) * mask_cols] for i in range(13)]
    own_lift_gate, own_lift_upper, own_down_outward = [
        own_tables[i * mask_cols : (i + 1) * mask_cols] for i in range(3)]
    cotangents = lax.all_gather(ordered(out_grad, stack), "group", axis=1, tiled=True)

    row_seq = lax.broadcasted_iota(jnp.int32, (rows, mask_cols), 0) // stretch
    col_seq = lax.broadcasted_iota(jnp.int32, (rows, mask_cols), 1) // ranks
    own = (row_seq == col_seq).astype(F32)
    own_two = jnp.concatenate([own, own], 1)

    begin = place * stretch
    padded_ids = jnp.pad(segment_ids, ((0, 0), (taps - 1, taps - 1)), constant_values=-1)
    window = lax.dynamic_slice_in_dim(padded_ids, begin, stretch + 2 * (taps - 1), 1)
    current = window[:, taps - 1 : taps - 1 + stretch + taps - 1]
    agree = [
        ((current == window[:, taps - 1 - j : taps - 1 - j + stretch + taps - 1]) & (current >= 0)).astype(F32)
        for j in range(taps)
    ]
    restart = (1.0 - agree[1][:, :stretch]).reshape(rows, 1)

    x_float = inputs.reshape(rows, width).astype(F32)
    normed_f, _ = norm_rows(x_float, gain_mix)
    normed = normed_f.astype(BF16)
    inner_one = (dot(normed, stack[: 2 * mask_cols], NT) * own_two).astype(BF16)
    inner_branch, inner_input = inner_one[:, :mask_cols], inner_one[:, mask_cols:]
    branch_pre = dot(normed, full_branch) + dot(inner_branch, p_lift_branch)
    fed = (dot(normed, full_input) + dot(inner_input, p_lift_input)).astype(BF16)
    fed = fed.reshape(seqs, stretch, width)
    halo = passed_along(fed[:, stretch - (taps - 1) :], "group", 1)
    extended = jnp.concatenate([halo, fed], axis=1).astype(F32)
    convolved = sum(
        conv_taps[j] * agree[j][:, :stretch, None] * extended[:, taps - 1 - j : taps - 1 - j + stretch]
        for j in range(taps)
    ).reshape(rows, width)
    rounded = convolved.astype(BF16)
    softrate = jax.nn.softplus(decay_param).reshape(1, width)
    inner_gates = (dot(rounded, stack[2 * mask_cols : 4 * mask_cols], NT) * own_two).astype(BF16)
    lift_gates = stack[9 * mask_cols : 11 * mask_cols]
    cum, local = forward_gates(seqs, convolved, inner_gates, lift_gates, decay_heads, admit_heads, softrate, restart)
    ends = jnp.concatenate(
        [cum.reshape(seqs, stretch, width)[:, -1], local.reshape(seqs, stretch, width)[:, -1]], 0)
    all_ends = lax.all_gather(ends, "group")
    carried = jnp.zeros((seqs, width), F32)
    for g in range(group - 1):
        longer = all_ends[g, :seqs] * carried + all_ends[g, seqs:]
        carried = jnp.where(g < place, longer, carried)
    carried_rows = jnp.repeat(carried, stretch, axis=0)
    state = local + cum * carried_rows
    merged = (state * gelu(branch_pre)).astype(BF16)
    inner_mixer = (dot(merged, p_down_mixer, NT) * own).astype(BF16)
    mixed = dot(merged, full_mixer) + dot(inner_mixer, p_lift_mixer)
    resid = x_float + mixed
    normed_two_f, _ = norm_rows(resid, gain_mlp)
    normed_two = normed_two_f.astype(BF16).reshape(seqs, stretch, width)

    spans = [slice(s * ranks, (s + 1) * ranks) for s in range(seqs)]
    grad_hiddens, through_out, first_tokens = grad_hidden_call(
        cotangents, w_down, p_lift_outward, own_down_outward, normed_two[0])
    all_tokens = [first_tokens] + [
        lax.all_gather(ordered(normed_two[s], first_tokens), "group", axis=0, tiled=True) for s in range(1, seqs)]
    backs, hiddens, throughs, wides = [], [], [], []
    for s, at in enumerate(spans):
        two_downs = jnp.concatenate([p_down_gate[at], p_down_upper[at]], 0)
        hidden, back, wide, through = feed_call(
            s, all_tokens[s], grad_hiddens, w_gate, w_upper, two_downs, own_lift_gate[at], own_lift_upper[at],
            through_out)
        if s < seqs - 1:
            backs.append(lax.psum_scatter(back, "group", scatter_dimension=0, tiled=True))
        hiddens.append(hidden)
        throughs.append(through)
        wides.append(wide)
    outward, _, early, reduced = outward_call(
        hiddens, all_tokens, throughs, cotangents, w_down, own_down_outward, p_lift_outward, back)
    backs.append(reduced)
    named = jnp.broadcast_to(jnp.pad(adapter_ids, (0, -seqs % 16)).astype(BF16)[:, None], (-(-seqs // 16) * 16,
                                                                                   wides[0].shape[1]))
    wide = jnp.concatenate(
        [wides[s][i * ranks : (i + 1) * ranks] for i in range(3) for s in range(seqs)] + [named], 0)
    grad_normed_two = jnp.concatenate(backs, 0)
    grad_resid, grad_mixed = resid_grad(
        resid, out_grad.reshape(rows, width), gain_mlp.reshape(1, width), grad_normed_two, ())
    outward = lax.psum_scatter(outward, "group", scatter_dimension=1, tiled=True).reshape(rows, width)
    block_out = block_call(resid, outward)

    through_mixer = (dot(grad_mixed, p_lift_mixer, NT) * own).astype(BF16)
    if group == 4 and 2 * seqs <= 8 and stretch % 8 == 0:
        agree_cols = jnp.stack([agree[j][:, j : j + stretch].reshape(rows) for j in range(taps)], 1)
        grad_branch_pre, through_one, through_gates, grad_lift_gates, grad_fed = mixer_back(
            seqs, grad_mixed, full_mixer, through_mixer, p_down_mixer, convolved, inner_gates, lift_gates, decay_heads,
            admit_heads, softrate, restart, cum, local, carried, branch_pre, p_lift_branch, p_lift_input,
            stack[2 * mask_cols : 4 * mask_cols], conv_taps, agree_cols)
    else:
        grad_merged = dot(grad_mixed, full_mixer, NT) + dot(through_mixer, p_down_mixer)
        span, total, firsts, grad_branch_pre = backward_scan(
            seqs, convolved, inner_gates, lift_gates, decay_heads, softrate, restart, cum, local, carried, branch_pre,
            grad_merged)
        all_firsts = lax.all_gather(firsts, "group")
        incoming = jnp.zeros((seqs, width), F32)
        for lap in range(group - 1):
            g = group - 1 - lap
            longer = all_firsts[g, :seqs] * incoming + all_firsts[g, seqs:]
            incoming = jnp.where(g > place, longer, incoming)
        grad_direct, through_gates, grad_lift_gates = backward_gates(
            seqs, convolved, inner_gates, lift_gates, decay_heads, admit_heads, softrate, restart, cum, local, carried,
            span, total, incoming)
        through_gates = (through_gates * own_two).astype(BF16)
        grad_convolved = grad_direct + dot(through_gates, stack[2 * mask_cols : 4 * mask_cols])
        grad_convolved = grad_convolved.reshape(seqs, stretch, width)
        below = passed_along(grad_convolved[:, : taps - 1].astype(BF16), "group", -1).astype(F32)
        grad_extended = jnp.concatenate([grad_convolved, below], axis=1)
        grad_fed = sum(
            conv_taps[j] * agree[j][:, j : j + stretch, None] * grad_extended[:, j : j + stretch] for j in range(taps)
        ).astype(BF16).reshape(rows, width)
        through_branch = (dot(grad_branch_pre, p_lift_branch, NT) * own).astype(BF16)
        through_input = (dot(grad_fed, p_lift_input, NT) * own).astype(BF16)
        through_one = jnp.concatenate([through_branch, through_input], 1)
    grad_normed = (dot(grad_branch_pre, full_branch, NT) + dot(grad_fed, full_input, NT)
                   + dot(through_one, stack[: 2 * mask_cols]))
    grad_inputs = finish(grad_resid, inputs.reshape(rows, width), gain_mix.reshape(1, width), grad_normed)

    all_wide, wide_source = over_replicas(wide, True, through_gates)
    both = 2 * mask_cols
    got_ids = jnp.concatenate([part[:, 3 * mask_cols : 3 * mask_cols + seqs, 0] for part in all_wide], 0)
    in_order = wide_source[:, None] == jnp.arange(wide_source.shape[0], dtype=jnp.int32)[None, :]
    all_ids = jnp.sum(jnp.where(in_order[:, :, None], got_ids.astype(jnp.int32)[:, None, :], 0), 0).reshape(-1)
    partial = products(
        [(through_one, 0, both, normed), (through_gates, 0, both, rounded), (through_mixer, 0, mask_cols, merged),
         (inner_branch, 0, mask_cols, grad_branch_pre), (inner_input, 0, mask_cols, grad_fed), (grad_lift_gates,),
         (inner_mixer, 0, mask_cols, grad_mixed), (early,)], all_wide, group)
    owned = lax.psum_scatter(ordered(partial, outward), "group", scatter_dimension=0, tiled=False)
    wides = spread(all_ids, wide_source, all_wide, 3, sets, seqs, ranks)
    all_owned, owned_source = over_replicas(ordered(owned, grad_normed), False)
    totals = spread(all_ids, owned_source, all_owned, 13, sets, seqs, ranks, (block_out, wides[0], grad_inputs))
    (t_down_branch, t_down_input, t_down_decay, t_down_admit, t_down_mixer, t_lift_branch, t_lift_input, t_lift_decay,
     t_lift_admit, t_lift_mixer, t_down_gate, t_down_upper, t_lift_outward) = totals
    return (
        block_out.reshape(seqs, stretch, width), grad_inputs.reshape(seqs, stretch, width),
        turned(t_down_branch), t_lift_branch, turned(t_down_input), t_lift_input, turned(t_down_decay), t_lift_decay,
        turned(t_down_admit), t_lift_admit, turned(t_down_mixer), t_lift_mixer, turned(t_down_gate), wides[0],
        turned(t_down_upper), wides[1], turned(wides[2]), t_lift_outward,
    )


def solution(mesh):
    tokens = P("replica", "group", None)
    down, lift = P(None, "group", None), P(None, None, "group")
    cols, split = P(None, "group"), P("group", None)
    in_specs = (
        tokens, P("replica", None), P("replica"), P(), P(), cols, cols, P(), P(), P(), P(), split, cols, cols, split,
    ) + (down, lift) * 8 + (tokens,)
    out_specs = (tokens, tokens) + (down, lift) * 8
    return jax.shard_map(body, mesh=mesh, in_specs=in_specs, out_specs=out_specs, check_vma=False)
```

```python
import functools

import jax
import jax.numpy as jnp
from jax import lax
from jax.experimental import pallas as pl
from jax.experimental.pallas import tpu as pltpu
from jax.sharding import PartitionSpec as P

EPS = 1e-06
F32 = jnp.float32
BF16 = jnp.bfloat16
GELU_C = 0.7978845608028654
GELU_A = 0.044715
NT = (((1,), (1,)), ((), ()))
NN = (((1,), (0,)), ((), ()))
TN = (((0,), (0,)), ((), ()))
ANYWHERE = pl.BlockSpec(memory_space=pl.ANY)
VMEM = 62 * 2**20


def dot(a, b, dims=NN):
    return lax.dot_general(a, b, dims, preferred_element_type=F32)


def gelu(v):
    return 0.5 * v * (1.0 + jnp.tanh(GELU_C * (v + GELU_A * v * v * v)))


def gelu_both(v):
    square = v * v
    half = 0.5 + 0.5 * jnp.tanh(v * (GELU_C + GELU_C * GELU_A * square))
    value = v * half
    return value, half + (value - value * half) * (2.0 * GELU_C + 6.0 * GELU_C * GELU_A * square)


def norm_rows(values, gain):
    rate = lax.rsqrt(jnp.mean(values * values, axis=-1, keepdims=True) + EPS)
    return values * rate * gain, rate


def norm_back(values, gain, rate, grads):
    scaled = grads * gain
    along = jnp.mean(scaled * values, axis=-1, keepdims=True)
    return rate * scaled - values * (rate * rate * rate * along)


def rows_shifted(values, by, fill):
    rows, width = values.shape
    if by % 8 == 0:
        return jnp.concatenate([jnp.full((by, width), fill, values.dtype), values[: rows - by]], 0)
    place = lax.broadcasted_iota(jnp.int32, values.shape, 0)
    return jnp.where(place >= by, pltpu.roll(values, by, 0), fill)


def rows_advanced(values, by, fill):
    rows, width = values.shape
    if by % 8 == 0:
        return jnp.concatenate([values[by:], jnp.full((by, width), fill, values.dtype)], 0)
    place = lax.broadcasted_iota(jnp.int32, values.shape, 0)
    return jnp.where(place < rows - by, pltpu.roll(values, rows - by, 0), fill)


def scan_rows(a, b, moved):
    by = 1
    while by < a.shape[0]:
        b = a * moved(b, by, 0.0) + b
        a = a * moved(a, by, 1.0)
        by *= 2
    return a, b


def gate_values(conv, inner, lift, table_d, table_a, softrate, restart):
    rounded = conv.astype(BF16)
    half = lift.shape[0] // 2
    pre_d = dot(rounded, table_d) + dot(inner[:, :half], lift[:half])
    pre_a = dot(rounded, table_a) + dot(inner[:, half:], lift[half:])
    decay_gate = 1.0 / (1.0 + jnp.exp(-pre_d))
    admit_gate = 1.0 / (1.0 + jnp.exp(-pre_a))
    safe = jnp.where(restart, -1.0, -8.0 * decay_gate * softrate)
    grown = jnp.exp(safe)
    scale = jnp.sqrt(jnp.tanh(-safe) * (1.0 + grown * grown))
    return decay_gate, admit_gate, grown, scale


def forward_gates_kernel(seqs, conv_ref, inner_ref, lift_ref, table_d_ref, table_a_ref, soft_ref, restart_ref,
                         cum_ref, local_ref):
    stretch = conv_ref.shape[0] // seqs
    for s in range(seqs):
        rows = pl.ds(s * stretch, stretch)
        conv = conv_ref[rows, :]
        restart = restart_ref[rows, :] > 0.5
        _, admit, grown, scale = gate_values(
            conv, inner_ref[rows, :], lift_ref[...], table_d_ref[0], table_a_ref[0], soft_ref[...], restart)
        decays = jnp.where(restart, 0.0, grown)
        drive = conv * admit * jnp.where(restart, 1.0, scale)
        cum, local = scan_rows(decays, drive, rows_shifted)
        cum_ref[rows, :] = cum
        local_ref[rows, :] = local


def forward_gates(seqs, conv, inner, lift, table_d, table_a, softrate, restart):
    rows, width = conv.shape
    heads, size = table_d.shape[:2]
    tile = pl.BlockSpec((rows, size), lambda h: (0, h))
    table = pl.BlockSpec((1, size, size), lambda h: (h, 0, 0))
    out = jax.ShapeDtypeStruct((rows, width), F32)
    return pl.pallas_call(
        functools.partial(forward_gates_kernel, seqs),
        out_shape=(out, out),
        grid=(heads,),
        in_specs=[
            tile,
            pl.BlockSpec(inner.shape, lambda h: (0, 0)),
            pl.BlockSpec((lift.shape[0], size), lambda h: (0, h)),
            table,
            table,
            pl.BlockSpec((1, size), lambda h: (0, h)),
            pl.BlockSpec(restart.shape, lambda h: (0, 0)),
        ],
        out_specs=(tile, tile),
        compiler_params=pltpu.CompilerParams(vmem_limit_bytes=40 * 2**20),
        cost_estimate=pl.CostEstimate(
            flops=4 * rows * width * size + 60 * rows * width,
            bytes_accessed=12 * rows * width,
            transcendentals=6 * rows * width),
    )(conv, inner, lift, table_d, table_a, softrate, restart)


def backward_scan_kernel(seqs, conv_ref, inner_ref, lift_ref, table_d_ref, soft_ref, restart_ref, cum_ref, local_ref,
                         carried_ref, pre_ref, grad_ref, span_ref, total_ref, first_ref, branch_grad_ref):
    stretch = conv_ref.shape[0] // seqs
    half = lift_ref.shape[0] // 2
    for s in range(seqs):
        rows = pl.ds(s * stretch, stretch)
        restart = restart_ref[rows, :] > 0.5
        rounded = conv_ref[rows, :].astype(BF16)
        pre_d = dot(rounded, table_d_ref[0]) + dot(inner_ref[rows, :half], lift_ref[:half, :])
        grown = jnp.exp(-8.0 * soft_ref[...] / (1.0 + jnp.exp(-pre_d)))
        decays = jnp.where(restart, 0.0, grown)
        state = local_ref[rows, :] + cum_ref[rows, :] * carried_ref[s : s + 1, :]
        value, slope = gelu_both(pre_ref[rows, :])
        grads = grad_ref[rows, :]
        branch_grad_ref[rows, :] = (grads * state * slope).astype(BF16)
        span, total = scan_rows(rows_advanced(decays, 1, 1.0), grads * value, rows_advanced)
        span_ref[rows, :] = span
        total_ref[rows, :] = total
        first_ref[s : s + 1, :] = decays[:1] * span[:1]
        first_ref[seqs + s : seqs + s + 1, :] = decays[:1] * total[:1]


def backward_scan(seqs, conv, inner, lift, table_d, softrate, restart, cum, local, carried, pre, grads):
    rows, width = conv.shape
    heads, size = table_d.shape[:2]
    tile = pl.BlockSpec((rows, size), lambda h: (0, h))
    table = pl.BlockSpec((1, size, size), lambda h: (h, 0, 0))
    out = jax.ShapeDtypeStruct((rows, width), F32)
    return pl.pallas_call(
        functools.partial(backward_scan_kernel, seqs),
        out_shape=(out, out, jax.ShapeDtypeStruct((2 * seqs, width), F32), jax.ShapeDtypeStruct((rows, width), BF16)),
        grid=(heads,),
        in_specs=[
            tile,
            pl.BlockSpec(inner.shape, lambda h: (0, 0)),
            pl.BlockSpec((lift.shape[0], size), lambda h: (0, h)),
            table,
            pl.BlockSpec((1, size), lambda h: (0, h)),
            pl.BlockSpec(restart.shape, lambda h: (0, 0)),
            tile,
            tile,
            pl.BlockSpec((seqs, size), lambda h: (0, h)),
            tile,
            tile,
        ],
        out_specs=(tile, tile, pl.BlockSpec((2 * seqs, size), lambda h: (0, h)), tile),
        compiler_params=pltpu.CompilerParams(vmem_limit_bytes=48 * 2**20),
        cost_estimate=pl.CostEstimate(
            flops=2 * rows * width * size + 80 * rows * width,
            bytes_accessed=30 * rows * width,
            transcendentals=4 * rows * width),
    )(conv, inner, lift, table_d, softrate, restart, cum, local, carried, pre, grads)


def backward_gates_kernel(seqs, conv_ref, inner_ref, lift_ref, table_d_ref, table_a_ref, soft_ref, restart_ref,
                          cum_ref, local_ref, carried_ref, span_ref, total_ref, incoming_ref,
                          conv_grad_ref, through_ref, lift_grad_ref):
    stretch = conv_ref.shape[0] // seqs
    half = lift_ref.shape[0] // 2

    @pl.when(pl.program_id(0) == 0)
    def _():
        through_ref[...] = jnp.zeros_like(through_ref)

    for s in range(seqs):
        rows = pl.ds(s * stretch, stretch)
        conv = conv_ref[rows, :]
        inner = inner_ref[rows, :]
        restart = restart_ref[rows, :] > 0.5
        softrate = soft_ref[...]
        decay_gate, admit, grown, scale = gate_values(
            conv, inner, lift_ref[...], table_d_ref[0], table_a_ref[0], softrate, restart)
        carried = carried_ref[s : s + 1, :]
        state = local_ref[rows, :] + cum_ref[rows, :] * carried
        place = lax.broadcasted_iota(jnp.int32, state.shape, 0)
        before = jnp.where(place >= 1, pltpu.roll(state, 1, 0), carried)
        grads = total_ref[rows, :] + span_ref[rows, :] * incoming_ref[s : s + 1, :]
        driven = grads * jnp.where(restart, 1.0, scale)
        grad_log = jnp.where(
            restart, 0.0, grads * (before * grown - conv * admit * grown * grown / scale))
        grad_d = (-8.0 * softrate) * grad_log * decay_gate * (1.0 - decay_gate)
        grad_a = driven * conv * admit * (1.0 - admit)
        low_d, low_a = grad_d.astype(BF16), grad_a.astype(BF16)
        conv_grad_ref[rows, :] = driven * admit + dot(low_d, table_d_ref[0], NT) + dot(low_a, table_a_ref[0], NT)
        through_ref[rows, :half] += dot(low_d, lift_ref[:half, :], NT)
        through_ref[rows, half:] += dot(low_a, lift_ref[half:, :], NT)
        first = dot(inner[:, :half], low_d, TN)
        second = dot(inner[:, half:], low_a, TN)
        if s == 0:
            lift_grad_ref[:half, :] = first
            lift_grad_ref[half:, :] = second
        else:
            lift_grad_ref[:half, :] += first
            lift_grad_ref[half:, :] += second


def backward_gates(seqs, conv, inner, lift, table_d, table_a, softrate, restart, cum, local, carried, span, total,
                   incoming):
    rows, width = conv.shape
    heads, size = table_d.shape[:2]
    tile = pl.BlockSpec((rows, size), lambda h: (0, h))
    table = pl.BlockSpec((1, size, size), lambda h: (h, 0, 0))
    edge = pl.BlockSpec((seqs, size), lambda h: (0, h))
    ranks = pl.BlockSpec((lift.shape[0], size), lambda h: (0, h))
    return pl.pallas_call(
        functools.partial(backward_gates_kernel, seqs),
        out_shape=(
            jax.ShapeDtypeStruct((rows, width), F32),
            jax.ShapeDtypeStruct(inner.shape, F32),
            jax.ShapeDtypeStruct(lift.shape, F32),
        ),
        grid=(heads,),
        in_specs=[
            tile,
            pl.BlockSpec(inner.shape, lambda h: (0, 0)),
            ranks,
            table,
            table,
            pl.BlockSpec((1, size), lambda h: (0, h)),
            pl.BlockSpec(restart.shape, lambda h: (0, 0)),
            tile,
            tile,
            edge,
            tile,
            tile,
            edge,
        ],
        out_specs=(tile, pl.BlockSpec(inner.shape, lambda h: (0, 0)), ranks),
        compiler_params=pltpu.CompilerParams(vmem_limit_bytes=48 * 2**20),
        cost_estimate=pl.CostEstimate(
            flops=8 * rows * width * size + 80 * rows * width,
            bytes_accessed=24 * rows * width,
            transcendentals=6 * rows * width),
    )(conv, inner, lift, table_d, table_a, softrate, restart, cum, local, carried, span, total, incoming)


def sequence_mask(rows, cols, seqs):
    row = lax.broadcasted_iota(jnp.int32, (rows, cols), 0) // (rows // seqs)
    col = lax.broadcasted_iota(jnp.int32, (rows, cols), 1) % (cols // 2) // (cols // 2 // seqs)
    return (row == col).astype(F32)


def mixer_back_kernel(
    seqs, heads, mixed_ref, w_ref, lift_mixer_ref, down_mixer_ref, conv_ref, inner_ref, lift_ref, table_d_ref,
    table_a_ref, soft_ref, restart_ref, cum_ref, local_ref, carried_ref, pre_ref, lift_branch_ref, lift_input_ref,
    down_gates_ref, taps_ref, agree_ref,
    branch_grad_ref, through_one_ref, through_gates_ref, lift_grad_ref, fed_grad_ref, thr_mixer_ref,
    span_ref, total_ref, ends_ref, all_ends_ref, incoming_ref, halo_ref, below_ref, one_ref, gates_ref, send, recv,
):
    rows, size = conv_ref.shape
    stretch = rows // seqs
    half = lift_ref.shape[0] // 2
    ranks = lift_branch_ref.shape[0]
    step = pl.program_id(0)
    group, replica = lax.axis_index("group"), lax.axis_index("replica")
    partners = [(group + 1 - 2 * (group % 2), replica), ((group + 2) % 4, replica), (3 - group, replica)]

    def copy(src, dst, slot, partner):
        return pltpu.make_async_remote_copy(
            src_ref=src, dst_ref=dst, send_sem=send.at[slot], recv_sem=recv.at[slot], device_id=partner,
            device_id_type=pl.DeviceIdType.MESH)

    exchange = [copy(ends_ref, all_ends_ref.at[group], slot, partner) for slot, partner in enumerate(partners)]
    downward = copy(halo_ref, below_ref, 3, ((group + 3) % 4, replica))

    @pl.when(step == 0)
    def _():
        barrier = pltpu.get_barrier_semaphore()
        for partner in partners:
            pl.semaphore_signal(barrier, inc=1, device_id=partner, device_id_type=pl.DeviceIdType.MESH)
        pl.semaphore_wait(barrier, 3)
        one_ref[...] = jnp.zeros_like(one_ref)
        gates_ref[...] = jnp.zeros_like(gates_ref)
        ends_ref[...] = jnp.zeros_like(ends_ref)
        row = lax.broadcasted_iota(jnp.int32, thr_mixer_ref.shape, 0) // stretch
        col = lax.broadcasted_iota(jnp.int32, thr_mixer_ref.shape, 1) // (thr_mixer_ref.shape[1] // seqs)
        through = dot(mixed_ref[...], lift_mixer_ref[...], NT)
        thr_mixer_ref[...] = jnp.where(row == col, through, 0.0).astype(BF16)

    @pl.when(step < heads)
    def _():
        cols = pl.ds(pl.multiple_of(step * size, size), size)
        merged = dot(mixed_ref[...], w_ref[...], NT) + dot(thr_mixer_ref[...], down_mixer_ref[...])
        for s in range(seqs):
            at = slice(s * stretch, (s + 1) * stretch)
            restart = restart_ref[at, :] > 0.5
            rounded = conv_ref[at, :].astype(BF16)
            pre_d = dot(rounded, table_d_ref[0]) + dot(inner_ref[at, :half], lift_ref[:half, :])
            grown = jnp.exp(-8.0 * soft_ref[...] / (1.0 + jnp.exp(-pre_d)))
            decays = jnp.where(restart, 0.0, grown)
            state = local_ref[at, :] + cum_ref[at, :] * carried_ref[s : s + 1, :]
            value, slope = gelu_both(pre_ref[at, :])
            grads = merged[at, :]
            low = (grads * state * slope).astype(BF16)
            branch_grad_ref[at, :] = low
            one_ref[at, :ranks] += dot(low, lift_branch_ref[...], NT)
            span, total = scan_rows(rows_advanced(decays, 1, 1.0), grads * value, rows_advanced)
            span_ref[step, at, :] = span
            total_ref[step, at, :] = total
            ends_ref[s : s + 1, cols] = decays[:1] * span[:1]
            ends_ref[seqs + s : seqs + s + 1, cols] = decays[:1] * total[:1]

    @pl.when(step == heads - 1)
    def _():
        for one in exchange:
            one.start()

    @pl.when(step == heads)
    def _():
        for one in exchange:
            one.wait_recv()
        incoming = jnp.zeros(incoming_ref.shape, F32)
        for g in (3, 2, 1):
            longer = all_ends_ref[g, :seqs, :] * incoming + all_ends_ref[g, seqs : 2 * seqs, :]
            incoming = jnp.where(group < g, longer, incoming)
        incoming_ref[...] = incoming

    @pl.when((step >= heads) & (step < 2 * heads))
    def _():
        head = step - heads
        cols = pl.ds(pl.multiple_of(head * size, size), size)
        softrate = soft_ref[...]
        for s in range(seqs):
            at = slice(s * stretch, (s + 1) * stretch)
            conv, inner = conv_ref[at, :], inner_ref[at, :]
            restart = restart_ref[at, :] > 0.5
            decay_gate, admit, grown, scale = gate_values(
                conv, inner, lift_ref[...], table_d_ref[0], table_a_ref[0], softrate, restart)
            carried = carried_ref[s : s + 1, :]
            state = local_ref[at, :] + cum_ref[at, :] * carried
            place = lax.broadcasted_iota(jnp.int32, state.shape, 0)
            before = jnp.where(place >= 1, pltpu.roll(state, 1, 0), carried)
            grads = total_ref[head, at, :] + span_ref[head, at, :] * incoming_ref[s : s + 1, cols]
            driven = grads * jnp.where(restart, 1.0, scale)
            grad_log = jnp.where(
                restart, 0.0, grads * (before * grown - conv * admit * grown * grown / scale))
            grad_d = (-8.0 * softrate) * grad_log * decay_gate * (1.0 - decay_gate)
            grad_a = driven * conv * admit * (1.0 - admit)
            low_d, low_a = grad_d.astype(BF16), grad_a.astype(BF16)
            total_ref[head, at, :] = (
                driven * admit + dot(low_d, table_d_ref[0], NT) + dot(low_a, table_a_ref[0], NT))
            gates_ref[at, :half] += dot(low_d, lift_ref[:half, :], NT)
            gates_ref[at, half:] += dot(low_a, lift_ref[half:, :], NT)
            first = dot(inner[:, :half], low_d, TN)
            second = dot(inner[:, half:], low_a, TN)
            if s == 0:
                lift_grad_ref[:half, :] = first
                lift_grad_ref[half:, :] = second
            else:
                lift_grad_ref[:half, :] += first
                lift_grad_ref[half:, :] += second

    @pl.when(step == 2 * heads)
    def _():
        through_gates_ref[...] = (gates_ref[...] * sequence_mask(rows, 2 * half, seqs)).astype(BF16)
        tops = []
        for s in range(seqs):
            top = slice(s * stretch, s * stretch + 8)
            direct = jnp.concatenate([total_ref[h, top, :] for h in range(heads)], 1)
            tops.append(direct + dot(through_gates_ref[top, :], down_gates_ref[...]))
        halo_ref[...] = jnp.concatenate(tops, 0).astype(BF16)
        downward.start()
        downward.wait_recv()

    @pl.when(step >= 2 * heads)
    def _():
        head = step - 2 * heads
        cols = pl.ds(pl.multiple_of(head * size, size), size)
        grads = total_ref[head] + dot(through_gates_ref[...], down_gates_ref[:, cols])
        for s in range(seqs):
            at = slice(s * stretch, (s + 1) * stretch)
            longer = jnp.concatenate([grads[at, :], below_ref[s * 8 : (s + 1) * 8, cols].astype(F32)], 0)
            total = taps_ref[0:1, :] * agree_ref[at, 0:1] * grads[at, :]
            for j in range(1, taps_ref.shape[0]):
                moved = pltpu.roll(longer, stretch + 8 - j, 0)[:stretch]
                total += taps_ref[j : j + 1, :] * agree_ref[at, j : j + 1] * moved
            low = total.astype(BF16)
            fed_grad_ref[at, :] = low
            one_ref[at, ranks:] += dot(low, lift_input_ref[...], NT)

    @pl.when(step == 3 * heads - 1)
    def _():
        through_one_ref[...] = (one_ref[...] * sequence_mask(rows, 2 * ranks, seqs)).astype(BF16)
        for one in exchange:
            one.wait_send()
        downward.wait_send()


def mixer_back(seqs, mixed, w_mixer, lift_mixer, down_mixer, conv, inner, lift, table_d, table_a, softrate, restart,
               cum, local, carried, pre, lift_branch, lift_input, down_gates, taps, agree):
    rows, width = conv.shape
    heads, size = table_d.shape[:2]
    first = lambda i: jnp.minimum(i, heads - 1)
    second = lambda i: jnp.clip(i - heads, 0, heads - 1)
    third = lambda i: jnp.maximum(i - 2 * heads, 0)
    either = lambda i: jnp.minimum(i, 2 * heads - 1) % heads
    full = lambda array: pl.BlockSpec(array.shape, lambda i: (0, 0), pipeline_mode=pl.Buffered(1))
    cols = lambda array, at: pl.BlockSpec((array.shape[0], size), lambda i: (0, at(i)))
    table = pl.BlockSpec((1, size, size), lambda i: (either(i), 0, 0))
    middle = inner.shape[1]
    tile = lambda at: pl.BlockSpec((rows, size), lambda i: (0, at(i)))
    whole = lambda count: pl.BlockSpec((rows, count), lambda i: (0, 0))
    return pl.pallas_call(
        functools.partial(mixer_back_kernel, seqs, heads),
        grid=(3 * heads,),
        out_shape=[
            jax.ShapeDtypeStruct((rows, width), BF16),
            jax.ShapeDtypeStruct((rows, 2 * lift_branch.shape[0]), BF16),
            jax.ShapeDtypeStruct((rows, middle), BF16),
            jax.ShapeDtypeStruct(lift.shape, F32),
            jax.ShapeDtypeStruct((rows, width), BF16),
            jax.ShapeDtypeStruct((rows, lift_mixer.shape[0]), BF16),
        ],
        in_specs=[
            full(mixed), pl.BlockSpec((size, width), lambda i: (first(i), 0)), full(lift_mixer), cols(down_mixer, first),
            cols(conv, either), full(inner), cols(lift, either), table, table, cols(softrate, either), full(restart),
            cols(cum, either), cols(local, either), cols(carried, either), cols(pre, first), cols(lift_branch, first),
            cols(lift_input, third), full(down_gates), cols(taps, third), full(agree),
        ],
        out_specs=[tile(first), whole(2 * lift_branch.shape[0]), whole(middle),
                   pl.BlockSpec((lift.shape[0], size), lambda i: (0, second(i))), tile(third),
                   whole(lift_mixer.shape[0])],
        scratch_shapes=[
            pltpu.VMEM((heads, rows, size), F32), pltpu.VMEM((heads, rows, size), F32), pltpu.VMEM((8, width), F32),
            pltpu.VMEM((4, 8, width), F32), pltpu.VMEM((seqs, width), F32), pltpu.VMEM((8 * seqs, width), BF16),
            pltpu.VMEM((8 * seqs, width), BF16), pltpu.VMEM((rows, 2 * lift_branch.shape[0]), F32),
            pltpu.VMEM((rows, middle), F32), pltpu.SemaphoreType.DMA((4,)), pltpu.SemaphoreType.DMA((4,))],
        compiler_params=pltpu.CompilerParams(
            vmem_limit_bytes=VMEM, collective_id=3, has_side_effects=True),
        cost_estimate=pl.CostEstimate(
            flops=2 * rows * width * width + 20 * rows * width * size + 200 * rows * width,
            bytes_accessed=40 * rows * width + 2 * width * width, transcendentals=12 * rows * width),
    )(mixed, w_mixer, lift_mixer, down_mixer, conv, inner, lift, table_d, table_a, softrate, restart, cum, local,
      carried, pre, lift_branch, lift_input, down_gates, taps, agree)


def resident(array):
    return pl.BlockSpec(array.shape, lambda i: (0, 0), pipeline_mode=pl.Buffered(1))


def tile_of(count, tile):
    return tile if count % 128 == 0 and count > tile else count


def grad_hidden_kernel(seqs, gather, steps, *refs):
    if gather:
        cot_ref, wd_ref, lift_out_ref, do_ref, block_ref, out_ref, through_ref, all_ref = refs[:8]
        staged_ref, send, recv, local = refs[8:]
    else:
        cot_ref, wd_ref, lift_out_ref, do_ref, out_ref, through_ref = refs
    ranks = do_ref.shape[0] // seqs
    step = pl.program_id(0)

    if gather:
        group, replica = lax.axis_index("group"), lax.axis_index("replica")
        beside, above = group + 1 - 2 * (group % 2), (group + 2) % 4
        at_beside, at_above = (beside, replica), (above, replica)
        rows = block_ref.shape[0]
        half = rows // 2

        def place(owner, part):
            return all_ref.at[pl.ds(pl.multiple_of(owner * rows + part * half, half), half), :]

        def own(part):
            return block_ref.at[pl.ds(part * half, half), :]

        def copy(src, dst, slot, partner):
            return pltpu.make_async_remote_copy(
                src_ref=src, dst_ref=dst, send_sem=send.at[slot], recv_sem=recv.at[slot], device_id=partner,
                device_id_type=pl.DeviceIdType.MESH)

        firsts = [copy(own(1), place(group, 1), 0, at_beside), copy(own(0), place(group, 0), 1, at_above),
                  copy(own(0), place(group, 0), 2, at_beside), copy(own(1), place(group, 1), 3, at_above)]
        seconds = [copy(place(beside, 1), place(beside, 1), 4, at_above),
                   copy(place(above, 0), place(above, 0), 5, at_beside)]
        stage = pltpu.make_async_copy(block_ref, staged_ref, local.at[0])
        keep = pltpu.make_async_copy(
            staged_ref, all_ref.at[pl.ds(pl.multiple_of(group * rows, rows), rows), :], local.at[1])

        @pl.when(step == 0)
        def _():
            barrier = pltpu.get_barrier_semaphore()
            for partner in (at_beside, at_above):
                pl.semaphore_signal(barrier, inc=1, device_id=partner, device_id_type=pl.DeviceIdType.MESH)
            pl.semaphore_wait(barrier, 2)
            for one in firsts[:2]:
                one.start()
            stage.start()

    @pl.when(step == 0)
    def _():
        for s in range(seqs):
            through_ref[s] = dot(cot_ref[s], lift_out_ref[s * ranks : (s + 1) * ranks, :], NT).astype(BF16)

    for s in range(seqs):
        out_ref[s] = (dot(cot_ref[s], wd_ref[...], NT)
                      + dot(through_ref[s], do_ref[s * ranks : (s + 1) * ranks, :])).astype(BF16)

    if gather:
        @pl.when(step == 0)
        def _():
            stage.wait()
            keep.start()
            for one in firsts[2:]:
                one.start()

        @pl.when(step == min(1, steps - 1))
        def _():
            for one, then in zip(firsts[:2], seconds):
                one.wait_recv()
                then.start()

        @pl.when(step == steps - 1)
        def _():
            for one in firsts[2:] + seconds:
                one.wait_recv()
            for one in firsts + seconds:
                one.wait_send()
            keep.wait()


def grad_hidden_call(cot, wd, lift_out, do, block):
    seqs, rows, width = cot.shape
    units, ranks = wd.shape[0], do.shape[0] // seqs
    tile = tile_of(units, 512)
    gather = lax.axis_size("group") == 4
    got = pl.pallas_call(
        functools.partial(grad_hidden_kernel, seqs, gather, pl.cdiv(units, tile)),
        grid=(pl.cdiv(units, tile),),
        out_shape=[jax.ShapeDtypeStruct((seqs, rows, units), BF16), jax.ShapeDtypeStruct((seqs, rows, ranks), BF16)]
        + [jax.ShapeDtypeStruct((rows, width), BF16)] * gather,
        in_specs=[pl.BlockSpec(cot.shape, lambda i: (0, 0, 0), pipeline_mode=pl.Buffered(1)),
                  pl.BlockSpec((tile, width), lambda i: (i, 0)), resident(lift_out),
                  pl.BlockSpec((seqs * ranks, tile), lambda i: (0, i))] + [ANYWHERE] * gather,
        out_specs=[pl.BlockSpec((seqs, rows, tile), lambda i: (0, 0, i)),
                   pl.BlockSpec((seqs, rows, ranks), lambda i: (0, 0, 0))] + [ANYWHERE] * gather,
        scratch_shapes=[pltpu.VMEM(block.shape, BF16), pltpu.SemaphoreType.DMA((6,)), pltpu.SemaphoreType.DMA((6,)),
                        pltpu.SemaphoreType.DMA((2,))] if gather else [],
        compiler_params=pltpu.CompilerParams(
            vmem_limit_bytes=VMEM, **(dict(collective_id=1, has_side_effects=True) if gather else {})),
        cost_estimate=pl.CostEstimate(
            flops=2 * seqs * rows * width * units,
            bytes_accessed=2 * width * units + 2 * seqs * rows * (units + width), transcendentals=0),
    )(cot, wd, lift_out, do, *([block] if gather else []))
    return got if gather else list(got) + [lax.all_gather(block, "group", axis=0, tiled=True)]


def feed_kernel(steps, tile, units, tok_ref, gh_ref, wg_ref, wu_ref, wg_rows_ref, wu_rows_ref, down_ref, lg_ref,
                lu_ref, through_out_ref, lg_full_ref, lu_full_ref, down_cols_ref, *refs):
    hidden_ref, back_ref, wide_ref, through_ref, inner_ref, gg_ref, gu_ref = refs[-7:]
    ranks = lg_ref.shape[0]
    step = pl.program_id(0)

    @pl.when(step == 0)
    def _():
        inner_ref[...] = dot(tok_ref[...], down_ref[...], NT).astype(BF16)

    @pl.when(step < steps)
    def _():
        tokens, inner = tok_ref[...], inner_ref[...]
        gate = dot(tokens, wg_ref[...]) + dot(inner[:, :ranks], lg_ref[...])
        upper = dot(tokens, wu_ref[...]) + dot(inner[:, ranks:], lu_ref[...])
        grad_hidden = gh_ref[...].astype(F32)
        value, slope = gelu_both(gate)
        hidden = (value * upper).astype(BF16)
        grad_gate = (grad_hidden * upper * slope).astype(BF16)
        grad_upper = (grad_hidden * value).astype(BF16)
        hidden_ref[...] = hidden
        cols = pl.ds(pl.multiple_of(step * tile, tile), tile) if steps > 1 else slice(0, tile)
        gg_ref[:, cols] = grad_gate
        gu_ref[:, cols] = grad_upper
        wide_ref[:ranks, :] = dot(inner[:, :ranks], grad_gate, TN).astype(BF16)
        wide_ref[ranks : 2 * ranks, :] = dot(inner[:, ranks:], grad_upper, TN).astype(BF16)
        wide_ref[2 * ranks :, :] = dot(through_out_ref[...], hidden, TN).astype(BF16)

    @pl.when(step == steps)
    def _():
        through_ref[:, :ranks] = dot(gg_ref[:, :units], lg_full_ref[...], NT).astype(BF16)
        through_ref[:, ranks:] = dot(gu_ref[:, :units], lu_full_ref[...], NT).astype(BF16)

    @pl.when(step >= steps)
    def _():
        back_ref[...] = (dot(gg_ref[:, :units], wg_rows_ref[...], NT) + dot(gu_ref[:, :units], wu_rows_ref[...], NT)
                         + dot(through_ref[...], down_cols_ref[...])).astype(BF16)


def feed_call(s, tok, gh, wg, wu, down, lg, lu, through_out):
    rows, width = tok.shape
    units, ranks = wg.shape[1], lg.shape[0]
    tile, span = tile_of(units, 512), tile_of(width, 512)
    steps, laps = pl.cdiv(units, tile), pl.cdiv(width, span)
    first = lambda i: jnp.minimum(i, steps - 1)
    second = lambda i: jnp.maximum(i - steps, 0)
    cols = pl.BlockSpec((width, tile), lambda i: (0, first(i)))
    across = pl.BlockSpec((span, units), lambda i: (second(i), 0))
    rank = pl.BlockSpec((ranks, tile), lambda i: (0, first(i)))
    out = pl.BlockSpec((rows, tile), lambda i: (0, first(i)))
    return pl.pallas_call(
        functools.partial(feed_kernel, steps, tile, units),
        grid=(steps + laps,),
        out_shape=[jax.ShapeDtypeStruct((rows, units), BF16), jax.ShapeDtypeStruct((rows, width), BF16),
                   jax.ShapeDtypeStruct((3 * ranks, units), BF16), jax.ShapeDtypeStruct((rows, 2 * ranks), BF16)],
        in_specs=[resident(tok), pl.BlockSpec((None, rows, tile), lambda i: (s, 0, first(i))), cols, cols, across,
                  across, resident(down), rank, rank, pl.BlockSpec((None, rows, ranks), lambda i: (s, 0, 0)),
                  resident(lg), resident(lu), pl.BlockSpec((2 * ranks, span), lambda i: (0, second(i)))],
        out_specs=[out, pl.BlockSpec((rows, span), lambda i: (0, second(i))),
                   pl.BlockSpec((3 * ranks, tile), lambda i: (0, first(i))),
                   pl.BlockSpec((rows, 2 * ranks), lambda i: (0, 0))],
        scratch_shapes=[pltpu.VMEM((rows, 2 * ranks), BF16), pltpu.VMEM((rows, steps * tile), BF16),
                        pltpu.VMEM((rows, steps * tile), BF16)],
        compiler_params=pltpu.CompilerParams(vmem_limit_bytes=VMEM),
        cost_estimate=pl.CostEstimate(
            flops=8 * rows * width * units, bytes_accessed=8 * width * units + 6 * rows * units,
            transcendentals=rows * units),
    )(tok, gh, wg, wu, wg, wu, down, lg, lu, through_out, lg, lu, down)


def outward_kernel(seqs, reduce, steps, *refs):
    hiddens, tokens, throughs, cot_ref, refs = (
        refs[:seqs], refs[seqs : 2 * seqs], refs[2 * seqs : 3 * seqs], refs[3 * seqs], refs[3 * seqs + 1 :])
    if reduce:
        wd_ref, do_ref, lift_out_ref, back_ref, out_ref, inner_ref, early_ref, sum_ref = refs[:8]
        first_a, first_b, second_a, second_b, pass_a, pass_b, own_ref, send, recv, local = refs[8:]
    else:
        wd_ref, do_ref, lift_out_ref, out_ref, inner_ref, early_ref = refs
    ranks = do_ref.shape[0] // seqs
    step = pl.program_id(0)

    if reduce:
        group, replica = lax.axis_index("group"), lax.axis_index("replica")
        beside, above, across = group + 1 - 2 * (group % 2), (group + 2) % 4, 3 - group
        at_beside, at_above = (beside, replica), (above, replica)
        rows, width = own_ref.shape
        half = width // 2

        def part(owner, side):
            return back_ref.at[pl.ds(pl.multiple_of(owner * rows, rows), rows), pl.ds(side * half, half)]

        def copy(src, dst, slot, partner):
            return pltpu.make_async_remote_copy(
                src_ref=src, dst_ref=dst, send_sem=send.at[slot], recv_sem=recv.at[slot], device_id=partner,
                device_id_type=pl.DeviceIdType.MESH)

        firsts = [copy(part(across, 0), first_a.at[1], 0, at_beside), copy(part(across, 1), first_b.at[1], 1, at_above),
                  copy(part(beside, 0), first_a.at[0], 2, at_beside), copy(part(above, 1), first_b.at[0], 3, at_above)]
        seconds = [copy(pass_a, second_a, 4, at_above), copy(pass_b, second_b, 5, at_beside)]
        loads = [pltpu.make_async_copy(part(above, 0), pass_a, local.at[0]),
                 pltpu.make_async_copy(part(beside, 1), pass_b, local.at[1]),
                 pltpu.make_async_copy(
                     back_ref.at[pl.ds(pl.multiple_of(group * rows, rows), rows), :], own_ref, local.at[2])]

        @pl.when(step == 0)
        def _():
            barrier = pltpu.get_barrier_semaphore()
            for partner in (at_beside, at_above):
                pl.semaphore_signal(barrier, inc=1, device_id=partner, device_id_type=pl.DeviceIdType.MESH)
            pl.semaphore_wait(barrier, 2)
            for one in firsts:
                one.start()
            for one in loads:
                one.start()

    @pl.when(step == 0)
    def _():
        for s, hidden_ref in enumerate(hiddens):
            inner_ref[s] = dot(hidden_ref[...], do_ref[s * ranks : (s + 1) * ranks, :], NT).astype(BF16)

    for s, hidden_ref in enumerate(hiddens):
        out_ref[s] = (dot(hidden_ref[...], wd_ref[...])
                      + dot(inner_ref[s], lift_out_ref[s * ranks : (s + 1) * ranks, :])).astype(BF16)
        both = dot(throughs[s][...], tokens[s][...], TN).astype(BF16)
        for kind, rows_of in enumerate((both[:ranks], both[ranks:], dot(inner_ref[s], cot_ref[s], TN).astype(BF16))):
            row = (kind * seqs + s) * ranks
            early_ref[row : row + ranks, :] = rows_of

    if reduce:
        @pl.when(step == max(steps - 2, 0))
        def _():
            for one in loads:
                one.wait()
            for one in firsts:
                one.wait_recv()
            pass_a[...] = (pass_a[...].astype(F32) + first_a[1].astype(F32)).astype(BF16)
            pass_b[...] = (pass_b[...].astype(F32) + first_b[1].astype(F32)).astype(BF16)
            for one in seconds:
                one.start()

        @pl.when(step == steps - 1)
        def _():
            for one in seconds:
                one.wait_recv()
            sum_ref[:, :half] = (own_ref[:, :half].astype(F32) + first_a[0].astype(F32)
                                 + second_a[...].astype(F32)).astype(BF16)
            sum_ref[:, half:] = (own_ref[:, half:].astype(F32) + first_b[0].astype(F32)
                                 + second_b[...].astype(F32)).astype(BF16)
            for one in firsts + seconds:
                one.wait_send()


def outward_call(hiddens, tokens, throughs, cot, wd, do, lift_out, back):
    rows, units = hiddens[0].shape
    seqs = len(hiddens)
    width, ranks = wd.shape[1], do.shape[0] // seqs
    tile = tile_of(width, 512)
    steps = pl.cdiv(width, tile)
    group = lax.axis_size("group")
    reduce = group == 4 and width % 256 == 0
    own, half = rows // group, width // 2
    scratch = [pltpu.VMEM((2, own, half), BF16)] * 2 + [pltpu.VMEM((own, half), BF16)] * 4 + [
        pltpu.VMEM((own, width), BF16), pltpu.SemaphoreType.DMA((6,)), pltpu.SemaphoreType.DMA((6,)),
        pltpu.SemaphoreType.DMA((3,))]
    got = pl.pallas_call(
        functools.partial(outward_kernel, seqs, reduce, steps),
        grid=(steps,),
        out_shape=[jax.ShapeDtypeStruct((seqs, rows, width), BF16), jax.ShapeDtypeStruct((seqs, rows, ranks), BF16),
                   jax.ShapeDtypeStruct((3 * seqs * ranks, width), BF16)]
        + [jax.ShapeDtypeStruct((own, width), BF16)] * reduce,
        in_specs=[resident(hidden) for hidden in hiddens] + [pl.BlockSpec((rows, tile), lambda i: (0, i))] * seqs
        + [resident(through) for through in throughs] + [pl.BlockSpec((seqs, rows, tile), lambda i: (0, 0, i))]
        + [pl.BlockSpec((units, tile), lambda i: (0, i)), resident(do),
           pl.BlockSpec((seqs * ranks, tile), lambda i: (0, i))] + [ANYWHERE] * reduce,
        out_specs=[pl.BlockSpec((seqs, rows, tile), lambda i: (0, 0, i)),
                   pl.BlockSpec((seqs, rows, ranks), lambda i: (0, 0, 0)),
                   pl.BlockSpec((3 * seqs * ranks, tile), lambda i: (0, i))]
        + [pl.BlockSpec((own, width), lambda i: (0, 0))] * reduce,
        scratch_shapes=scratch if reduce else [],
        compiler_params=pltpu.CompilerParams(
            vmem_limit_bytes=VMEM, **(dict(collective_id=2, has_side_effects=True) if reduce else {})),
        cost_estimate=pl.CostEstimate(
            flops=2 * seqs * rows * width * units,
            bytes_accessed=2 * width * units + 2 * seqs * rows * (units + width), transcendentals=0),
    )(*hiddens, *tokens, *throughs, cot, wd, do, lift_out, *([back] if reduce else []))
    return got if reduce else list(got) + [lax.psum_scatter(back, "group", scatter_dimension=0, tiled=True)]


def pick_kernel(counts, ids_ref, *refs):
    tables, (stack_ref, wide_ref) = refs[: sum(counts)], refs[sum(counts) :]
    for i, table in enumerate(tables):
        if i < counts[0]:
            stack_ref[i, 0] = table[0]
        else:
            wide_ref[i - counts[0], 0] = table[0]


def pick(ids, narrow, wide):
    seqs, ranks = ids.shape[0], narrow[0].shape[1]
    counts = (len(narrow), len(wide))
    widths = (narrow[0].shape[2], wide[0].shape[2])
    tables = [pl.BlockSpec((1, ranks, table.shape[2]), lambda s, ids: (ids[s], 0, 0)) for table in narrow + wide]
    picked = pl.pallas_call(
        functools.partial(pick_kernel, counts),
        out_shape=[jax.ShapeDtypeStruct((count, seqs, ranks, width), BF16) for count, width in zip(counts, widths)],
        grid_spec=pltpu.PrefetchScalarGridSpec(
            num_scalar_prefetch=1,
            grid=(seqs,),
            in_specs=tables,
            out_specs=[pl.BlockSpec((count, 1, ranks, width), lambda s, ids: (0, s, 0, 0))
                       for count, width in zip(counts, widths)],
        ),
    )(ids, *narrow, *wide)
    return [part.reshape(-1, part.shape[-1]) for part in picked]


def gather_kernel(units, *refs):
    weights, passed, wholes, handed_out = refs[:4], refs[4], refs[5:9], refs[9]
    staged, handed, (send, recv, local) = refs[10:14], refs[14], refs[15:]
    group, replica = lax.axis_index("group"), lax.axis_index("replica")
    beside, above, across = group + 1 - 2 * (group % 2), (group + 2) % 4, 3 - group
    core, level = replica % 2, (replica // 2) % 2
    at_beside, at_above = (beside, replica), (above, replica)
    at_core, at_level = (group, replica + 1 - 2 * core), (group, replica + 2 - 4 * level)
    partners = (at_beside, at_above, at_core, at_level)
    mine, other = 2 * core + level, 2 * core + 1 - level

    barrier = pltpu.get_barrier_semaphore()
    for partner in partners:
        pl.semaphore_signal(barrier, inc=1, device_id=partner, device_id_type=pl.DeviceIdType.MESH)
    pl.semaphore_wait(barrier, 4)

    kept = [pltpu.make_async_copy(weight, stage, local.at[m])
            for m, (weight, stage) in enumerate(zip(weights, staged))]
    for one in kept:
        one.start()

    def keep(m):
        whole = wholes[m]
        rows, cols = weights[m].shape
        if m == 2:
            into = whole.at[pl.ds(pl.multiple_of(group * rows, rows), rows), :]
        else:
            into = whole.at[:, pl.ds(pl.multiple_of(group * cols, cols), cols)]
        kept[m].wait()
        kept[m] = pltpu.make_async_copy(staged[m], into, local.at[m])
        kept[m].start()

    def own(m, part, quarter):
        weight = weights[m]
        size = wholes[m].shape[0] // 4
        step = size // units
        if m < 2:
            return weight.at[pl.ds(pl.multiple_of(quarter * size + part * step, step), step), :]
        return weight.at[pl.ds(part * step, step), pl.ds(pl.multiple_of(quarter * size, size), size)]

    def piece(m, part, shard, quarter):
        whole = wholes[m]
        size = whole.shape[0] // 4
        step = size // units
        down, along = (quarter, shard) if m < 2 else (shard, quarter)
        return whole.at[pl.ds(pl.multiple_of(down * size + part * step, step), step),
                        pl.ds(pl.multiple_of(along * size, size), size)]

    def copy(src, dst, k, slot, partner):
        made = pltpu.make_async_remote_copy(
            src_ref=src, dst_ref=dst, send_sem=send.at[k, slot], recv_sem=recv.at[k, slot], device_id=partner,
            device_id_type=pl.DeviceIdType.MESH)
        made.start()
        return made

    def forward(m, part, shard, quarter, k, slot, partner):
        where = piece(m, part, shard, quarter)
        return copy(where, where, k, slot, partner)

    ranks, cols = weights[3].shape
    last = 3 * units

    def stack_piece(first, count, shard):
        return wholes[3].at[pl.ds(first, count), pl.ds(pl.multiple_of(shard * cols, cols), cols)]

    steps = [(m, part) for m in range(3) for part in range(units)]
    made = {}

    def begin(k):
        m, part = steps[k]
        made[k, 0] = copy(own(m, part, mine), piece(m, part, group, mine), k, 0, at_above)
        made[k, 2] = copy(own(m, part, mine), piece(m, part, group, mine), k, 2, at_beside)
        made[k, 1] = copy(own(m, part, other), piece(m, part, group, other), k, 1, at_above)

    begin(0)
    begin(1)
    for m in range(4):
        keep(m)
    onward = pltpu.make_async_copy(passed, handed, local.at[4])
    onward.start()
    for t in range(len(steps) + 2):
        if t < len(steps):
            m, part = steps[t]
            made[t, 0].wait_recv()
            made[t, 4] = forward(m, part, above, mine, t, 4, at_beside)
            made[t, 6] = forward(m, part, above, mine, t, 6, at_core)
            made[t, 2].wait_recv()
            made[t, 3] = forward(m, part, beside, mine, t, 3, at_level)
            made[t, 8] = forward(m, part, beside, mine, t, 8, at_core)
            if t + 2 < len(steps):
                begin(t + 2)
            if t + 3 == len(steps):
                stack_beside = copy(weights[3], stack_piece(0, ranks, group), last, 0, at_beside)
                stack_above = copy(weights[3], stack_piece(0, ranks, group), last, 1, at_above)
            made[t, 1].wait_recv()
            made[t, 7] = forward(m, part, above, other, t, 7, at_core)
        if 1 <= t <= len(steps):
            m, part = steps[t - 1]
            made[t - 1, 4].wait_recv()
            made[t - 1, 5] = forward(m, part, across, mine, t - 1, 5, at_level)
            made[t - 1, 10] = forward(m, part, across, mine, t - 1, 10, at_core)
            made[t - 1, 3].wait_recv()
            made[t - 1, 9] = forward(m, part, beside, other, t - 1, 9, at_core)
        if 2 <= t:
            m, part = steps[t - 2]
            made[t - 2, 5].wait_recv()
            made[t - 2, 11] = forward(m, part, across, other, t - 2, 11, at_core)
        if t == len(steps):
            stack_beside.wait_recv()
            stack_above.wait_recv()
            half = ranks // 2
            lower = stack_piece(0, half, above)
            upper = stack_piece(half, half, beside)
            stack_lower = copy(lower, lower, last, 2, at_beside)
            stack_upper = copy(upper, upper, last, 3, at_above)
    onward.wait()
    onward = pltpu.make_async_copy(handed, handed_out, local.at[4])
    onward.start()
    for k in range(len(steps)):
        for slot in range(6, 12):
            made[k, slot].wait_recv()
    for k in range(len(steps)):
        for slot in range(12):
            made[k, slot].wait_send()
    for one in (stack_lower, stack_upper):
        one.wait_recv()
    for one in (stack_beside, stack_above, stack_lower, stack_upper):
        one.wait_send()
    for one in kept + [onward]:
        one.wait()


def gather_weights(w_branch, w_input, w_mixer, stack, passed):
    width = w_branch.shape[0]
    if lax.axis_size("group") != 4 or lax.axis_size("replica") % 4 != 0:
        return (lax.all_gather(w_branch, "group", axis=1, tiled=True),
                lax.all_gather(w_input, "group", axis=1, tiled=True),
                lax.all_gather(w_mixer, "group", axis=0, tiled=True),
                lax.all_gather(stack, "group", axis=1, tiled=True), passed)
    units = 4
    operands = (w_branch, w_input, w_mixer, stack, passed)
    return pl.pallas_call(
        functools.partial(gather_kernel, units),
        out_shape=[jax.ShapeDtypeStruct((width, width), BF16)] * 3
        + [jax.ShapeDtypeStruct((stack.shape[0], width), BF16), jax.ShapeDtypeStruct(passed.shape, passed.dtype)],
        in_specs=[ANYWHERE] * 5,
        out_specs=[ANYWHERE] * 5,
        scratch_shapes=[pltpu.VMEM(operand.shape, BF16) for operand in operands]
        + [pltpu.SemaphoreType.DMA((3 * units + 1, 12)), pltpu.SemaphoreType.DMA((3 * units + 1, 12)),
           pltpu.SemaphoreType.DMA((5,))],
        compiler_params=pltpu.CompilerParams(
            collective_id=0, has_side_effects=True, vmem_limit_bytes=VMEM),
        cost_estimate=pl.CostEstimate(flops=0, bytes_accessed=400 * 2**20, transcendentals=0),
    )(*operands)


def ordered_kernel(*refs):
    del refs


def ordered(value, *earlier):
    return pl.pallas_call(
        ordered_kernel,
        out_shape=jax.ShapeDtypeStruct(value.shape, value.dtype),
        in_specs=[ANYWHERE] * (1 + len(earlier)),
        out_specs=ANYWHERE,
        input_output_aliases={0: 0},
    )(value, *earlier)


def ordered_stack_kernel(count, *refs):
    for i in range(count):
        refs[-1][i] = refs[i][...]


def ordered_stack(values, *earlier):
    vmem = pl.BlockSpec(memory_space=pltpu.VMEM)
    return pl.pallas_call(
        functools.partial(ordered_stack_kernel, len(values)),
        out_shape=jax.ShapeDtypeStruct((len(values),) + values[0].shape, values[0].dtype),
        in_specs=[vmem] * len(values) + [ANYWHERE] * len(earlier),
        out_specs=vmem,
    )(*values, *earlier)


def row_tiles(rows, width, count):
    step = min(rows, 128)
    return (rows // step,), [pl.BlockSpec((step, width), lambda i: (i, 0))] * count


def resid_grad_kernel(per, resid_ref, cot_ref, gain_ref, *refs):
    pieces, (full_ref, low_ref) = refs[:-2], refs[-2:]
    grads = pieces[0][...]
    for s, piece in enumerate(pieces[1:], 1):
        grads = jnp.where(pl.program_id(0) >= s * per, piece[...], grads)
    values = resid_ref[...]
    rate = lax.rsqrt(jnp.mean(values * values, axis=-1, keepdims=True) + EPS)
    grads = cot_ref[...].astype(F32) + norm_back(values, gain_ref[...], rate, grads.astype(F32))
    full_ref[...] = grads
    low_ref[...] = grads.astype(BF16)


def resid_grad(resid, cot, gain, pieces):
    rows, width = resid.shape
    step = min(pieces[0].shape[0], 128)
    per = pieces[0].shape[0] // step
    tile = pl.BlockSpec((step, width), lambda i: (i, 0))
    return pl.pallas_call(
        functools.partial(resid_grad_kernel, per),
        grid=(rows // step,),
        out_shape=[jax.ShapeDtypeStruct((rows, width), F32), jax.ShapeDtypeStruct((rows, width), BF16)],
        in_specs=[tile, tile, pl.BlockSpec((1, width), lambda i: (0, 0))] + [
            pl.BlockSpec((step, width), lambda i, s=s: (jnp.clip(i - s * per, 0, per - 1), 0))
            for s in range(len(pieces))],
        out_specs=[tile, tile],
        compiler_params=pltpu.CompilerParams(vmem_limit_bytes=VMEM),
        cost_estimate=pl.CostEstimate(
            flops=20 * rows * width, bytes_accessed=14 * rows * width, transcendentals=rows),
    )(resid, cot, gain, *pieces)


def finish_kernel(grad_resid_ref, inputs_ref, gain_ref, grads_ref, resid_ref, outward_ref, out_ref, block_ref):
    values = inputs_ref[...].astype(F32)
    rate = lax.rsqrt(jnp.mean(values * values, axis=-1, keepdims=True) + EPS)
    out_ref[...] = grad_resid_ref[...] + norm_back(values, gain_ref[...], rate, grads_ref[...])
    block_ref[...] = (resid_ref[...] + outward_ref[...].astype(F32)).astype(BF16)


def finish(grad_resid, inputs, gain, grads, resid, outward):
    rows, width = inputs.shape
    grid, tiles = row_tiles(rows, width, 5)
    return pl.pallas_call(
        finish_kernel,
        grid=grid,
        out_shape=[jax.ShapeDtypeStruct((rows, width), F32), jax.ShapeDtypeStruct((rows, width), BF16)],
        in_specs=tiles[:2] + [pl.BlockSpec((1, width), lambda i: (0, 0))] + tiles[:3],
        out_specs=tiles[:2],
        compiler_params=pltpu.CompilerParams(vmem_limit_bytes=VMEM),
        cost_estimate=pl.CostEstimate(
            flops=21 * rows * width, bytes_accessed=22 * rows * width, transcendentals=rows),
    )(grad_resid, inputs, gain, grads, resid, outward)


def tail_kernel(
    steps, branch_grad_ref, fed_grad_ref, w_branch_ref, w_input_ref, through_ref, down_ref, partial_ref,
    out_ref, got_ref, first_a, first_b, second_a, second_b, pass_a, pass_b, own_ref, send, recv, up_send, low_recv,
    down_send, high_recv, core_send, core_recv, local,
):
    step = pl.program_id(0)
    group, replica = lax.axis_index("group"), lax.axis_index("replica")
    beside, above, across = group + 1 - 2 * (group % 2), (group + 2) % 4, 3 - group
    at_beside, at_above = (beside, replica), (above, replica)
    count = got_ref.shape[0]
    levels = count // 2
    core, level = replica % 2, replica // 2
    at_core = (group, replica + 1 - 2 * core)
    at_up, at_down = (group, (replica + 2) % count), (group, (replica + count - 2) % count)
    rows = own_ref.shape[0]
    half = rows // 2

    def part(owner, side):
        return partial_ref.at[owner, pl.ds(side * half, half), :]

    def copy(src, dst, send_sem, recv_sem, partner):
        return pltpu.make_async_remote_copy(
            src_ref=src, dst_ref=dst, send_sem=send_sem, recv_sem=recv_sem, device_id=partner,
            device_id_type=pl.DeviceIdType.MESH)

    pairs = [(part(across, 0), first_a.at[1], at_beside), (part(across, 1), first_b.at[1], at_above),
             (part(beside, 0), first_a.at[0], at_beside), (part(above, 1), first_b.at[0], at_above),
             (pass_a, second_a, at_above), (pass_b, second_b, at_beside)]
    moves = [copy(src, dst, send.at[slot], recv.at[slot], partner) for slot, (src, dst, partner) in enumerate(pairs)]
    firsts, seconds = moves[:4], moves[4:]
    loads = [pltpu.make_async_copy(part(above, 0), pass_a, local.at[0]),
             pltpu.make_async_copy(part(beside, 1), pass_b, local.at[1]),
             pltpu.make_async_copy(partial_ref.at[group], own_ref, local.at[2])]

    @pl.when(step == 0)
    def _():
        barrier = pltpu.get_barrier_semaphore()

        def greet(partner):
            pl.semaphore_signal(barrier, inc=1, device_id=partner, device_id_type=pl.DeviceIdType.MESH)

        for partner in (at_beside, at_above, at_core):
            greet(partner)

        @pl.when(level > 0)
        def _():
            greet(at_down)

        @pl.when(level < levels - 1)
        def _():
            greet(at_up)

        ends = (level + levels - 1) // levels + (2 * levels - 2 - level) // levels
        pl.semaphore_wait(barrier, 3 + ends)
        for one in firsts + loads:
            one.start()

    out_ref[...] = (dot(branch_grad_ref[...], w_branch_ref[...], NT) + dot(fed_grad_ref[...], w_input_ref[...], NT)
                    + dot(through_ref[...], down_ref[...]))

    @pl.when(step == max(steps - 2, 0))
    def _():
        for one in loads:
            one.wait()
        for one in firsts:
            one.wait_recv()
        pass_a[...] = (pass_a[...].astype(F32) + first_a[1].astype(F32)).astype(BF16)
        pass_b[...] = (pass_b[...].astype(F32) + first_b[1].astype(F32)).astype(BF16)
        for one in seconds:
            one.start()

    @pl.when(step == steps - 1)
    def _():
        for one in seconds:
            one.wait_recv()
        own_ref[:half] = (own_ref[:half].astype(F32) + first_a[0].astype(F32) + second_a[...].astype(F32)).astype(BF16)
        own_ref[half:] = (own_ref[half:].astype(F32) + first_b[0].astype(F32) + second_b[...].astype(F32)).astype(BF16)
        keep = pltpu.make_async_copy(own_ref, got_ref.at[replica], local.at[3])
        keep.start()

        def piece(source):
            return got_ref.at[(source + count) % count]

        to_up = [copy(own_ref, piece(replica), up_send.at[0], low_recv.at[0], at_up)]
        to_down = [copy(own_ref, piece(replica), down_send.at[0], high_recv.at[0], at_down)]
        to_core = [copy(own_ref, piece(replica), core_send.at[0], core_recv.at[0], at_core)]
        has_up, has_down = level < levels - 1, level > 0

        def when(condition, action):
            pl.when(condition)(action)

        when(has_up, to_up[0].start)
        when(has_down, to_down[0].start)
        to_core[0].start()
        for d in range(1, levels):
            low, high = piece(replica - 2 * d), piece(replica + 2 * d)
            to_up.append(copy(low, low, up_send.at[d], low_recv.at[d], at_up))
            to_down.append(copy(high, high, down_send.at[d], high_recv.at[d], at_down))
            core_low = copy(low, low, core_send.at[2 * d - 1], core_recv.at[2 * d - 1], at_core)
            core_high = copy(high, high, core_send.at[2 * d], core_recv.at[2 * d], at_core)
            to_core += [core_low, core_high]
            from_low, from_high = level >= d, level + d < levels

            @pl.when(from_low)
            def _(d=d, core_low=core_low):
                to_up[d - 1].wait_recv()
                when(has_up, to_up[d].start)
                core_low.start()

            @pl.when(from_high)
            def _(d=d, core_high=core_high):
                to_down[d - 1].wait_recv()
                when(has_down, to_down[d].start)
                core_high.start()

        to_core[0].wait()
        when(has_up, to_up[0].wait_send)
        when(has_down, to_down[0].wait_send)
        for d in range(1, levels):
            when(level >= d, to_core[2 * d - 1].wait)
            when(level + d < levels, to_core[2 * d].wait)
            when((level >= d) & has_up, to_up[d].wait_send)
            when((level + d < levels) & has_down, to_down[d].wait_send)
        for one in firsts + seconds:
            one.wait_send()
        keep.wait()


def tail_call(branch_grad, fed_grad, w_branch, w_input, through, down, partial):
    rows, width = branch_grad.shape
    ranks, cols = partial.shape[1:]
    count = lax.axis_size("replica")
    levels = count // 2
    tile = tile_of(width, 512)
    steps = pl.cdiv(width, tile)
    weight = pl.BlockSpec((tile, width), lambda i: (i, 0))
    half = ranks // 2
    dma = pltpu.SemaphoreType.DMA
    return pl.pallas_call(
        functools.partial(tail_kernel, steps),
        grid=(steps,),
        out_shape=[jax.ShapeDtypeStruct((rows, width), F32), jax.ShapeDtypeStruct((count, ranks, cols), BF16)],
        in_specs=[resident(branch_grad), resident(fed_grad), weight, weight, resident(through),
                  pl.BlockSpec((down.shape[0], tile), lambda i: (0, i)), ANYWHERE],
        out_specs=[pl.BlockSpec((rows, tile), lambda i: (0, i)), ANYWHERE],
        scratch_shapes=[pltpu.VMEM((2, half, cols), BF16)] * 2 + [pltpu.VMEM((half, cols), BF16)] * 4
        + [pltpu.VMEM((ranks, cols), BF16), dma((6,)), dma((6,)), dma((levels,)), dma((levels,)), dma((levels,)),
           dma((levels,)), dma((count,)), dma((count,)), dma((4,))],
        compiler_params=pltpu.CompilerParams(
            vmem_limit_bytes=VMEM, collective_id=4, has_side_effects=True),
        cost_estimate=pl.CostEstimate(
            flops=4 * rows * width * width, bytes_accessed=4 * width * width + 8 * rows * width, transcendentals=0),
    )(branch_grad, fed_grad, w_branch, w_input, through, down, partial)


def spread_kernel(tables, pieces, ids_ref, from_ref, *refs):
    gots, out_refs = refs[:pieces], refs[-tables:]
    ranks = out_refs[0].shape[1]
    replicas = from_ref.shape[0]
    seqs = ids_ref.shape[0] // replicas
    for table in range(tables):
        out_refs[table][...] = jnp.zeros_like(out_refs[table])
    replica = 0
    for got_ref in gots:
        for at in range(got_ref.shape[0]):
            for s in range(seqs):
                place = ids_ref[from_ref[replica] * seqs + s]
                for table in range(tables):
                    rows = pl.ds((table * seqs + s) * ranks, ranks)
                    out_refs[table][place] += got_ref[at, rows, :].astype(F32)
            replica += 1


def spread(ids, source, gots, tables, sets, seqs, ranks, earlier=()):
    rows, width = gots[0].shape[1:]
    replicas = source.shape[0]
    scalars = pl.BlockSpec(memory_space=pltpu.SMEM)
    return pl.pallas_call(
        functools.partial(spread_kernel, tables, len(gots)),
        out_shape=[jax.ShapeDtypeStruct((sets, ranks, width), F32)] * tables,
        in_specs=[scalars, scalars] + [pl.BlockSpec(memory_space=pltpu.VMEM)] * len(gots)
        + [ANYWHERE] * len(earlier),
        out_specs=[pl.BlockSpec(memory_space=pltpu.VMEM)] * tables,
        compiler_params=pltpu.CompilerParams(vmem_limit_bytes=56 * 2**20),
        cost_estimate=pl.CostEstimate(
            flops=replicas * rows * width,
            bytes_accessed=2 * replicas * rows * width + 4 * tables * sets * ranks * width, transcendentals=0),
    )(ids, source, *gots, *earlier)


def products_kernel(plan, *refs):
    out_ref, row = refs[-1], 0
    for place, (kind, first, last) in plan:
        if kind == "product":
            result = dot(refs[place][:, first:last], refs[place + 1][...], TN)
        else:
            result = refs[place][...]
        count = last - first
        out_ref[row : row + count, :] = result.astype(BF16)
        row += count


def products(items, earlier=(), blocks=1):
    operands, specs, plan, total = [], [], [], 0
    width = items[0][3].shape[-1]
    tile = width // blocks if blocks > 1 and width % (128 * blocks) == 0 else tile_of(width, 512)
    for item in items:
        if len(item) == 1:
            plan.append((len(operands), ("rows", 0, item[0].shape[0])))
            operands.append(item[0])
            specs.append(pl.BlockSpec((item[0].shape[0], tile), lambda i: (0, i)))
        else:
            lhs, first, last, rhs = item
            plan.append((len(operands), ("product", first, last)))
            if isinstance(rhs, tuple):
                rhs, s = rhs
                block = pl.BlockSpec((None, rhs.shape[1], tile), lambda i, s=s: (s, 0, i))
            else:
                block = pl.BlockSpec((rhs.shape[0], tile), lambda i: (0, i))
            operands += [lhs, rhs]
            specs += [resident(lhs), block]
        total += plan[-1][1][2] - plan[-1][1][1]
    cells = sum(operand.size for operand in operands)
    direct = blocks > 1 and tile * blocks == width
    result = pl.pallas_call(
        functools.partial(products_kernel, plan),
        grid=(pl.cdiv(width, tile),),
        out_shape=jax.ShapeDtypeStruct((blocks, total, tile) if direct else (total, width), BF16),
        in_specs=specs + [ANYWHERE] * len(earlier),
        out_specs=(pl.BlockSpec((None, total, tile), lambda i: (i, 0, 0)) if direct
                   else pl.BlockSpec((total, tile), lambda i: (0, i))),
        compiler_params=pltpu.CompilerParams(vmem_limit_bytes=VMEM),
        cost_estimate=pl.CostEstimate(flops=64 * cells, bytes_accessed=2 * cells, transcendentals=0),
    )(*operands, *earlier)
    if blocks > 1 and not direct:
        result = jnp.swapaxes(result.reshape(total, blocks, width // blocks), 0, 1)
    return result


def passed_along(block, axis, distance):
    devices = range(lax.axis_size(axis))
    route = [(i - distance, i) for i in devices if i - distance in devices]
    return lax.ppermute(block, axis, route)


def over_replicas(value, direct, *earlier):
    count, here = lax.axis_size("replica"), lax.axis_index("replica")
    if count % 2:
        return [lax.all_gather(value, "replica")], jnp.arange(count, dtype=jnp.int32)
    steps = jnp.arange(count // 2, dtype=jnp.int32)
    if direct:
        got = ordered_stack([value] + [
            lax.ppermute(value, "replica", [(i, (i + 2 * step) % count) for i in range(count)])
            for step in range(1, count // 2)], *earlier)
        source = (here + count - 2 * steps) % count
    else:
        got = lax.all_gather(value, "replica", axis_index_groups=[list(range(p, count, 2)) for p in range(2)])
        source = here % 2 + 2 * steps
    swapped = lax.ppermute(got, "replica", [(i, i ^ 1) for i in range(count)])
    return [got, swapped], jnp.concatenate([source, source + 1 - 2 * (here % 2)], 0)


def body(
    inputs, segment_ids, adapter_ids, gain_mix, gain_mlp, w_branch, w_input, conv_taps, decay_heads, admit_heads,
    decay_param, w_mixer, w_gate, w_upper, w_down, down_branch, lift_branch, down_input, lift_input, down_decay,
    lift_decay, down_admit, lift_admit, down_mixer, lift_mixer, down_gate, lift_gate, down_upper, lift_upper,
    down_outward, lift_outward, out_grad,
):
    seqs, stretch, width = inputs.shape
    rows = seqs * stretch
    taps = conv_taps.shape[0]
    sets, _, ranks = down_branch.shape
    group, place = lax.axis_size("group"), lax.axis_index("group")
    mask_cols = seqs * ranks

    turned = lambda table: jnp.swapaxes(table, 1, 2)
    stack, own_tables = pick(
        adapter_ids,
        [turned(down_branch), turned(down_input), turned(down_decay), turned(down_admit), turned(down_mixer),
         turned(down_gate), turned(down_upper), lift_branch, lift_input, lift_decay, lift_admit, lift_mixer,
         lift_outward],
        [lift_gate, lift_upper, turned(down_outward)])
    full_branch, full_input, full_mixer, stack, late_grad = gather_weights(
        w_branch, w_input, w_mixer, stack, out_grad)
    (p_down_branch, p_down_input, p_down_decay, p_down_admit, p_down_mixer, p_down_gate, p_down_upper,
     p_lift_branch, p_lift_input, p_lift_decay, p_lift_admit, p_lift_mixer, p_lift_outward) = [
        stack[i * mask_cols : (i + 1) * mask_cols] for i in range(13)]
    own_lift_gate, own_lift_upper, own_down_outward = [
        own_tables[i * mask_cols : (i + 1) * mask_cols] for i in range(3)]
    cotangents = lax.all_gather(late_grad, "group", axis=1, tiled=True)

    row_seq = lax.broadcasted_iota(jnp.int32, (rows, mask_cols), 0) // stretch
    col_seq = lax.broadcasted_iota(jnp.int32, (rows, mask_cols), 1) // ranks
    own = (row_seq == col_seq).astype(F32)
    own_two = jnp.concatenate([own, own], 1)

    begin = place * stretch
    padded_ids = jnp.pad(segment_ids, ((0, 0), (taps - 1, taps - 1)), constant_values=-1)
    window = lax.dynamic_slice_in_dim(padded_ids, begin, stretch + 2 * (taps - 1), 1)
    current = window[:, taps - 1 : taps - 1 + stretch + taps - 1]
    agree = [
        ((current == window[:, taps - 1 - j : taps - 1 - j + stretch + taps - 1]) & (current >= 0)).astype(F32)
        for j in range(taps)
    ]
    restart = (1.0 - agree[1][:, :stretch]).reshape(rows, 1)

    x_float = inputs.reshape(rows, width).astype(F32)
    normed_f, _ = norm_rows(x_float, gain_mix)
    normed = normed_f.astype(BF16)
    inner_one = (dot(normed, stack[: 2 * mask_cols], NT) * own_two).astype(BF16)
    inner_branch, inner_input = inner_one[:, :mask_cols], inner_one[:, mask_cols:]
    branch_pre = dot(normed, full_branch) + dot(inner_branch, p_lift_branch)
    fed = (dot(normed, full_input) + dot(inner_input, p_lift_input)).astype(BF16)
    fed = fed.reshape(seqs, stretch, width)
    halo = passed_along(fed[:, stretch - (taps - 1) :], "group", 1)
    extended = jnp.concatenate([halo, fed], axis=1).astype(F32)
    convolved = sum(
        conv_taps[j] * agree[j][:, :stretch, None] * extended[:, taps - 1 - j : taps - 1 - j + stretch]
        for j in range(taps)
    ).reshape(rows, width)
    rounded = convolved.astype(BF16)
    softrate = jax.nn.softplus(decay_param).reshape(1, width)
    inner_gates = (dot(rounded, stack[2 * mask_cols : 4 * mask_cols], NT) * own_two).astype(BF16)
    lift_gates = stack[9 * mask_cols : 11 * mask_cols]
    cum, local = forward_gates(seqs, convolved, inner_gates, lift_gates, decay_heads, admit_heads, softrate, restart)
    ends = jnp.concatenate(
        [cum.reshape(seqs, stretch, width)[:, -1], local.reshape(seqs, stretch, width)[:, -1]], 0)
    all_ends = lax.all_gather(ends, "group")
    carried = jnp.zeros((seqs, width), F32)
    for g in range(group - 1):
        longer = all_ends[g, :seqs] * carried + all_ends[g, seqs:]
        carried = jnp.where(g < place, longer, carried)
    carried_rows = jnp.repeat(carried, stretch, axis=0)
    state = local + cum * carried_rows
    merged = (state * gelu(branch_pre)).astype(BF16)
    inner_mixer = (dot(merged, p_down_mixer, NT) * own).astype(BF16)
    mixed = dot(merged, full_mixer) + dot(inner_mixer, p_lift_mixer)
    resid = x_float + mixed
    normed_two_f, _ = norm_rows(resid, gain_mlp)
    normed_two = normed_two_f.astype(BF16).reshape(seqs, stretch, width)

    spans = [slice(s * ranks, (s + 1) * ranks) for s in range(seqs)]
    grad_hiddens, through_out, first_tokens = grad_hidden_call(
        cotangents, w_down, p_lift_outward, own_down_outward, normed_two[0])
    all_tokens = [first_tokens] + [
        lax.all_gather(ordered(normed_two[s], first_tokens), "group", axis=0, tiled=True) for s in range(1, seqs)]
    backs, hiddens, throughs, wides = [], [], [], []
    for s, at in enumerate(spans):
        two_downs = jnp.concatenate([p_down_gate[at], p_down_upper[at]], 0)
        hidden, back, wide, through = feed_call(
            s, all_tokens[s], grad_hiddens, w_gate, w_upper, two_downs, own_lift_gate[at], own_lift_upper[at],
            through_out)
        if s < seqs - 1:
            backs.append(lax.psum_scatter(back, "group", scatter_dimension=0, tiled=True))
        hiddens.append(hidden)
        throughs.append(through)
        wides.append(wide)
    outward, _, early, reduced = outward_call(
        hiddens, all_tokens, throughs, cotangents, w_down, own_down_outward, p_lift_outward, back)
    backs.append(reduced)
    named = jnp.broadcast_to(jnp.pad(adapter_ids, (0, -seqs % 16)).astype(BF16)[:, None], (-(-seqs // 16) * 16,
                                                                                   wides[0].shape[1]))
    wide = jnp.concatenate(
        [wides[s][i * ranks : (i + 1) * ranks] for i in range(3) for s in range(seqs)] + [named], 0)
    grad_resid, grad_mixed = resid_grad(
        resid, out_grad.reshape(rows, width), gain_mlp.reshape(1, width), backs)
    outward = lax.psum_scatter(outward, "group", scatter_dimension=1, tiled=True).reshape(rows, width)

    if group == 4 and 2 * seqs <= 8 and stretch % 8 == 0:
        agree_cols = jnp.stack([agree[j][:, j : j + stretch].reshape(rows) for j in range(taps)], 1)
        grad_branch_pre, through_one, through_gates, grad_lift_gates, grad_fed, through_mixer = mixer_back(
            seqs, grad_mixed, full_mixer, p_lift_mixer, p_down_mixer, convolved, inner_gates, lift_gates, decay_heads,
            admit_heads, softrate, restart, cum, local, carried, branch_pre, p_lift_branch, p_lift_input,
            stack[2 * mask_cols : 4 * mask_cols], conv_taps, agree_cols)
    else:
        through_mixer = (dot(grad_mixed, p_lift_mixer, NT) * own).astype(BF16)
        grad_merged = dot(grad_mixed, full_mixer, NT) + dot(through_mixer, p_down_mixer)
        span, total, firsts, grad_branch_pre = backward_scan(
            seqs, convolved, inner_gates, lift_gates, decay_heads, softrate, restart, cum, local, carried, branch_pre,
            grad_merged)
        all_firsts = lax.all_gather(firsts, "group")
        incoming = jnp.zeros((seqs, width), F32)
        for lap in range(group - 1):
            g = group - 1 - lap
            longer = all_firsts[g, :seqs] * incoming + all_firsts[g, seqs:]
            incoming = jnp.where(g > place, longer, incoming)
        grad_direct, through_gates, grad_lift_gates = backward_gates(
            seqs, convolved, inner_gates, lift_gates, decay_heads, admit_heads, softrate, restart, cum, local, carried,
            span, total, incoming)
        through_gates = (through_gates * own_two).astype(BF16)
        grad_convolved = grad_direct + dot(through_gates, stack[2 * mask_cols : 4 * mask_cols])
        grad_convolved = grad_convolved.reshape(seqs, stretch, width)
        below = passed_along(grad_convolved[:, : taps - 1].astype(BF16), "group", -1).astype(F32)
        grad_extended = jnp.concatenate([grad_convolved, below], axis=1)
        grad_fed = sum(
            conv_taps[j] * agree[j][:, j : j + stretch, None] * grad_extended[:, j : j + stretch] for j in range(taps)
        ).astype(BF16).reshape(rows, width)
        through_branch = (dot(grad_branch_pre, p_lift_branch, NT) * own).astype(BF16)
        through_input = (dot(grad_fed, p_lift_input, NT) * own).astype(BF16)
        through_one = jnp.concatenate([through_branch, through_input], 1)
    all_wide, wide_source = over_replicas(wide, True, through_gates)
    both = 2 * mask_cols
    got_ids = jnp.concatenate([part[:, 3 * mask_cols : 3 * mask_cols + seqs, 0] for part in all_wide], 0)
    in_order = wide_source[:, None] == jnp.arange(wide_source.shape[0], dtype=jnp.int32)[None, :]
    all_ids = jnp.sum(jnp.where(in_order[:, :, None], got_ids.astype(jnp.int32)[:, None, :], 0), 0).reshape(-1)
    partial = products(
        [(through_one, 0, both, normed), (through_gates, 0, both, rounded), (through_mixer, 0, mask_cols, merged),
         (inner_branch, 0, mask_cols, grad_branch_pre), (inner_input, 0, mask_cols, grad_fed), (grad_lift_gates,),
         (inner_mixer, 0, mask_cols, grad_mixed), (early,)], (), group)
    if group == 4 and lax.axis_size("replica") % 2 == 0 and partial.shape[1] % 32 == 0:
        grad_normed, got = tail_call(
            grad_branch_pre, grad_fed, full_branch, full_input, through_one, stack[:both], partial)
        all_owned, owned_source = [got], jnp.arange(lax.axis_size("replica"), dtype=jnp.int32)
    else:
        grad_normed = (dot(grad_branch_pre, full_branch, NT) + dot(grad_fed, full_input, NT)
                       + dot(through_one, stack[:both]))
        owned = lax.psum_scatter(partial, "group", scatter_dimension=0, tiled=False)
        all_owned, owned_source = over_replicas(owned, False)
    grad_inputs, block_out = finish(
        grad_resid, inputs.reshape(rows, width), gain_mix.reshape(1, width), grad_normed, resid, outward)
    wides = spread(all_ids, wide_source, all_wide, 3, sets, seqs, ranks)
    totals = spread(all_ids, owned_source, all_owned, 13, sets, seqs, ranks)
    (t_down_branch, t_down_input, t_down_decay, t_down_admit, t_down_mixer, t_lift_branch, t_lift_input, t_lift_decay,
     t_lift_admit, t_lift_mixer, t_down_gate, t_down_upper, t_lift_outward) = totals
    return (
        block_out.reshape(seqs, stretch, width), grad_inputs.reshape(seqs, stretch, width),
        turned(t_down_branch), t_lift_branch, turned(t_down_input), t_lift_input, turned(t_down_decay), t_lift_decay,
        turned(t_down_admit), t_lift_admit, turned(t_down_mixer), t_lift_mixer, turned(t_down_gate), wides[0],
        turned(t_down_upper), wides[1], turned(wides[2]), t_lift_outward,
    )


def solution(mesh):
    tokens = P("replica", "group", None)
    down, lift = P(None, "group", None), P(None, None, "group")
    cols, split = P(None, "group"), P("group", None)
    in_specs = (
        tokens, P("replica", None), P("replica"), P(), P(), cols, cols, P(), P(), P(), P(), split, cols, cols, split,
    ) + (down, lift) * 8 + (tokens,)
    out_specs = (tokens, tokens) + (down, lift) * 8
    return jax.shard_map(body, mesh=mesh, in_specs=in_specs, out_specs=out_specs, check_vma=False)
```

```python
import functools

import jax
import jax.numpy as jnp
from jax import lax
from jax.experimental import pallas as pl
from jax.experimental.pallas import tpu as pltpu
from jax.sharding import PartitionSpec as P

EPS = 1e-06
F32 = jnp.float32
BF16 = jnp.bfloat16
GELU_C = 0.7978845608028654
GELU_A = 0.044715
NT = (((1,), (1,)), ((), ()))
NN = (((1,), (0,)), ((), ()))
TN = (((0,), (0,)), ((), ()))
ANYWHERE = pl.BlockSpec(memory_space=pl.ANY)
VMEM = 62 * 2**20


def dot(a, b, dims=NN):
    return lax.dot_general(a, b, dims, preferred_element_type=F32)


def gelu(v):
    return 0.5 * v * (1.0 + jnp.tanh(GELU_C * (v + GELU_A * v * v * v)))


def gelu_both(v):
    square = v * v
    half = 0.5 + 0.5 * jnp.tanh(v * (GELU_C + GELU_C * GELU_A * square))
    value = v * half
    return value, half + (value - value * half) * (2.0 * GELU_C + 6.0 * GELU_C * GELU_A * square)


def norm_rows(values, gain):
    rate = lax.rsqrt(jnp.mean(values * values, axis=-1, keepdims=True) + EPS)
    return values * rate * gain, rate


def norm_back(values, gain, rate, grads):
    scaled = grads * gain
    along = jnp.mean(scaled * values, axis=-1, keepdims=True)
    return rate * scaled - values * (rate * rate * rate * along)


def rows_shifted(values, by, fill):
    rows, width = values.shape
    if by % 8 == 0:
        return jnp.concatenate([jnp.full((by, width), fill, values.dtype), values[: rows - by]], 0)
    place = lax.broadcasted_iota(jnp.int32, values.shape, 0)
    return jnp.where(place >= by, pltpu.roll(values, by, 0), fill)


def rows_advanced(values, by, fill):
    rows, width = values.shape
    if by % 8 == 0:
        return jnp.concatenate([values[by:], jnp.full((by, width), fill, values.dtype)], 0)
    place = lax.broadcasted_iota(jnp.int32, values.shape, 0)
    return jnp.where(place < rows - by, pltpu.roll(values, rows - by, 0), fill)


def scan_rows(a, b, moved):
    by = 1
    while by < a.shape[0]:
        b = a * moved(b, by, 0.0) + b
        a = a * moved(a, by, 1.0)
        by *= 2
    return a, b


def gate_steps(pre_d, pre_a, softrate, restart):
    decay_gate = 1.0 / (1.0 + jnp.exp(-pre_d))
    admit_gate = 1.0 / (1.0 + jnp.exp(-pre_a))
    safe = jnp.where(restart, -1.0, -8.0 * decay_gate * softrate)
    grown = jnp.exp(safe)
    scale = jnp.sqrt(jnp.tanh(-safe) * (1.0 + grown * grown))
    return decay_gate, admit_gate, grown, scale


def gate_values(conv, inner, lift, table_d, table_a, softrate, restart):
    rounded = conv.astype(BF16)
    half = lift.shape[0] // 2
    pre_d = dot(rounded, table_d) + dot(inner[:, :half], lift[:half])
    pre_a = dot(rounded, table_a) + dot(inner[:, half:], lift[half:])
    return gate_steps(pre_d, pre_a, softrate, restart)


GROUP = 16
UNROLL = 16


def scan_group(a, b, carry_a, carry_b, moved):
    by = 1
    while by < a.shape[0]:
        b = a * moved(b, by, 0.0) + b
        a = a * moved(a, by, 1.0)
        by *= 2
    return a * carry_a, a * carry_b + b


def forward_gates_kernel(seqs, conv_ref, inner_ref, lift_ref, table_d_ref, table_a_ref, soft_ref, restart_ref,
                         cum_ref, local_ref, pre_d_ref, pre_a_ref):
    rows, size = conv_ref.shape
    stretch = rows // seqs
    half = lift_ref.shape[0] // 2
    rounded = conv_ref[...].astype(BF16)
    pre_d_ref[...] = dot(rounded, table_d_ref[0]) + dot(inner_ref[:, :half], lift_ref[:half, :])
    pre_a_ref[...] = dot(rounded, table_a_ref[0]) + dot(inner_ref[:, half:], lift_ref[half:, :])
    softrate = soft_ref[...]

    def group(k, carries):
        after = []
        for s in range(seqs):
            at = pl.ds(pl.multiple_of(s * stretch + k * GROUP, GROUP), GROUP)
            restart = restart_ref[at, :] > 0.5
            _, admit, grown, scale = gate_steps(pre_d_ref[at, :], pre_a_ref[at, :], softrate, restart)
            decays = jnp.where(restart, 0.0, grown)
            drive = conv_ref[at, :] * admit * jnp.where(restart, 1.0, scale)
            cum, local = scan_group(decays, drive, *carries[s], rows_shifted)
            cum_ref[at, :] = cum
            local_ref[at, :] = local
            after.append((cum[GROUP - 1 :], local[GROUP - 1 :]))
        return tuple(after)

    start = (jnp.ones((1, size), F32), jnp.zeros((1, size), F32))
    lax.fori_loop(0, stretch // GROUP, group, (start,) * seqs, unroll=UNROLL)


def forward_gates(seqs, conv, inner, lift, table_d, table_a, softrate, restart):
    rows, width = conv.shape
    heads, size = table_d.shape[:2]
    tile = pl.BlockSpec((rows, size), lambda h: (0, h))
    table = pl.BlockSpec((1, size, size), lambda h: (h, 0, 0))
    out = jax.ShapeDtypeStruct((rows, width), F32)
    return pl.pallas_call(
        functools.partial(forward_gates_kernel, seqs),
        out_shape=(out, out),
        grid=(heads,),
        in_specs=[
            tile,
            pl.BlockSpec(inner.shape, lambda h: (0, 0)),
            pl.BlockSpec((lift.shape[0], size), lambda h: (0, h)),
            table,
            table,
            pl.BlockSpec((1, size), lambda h: (0, h)),
            pl.BlockSpec(restart.shape, lambda h: (0, 0)),
        ],
        out_specs=(tile, tile),
        scratch_shapes=[pltpu.VMEM((rows, size), F32)] * 2,
        compiler_params=pltpu.CompilerParams(vmem_limit_bytes=40 * 2**20),
        cost_estimate=pl.CostEstimate(
            flops=4 * rows * width * size + 60 * rows * width,
            bytes_accessed=12 * rows * width,
            transcendentals=6 * rows * width),
    )(conv, inner, lift, table_d, table_a, softrate, restart)


def backward_scan_kernel(seqs, conv_ref, inner_ref, lift_ref, table_d_ref, soft_ref, restart_ref, cum_ref, local_ref,
                         carried_ref, pre_ref, grad_ref, span_ref, total_ref, first_ref, branch_grad_ref):
    stretch = conv_ref.shape[0] // seqs
    half = lift_ref.shape[0] // 2
    for s in range(seqs):
        rows = pl.ds(s * stretch, stretch)
        restart = restart_ref[rows, :] > 0.5
        rounded = conv_ref[rows, :].astype(BF16)
        pre_d = dot(rounded, table_d_ref[0]) + dot(inner_ref[rows, :half], lift_ref[:half, :])
        grown = jnp.exp(-8.0 * soft_ref[...] / (1.0 + jnp.exp(-pre_d)))
        decays = jnp.where(restart, 0.0, grown)
        state = local_ref[rows, :] + cum_ref[rows, :] * carried_ref[s : s + 1, :]
        value, slope = gelu_both(pre_ref[rows, :])
        grads = grad_ref[rows, :]
        branch_grad_ref[rows, :] = (grads * state * slope).astype(BF16)
        span, total = scan_rows(rows_advanced(decays, 1, 1.0), grads * value, rows_advanced)
        span_ref[rows, :] = span
        total_ref[rows, :] = total
        first_ref[s : s + 1, :] = decays[:1] * span[:1]
        first_ref[seqs + s : seqs + s + 1, :] = decays[:1] * total[:1]


def backward_scan(seqs, conv, inner, lift, table_d, softrate, restart, cum, local, carried, pre, grads):
    rows, width = conv.shape
    heads, size = table_d.shape[:2]
    tile = pl.BlockSpec((rows, size), lambda h: (0, h))
    table = pl.BlockSpec((1, size, size), lambda h: (h, 0, 0))
    out = jax.ShapeDtypeStruct((rows, width), F32)
    return pl.pallas_call(
        functools.partial(backward_scan_kernel, seqs),
        out_shape=(out, out, jax.ShapeDtypeStruct((2 * seqs, width), F32), jax.ShapeDtypeStruct((rows, width), BF16)),
        grid=(heads,),
        in_specs=[
            tile,
            pl.BlockSpec(inner.shape, lambda h: (0, 0)),
            pl.BlockSpec((lift.shape[0], size), lambda h: (0, h)),
            table,
            pl.BlockSpec((1, size), lambda h: (0, h)),
            pl.BlockSpec(restart.shape, lambda h: (0, 0)),
            tile,
            tile,
            pl.BlockSpec((seqs, size), lambda h: (0, h)),
            tile,
            tile,
        ],
        out_specs=(tile, tile, pl.BlockSpec((2 * seqs, size), lambda h: (0, h)), tile),
        compiler_params=pltpu.CompilerParams(vmem_limit_bytes=48 * 2**20),
        cost_estimate=pl.CostEstimate(
            flops=2 * rows * width * size + 80 * rows * width,
            bytes_accessed=30 * rows * width,
            transcendentals=4 * rows * width),
    )(conv, inner, lift, table_d, softrate, restart, cum, local, carried, pre, grads)


def backward_gates_kernel(seqs, conv_ref, inner_ref, lift_ref, table_d_ref, table_a_ref, soft_ref, restart_ref,
                          cum_ref, local_ref, carried_ref, span_ref, total_ref, incoming_ref,
                          conv_grad_ref, through_ref, lift_grad_ref):
    stretch = conv_ref.shape[0] // seqs
    half = lift_ref.shape[0] // 2

    @pl.when(pl.program_id(0) == 0)
    def _():
        through_ref[...] = jnp.zeros_like(through_ref)

    for s in range(seqs):
        rows = pl.ds(s * stretch, stretch)
        conv = conv_ref[rows, :]
        inner = inner_ref[rows, :]
        restart = restart_ref[rows, :] > 0.5
        softrate = soft_ref[...]
        decay_gate, admit, grown, scale = gate_values(
            conv, inner, lift_ref[...], table_d_ref[0], table_a_ref[0], softrate, restart)
        carried = carried_ref[s : s + 1, :]
        state = local_ref[rows, :] + cum_ref[rows, :] * carried
        place = lax.broadcasted_iota(jnp.int32, state.shape, 0)
        before = jnp.where(place >= 1, pltpu.roll(state, 1, 0), carried)
        grads = total_ref[rows, :] + span_ref[rows, :] * incoming_ref[s : s + 1, :]
        driven = grads * jnp.where(restart, 1.0, scale)
        grad_log = jnp.where(
            restart, 0.0, grads * (before * grown - conv * admit * grown * grown / scale))
        grad_d = (-8.0 * softrate) * grad_log * decay_gate * (1.0 - decay_gate)
        grad_a = driven * conv * admit * (1.0 - admit)
        low_d, low_a = grad_d.astype(BF16), grad_a.astype(BF16)
        conv_grad_ref[rows, :] = driven * admit + dot(low_d, table_d_ref[0], NT) + dot(low_a, table_a_ref[0], NT)
        through_ref[rows, :half] += dot(low_d, lift_ref[:half, :], NT)
        through_ref[rows, half:] += dot(low_a, lift_ref[half:, :], NT)
        first = dot(inner[:, :half], low_d, TN)
        second = dot(inner[:, half:], low_a, TN)
        if s == 0:
            lift_grad_ref[:half, :] = first
            lift_grad_ref[half:, :] = second
        else:
            lift_grad_ref[:half, :] += first
            lift_grad_ref[half:, :] += second


def backward_gates(seqs, conv, inner, lift, table_d, table_a, softrate, restart, cum, local, carried, span, total,
                   incoming):
    rows, width = conv.shape
    heads, size = table_d.shape[:2]
    tile = pl.BlockSpec((rows, size), lambda h: (0, h))
    table = pl.BlockSpec((1, size, size), lambda h: (h, 0, 0))
    edge = pl.BlockSpec((seqs, size), lambda h: (0, h))
    ranks = pl.BlockSpec((lift.shape[0], size), lambda h: (0, h))
    return pl.pallas_call(
        functools.partial(backward_gates_kernel, seqs),
        out_shape=(
            jax.ShapeDtypeStruct((rows, width), F32),
            jax.ShapeDtypeStruct(inner.shape, F32),
            jax.ShapeDtypeStruct(lift.shape, F32),
        ),
        grid=(heads,),
        in_specs=[
            tile,
            pl.BlockSpec(inner.shape, lambda h: (0, 0)),
            ranks,
            table,
            table,
            pl.BlockSpec((1, size), lambda h: (0, h)),
            pl.BlockSpec(restart.shape, lambda h: (0, 0)),
            tile,
            tile,
            edge,
            tile,
            tile,
            edge,
        ],
        out_specs=(tile, pl.BlockSpec(inner.shape, lambda h: (0, 0)), ranks),
        compiler_params=pltpu.CompilerParams(vmem_limit_bytes=48 * 2**20),
        cost_estimate=pl.CostEstimate(
            flops=8 * rows * width * size + 80 * rows * width,
            bytes_accessed=24 * rows * width,
            transcendentals=6 * rows * width),
    )(conv, inner, lift, table_d, table_a, softrate, restart, cum, local, carried, span, total, incoming)


def remote(src, dst, send_sem, recv_sem, partner):
    return pltpu.make_async_remote_copy(
        src_ref=src, dst_ref=dst, send_sem=send_sem, recv_sem=recv_sem, device_id=partner,
        device_id_type=pl.DeviceIdType.MESH)


class GroupSum:
    def __init__(self, block, scratch):
        first_a, first_b, second_a, second_b, pass_a, pass_b, own, send, recv, local = scratch
        group, replica = lax.axis_index("group"), lax.axis_index("replica")
        beside, above, across = group + 1 - 2 * (group % 2), (group + 2) % 4, 3 - group
        at_beside, at_above = (beside, replica), (above, replica)
        self.scratch, self.half = scratch, own.shape[0] // 2
        pairs = [(block(across, 0), first_a.at[1], at_beside), (block(across, 1), first_b.at[1], at_above),
                 (block(beside, 0), first_a.at[0], at_beside), (block(above, 1), first_b.at[0], at_above),
                 (pass_a, second_a, at_above), (pass_b, second_b, at_beside)]
        moves = [remote(src, dst, send.at[slot], recv.at[slot], partner)
                 for slot, (src, dst, partner) in enumerate(pairs)]
        self.firsts, self.seconds = moves[:4], moves[4:]
        pieces = [(block(above, 0), pass_a), (block(beside, 1), pass_b), (block(group, 0), own.at[pl.ds(0, self.half)]),
                  (block(group, 1), own.at[pl.ds(self.half, self.half)])]
        self.loads = [pltpu.make_async_copy(src, dst, local.at[i]) for i, (src, dst) in enumerate(pieces)]

    def begin(self):
        for one in self.firsts + self.loads:
            one.start()

    def middle(self):
        first_a, first_b, _, _, pass_a, pass_b = self.scratch[:6]
        for one in self.loads:
            one.wait()
        for one in self.firsts:
            one.wait_recv()
        pass_a[...] = (pass_a[...].astype(F32) + first_a[1].astype(F32)).astype(BF16)
        pass_b[...] = (pass_b[...].astype(F32) + first_b[1].astype(F32)).astype(BF16)
        for one in self.seconds:
            one.start()

    def end(self):
        first_a, first_b, second_a, second_b, _, _, own = self.scratch[:7]
        half = self.half
        for one in self.seconds:
            one.wait_recv()
        own[:half] = (own[:half].astype(F32) + first_a[0].astype(F32) + second_a[...].astype(F32)).astype(BF16)
        own[half:] = (own[half:].astype(F32) + first_b[0].astype(F32) + second_b[...].astype(F32)).astype(BF16)

    def clear(self):
        for one in self.firsts + self.seconds:
            one.wait_send()

    @staticmethod
    def shapes(ranks, cols):
        half = ranks // 2
        return [pltpu.VMEM((2, half, cols), BF16)] * 2 + [pltpu.VMEM((half, cols), BF16)] * 4 + [
            pltpu.VMEM((ranks, cols), BF16), pltpu.SemaphoreType.DMA((6,)), pltpu.SemaphoreType.DMA((6,)),
            pltpu.SemaphoreType.DMA((4,))]


class ReplicaChain:
    def __init__(self, own, got, sems):
        up_send, low_recv, down_send, high_recv, core_send, core_recv, local = sems
        group, replica = lax.axis_index("group"), lax.axis_index("replica")
        count = got.shape[0]
        self.levels, self.level = count // 2, replica // 2
        at_core = (group, replica + 1 - 2 * (replica % 2))
        at_up, at_down = (group, (replica + 2) % count), (group, (replica + count - 2) % count)
        self.has_up, self.has_down = self.level < self.levels - 1, self.level > 0
        piece = lambda source: got.at[(source + count) % count]
        self.to_up = [remote(own, piece(replica), up_send.at[0], low_recv.at[0], at_up)]
        self.to_down = [remote(own, piece(replica), down_send.at[0], high_recv.at[0], at_down)]
        self.to_core = [remote(own, piece(replica), core_send.at[0], core_recv.at[0], at_core)]
        self.keep = pltpu.make_async_copy(own, piece(replica), local.at[0])
        for d in range(1, self.levels):
            low, high = piece(replica - 2 * d), piece(replica + 2 * d)
            self.to_up.append(remote(low, low, up_send.at[d], low_recv.at[d], at_up))
            self.to_down.append(remote(high, high, down_send.at[d], high_recv.at[d], at_down))
            self.to_core += [remote(low, low, core_send.at[2 * d - 1], core_recv.at[2 * d - 1], at_core),
                             remote(high, high, core_send.at[2 * d], core_recv.at[2 * d], at_core)]

    def begin(self):
        self.keep.start()
        pl.when(self.has_up)(self.to_up[0].start)
        pl.when(self.has_down)(self.to_down[0].start)
        self.to_core[0].start()

    def hop(self, d):
        @pl.when(self.level >= d)
        def _():
            self.to_up[d - 1].wait_recv()
            pl.when(self.has_up)(self.to_up[d].start)
            self.to_core[2 * d - 1].start()

        @pl.when(self.level + d < self.levels)
        def _():
            self.to_down[d - 1].wait_recv()
            pl.when(self.has_down)(self.to_down[d].start)
            self.to_core[2 * d].start()

    def end(self):
        self.to_core[0].wait()
        pl.when(self.has_up)(self.to_up[0].wait_send)
        pl.when(self.has_down)(self.to_down[0].wait_send)
        for d in range(1, self.levels):
            from_low, from_high = self.level >= d, self.level + d < self.levels
            pl.when(from_low)(self.to_core[2 * d - 1].wait)
            pl.when(from_high)(self.to_core[2 * d].wait)
            pl.when(from_low & self.has_up)(self.to_up[d].wait_send)
            pl.when(from_high & self.has_down)(self.to_down[d].wait_send)
        self.keep.wait()

    @staticmethod
    def shapes(count):
        return [pltpu.SemaphoreType.DMA((count // 2,))] * 4 + [pltpu.SemaphoreType.DMA((count,))] * 2 + [
            pltpu.SemaphoreType.DMA((1,))]


def greet_all(levels, group_partners):
    group, replica = lax.axis_index("group"), lax.axis_index("replica")
    level = replica // 2
    barrier = pltpu.get_barrier_semaphore()

    def greet(partner):
        pl.semaphore_signal(barrier, inc=1, device_id=partner, device_id_type=pl.DeviceIdType.MESH)

    for partner in group_partners + [(group, replica + 1 - 2 * (replica % 2))]:
        greet(partner)

    @pl.when(level > 0)
    def _():
        greet((group, (replica + 2 * levels - 2) % (2 * levels)))

    @pl.when(level < levels - 1)
    def _():
        greet((group, (replica + 2) % (2 * levels)))

    ends = (level + levels - 1) // levels + (2 * levels - 2 - level) // levels
    pl.semaphore_wait(barrier, len(group_partners) + 1 + ends)


def sequence_mask(rows, cols, seqs):
    row = lax.broadcasted_iota(jnp.int32, (rows, cols), 0) // (rows // seqs)
    col = lax.broadcasted_iota(jnp.int32, (rows, cols), 1) % (cols // 2) // (cols // 2 // seqs)
    return (row == col).astype(F32)


def mixer_back_kernel(
    seqs, heads, mixed_ref, w_ref, lift_mixer_ref, down_mixer_ref, conv_ref, inner_ref, lift_ref, table_d_ref,
    table_a_ref, soft_ref, restart_ref, cum_ref, local_ref, carried_ref, pre_ref, lift_branch_ref, lift_input_ref,
    down_gates_ref, taps_ref, agree_ref, early_ref, wide_ref,
    branch_grad_ref, through_one_ref, through_gates_ref, lift_grad_ref, fed_grad_ref, thr_mixer_ref,
    got_early_ref, got_wide_ref, span_ref, total_ref, ends_ref, all_ends_ref, incoming_ref, halo_ref, below_ref, one_ref, gates_ref, first_ref,
    second_ref, low_d_ref, low_a_ref, longer_ref, send, recv, *scratch,
):
    rows, size = conv_ref.shape
    stretch = rows // seqs
    half = lift_ref.shape[0] // 2
    ranks = lift_branch_ref.shape[0]
    step = pl.program_id(0)
    group, replica = lax.axis_index("group"), lax.axis_index("replica")
    partners = [(group + 1 - 2 * (group % 2), replica), ((group + 2) % 4, replica), (3 - group, replica)]

    def copy(src, dst, slot, partner):
        return pltpu.make_async_remote_copy(
            src_ref=src, dst_ref=dst, send_sem=send.at[slot], recv_sem=recv.at[slot], device_id=partner,
            device_id_type=pl.DeviceIdType.MESH)

    early_rows, early_cols = got_early_ref.shape[1:]
    early_half = early_rows // 2
    total_early = GroupSum(
        lambda owner, side: early_ref.at[
            pl.ds(side * early_half, early_half), pl.ds(pl.multiple_of(owner * early_cols, early_cols), early_cols)],
        scratch[:10])
    levels = got_early_ref.shape[0] // 2
    chains = [ReplicaChain(scratch[6], got_early_ref, scratch[10:17]),
              ReplicaChain(wide_ref, got_wide_ref, scratch[17:])]

    exchange = [copy(ends_ref, all_ends_ref.at[group], slot, partner) for slot, partner in enumerate(partners)]
    downward = copy(halo_ref, below_ref, 3, ((group + 3) % 4, replica))

    @pl.when(step == 0)
    def _():
        greet_all(levels, partners)
        total_early.begin()
        chains[1].begin()
        one_ref[...] = jnp.zeros_like(one_ref)
        gates_ref[...] = jnp.zeros_like(gates_ref)
        ends_ref[...] = jnp.zeros_like(ends_ref)
        row = lax.broadcasted_iota(jnp.int32, thr_mixer_ref.shape, 0) // stretch
        col = lax.broadcasted_iota(jnp.int32, thr_mixer_ref.shape, 1) // (thr_mixer_ref.shape[1] // seqs)
        through = dot(mixed_ref[...], lift_mixer_ref[...], NT)
        thr_mixer_ref[...] = jnp.where(row == col, through, 0.0).astype(BF16)

    stops = 3 * heads // (levels + 2)

    @pl.when(step == stops // 2)
    def _():
        total_early.middle()

    @pl.when(step == stops)
    def _():
        total_early.end()
        chains[0].begin()

    for d in range(1, levels):
        @pl.when(step == (d + 1) * stops)
        def _(d=d):
            for chain in chains:
                chain.hop(d)

    groups = stretch // GROUP

    def rows_of(s, k):
        return pl.ds(pl.multiple_of(s * stretch + k * GROUP, GROUP), GROUP)

    @pl.when(step < heads)
    def _():
        cols = pl.ds(pl.multiple_of(step * size, size), size)
        first_ref[...] = dot(mixed_ref[...], w_ref[...], NT) + dot(thr_mixer_ref[...], down_mixer_ref[...])
        second_ref[...] = (dot(conv_ref[...].astype(BF16), table_d_ref[0])
                           + dot(inner_ref[:, :half], lift_ref[:half, :]))
        softrate = soft_ref[...]

        def group(lap, carries):
            k = groups - 1 - lap
            after = []
            for s in range(seqs):
                at = rows_of(s, k)
                restart = restart_ref[at, :] > 0.5
                grown = jnp.exp(-8.0 * softrate / (1.0 + jnp.exp(-second_ref[at, :])))
                decays = jnp.where(restart, 0.0, grown)
                state = local_ref[at, :] + cum_ref[at, :] * carried_ref[s : s + 1, :]
                value, slope = gelu_both(pre_ref[at, :])
                merged = first_ref[at, :]
                branch_grad_ref[at, :] = (merged * state * slope).astype(BF16)
                grads = merged * value
                carry_a, carry_b = carries[s]
                a, b = scan_group(decays, decays * grads, carry_a, carry_b, rows_advanced)
                last = lax.broadcasted_iota(jnp.int32, a.shape, 0) == GROUP - 1
                span_ref[step, at, :] = jnp.where(last, carry_a, pltpu.roll(a, GROUP - 1, 0))
                total_ref[step, at, :] = grads + jnp.where(last, carry_b, pltpu.roll(b, GROUP - 1, 0))
                after.append((a[:1], b[:1]))
            return tuple(after)

        start = (jnp.ones((1, size), F32), jnp.zeros((1, size), F32))
        ends = lax.fori_loop(0, groups, group, (start,) * seqs, unroll=UNROLL)
        for s in range(seqs):
            ends_ref[s : s + 1, cols] = ends[s][0]
            ends_ref[seqs + s : seqs + s + 1, cols] = ends[s][1]
        one_ref[:, :ranks] += dot(branch_grad_ref[...], lift_branch_ref[...], NT)

    @pl.when(step == heads - 1)
    def _():
        for one in exchange:
            one.start()

    @pl.when(step == heads)
    def _():
        for one in exchange:
            one.wait_recv()
        incoming = jnp.zeros(incoming_ref.shape, F32)
        for g in (3, 2, 1):
            longer = all_ends_ref[g, :seqs, :] * incoming + all_ends_ref[g, seqs : 2 * seqs, :]
            incoming = jnp.where(group < g, longer, incoming)
        incoming_ref[...] = incoming

    @pl.when((step >= heads) & (step < 2 * heads))
    def _():
        head = step - heads
        cols = pl.ds(pl.multiple_of(head * size, size), size)
        rounded = conv_ref[...].astype(BF16)
        first_ref[...] = dot(rounded, table_d_ref[0]) + dot(inner_ref[:, :half], lift_ref[:half, :])
        second_ref[...] = dot(rounded, table_a_ref[0]) + dot(inner_ref[:, half:], lift_ref[half:, :])
        softrate = soft_ref[...]
        rate = -8.0 * softrate

        def group(k, carries):
            after = []
            for s in range(seqs):
                at = rows_of(s, k)
                conv = conv_ref[at, :]
                restart = restart_ref[at, :] > 0.5
                decay_gate, admit, grown, scale = gate_steps(
                    first_ref[at, :], second_ref[at, :], softrate, restart)
                state = local_ref[at, :] + cum_ref[at, :] * carried_ref[s : s + 1, :]
                place = lax.broadcasted_iota(jnp.int32, state.shape, 0)
                before = jnp.where(place >= 1, pltpu.roll(state, 1, 0), carries[s])
                grads = total_ref[head, at, :] + span_ref[head, at, :] * incoming_ref[s : s + 1, cols]
                driven = grads * jnp.where(restart, 1.0, scale)
                admitted = conv * admit
                grad_log = jnp.where(restart, 0.0, grads * (before * grown - admitted * grown * grown / scale))
                low_d_ref[at, :] = (rate * grad_log * decay_gate * (1.0 - decay_gate)).astype(BF16)
                low_a_ref[at, :] = (driven * admitted * (1.0 - admit)).astype(BF16)
                total_ref[head, at, :] = driven * admit
                after.append(state[GROUP - 1 :])
            return tuple(after)

        lax.fori_loop(0, groups, group, tuple(carried_ref[s : s + 1, :] for s in range(seqs)), unroll=UNROLL)
        low_d, low_a = low_d_ref[...], low_a_ref[...]
        total_ref[head] += dot(low_d, table_d_ref[0], NT) + dot(low_a, table_a_ref[0], NT)
        gates_ref[:, :half] += dot(low_d, lift_ref[:half, :], NT)
        gates_ref[:, half:] += dot(low_a, lift_ref[half:, :], NT)
        lift_grad_ref[:half, :] = dot(inner_ref[:, :half], low_d, TN)
        lift_grad_ref[half:, :] = dot(inner_ref[:, half:], low_a, TN)

    @pl.when(step == 2 * heads)
    def _():
        through_gates_ref[...] = (gates_ref[...] * sequence_mask(rows, 2 * half, seqs)).astype(BF16)
        tops = []
        for s in range(seqs):
            top = slice(s * stretch, s * stretch + 8)
            direct = jnp.concatenate([total_ref[h, top, :] for h in range(heads)], 1)
            tops.append(direct + dot(through_gates_ref[top, :], down_gates_ref[...]))
        halo_ref[...] = jnp.concatenate(tops, 0).astype(BF16)
        downward.start()
        downward.wait_recv()

    @pl.when(step >= 2 * heads)
    def _():
        head = step - 2 * heads
        cols = pl.ds(pl.multiple_of(head * size, size), size)
        grads = total_ref[head] + dot(through_gates_ref[...], down_gates_ref[:, cols])
        for s in range(seqs):
            longer_ref[s, :stretch, :] = grads[s * stretch : (s + 1) * stretch, :]
            longer_ref[s, stretch:, :] = below_ref[s * 8 : (s + 1) * 8, cols].astype(F32)

        def group(k, _):
            for s in range(seqs):
                at = rows_of(s, k)
                ahead = longer_ref[s, pl.ds(pl.multiple_of(k * GROUP, GROUP), GROUP + 8), :]
                total = taps_ref[0:1, :] * agree_ref[at, 0:1] * ahead[:GROUP]
                for j in range(1, taps_ref.shape[0]):
                    moved = pltpu.roll(ahead, GROUP + 8 - j, 0)[:GROUP]
                    total += taps_ref[j : j + 1, :] * agree_ref[at, j : j + 1] * moved
                fed_grad_ref[at, :] = total.astype(BF16)
            return 0

        lax.fori_loop(0, groups, group, 0, unroll=UNROLL)
        one_ref[:, ranks:] += dot(fed_grad_ref[...], lift_input_ref[...], NT)

    @pl.when(step == 3 * heads - 1)
    def _():
        through_one_ref[...] = (one_ref[...] * sequence_mask(rows, 2 * ranks, seqs)).astype(BF16)
        for one in exchange:
            one.wait_send()
        downward.wait_send()
        total_early.clear()
        for chain in chains:
            chain.end()


def mixer_back(seqs, mixed, w_mixer, lift_mixer, down_mixer, conv, inner, lift, table_d, table_a, softrate, restart,
               cum, local, carried, pre, lift_branch, lift_input, down_gates, taps, agree, early, wide):
    rows, width = conv.shape
    count, early_cols = lax.axis_size("replica"), width // 4
    heads, size = table_d.shape[:2]
    first = lambda i: jnp.minimum(i, heads - 1)
    second = lambda i: jnp.clip(i - heads, 0, heads - 1)
    third = lambda i: jnp.maximum(i - 2 * heads, 0)
    either = lambda i: jnp.minimum(i, 2 * heads - 1) % heads
    full = lambda array: pl.BlockSpec(array.shape, lambda i: (0, 0), pipeline_mode=pl.Buffered(1))
    cols = lambda array, at: pl.BlockSpec((array.shape[0], size), lambda i: (0, at(i)))
    table = pl.BlockSpec((1, size, size), lambda i: (either(i), 0, 0))
    middle = inner.shape[1]
    tile = lambda at: pl.BlockSpec((rows, size), lambda i: (0, at(i)))
    whole = lambda count: pl.BlockSpec((rows, count), lambda i: (0, 0))
    return pl.pallas_call(
        functools.partial(mixer_back_kernel, seqs, heads),
        grid=(3 * heads,),
        out_shape=[
            jax.ShapeDtypeStruct((rows, width), BF16),
            jax.ShapeDtypeStruct((rows, 2 * lift_branch.shape[0]), BF16),
            jax.ShapeDtypeStruct((rows, middle), BF16),
            jax.ShapeDtypeStruct(lift.shape, F32),
            jax.ShapeDtypeStruct((rows, width), BF16),
            jax.ShapeDtypeStruct((rows, lift_mixer.shape[0]), BF16),
            jax.ShapeDtypeStruct((count, early.shape[0], early_cols), BF16),
            jax.ShapeDtypeStruct((count,) + wide.shape, BF16),
        ],
        in_specs=[
            full(mixed), pl.BlockSpec((size, width), lambda i: (first(i), 0)), full(lift_mixer), cols(down_mixer, first),
            cols(conv, either), full(inner), cols(lift, either), table, table, cols(softrate, either), full(restart),
            cols(cum, either), cols(local, either), cols(carried, either), cols(pre, first), cols(lift_branch, first),
            cols(lift_input, third), full(down_gates), cols(taps, third), full(agree), ANYWHERE, ANYWHERE,
        ],
        out_specs=[tile(first), whole(2 * lift_branch.shape[0]), whole(middle),
                   pl.BlockSpec((lift.shape[0], size), lambda i: (0, second(i))), tile(third),
                   whole(lift_mixer.shape[0]), ANYWHERE, ANYWHERE],
        scratch_shapes=[
            pltpu.VMEM((heads, rows, size), F32), pltpu.VMEM((heads, rows, size), F32), pltpu.VMEM((8, width), F32),
            pltpu.VMEM((4, 8, width), F32), pltpu.VMEM((seqs, width), F32), pltpu.VMEM((8 * seqs, width), BF16),
            pltpu.VMEM((8 * seqs, width), BF16), pltpu.VMEM((rows, 2 * lift_branch.shape[0]), F32),
            pltpu.VMEM((rows, middle), F32), pltpu.VMEM((rows, size), F32), pltpu.VMEM((rows, size), F32),
            pltpu.VMEM((rows, size), BF16), pltpu.VMEM((rows, size), BF16),
            pltpu.VMEM((seqs, rows // seqs + 8, size), F32), pltpu.SemaphoreType.DMA((4,)),
            pltpu.SemaphoreType.DMA((4,))]
        + GroupSum.shapes(early.shape[0], early_cols) + ReplicaChain.shapes(count) + ReplicaChain.shapes(count),
        compiler_params=pltpu.CompilerParams(
            vmem_limit_bytes=VMEM, collective_id=3, has_side_effects=True),
        cost_estimate=pl.CostEstimate(
            flops=2 * rows * width * width + 20 * rows * width * size + 200 * rows * width,
            bytes_accessed=40 * rows * width + 2 * width * width, transcendentals=12 * rows * width),
    )(mixed, w_mixer, lift_mixer, down_mixer, conv, inner, lift, table_d, table_a, softrate, restart, cum, local,
      carried, pre, lift_branch, lift_input, down_gates, taps, agree, early, wide)


def resident(array):
    return pl.BlockSpec(array.shape, lambda i: (0, 0), pipeline_mode=pl.Buffered(1))


def tile_of(count, tile):
    return tile if count % 128 == 0 and count > tile else count


def grad_hidden_kernel(seqs, gather, steps, *refs):
    if gather:
        cot_ref, wd_ref, lift_out_ref, do_ref, block_ref, out_ref, through_ref, all_ref = refs[:8]
        staged_ref, send, recv, local = refs[8:]
    else:
        cot_ref, wd_ref, lift_out_ref, do_ref, out_ref, through_ref = refs
    ranks = do_ref.shape[0] // seqs
    step = pl.program_id(0)

    if gather:
        group, replica = lax.axis_index("group"), lax.axis_index("replica")
        beside, above = group + 1 - 2 * (group % 2), (group + 2) % 4
        at_beside, at_above = (beside, replica), (above, replica)
        rows = block_ref.shape[0]
        half = rows // 2

        def place(owner, part):
            return all_ref.at[pl.ds(pl.multiple_of(owner * rows + part * half, half), half), :]

        def own(part):
            return block_ref.at[pl.ds(part * half, half), :]

        def copy(src, dst, slot, partner):
            return pltpu.make_async_remote_copy(
                src_ref=src, dst_ref=dst, send_sem=send.at[slot], recv_sem=recv.at[slot], device_id=partner,
                device_id_type=pl.DeviceIdType.MESH)

        firsts = [copy(own(1), place(group, 1), 0, at_beside), copy(own(0), place(group, 0), 1, at_above),
                  copy(own(0), place(group, 0), 2, at_beside), copy(own(1), place(group, 1), 3, at_above)]
        seconds = [copy(place(beside, 1), place(beside, 1), 4, at_above),
                   copy(place(above, 0), place(above, 0), 5, at_beside)]
        stage = pltpu.make_async_copy(block_ref, staged_ref, local.at[0])
        keep = pltpu.make_async_copy(
            staged_ref, all_ref.at[pl.ds(pl.multiple_of(group * rows, rows), rows), :], local.at[1])

        @pl.when(step == 0)
        def _():
            barrier = pltpu.get_barrier_semaphore()
            for partner in (at_beside, at_above):
                pl.semaphore_signal(barrier, inc=1, device_id=partner, device_id_type=pl.DeviceIdType.MESH)
            pl.semaphore_wait(barrier, 2)
            for one in firsts[:2]:
                one.start()
            stage.start()

    @pl.when(step == 0)
    def _():
        for s in range(seqs):
            through_ref[s] = dot(cot_ref[s], lift_out_ref[s * ranks : (s + 1) * ranks, :], NT).astype(BF16)

    for s in range(seqs):
        out_ref[s] = (dot(cot_ref[s], wd_ref[...], NT)
                      + dot(through_ref[s], do_ref[s * ranks : (s + 1) * ranks, :])).astype(BF16)

    if gather:
        @pl.when(step == 0)
        def _():
            stage.wait()
            keep.start()
            for one in firsts[2:]:
                one.start()

        @pl.when(step == min(1, steps - 1))
        def _():
            for one, then in zip(firsts[:2], seconds):
                one.wait_recv()
                then.start()

        @pl.when(step == steps - 1)
        def _():
            for one in firsts[2:] + seconds:
                one.wait_recv()
            for one in firsts + seconds:
                one.wait_send()
            keep.wait()


def grad_hidden_call(cot, wd, lift_out, do, block):
    seqs, rows, width = cot.shape
    units, ranks = wd.shape[0], do.shape[0] // seqs
    tile = tile_of(units, 512)
    gather = lax.axis_size("group") == 4
    got = pl.pallas_call(
        functools.partial(grad_hidden_kernel, seqs, gather, pl.cdiv(units, tile)),
        grid=(pl.cdiv(units, tile),),
        out_shape=[jax.ShapeDtypeStruct((seqs, rows, units), BF16), jax.ShapeDtypeStruct((seqs, rows, ranks), BF16)]
        + [jax.ShapeDtypeStruct((rows, width), BF16)] * gather,
        in_specs=[pl.BlockSpec(cot.shape, lambda i: (0, 0, 0), pipeline_mode=pl.Buffered(1)),
                  pl.BlockSpec((tile, width), lambda i: (i, 0)), resident(lift_out),
                  pl.BlockSpec((seqs * ranks, tile), lambda i: (0, i))] + [ANYWHERE] * gather,
        out_specs=[pl.BlockSpec((seqs, rows, tile), lambda i: (0, 0, i)),
                   pl.BlockSpec((seqs, rows, ranks), lambda i: (0, 0, 0))] + [ANYWHERE] * gather,
        scratch_shapes=[pltpu.VMEM(block.shape, BF16), pltpu.SemaphoreType.DMA((6,)), pltpu.SemaphoreType.DMA((6,)),
                        pltpu.SemaphoreType.DMA((2,))] if gather else [],
        compiler_params=pltpu.CompilerParams(
            vmem_limit_bytes=VMEM, **(dict(collective_id=1, has_side_effects=True) if gather else {})),
        cost_estimate=pl.CostEstimate(
            flops=2 * seqs * rows * width * units,
            bytes_accessed=2 * width * units + 2 * seqs * rows * (units + width), transcendentals=0),
    )(cot, wd, lift_out, do, *([block] if gather else []))
    return got if gather else list(got) + [lax.all_gather(block, "group", axis=0, tiled=True)]


def feed_kernel(steps, tile, units, tok_ref, gh_ref, wg_ref, wu_ref, wg_rows_ref, wu_rows_ref, down_ref, lg_ref,
                lu_ref, through_out_ref, lg_full_ref, lu_full_ref, down_cols_ref, *refs):
    hidden_ref, back_ref, wide_ref, through_ref, inner_ref, gg_ref, gu_ref = refs[-7:]
    ranks = lg_ref.shape[0]
    step = pl.program_id(0)

    @pl.when(step == 0)
    def _():
        inner_ref[...] = dot(tok_ref[...], down_ref[...], NT).astype(BF16)

    @pl.when(step < steps)
    def _():
        tokens, inner = tok_ref[...], inner_ref[...]
        gate = dot(tokens, wg_ref[...]) + dot(inner[:, :ranks], lg_ref[...])
        upper = dot(tokens, wu_ref[...]) + dot(inner[:, ranks:], lu_ref[...])
        grad_hidden = gh_ref[...].astype(F32)
        value, slope = gelu_both(gate)
        hidden = (value * upper).astype(BF16)
        grad_gate = (grad_hidden * upper * slope).astype(BF16)
        grad_upper = (grad_hidden * value).astype(BF16)
        hidden_ref[...] = hidden
        cols = pl.ds(pl.multiple_of(step * tile, tile), tile) if steps > 1 else slice(0, tile)
        gg_ref[:, cols] = grad_gate
        gu_ref[:, cols] = grad_upper
        wide_ref[:ranks, :] = dot(inner[:, :ranks], grad_gate, TN).astype(BF16)
        wide_ref[ranks : 2 * ranks, :] = dot(inner[:, ranks:], grad_upper, TN).astype(BF16)
        wide_ref[2 * ranks :, :] = dot(through_out_ref[...], hidden, TN).astype(BF16)

    @pl.when(step == steps)
    def _():
        through_ref[:, :ranks] = dot(gg_ref[:, :units], lg_full_ref[...], NT).astype(BF16)
        through_ref[:, ranks:] = dot(gu_ref[:, :units], lu_full_ref[...], NT).astype(BF16)

    @pl.when(step >= steps)
    def _():
        back_ref[...] = (dot(gg_ref[:, :units], wg_rows_ref[...], NT) + dot(gu_ref[:, :units], wu_rows_ref[...], NT)
                         + dot(through_ref[...], down_cols_ref[...])).astype(BF16)


def feed_call(s, tok, gh, wg, wu, down, lg, lu, through_out):
    rows, width = tok.shape
    units, ranks = wg.shape[1], lg.shape[0]
    tile, span = tile_of(units, 512), tile_of(width, 512)
    steps, laps = pl.cdiv(units, tile), pl.cdiv(width, span)
    first = lambda i: jnp.minimum(i, steps - 1)
    second = lambda i: jnp.maximum(i - steps, 0)
    cols = pl.BlockSpec((width, tile), lambda i: (0, first(i)))
    across = pl.BlockSpec((span, units), lambda i: (second(i), 0))
    rank = pl.BlockSpec((ranks, tile), lambda i: (0, first(i)))
    out = pl.BlockSpec((rows, tile), lambda i: (0, first(i)))
    return pl.pallas_call(
        functools.partial(feed_kernel, steps, tile, units),
        grid=(steps + laps,),
        out_shape=[jax.ShapeDtypeStruct((rows, units), BF16), jax.ShapeDtypeStruct((rows, width), BF16),
                   jax.ShapeDtypeStruct((3 * ranks, units), BF16), jax.ShapeDtypeStruct((rows, 2 * ranks), BF16)],
        in_specs=[resident(tok), pl.BlockSpec((None, rows, tile), lambda i: (s, 0, first(i))), cols, cols, across,
                  across, resident(down), rank, rank, pl.BlockSpec((None, rows, ranks), lambda i: (s, 0, 0)),
                  resident(lg), resident(lu), pl.BlockSpec((2 * ranks, span), lambda i: (0, second(i)))],
        out_specs=[out, pl.BlockSpec((rows, span), lambda i: (0, second(i))),
                   pl.BlockSpec((3 * ranks, tile), lambda i: (0, first(i))),
                   pl.BlockSpec((rows, 2 * ranks), lambda i: (0, 0))],
        scratch_shapes=[pltpu.VMEM((rows, 2 * ranks), BF16), pltpu.VMEM((rows, steps * tile), BF16),
                        pltpu.VMEM((rows, steps * tile), BF16)],
        compiler_params=pltpu.CompilerParams(vmem_limit_bytes=VMEM),
        cost_estimate=pl.CostEstimate(
            flops=8 * rows * width * units, bytes_accessed=8 * width * units + 6 * rows * units,
            transcendentals=rows * units),
    )(tok, gh, wg, wu, wg, wu, down, lg, lu, through_out, lg, lu, down)


def outward_kernel(seqs, reduce, steps, *refs):
    hiddens, tokens, throughs, cot_ref, refs = (
        refs[:seqs], refs[seqs : 2 * seqs], refs[2 * seqs : 3 * seqs], refs[3 * seqs], refs[3 * seqs + 1 :])
    if reduce:
        wd_ref, do_ref, lift_out_ref, back_ref, out_ref, inner_ref, early_ref, sum_ref = refs[:8]
        first_a, first_b, second_a, second_b, pass_a, pass_b, own_ref, send, recv, local = refs[8:]
    else:
        wd_ref, do_ref, lift_out_ref, out_ref, inner_ref, early_ref = refs
    ranks = do_ref.shape[0] // seqs
    step = pl.program_id(0)

    if reduce:
        group, replica = lax.axis_index("group"), lax.axis_index("replica")
        beside, above, across = group + 1 - 2 * (group % 2), (group + 2) % 4, 3 - group
        at_beside, at_above = (beside, replica), (above, replica)
        rows, width = own_ref.shape
        half = width // 2

        def part(owner, side):
            return back_ref.at[pl.ds(pl.multiple_of(owner * rows, rows), rows), pl.ds(side * half, half)]

        def copy(src, dst, slot, partner):
            return pltpu.make_async_remote_copy(
                src_ref=src, dst_ref=dst, send_sem=send.at[slot], recv_sem=recv.at[slot], device_id=partner,
                device_id_type=pl.DeviceIdType.MESH)

        firsts = [copy(part(across, 0), first_a.at[1], 0, at_beside), copy(part(across, 1), first_b.at[1], 1, at_above),
                  copy(part(beside, 0), first_a.at[0], 2, at_beside), copy(part(above, 1), first_b.at[0], 3, at_above)]
        seconds = [copy(pass_a, second_a, 4, at_above), copy(pass_b, second_b, 5, at_beside)]
        loads = [pltpu.make_async_copy(part(above, 0), pass_a, local.at[0]),
                 pltpu.make_async_copy(part(beside, 1), pass_b, local.at[1]),
                 pltpu.make_async_copy(
                     back_ref.at[pl.ds(pl.multiple_of(group * rows, rows), rows), :], own_ref, local.at[2])]

        @pl.when(step == 0)
        def _():
            barrier = pltpu.get_barrier_semaphore()
            for partner in (at_beside, at_above):
                pl.semaphore_signal(barrier, inc=1, device_id=partner, device_id_type=pl.DeviceIdType.MESH)
            pl.semaphore_wait(barrier, 2)
            for one in firsts:
                one.start()
            for one in loads:
                one.start()

    @pl.when(step == 0)
    def _():
        for s, hidden_ref in enumerate(hiddens):
            inner_ref[s] = dot(hidden_ref[...], do_ref[s * ranks : (s + 1) * ranks, :], NT).astype(BF16)

    for s, hidden_ref in enumerate(hiddens):
        out_ref[s] = (dot(hidden_ref[...], wd_ref[...])
                      + dot(inner_ref[s], lift_out_ref[s * ranks : (s + 1) * ranks, :])).astype(BF16)
        both = dot(throughs[s][...], tokens[s][...], TN).astype(BF16)
        for kind, rows_of in enumerate((both[:ranks], both[ranks:], dot(inner_ref[s], cot_ref[s], TN).astype(BF16))):
            row = (kind * seqs + s) * ranks
            early_ref[row : row + ranks, :] = rows_of

    if reduce:
        @pl.when(step == max(steps - 2, 0))
        def _():
            for one in loads:
                one.wait()
            for one in firsts:
                one.wait_recv()
            pass_a[...] = (pass_a[...].astype(F32) + first_a[1].astype(F32)).astype(BF16)
            pass_b[...] = (pass_b[...].astype(F32) + first_b[1].astype(F32)).astype(BF16)
            for one in seconds:
                one.start()

        @pl.when(step == steps - 1)
        def _():
            for one in seconds:
                one.wait_recv()
            sum_ref[:, :half] = (own_ref[:, :half].astype(F32) + first_a[0].astype(F32)
                                 + second_a[...].astype(F32)).astype(BF16)
            sum_ref[:, half:] = (own_ref[:, half:].astype(F32) + first_b[0].astype(F32)
                                 + second_b[...].astype(F32)).astype(BF16)
            for one in firsts + seconds:
                one.wait_send()


def outward_call(hiddens, tokens, throughs, cot, wd, do, lift_out, back):
    rows, units = hiddens[0].shape
    seqs = len(hiddens)
    width, ranks = wd.shape[1], do.shape[0] // seqs
    tile = tile_of(width, 512)
    steps = pl.cdiv(width, tile)
    group = lax.axis_size("group")
    reduce = group == 4 and width % 256 == 0
    own, half = rows // group, width // 2
    scratch = [pltpu.VMEM((2, own, half), BF16)] * 2 + [pltpu.VMEM((own, half), BF16)] * 4 + [
        pltpu.VMEM((own, width), BF16), pltpu.SemaphoreType.DMA((6,)), pltpu.SemaphoreType.DMA((6,)),
        pltpu.SemaphoreType.DMA((3,))]
    got = pl.pallas_call(
        functools.partial(outward_kernel, seqs, reduce, steps),
        grid=(steps,),
        out_shape=[jax.ShapeDtypeStruct((seqs, rows, width), BF16), jax.ShapeDtypeStruct((seqs, rows, ranks), BF16),
                   jax.ShapeDtypeStruct((3 * seqs * ranks, width), BF16)]
        + [jax.ShapeDtypeStruct((own, width), BF16)] * reduce,
        in_specs=[resident(hidden) for hidden in hiddens] + [pl.BlockSpec((rows, tile), lambda i: (0, i))] * seqs
        + [resident(through) for through in throughs] + [pl.BlockSpec((seqs, rows, tile), lambda i: (0, 0, i))]
        + [pl.BlockSpec((units, tile), lambda i: (0, i)), resident(do),
           pl.BlockSpec((seqs * ranks, tile), lambda i: (0, i))] + [ANYWHERE] * reduce,
        out_specs=[pl.BlockSpec((seqs, rows, tile), lambda i: (0, 0, i)),
                   pl.BlockSpec((seqs, rows, ranks), lambda i: (0, 0, 0)),
                   pl.BlockSpec((3 * seqs * ranks, tile), lambda i: (0, i))]
        + [pl.BlockSpec((own, width), lambda i: (0, 0))] * reduce,
        scratch_shapes=scratch if reduce else [],
        compiler_params=pltpu.CompilerParams(
            vmem_limit_bytes=VMEM, **(dict(collective_id=2, has_side_effects=True) if reduce else {})),
        cost_estimate=pl.CostEstimate(
            flops=2 * seqs * rows * width * units,
            bytes_accessed=2 * width * units + 2 * seqs * rows * (units + width), transcendentals=0),
    )(*hiddens, *tokens, *throughs, cot, wd, do, lift_out, *([back] if reduce else []))
    return got if reduce else list(got) + [lax.psum_scatter(back, "group", scatter_dimension=0, tiled=True)]


def pick_kernel(counts, ids_ref, *refs):
    tables, (stack_ref, wide_ref) = refs[: sum(counts)], refs[sum(counts) :]
    for i, table in enumerate(tables):
        if i < counts[0]:
            stack_ref[i, 0] = table[0]
        else:
            wide_ref[i - counts[0], 0] = table[0]


def pick(ids, narrow, wide):
    seqs, ranks = ids.shape[0], narrow[0].shape[1]
    counts = (len(narrow), len(wide))
    widths = (narrow[0].shape[2], wide[0].shape[2])
    tables = [pl.BlockSpec((1, ranks, table.shape[2]), lambda s, ids: (ids[s], 0, 0)) for table in narrow + wide]
    picked = pl.pallas_call(
        functools.partial(pick_kernel, counts),
        out_shape=[jax.ShapeDtypeStruct((count, seqs, ranks, width), BF16) for count, width in zip(counts, widths)],
        grid_spec=pltpu.PrefetchScalarGridSpec(
            num_scalar_prefetch=1,
            grid=(seqs,),
            in_specs=tables,
            out_specs=[pl.BlockSpec((count, 1, ranks, width), lambda s, ids: (0, s, 0, 0))
                       for count, width in zip(counts, widths)],
        ),
    )(ids, *narrow, *wide)
    return [part.reshape(-1, part.shape[-1]) for part in picked]


def gather_kernel(units, *refs):
    weights, passed, wholes, handed_out = refs[:4], refs[4], refs[5:9], refs[9]
    staged, handed, (send, recv, local) = refs[10:14], refs[14], refs[15:]
    group, replica = lax.axis_index("group"), lax.axis_index("replica")
    beside, above, across = group + 1 - 2 * (group % 2), (group + 2) % 4, 3 - group
    core, level = replica % 2, (replica // 2) % 2
    at_beside, at_above = (beside, replica), (above, replica)
    at_core, at_level = (group, replica + 1 - 2 * core), (group, replica + 2 - 4 * level)
    partners = (at_beside, at_above, at_core, at_level)
    mine, other = 2 * core + level, 2 * core + 1 - level

    barrier = pltpu.get_barrier_semaphore()
    for partner in partners:
        pl.semaphore_signal(barrier, inc=1, device_id=partner, device_id_type=pl.DeviceIdType.MESH)
    pl.semaphore_wait(barrier, 4)

    kept = [pltpu.make_async_copy(weight, stage, local.at[m])
            for m, (weight, stage) in enumerate(zip(weights, staged))]
    for one in kept:
        one.start()

    def keep(m):
        whole = wholes[m]
        rows, cols = weights[m].shape
        if m == 2:
            into = whole.at[pl.ds(pl.multiple_of(group * rows, rows), rows), :]
        else:
            into = whole.at[:, pl.ds(pl.multiple_of(group * cols, cols), cols)]
        kept[m].wait()
        kept[m] = pltpu.make_async_copy(staged[m], into, local.at[m])
        kept[m].start()

    def own(m, part, quarter):
        weight = weights[m]
        size = wholes[m].shape[0] // 4
        step = size // units
        if m < 2:
            return weight.at[pl.ds(pl.multiple_of(quarter * size + part * step, step), step), :]
        return weight.at[pl.ds(part * step, step), pl.ds(pl.multiple_of(quarter * size, size), size)]

    def piece(m, part, shard, quarter):
        whole = wholes[m]
        size = whole.shape[0] // 4
        step = size // units
        down, along = (quarter, shard) if m < 2 else (shard, quarter)
        return whole.at[pl.ds(pl.multiple_of(down * size + part * step, step), step),
                        pl.ds(pl.multiple_of(along * size, size), size)]

    def copy(src, dst, k, slot, partner):
        made = pltpu.make_async_remote_copy(
            src_ref=src, dst_ref=dst, send_sem=send.at[k, slot], recv_sem=recv.at[k, slot], device_id=partner,
            device_id_type=pl.DeviceIdType.MESH)
        made.start()
        return made

    def forward(m, part, shard, quarter, k, slot, partner):
        where = piece(m, part, shard, quarter)
        return copy(where, where, k, slot, partner)

    ranks, cols = weights[3].shape
    last = 3 * units

    def stack_piece(first, count, shard):
        return wholes[3].at[pl.ds(first, count), pl.ds(pl.multiple_of(shard * cols, cols), cols)]

    steps = [(m, part) for m in range(3) for part in range(units)]
    made = {}

    def begin(k):
        m, part = steps[k]
        made[k, 0] = copy(own(m, part, mine), piece(m, part, group, mine), k, 0, at_above)
        made[k, 2] = copy(own(m, part, mine), piece(m, part, group, mine), k, 2, at_beside)
        made[k, 1] = copy(own(m, part, other), piece(m, part, group, other), k, 1, at_above)

    begin(0)
    begin(1)
    for m in range(4):
        keep(m)
    onward = pltpu.make_async_copy(passed, handed, local.at[4])
    onward.start()
    for t in range(len(steps) + 2):
        if t < len(steps):
            m, part = steps[t]
            made[t, 0].wait_recv()
            made[t, 4] = forward(m, part, above, mine, t, 4, at_beside)
            made[t, 6] = forward(m, part, above, mine, t, 6, at_core)
            made[t, 2].wait_recv()
            made[t, 3] = forward(m, part, beside, mine, t, 3, at_level)
            made[t, 8] = forward(m, part, beside, mine, t, 8, at_core)
            if t + 2 < len(steps):
                begin(t + 2)
            if t + 3 == len(steps):
                stack_beside = copy(weights[3], stack_piece(0, ranks, group), last, 0, at_beside)
                stack_above = copy(weights[3], stack_piece(0, ranks, group), last, 1, at_above)
            made[t, 1].wait_recv()
            made[t, 7] = forward(m, part, above, other, t, 7, at_core)
        if 1 <= t <= len(steps):
            m, part = steps[t - 1]
            made[t - 1, 4].wait_recv()
            made[t - 1, 5] = forward(m, part, across, mine, t - 1, 5, at_level)
            made[t - 1, 10] = forward(m, part, across, mine, t - 1, 10, at_core)
            made[t - 1, 3].wait_recv()
            made[t - 1, 9] = forward(m, part, beside, other, t - 1, 9, at_core)
        if 2 <= t:
            m, part = steps[t - 2]
            made[t - 2, 5].wait_recv()
            made[t - 2, 11] = forward(m, part, across, other, t - 2, 11, at_core)
        if t == len(steps):
            stack_beside.wait_recv()
            stack_above.wait_recv()
            half = ranks // 2
            lower = stack_piece(0, half, above)
            upper = stack_piece(half, half, beside)
            stack_lower = copy(lower, lower, last, 2, at_beside)
            stack_upper = copy(upper, upper, last, 3, at_above)
    onward.wait()
    onward = pltpu.make_async_copy(handed, handed_out, local.at[4])
    onward.start()
    for k in range(len(steps)):
        for slot in range(6, 12):
            made[k, slot].wait_recv()
    for k in range(len(steps)):
        for slot in range(12):
            made[k, slot].wait_send()
    for one in (stack_lower, stack_upper):
        one.wait_recv()
    for one in (stack_beside, stack_above, stack_lower, stack_upper):
        one.wait_send()
    for one in kept + [onward]:
        one.wait()


def gather_weights(w_branch, w_input, w_mixer, stack, passed):
    width = w_branch.shape[0]
    if lax.axis_size("group") != 4 or lax.axis_size("replica") % 4 != 0:
        return (lax.all_gather(w_branch, "group", axis=1, tiled=True),
                lax.all_gather(w_input, "group", axis=1, tiled=True),
                lax.all_gather(w_mixer, "group", axis=0, tiled=True),
                lax.all_gather(stack, "group", axis=1, tiled=True), passed)
    units = 4
    operands = (w_branch, w_input, w_mixer, stack, passed)
    return pl.pallas_call(
        functools.partial(gather_kernel, units),
        out_shape=[jax.ShapeDtypeStruct((width, width), BF16)] * 3
        + [jax.ShapeDtypeStruct((stack.shape[0], width), BF16), jax.ShapeDtypeStruct(passed.shape, passed.dtype)],
        in_specs=[ANYWHERE] * 5,
        out_specs=[ANYWHERE] * 5,
        scratch_shapes=[pltpu.VMEM(operand.shape, BF16) for operand in operands]
        + [pltpu.SemaphoreType.DMA((3 * units + 1, 12)), pltpu.SemaphoreType.DMA((3 * units + 1, 12)),
           pltpu.SemaphoreType.DMA((5,))],
        compiler_params=pltpu.CompilerParams(
            collective_id=0, has_side_effects=True, vmem_limit_bytes=VMEM),
        cost_estimate=pl.CostEstimate(flops=0, bytes_accessed=400 * 2**20, transcendentals=0),
    )(*operands)


def ordered_kernel(*refs):
    del refs


def ordered(value, *earlier):
    return pl.pallas_call(
        ordered_kernel,
        out_shape=jax.ShapeDtypeStruct(value.shape, value.dtype),
        in_specs=[ANYWHERE] * (1 + len(earlier)),
        out_specs=ANYWHERE,
        input_output_aliases={0: 0},
    )(value, *earlier)


def row_tiles(rows, width, count):
    step = min(rows, 128)
    return (rows // step,), [pl.BlockSpec((step, width), lambda i: (i, 0))] * count


def resid_grad_kernel(per, resid_ref, cot_ref, gain_ref, *refs):
    pieces, (full_ref, low_ref) = refs[:-2], refs[-2:]
    grads = pieces[0][...]
    for s, piece in enumerate(pieces[1:], 1):
        grads = jnp.where(pl.program_id(0) >= s * per, piece[...], grads)
    values = resid_ref[...]
    rate = lax.rsqrt(jnp.mean(values * values, axis=-1, keepdims=True) + EPS)
    grads = cot_ref[...].astype(F32) + norm_back(values, gain_ref[...], rate, grads.astype(F32))
    full_ref[...] = grads
    low_ref[...] = grads.astype(BF16)


def resid_grad(resid, cot, gain, pieces):
    rows, width = resid.shape
    step = min(pieces[0].shape[0], 128)
    per = pieces[0].shape[0] // step
    tile = pl.BlockSpec((step, width), lambda i: (i, 0))
    return pl.pallas_call(
        functools.partial(resid_grad_kernel, per),
        grid=(rows // step,),
        out_shape=[jax.ShapeDtypeStruct((rows, width), F32), jax.ShapeDtypeStruct((rows, width), BF16)],
        in_specs=[tile, tile, pl.BlockSpec((1, width), lambda i: (0, 0))] + [
            pl.BlockSpec((step, width), lambda i, s=s: (jnp.clip(i - s * per, 0, per - 1), 0))
            for s in range(len(pieces))],
        out_specs=[tile, tile],
        compiler_params=pltpu.CompilerParams(vmem_limit_bytes=VMEM),
        cost_estimate=pl.CostEstimate(
            flops=20 * rows * width, bytes_accessed=14 * rows * width, transcendentals=rows),
    )(resid, cot, gain, *pieces)


def finish_kernel(grad_resid_ref, inputs_ref, gain_ref, grads_ref, resid_ref, outward_ref, out_ref, block_ref):
    values = inputs_ref[...].astype(F32)
    rate = lax.rsqrt(jnp.mean(values * values, axis=-1, keepdims=True) + EPS)
    out_ref[...] = grad_resid_ref[...] + norm_back(values, gain_ref[...], rate, grads_ref[...])
    block_ref[...] = (resid_ref[...] + outward_ref[...].astype(F32)).astype(BF16)


def finish(grad_resid, inputs, gain, grads, resid, outward):
    rows, width = inputs.shape
    grid, tiles = row_tiles(rows, width, 5)
    return pl.pallas_call(
        finish_kernel,
        grid=grid,
        out_shape=[jax.ShapeDtypeStruct((rows, width), F32), jax.ShapeDtypeStruct((rows, width), BF16)],
        in_specs=tiles[:2] + [pl.BlockSpec((1, width), lambda i: (0, 0))] + tiles[:3],
        out_specs=tiles[:2],
        compiler_params=pltpu.CompilerParams(vmem_limit_bytes=VMEM),
        cost_estimate=pl.CostEstimate(
            flops=21 * rows * width, bytes_accessed=22 * rows * width, transcendentals=rows),
    )(grad_resid, inputs, gain, grads, resid, outward)


def tail_kernel(
    steps, branch_grad_ref, fed_grad_ref, w_branch_ref, w_input_ref, through_ref, down_ref, partial_ref,
    out_ref, got_ref, *scratch,
):
    step = pl.program_id(0)
    levels = got_ref.shape[0] // 2
    group, replica = lax.axis_index("group"), lax.axis_index("replica")
    ranks = got_ref.shape[1]
    half = ranks // 2
    total = GroupSum(lambda owner, side: partial_ref.at[owner, pl.ds(side * half, half), :], scratch[:10])
    chain = ReplicaChain(scratch[6], got_ref, scratch[10:])

    @pl.when(step == 0)
    def _():
        greet_all(levels, [(group + 1 - 2 * (group % 2), replica), ((group + 2) % 4, replica)])
        total.begin()

    out_ref[...] = (dot(branch_grad_ref[...], w_branch_ref[...], NT) + dot(fed_grad_ref[...], w_input_ref[...], NT)
                    + dot(through_ref[...], down_ref[...]))

    @pl.when(step == max(steps - 2, 0))
    def _():
        total.middle()

    @pl.when(step == steps - 1)
    def _():
        total.end()
        chain.begin()
        for d in range(1, levels):
            chain.hop(d)
        chain.end()
        total.clear()


def tail_call(branch_grad, fed_grad, w_branch, w_input, through, down, partial):
    rows, width = branch_grad.shape
    ranks, cols = partial.shape[1:]
    count = lax.axis_size("replica")
    tile = tile_of(width, 512)
    steps = pl.cdiv(width, tile)
    weight = pl.BlockSpec((tile, width), lambda i: (i, 0))
    return pl.pallas_call(
        functools.partial(tail_kernel, steps),
        grid=(steps,),
        out_shape=[jax.ShapeDtypeStruct((rows, width), F32), jax.ShapeDtypeStruct((count, ranks, cols), BF16)],
        in_specs=[resident(branch_grad), resident(fed_grad), weight, weight, resident(through),
                  pl.BlockSpec((down.shape[0], tile), lambda i: (0, i)), ANYWHERE],
        out_specs=[pl.BlockSpec((rows, tile), lambda i: (0, i)), ANYWHERE],
        scratch_shapes=GroupSum.shapes(ranks, cols) + ReplicaChain.shapes(count),
        compiler_params=pltpu.CompilerParams(
            vmem_limit_bytes=VMEM, collective_id=4, has_side_effects=True),
        cost_estimate=pl.CostEstimate(
            flops=4 * rows * width * width, bytes_accessed=4 * width * width + 8 * rows * width, transcendentals=0),
    )(branch_grad, fed_grad, w_branch, w_input, through, down, partial)


def spread_kernel(counts, ids_ref, *refs):
    gots, outs = refs[: len(counts)], refs[len(counts) :]
    ranks = outs[0].shape[1]
    replicas = gots[0].shape[0]
    seqs = ids_ref.shape[0] // replicas
    for out_ref in outs:
        out_ref[...] = jnp.zeros_like(out_ref)
    for replica in range(replicas):
        for s in range(seqs):
            place = ids_ref[replica * seqs + s]
            table = 0
            for count, got_ref in zip(counts, gots):
                for at in range(count):
                    rows = pl.ds((at * seqs + s) * ranks, ranks)
                    outs[table][place] += got_ref[replica, rows, :].astype(F32)
                    table += 1


def spread(ids, gots, counts, sets, ranks):
    vmem = pl.BlockSpec(memory_space=pltpu.VMEM)
    return pl.pallas_call(
        functools.partial(spread_kernel, counts),
        out_shape=[jax.ShapeDtypeStruct((sets, ranks, got.shape[2]), F32)
                   for got, count in zip(gots, counts) for _ in range(count)],
        in_specs=[pl.BlockSpec(memory_space=pltpu.SMEM)] + [vmem] * len(gots),
        out_specs=[vmem] * sum(counts),
        compiler_params=pltpu.CompilerParams(vmem_limit_bytes=VMEM),
        cost_estimate=pl.CostEstimate(
            flops=sum(got.size for got in gots), bytes_accessed=4 * sum(got.size for got in gots), transcendentals=0),
    )(ids, *gots)


def products_kernel(plan, *refs):
    out_ref, row = refs[-1], 0
    for place, (kind, first, last) in plan:
        if kind == "product":
            result = dot(refs[place][:, first:last], refs[place + 1][...], TN)
        else:
            result = refs[place][...]
        count = last - first
        out_ref[row : row + count, :] = result.astype(BF16)
        row += count


def products(items, earlier=(), blocks=1):
    operands, specs, plan, total = [], [], [], 0
    width = items[0][3].shape[-1]
    tile = width // blocks if blocks > 1 and width % (128 * blocks) == 0 else tile_of(width, 512)
    for item in items:
        if len(item) == 1:
            plan.append((len(operands), ("rows", 0, item[0].shape[0])))
            operands.append(item[0])
            specs.append(pl.BlockSpec((item[0].shape[0], tile), lambda i: (0, i)))
        else:
            lhs, first, last, rhs = item
            plan.append((len(operands), ("product", first, last)))
            if isinstance(rhs, tuple):
                rhs, s = rhs
                block = pl.BlockSpec((None, rhs.shape[1], tile), lambda i, s=s: (s, 0, i))
            else:
                block = pl.BlockSpec((rhs.shape[0], tile), lambda i: (0, i))
            operands += [lhs, rhs]
            specs += [resident(lhs), block]
        total += plan[-1][1][2] - plan[-1][1][1]
    cells = sum(operand.size for operand in operands)
    direct = blocks > 1 and tile * blocks == width
    result = pl.pallas_call(
        functools.partial(products_kernel, plan),
        grid=(pl.cdiv(width, tile),),
        out_shape=jax.ShapeDtypeStruct((blocks, total, tile) if direct else (total, width), BF16),
        in_specs=specs + [ANYWHERE] * len(earlier),
        out_specs=(pl.BlockSpec((None, total, tile), lambda i: (i, 0, 0)) if direct
                   else pl.BlockSpec((total, tile), lambda i: (0, i))),
        compiler_params=pltpu.CompilerParams(vmem_limit_bytes=VMEM),
        cost_estimate=pl.CostEstimate(flops=64 * cells, bytes_accessed=2 * cells, transcendentals=0),
    )(*operands, *earlier)
    if blocks > 1 and not direct:
        result = jnp.swapaxes(result.reshape(total, blocks, width // blocks), 0, 1)
    return result


def passed_along(block, axis, distance):
    devices = range(lax.axis_size(axis))
    route = [(i - distance, i) for i in devices if i - distance in devices]
    return lax.ppermute(block, axis, route)


def body(
    inputs, segment_ids, adapter_ids, gain_mix, gain_mlp, w_branch, w_input, conv_taps, decay_heads, admit_heads,
    decay_param, w_mixer, w_gate, w_upper, w_down, down_branch, lift_branch, down_input, lift_input, down_decay,
    lift_decay, down_admit, lift_admit, down_mixer, lift_mixer, down_gate, lift_gate, down_upper, lift_upper,
    down_outward, lift_outward, out_grad,
):
    seqs, stretch, width = inputs.shape
    rows = seqs * stretch
    taps = conv_taps.shape[0]
    sets, _, ranks = down_branch.shape
    group, place = lax.axis_size("group"), lax.axis_index("group")
    mask_cols = seqs * ranks

    turned = lambda table: jnp.swapaxes(table, 1, 2)
    stack, own_tables = pick(
        adapter_ids,
        [turned(down_branch), turned(down_input), turned(down_decay), turned(down_admit), turned(down_mixer),
         turned(down_gate), turned(down_upper), lift_branch, lift_input, lift_decay, lift_admit, lift_mixer,
         lift_outward],
        [lift_gate, lift_upper, turned(down_outward)])
    full_branch, full_input, full_mixer, stack, late_grad = gather_weights(
        w_branch, w_input, w_mixer, stack, out_grad)
    (p_down_branch, p_down_input, p_down_decay, p_down_admit, p_down_mixer, p_down_gate, p_down_upper,
     p_lift_branch, p_lift_input, p_lift_decay, p_lift_admit, p_lift_mixer, p_lift_outward) = [
        stack[i * mask_cols : (i + 1) * mask_cols] for i in range(13)]
    own_lift_gate, own_lift_upper, own_down_outward = [
        own_tables[i * mask_cols : (i + 1) * mask_cols] for i in range(3)]
    cotangents = lax.all_gather(late_grad, "group", axis=1, tiled=True)

    row_seq = lax.broadcasted_iota(jnp.int32, (rows, mask_cols), 0) // stretch
    col_seq = lax.broadcasted_iota(jnp.int32, (rows, mask_cols), 1) // ranks
    own = (row_seq == col_seq).astype(F32)
    own_two = jnp.concatenate([own, own], 1)

    begin = place * stretch
    padded_ids = jnp.pad(segment_ids, ((0, 0), (taps - 1, taps - 1)), constant_values=-1)
    window = lax.dynamic_slice_in_dim(padded_ids, begin, stretch + 2 * (taps - 1), 1)
    current = window[:, taps - 1 : taps - 1 + stretch + taps - 1]
    agree = [
        ((current == window[:, taps - 1 - j : taps - 1 - j + stretch + taps - 1]) & (current >= 0)).astype(F32)
        for j in range(taps)
    ]
    restart = (1.0 - agree[1][:, :stretch]).reshape(rows, 1)

    x_float = inputs.reshape(rows, width).astype(F32)
    normed_f, _ = norm_rows(x_float, gain_mix)
    normed = normed_f.astype(BF16)
    inner_one = (dot(normed, stack[: 2 * mask_cols], NT) * own_two).astype(BF16)
    inner_branch, inner_input = inner_one[:, :mask_cols], inner_one[:, mask_cols:]
    branch_pre = dot(normed, full_branch) + dot(inner_branch, p_lift_branch)
    fed = (dot(normed, full_input) + dot(inner_input, p_lift_input)).astype(BF16)
    fed = fed.reshape(seqs, stretch, width)
    halo = passed_along(fed[:, stretch - (taps - 1) :], "group", 1)
    extended = jnp.concatenate([halo, fed], axis=1).astype(F32)
    convolved = sum(
        conv_taps[j] * agree[j][:, :stretch, None] * extended[:, taps - 1 - j : taps - 1 - j + stretch]
        for j in range(taps)
    ).reshape(rows, width)
    rounded = convolved.astype(BF16)
    softrate = jax.nn.softplus(decay_param).reshape(1, width)
    inner_gates = (dot(rounded, stack[2 * mask_cols : 4 * mask_cols], NT) * own_two).astype(BF16)
    lift_gates = stack[9 * mask_cols : 11 * mask_cols]
    cum, local = forward_gates(seqs, convolved, inner_gates, lift_gates, decay_heads, admit_heads, softrate, restart)
    ends = jnp.concatenate(
        [cum.reshape(seqs, stretch, width)[:, -1], local.reshape(seqs, stretch, width)[:, -1]], 0)
    all_ends = lax.all_gather(ends, "group")
    carried = jnp.zeros((seqs, width), F32)
    for g in range(group - 1):
        longer = all_ends[g, :seqs] * carried + all_ends[g, seqs:]
        carried = jnp.where(g < place, longer, carried)
    carried_rows = jnp.repeat(carried, stretch, axis=0)
    state = local + cum * carried_rows
    merged = (state * gelu(branch_pre)).astype(BF16)
    inner_mixer = (dot(merged, p_down_mixer, NT) * own).astype(BF16)
    mixed = dot(merged, full_mixer) + dot(inner_mixer, p_lift_mixer)
    resid = x_float + mixed
    normed_two_f, _ = norm_rows(resid, gain_mlp)
    normed_two = normed_two_f.astype(BF16).reshape(seqs, stretch, width)

    spans = [slice(s * ranks, (s + 1) * ranks) for s in range(seqs)]
    grad_hiddens, through_out, first_tokens = grad_hidden_call(
        cotangents, w_down, p_lift_outward, own_down_outward, normed_two[0])
    all_tokens = [first_tokens] + [
        lax.all_gather(ordered(normed_two[s], first_tokens), "group", axis=0, tiled=True) for s in range(1, seqs)]
    backs, hiddens, throughs, wides = [], [], [], []
    for s, at in enumerate(spans):
        two_downs = jnp.concatenate([p_down_gate[at], p_down_upper[at]], 0)
        hidden, back, wide, through = feed_call(
            s, all_tokens[s], grad_hiddens, w_gate, w_upper, two_downs, own_lift_gate[at], own_lift_upper[at],
            through_out)
        if s < seqs - 1:
            backs.append(lax.psum_scatter(back, "group", scatter_dimension=0, tiled=True))
        hiddens.append(hidden)
        throughs.append(through)
        wides.append(wide)
    outward, _, early, reduced = outward_call(
        hiddens, all_tokens, throughs, cotangents, w_down, own_down_outward, p_lift_outward, back)
    backs.append(reduced)
    named = jnp.broadcast_to(jnp.pad(adapter_ids, (0, -seqs % 16)).astype(BF16)[:, None], (-(-seqs // 16) * 16,
                                                                                   wides[0].shape[1]))
    wide = jnp.concatenate(
        [wides[s][i * ranks : (i + 1) * ranks] for i in range(3) for s in range(seqs)] + [named], 0)
    grad_resid, grad_mixed = resid_grad(
        resid, out_grad.reshape(rows, width), gain_mlp.reshape(1, width), backs)
    outward = lax.psum_scatter(outward, "group", scatter_dimension=1, tiled=True).reshape(rows, width)

    kernels = (group == 4 and lax.axis_size("replica") % 2 == 0 and 2 * seqs <= 8 and stretch % GROUP == 0
               and width % 512 == 0 and seqs % 2 == 0)
    if kernels:
        agree_cols = jnp.stack([agree[j][:, j : j + stretch].reshape(rows) for j in range(taps)], 1)
        grad_branch_pre, through_one, through_gates, grad_lift_gates, grad_fed, through_mixer, got_early, got_wide = mixer_back(
            seqs, grad_mixed, full_mixer, p_lift_mixer, p_down_mixer, convolved, inner_gates, lift_gates, decay_heads,
            admit_heads, softrate, restart, cum, local, carried, branch_pre, p_lift_branch, p_lift_input,
            stack[2 * mask_cols : 4 * mask_cols], conv_taps, agree_cols, early, wide)
    else:
        through_mixer = (dot(grad_mixed, p_lift_mixer, NT) * own).astype(BF16)
        grad_merged = dot(grad_mixed, full_mixer, NT) + dot(through_mixer, p_down_mixer)
        span, total, firsts, grad_branch_pre = backward_scan(
            seqs, convolved, inner_gates, lift_gates, decay_heads, softrate, restart, cum, local, carried, branch_pre,
            grad_merged)
        all_firsts = lax.all_gather(firsts, "group")
        incoming = jnp.zeros((seqs, width), F32)
        for lap in range(group - 1):
            g = group - 1 - lap
            longer = all_firsts[g, :seqs] * incoming + all_firsts[g, seqs:]
            incoming = jnp.where(g > place, longer, incoming)
        grad_direct, through_gates, grad_lift_gates = backward_gates(
            seqs, convolved, inner_gates, lift_gates, decay_heads, admit_heads, softrate, restart, cum, local, carried,
            span, total, incoming)
        through_gates = (through_gates * own_two).astype(BF16)
        grad_convolved = grad_direct + dot(through_gates, stack[2 * mask_cols : 4 * mask_cols])
        grad_convolved = grad_convolved.reshape(seqs, stretch, width)
        below = passed_along(grad_convolved[:, : taps - 1].astype(BF16), "group", -1).astype(F32)
        grad_extended = jnp.concatenate([grad_convolved, below], axis=1)
        grad_fed = sum(
            conv_taps[j] * agree[j][:, j : j + stretch, None] * grad_extended[:, j : j + stretch] for j in range(taps)
        ).astype(BF16).reshape(rows, width)
        through_branch = (dot(grad_branch_pre, p_lift_branch, NT) * own).astype(BF16)
        through_input = (dot(grad_fed, p_lift_input, NT) * own).astype(BF16)
        through_one = jnp.concatenate([through_branch, through_input], 1)
    both = 2 * mask_cols
    late = products(
        [(through_one, 0, both, normed), (through_gates, 0, both, rounded), (through_mixer, 0, mask_cols, merged),
         (inner_branch, 0, mask_cols, grad_branch_pre), (inner_input, 0, mask_cols, grad_fed), (grad_lift_gates,),
         (inner_mixer, 0, mask_cols, grad_mixed)], (), group)
    if kernels:
        grad_normed, got_late = tail_call(
            grad_branch_pre, grad_fed, full_branch, full_input, through_one, stack[:both], late)
    else:
        grad_normed = (dot(grad_branch_pre, full_branch, NT) + dot(grad_fed, full_input, NT)
                       + dot(through_one, stack[:both]))
        got_late = lax.all_gather(lax.psum_scatter(late, "group", scatter_dimension=0, tiled=False), "replica")
        got_early = lax.all_gather(lax.psum_scatter(early, "group", scatter_dimension=1, tiled=True), "replica")
        got_wide = lax.all_gather(wide, "replica")
    grad_inputs, block_out = finish(
        grad_resid, inputs.reshape(rows, width), gain_mix.reshape(1, width), grad_normed, resid, outward)
    all_ids = got_wide[:, 3 * mask_cols : 3 * mask_cols + seqs, 0].astype(jnp.int32).reshape(-1)
    totals = spread(all_ids, [got_late, got_early, got_wide], (10, 3, 3), sets, ranks)
    (t_down_branch, t_down_input, t_down_decay, t_down_admit, t_down_mixer, t_lift_branch, t_lift_input, t_lift_decay,
     t_lift_admit, t_lift_mixer, t_down_gate, t_down_upper, t_lift_outward, *wides) = totals
    return (
        block_out.reshape(seqs, stretch, width), grad_inputs.reshape(seqs, stretch, width),
        turned(t_down_branch), t_lift_branch, turned(t_down_input), t_lift_input, turned(t_down_decay), t_lift_decay,
        turned(t_down_admit), t_lift_admit, turned(t_down_mixer), t_lift_mixer, turned(t_down_gate), wides[0],
        turned(t_down_upper), wides[1], turned(wides[2]), t_lift_outward,
    )


def solution(mesh):
    tokens = P("replica", "group", None)
    down, lift = P(None, "group", None), P(None, None, "group")
    cols, split = P(None, "group"), P("group", None)
    in_specs = (
        tokens, P("replica", None), P("replica"), P(), P(), cols, cols, P(), P(), P(), P(), split, cols, cols, split,
    ) + (down, lift) * 8 + (tokens,)
    out_specs = (tokens, tokens) + (down, lift) * 8
    return jax.shard_map(body, mesh=mesh, in_specs=in_specs, out_specs=out_specs, check_vma=False)
```

```python
import functools

import jax
import jax.numpy as jnp
from jax import lax
from jax.experimental import pallas as pl
from jax.experimental.pallas import tpu as pltpu
from jax.sharding import PartitionSpec as P

EPS = 1e-06
F32 = jnp.float32
BF16 = jnp.bfloat16
GELU_C = 0.7978845608028654
GELU_A = 0.044715
NT = (((1,), (1,)), ((), ()))
NN = (((1,), (0,)), ((), ()))
TN = (((0,), (0,)), ((), ()))
ANYWHERE = pl.BlockSpec(memory_space=pl.ANY)
VMEM = 62 * 2**20


def dot(a, b, dims=NN):
    return lax.dot_general(a, b, dims, preferred_element_type=F32)


def gelu(v):
    return 0.5 * v * (1.0 + jnp.tanh(GELU_C * (v + GELU_A * v * v * v)))


def gelu_both(v):
    square = v * v
    half = 0.5 + 0.5 * jnp.tanh(v * (GELU_C + GELU_C * GELU_A * square))
    value = v * half
    return value, half + (value - value * half) * (2.0 * GELU_C + 6.0 * GELU_C * GELU_A * square)


def norm_rows(values, gain):
    rate = lax.rsqrt(jnp.mean(values * values, axis=-1, keepdims=True) + EPS)
    return values * rate * gain, rate


def norm_back(values, gain, rate, grads):
    scaled = grads * gain
    along = jnp.mean(scaled * values, axis=-1, keepdims=True)
    return rate * scaled - values * (rate * rate * rate * along)


def rows_shifted(values, by, fill):
    rows, width = values.shape
    if by % 8 == 0:
        return jnp.concatenate([jnp.full((by, width), fill, values.dtype), values[: rows - by]], 0)
    place = lax.broadcasted_iota(jnp.int32, values.shape, 0)
    return jnp.where(place >= by, pltpu.roll(values, by, 0), fill)


def rows_advanced(values, by, fill):
    rows, width = values.shape
    if by % 8 == 0:
        return jnp.concatenate([values[by:], jnp.full((by, width), fill, values.dtype)], 0)
    place = lax.broadcasted_iota(jnp.int32, values.shape, 0)
    return jnp.where(place < rows - by, pltpu.roll(values, rows - by, 0), fill)


def scan_rows(a, b, moved):
    by = 1
    while by < a.shape[0]:
        b = a * moved(b, by, 0.0) + b
        a = a * moved(a, by, 1.0)
        by *= 2
    return a, b


def gate_steps(pre_d, pre_a, softrate, restart):
    decay_gate = 1.0 / (1.0 + jnp.exp(-pre_d))
    admit_gate = 1.0 / (1.0 + jnp.exp(-pre_a))
    safe = jnp.where(restart, -1.0, -8.0 * decay_gate * softrate)
    grown = jnp.exp(safe)
    scale = jnp.sqrt(jnp.tanh(-safe) * (1.0 + grown * grown))
    return decay_gate, admit_gate, grown, scale


def gate_values(conv, inner, lift, table_d, table_a, softrate, restart):
    rounded = conv.astype(BF16)
    half = lift.shape[0] // 2
    pre_d = dot(rounded, table_d) + dot(inner[:, :half], lift[:half])
    pre_a = dot(rounded, table_a) + dot(inner[:, half:], lift[half:])
    return gate_steps(pre_d, pre_a, softrate, restart)


GROUP = 16
UNROLL = 16


def scan_group(a, b, carry_a, carry_b, moved):
    by = 1
    while by < a.shape[0]:
        b = a * moved(b, by, 0.0) + b
        a = a * moved(a, by, 1.0)
        by *= 2
    return a * carry_a, a * carry_b + b


def forward_gates_kernel(seqs, conv_ref, inner_ref, lift_ref, table_d_ref, table_a_ref, soft_ref, restart_ref,
                         cum_ref, local_ref, pre_d_ref, pre_a_ref):
    rows, size = conv_ref.shape
    stretch = rows // seqs
    half = lift_ref.shape[0] // 2
    rounded = conv_ref[...].astype(BF16)
    pre_d_ref[...] = dot(rounded, table_d_ref[0]) + dot(inner_ref[:, :half], lift_ref[:half, :])
    pre_a_ref[...] = dot(rounded, table_a_ref[0]) + dot(inner_ref[:, half:], lift_ref[half:, :])
    softrate = soft_ref[...]

    def group(k, carries):
        after = []
        for s in range(seqs):
            at = pl.ds(pl.multiple_of(s * stretch + k * GROUP, GROUP), GROUP)
            restart = restart_ref[at, :] > 0.5
            _, admit, grown, scale = gate_steps(pre_d_ref[at, :], pre_a_ref[at, :], softrate, restart)
            decays = jnp.where(restart, 0.0, grown)
            drive = conv_ref[at, :] * admit * jnp.where(restart, 1.0, scale)
            cum, local = scan_group(decays, drive, *carries[s], rows_shifted)
            cum_ref[at, :] = cum
            local_ref[at, :] = local
            after.append((cum[GROUP - 1 :], local[GROUP - 1 :]))
        return tuple(after)

    start = (jnp.ones((1, size), F32), jnp.zeros((1, size), F32))
    lax.fori_loop(0, stretch // GROUP, group, (start,) * seqs, unroll=UNROLL)


def forward_gates(seqs, conv, inner, lift, table_d, table_a, softrate, restart):
    rows, width = conv.shape
    heads, size = table_d.shape[:2]
    tile = pl.BlockSpec((rows, size), lambda h: (0, h))
    table = pl.BlockSpec((1, size, size), lambda h: (h, 0, 0))
    out = jax.ShapeDtypeStruct((rows, width), F32)
    return pl.pallas_call(
        functools.partial(forward_gates_kernel, seqs),
        out_shape=(out, out),
        grid=(heads,),
        in_specs=[
            tile,
            pl.BlockSpec(inner.shape, lambda h: (0, 0)),
            pl.BlockSpec((lift.shape[0], size), lambda h: (0, h)),
            table,
            table,
            pl.BlockSpec((1, size), lambda h: (0, h)),
            pl.BlockSpec(restart.shape, lambda h: (0, 0)),
        ],
        out_specs=(tile, tile),
        scratch_shapes=[pltpu.VMEM((rows, size), F32)] * 2,
        compiler_params=pltpu.CompilerParams(vmem_limit_bytes=40 * 2**20),
        cost_estimate=pl.CostEstimate(
            flops=4 * rows * width * size + 60 * rows * width,
            bytes_accessed=12 * rows * width,
            transcendentals=6 * rows * width),
    )(conv, inner, lift, table_d, table_a, softrate, restart)


def backward_scan_kernel(seqs, conv_ref, inner_ref, lift_ref, table_d_ref, soft_ref, restart_ref, cum_ref, local_ref,
                         carried_ref, pre_ref, grad_ref, span_ref, total_ref, first_ref, branch_grad_ref):
    stretch = conv_ref.shape[0] // seqs
    half = lift_ref.shape[0] // 2
    for s in range(seqs):
        rows = pl.ds(s * stretch, stretch)
        restart = restart_ref[rows, :] > 0.5
        rounded = conv_ref[rows, :].astype(BF16)
        pre_d = dot(rounded, table_d_ref[0]) + dot(inner_ref[rows, :half], lift_ref[:half, :])
        grown = jnp.exp(-8.0 * soft_ref[...] / (1.0 + jnp.exp(-pre_d)))
        decays = jnp.where(restart, 0.0, grown)
        state = local_ref[rows, :] + cum_ref[rows, :] * carried_ref[s : s + 1, :]
        value, slope = gelu_both(pre_ref[rows, :])
        grads = grad_ref[rows, :]
        branch_grad_ref[rows, :] = (grads * state * slope).astype(BF16)
        span, total = scan_rows(rows_advanced(decays, 1, 1.0), grads * value, rows_advanced)
        span_ref[rows, :] = span
        total_ref[rows, :] = total
        first_ref[s : s + 1, :] = decays[:1] * span[:1]
        first_ref[seqs + s : seqs + s + 1, :] = decays[:1] * total[:1]


def backward_scan(seqs, conv, inner, lift, table_d, softrate, restart, cum, local, carried, pre, grads):
    rows, width = conv.shape
    heads, size = table_d.shape[:2]
    tile = pl.BlockSpec((rows, size), lambda h: (0, h))
    table = pl.BlockSpec((1, size, size), lambda h: (h, 0, 0))
    out = jax.ShapeDtypeStruct((rows, width), F32)
    return pl.pallas_call(
        functools.partial(backward_scan_kernel, seqs),
        out_shape=(out, out, jax.ShapeDtypeStruct((2 * seqs, width), F32), jax.ShapeDtypeStruct((rows, width), BF16)),
        grid=(heads,),
        in_specs=[
            tile,
            pl.BlockSpec(inner.shape, lambda h: (0, 0)),
            pl.BlockSpec((lift.shape[0], size), lambda h: (0, h)),
            table,
            pl.BlockSpec((1, size), lambda h: (0, h)),
            pl.BlockSpec(restart.shape, lambda h: (0, 0)),
            tile,
            tile,
            pl.BlockSpec((seqs, size), lambda h: (0, h)),
            tile,
            tile,
        ],
        out_specs=(tile, tile, pl.BlockSpec((2 * seqs, size), lambda h: (0, h)), tile),
        compiler_params=pltpu.CompilerParams(vmem_limit_bytes=48 * 2**20),
        cost_estimate=pl.CostEstimate(
            flops=2 * rows * width * size + 80 * rows * width,
            bytes_accessed=30 * rows * width,
            transcendentals=4 * rows * width),
    )(conv, inner, lift, table_d, softrate, restart, cum, local, carried, pre, grads)


def backward_gates_kernel(seqs, conv_ref, inner_ref, lift_ref, table_d_ref, table_a_ref, soft_ref, restart_ref,
                          cum_ref, local_ref, carried_ref, span_ref, total_ref, incoming_ref,
                          conv_grad_ref, through_ref, lift_grad_ref):
    stretch = conv_ref.shape[0] // seqs
    half = lift_ref.shape[0] // 2

    @pl.when(pl.program_id(0) == 0)
    def _():
        through_ref[...] = jnp.zeros_like(through_ref)

    for s in range(seqs):
        rows = pl.ds(s * stretch, stretch)
        conv = conv_ref[rows, :]
        inner = inner_ref[rows, :]
        restart = restart_ref[rows, :] > 0.5
        softrate = soft_ref[...]
        decay_gate, admit, grown, scale = gate_values(
            conv, inner, lift_ref[...], table_d_ref[0], table_a_ref[0], softrate, restart)
        carried = carried_ref[s : s + 1, :]
        state = local_ref[rows, :] + cum_ref[rows, :] * carried
        place = lax.broadcasted_iota(jnp.int32, state.shape, 0)
        before = jnp.where(place >= 1, pltpu.roll(state, 1, 0), carried)
        grads = total_ref[rows, :] + span_ref[rows, :] * incoming_ref[s : s + 1, :]
        driven = grads * jnp.where(restart, 1.0, scale)
        grad_log = jnp.where(
            restart, 0.0, grads * (before * grown - conv * admit * grown * grown / scale))
        grad_d = (-8.0 * softrate) * grad_log * decay_gate * (1.0 - decay_gate)
        grad_a = driven * conv * admit * (1.0 - admit)
        low_d, low_a = grad_d.astype(BF16), grad_a.astype(BF16)
        conv_grad_ref[rows, :] = driven * admit + dot(low_d, table_d_ref[0], NT) + dot(low_a, table_a_ref[0], NT)
        through_ref[rows, :half] += dot(low_d, lift_ref[:half, :], NT)
        through_ref[rows, half:] += dot(low_a, lift_ref[half:, :], NT)
        first = dot(inner[:, :half], low_d, TN)
        second = dot(inner[:, half:], low_a, TN)
        if s == 0:
            lift_grad_ref[:half, :] = first
            lift_grad_ref[half:, :] = second
        else:
            lift_grad_ref[:half, :] += first
            lift_grad_ref[half:, :] += second


def backward_gates(seqs, conv, inner, lift, table_d, table_a, softrate, restart, cum, local, carried, span, total,
                   incoming):
    rows, width = conv.shape
    heads, size = table_d.shape[:2]
    tile = pl.BlockSpec((rows, size), lambda h: (0, h))
    table = pl.BlockSpec((1, size, size), lambda h: (h, 0, 0))
    edge = pl.BlockSpec((seqs, size), lambda h: (0, h))
    ranks = pl.BlockSpec((lift.shape[0], size), lambda h: (0, h))
    return pl.pallas_call(
        functools.partial(backward_gates_kernel, seqs),
        out_shape=(
            jax.ShapeDtypeStruct((rows, width), F32),
            jax.ShapeDtypeStruct(inner.shape, F32),
            jax.ShapeDtypeStruct(lift.shape, F32),
        ),
        grid=(heads,),
        in_specs=[
            tile,
            pl.BlockSpec(inner.shape, lambda h: (0, 0)),
            ranks,
            table,
            table,
            pl.BlockSpec((1, size), lambda h: (0, h)),
            pl.BlockSpec(restart.shape, lambda h: (0, 0)),
            tile,
            tile,
            edge,
            tile,
            tile,
            edge,
        ],
        out_specs=(tile, pl.BlockSpec(inner.shape, lambda h: (0, 0)), ranks),
        compiler_params=pltpu.CompilerParams(vmem_limit_bytes=48 * 2**20),
        cost_estimate=pl.CostEstimate(
            flops=8 * rows * width * size + 80 * rows * width,
            bytes_accessed=24 * rows * width,
            transcendentals=6 * rows * width),
    )(conv, inner, lift, table_d, table_a, softrate, restart, cum, local, carried, span, total, incoming)


def remote(src, dst, send_sem, recv_sem, partner):
    return pltpu.make_async_remote_copy(
        src_ref=src, dst_ref=dst, send_sem=send_sem, recv_sem=recv_sem, device_id=partner,
        device_id_type=pl.DeviceIdType.MESH)


class GroupSum:
    def __init__(self, block, scratch):
        first_a, first_b, second_a, second_b, pass_a, pass_b, own, send, recv, local = scratch
        group, replica = lax.axis_index("group"), lax.axis_index("replica")
        beside, above, across = group + 1 - 2 * (group % 2), (group + 2) % 4, 3 - group
        at_beside, at_above = (beside, replica), (above, replica)
        self.scratch, self.half = scratch, own.shape[0] // 2
        pairs = [(block(across, 0), first_a.at[1], at_beside), (block(across, 1), first_b.at[1], at_above),
                 (block(beside, 0), first_a.at[0], at_beside), (block(above, 1), first_b.at[0], at_above),
                 (pass_a, second_a, at_above), (pass_b, second_b, at_beside)]
        moves = [remote(src, dst, send.at[slot], recv.at[slot], partner)
                 for slot, (src, dst, partner) in enumerate(pairs)]
        self.firsts, self.seconds = moves[:4], moves[4:]
        pieces = [(block(above, 0), pass_a), (block(beside, 1), pass_b), (block(group, 0), own.at[pl.ds(0, self.half)]),
                  (block(group, 1), own.at[pl.ds(self.half, self.half)])]
        self.loads = [pltpu.make_async_copy(src, dst, local.at[i]) for i, (src, dst) in enumerate(pieces)]

    def begin(self):
        for one in self.firsts + self.loads:
            one.start()

    def middle(self):
        first_a, first_b, _, _, pass_a, pass_b = self.scratch[:6]
        for one in self.loads:
            one.wait()
        for one in self.firsts:
            one.wait_recv()
        pass_a[...] = (pass_a[...].astype(F32) + first_a[1].astype(F32)).astype(BF16)
        pass_b[...] = (pass_b[...].astype(F32) + first_b[1].astype(F32)).astype(BF16)
        for one in self.seconds:
            one.start()

    def end(self):
        first_a, first_b, second_a, second_b, _, _, own = self.scratch[:7]
        half = self.half
        for one in self.seconds:
            one.wait_recv()
        own[:half] = (own[:half].astype(F32) + first_a[0].astype(F32) + second_a[...].astype(F32)).astype(BF16)
        own[half:] = (own[half:].astype(F32) + first_b[0].astype(F32) + second_b[...].astype(F32)).astype(BF16)

    def clear(self):
        for one in self.firsts + self.seconds:
            one.wait_send()

    @staticmethod
    def shapes(ranks, cols):
        half = ranks // 2
        return [pltpu.VMEM((2, half, cols), BF16)] * 2 + [pltpu.VMEM((half, cols), BF16)] * 4 + [
            pltpu.VMEM((ranks, cols), BF16), pltpu.SemaphoreType.DMA((6,)), pltpu.SemaphoreType.DMA((6,)),
            pltpu.SemaphoreType.DMA((4,))]


class ReplicaChain:
    def __init__(self, own, got, sems):
        up_send, low_recv, down_send, high_recv, core_send, core_recv, local = sems
        group, replica = lax.axis_index("group"), lax.axis_index("replica")
        count = got.shape[0]
        self.levels, self.level = count // 2, replica // 2
        at_core = (group, replica + 1 - 2 * (replica % 2))
        at_up, at_down = (group, (replica + 2) % count), (group, (replica + count - 2) % count)
        self.has_up, self.has_down = self.level < self.levels - 1, self.level > 0
        piece = lambda source: got.at[(source + count) % count]
        self.to_up = [remote(own, piece(replica), up_send.at[0], low_recv.at[0], at_up)]
        self.to_down = [remote(own, piece(replica), down_send.at[0], high_recv.at[0], at_down)]
        self.to_core = [remote(own, piece(replica), core_send.at[0], core_recv.at[0], at_core)]
        self.keep = pltpu.make_async_copy(own, piece(replica), local.at[0])
        for d in range(1, self.levels):
            low, high = piece(replica - 2 * d), piece(replica + 2 * d)
            self.to_up.append(remote(low, low, up_send.at[d], low_recv.at[d], at_up))
            self.to_down.append(remote(high, high, down_send.at[d], high_recv.at[d], at_down))
            self.to_core += [remote(low, low, core_send.at[2 * d - 1], core_recv.at[2 * d - 1], at_core),
                             remote(high, high, core_send.at[2 * d], core_recv.at[2 * d], at_core)]

    def begin(self):
        self.keep.start()
        pl.when(self.has_up)(self.to_up[0].start)
        pl.when(self.has_down)(self.to_down[0].start)
        self.to_core[0].start()

    def hop(self, d):
        @pl.when(self.level >= d)
        def _():
            self.to_up[d - 1].wait_recv()
            pl.when(self.has_up)(self.to_up[d].start)
            self.to_core[2 * d - 1].start()

        @pl.when(self.level + d < self.levels)
        def _():
            self.to_down[d - 1].wait_recv()
            pl.when(self.has_down)(self.to_down[d].start)
            self.to_core[2 * d].start()

    def end(self):
        self.to_core[0].wait()
        pl.when(self.has_up)(self.to_up[0].wait_send)
        pl.when(self.has_down)(self.to_down[0].wait_send)
        for d in range(1, self.levels):
            from_low, from_high = self.level >= d, self.level + d < self.levels
            pl.when(from_low)(self.to_core[2 * d - 1].wait)
            pl.when(from_high)(self.to_core[2 * d].wait)
            pl.when(from_low & self.has_up)(self.to_up[d].wait_send)
            pl.when(from_high & self.has_down)(self.to_down[d].wait_send)
        self.keep.wait()

    @staticmethod
    def shapes(count):
        return [pltpu.SemaphoreType.DMA((count // 2,))] * 4 + [pltpu.SemaphoreType.DMA((count,))] * 2 + [
            pltpu.SemaphoreType.DMA((1,))]


def greet_all(levels, group_partners):
    group, replica = lax.axis_index("group"), lax.axis_index("replica")
    level = replica // 2
    barrier = pltpu.get_barrier_semaphore()

    def greet(partner):
        pl.semaphore_signal(barrier, inc=1, device_id=partner, device_id_type=pl.DeviceIdType.MESH)

    for partner in group_partners + [(group, replica + 1 - 2 * (replica % 2))]:
        greet(partner)

    @pl.when(level > 0)
    def _():
        greet((group, (replica + 2 * levels - 2) % (2 * levels)))

    @pl.when(level < levels - 1)
    def _():
        greet((group, (replica + 2) % (2 * levels)))

    ends = (level + levels - 1) // levels + (2 * levels - 2 - level) // levels
    pl.semaphore_wait(barrier, len(group_partners) + 1 + ends)


def sequence_mask(rows, cols, seqs):
    row = lax.broadcasted_iota(jnp.int32, (rows, cols), 0) // (rows // seqs)
    col = lax.broadcasted_iota(jnp.int32, (rows, cols), 1) % (cols // 2) // (cols // 2 // seqs)
    return (row == col).astype(F32)


def mixer_back_kernel(
    seqs, heads, mixed_ref, w_ref, lift_mixer_ref, down_mixer_ref, conv_ref, inner_ref, lift_ref, table_d_ref,
    table_a_ref, soft_ref, restart_ref, cum_ref, local_ref, carried_ref, pre_ref, lift_branch_ref, lift_input_ref,
    down_gates_ref, taps_ref, agree_ref, early_ref, wide_ref,
    branch_grad_ref, through_one_ref, through_gates_ref, lift_grad_ref, fed_grad_ref, thr_mixer_ref,
    got_early_ref, got_wide_ref, span_ref, total_ref, ends_ref, all_ends_ref, incoming_ref, halo_ref, below_ref, one_ref, gates_ref, first_ref,
    second_ref, low_d_ref, low_a_ref, longer_ref, send, recv, *scratch,
):
    rows, size = conv_ref.shape
    stretch = rows // seqs
    half = lift_ref.shape[0] // 2
    ranks = lift_branch_ref.shape[0]
    each = table_d_ref.shape[1]
    lanes = [slice(q * each, (q + 1) * each) for q in range(size // each)]
    step = pl.program_id(0)
    group, replica = lax.axis_index("group"), lax.axis_index("replica")
    partners = [(group + 1 - 2 * (group % 2), replica), ((group + 2) % 4, replica), (3 - group, replica)]

    def copy(src, dst, slot, partner):
        return pltpu.make_async_remote_copy(
            src_ref=src, dst_ref=dst, send_sem=send.at[slot], recv_sem=recv.at[slot], device_id=partner,
            device_id_type=pl.DeviceIdType.MESH)

    early_rows, early_cols = got_early_ref.shape[1:]
    early_half = early_rows // 2
    total_early = GroupSum(
        lambda owner, side: early_ref.at[
            pl.ds(side * early_half, early_half), pl.ds(pl.multiple_of(owner * early_cols, early_cols), early_cols)],
        scratch[:10])
    levels = got_early_ref.shape[0] // 2
    chains = [ReplicaChain(scratch[6], got_early_ref, scratch[10:17]),
              ReplicaChain(wide_ref, got_wide_ref, scratch[17:])]

    exchange = [copy(ends_ref, all_ends_ref.at[group], slot, partner) for slot, partner in enumerate(partners)]
    downward = copy(halo_ref, below_ref, 3, ((group + 3) % 4, replica))

    @pl.when(step == 0)
    def _():
        greet_all(levels, partners)
        total_early.begin()
        chains[1].begin()
        one_ref[...] = jnp.zeros_like(one_ref)
        gates_ref[...] = jnp.zeros_like(gates_ref)
        ends_ref[...] = jnp.zeros_like(ends_ref)
        row = lax.broadcasted_iota(jnp.int32, thr_mixer_ref.shape, 0) // stretch
        col = lax.broadcasted_iota(jnp.int32, thr_mixer_ref.shape, 1) // (thr_mixer_ref.shape[1] // seqs)
        through = dot(mixed_ref[...], lift_mixer_ref[...], NT)
        thr_mixer_ref[...] = jnp.where(row == col, through, 0.0).astype(BF16)

    stops = 3 * heads / (levels + 2)

    @pl.when(step == int(stops / 2))
    def _():
        total_early.middle()

    @pl.when(step == int(stops))
    def _():
        total_early.end()
        chains[0].begin()

    for d in range(1, levels):
        @pl.when(step == int((d + 1) * stops))
        def _(d=d):
            for chain in chains:
                chain.hop(d)

    groups = stretch // GROUP

    def rows_of(s, k):
        return pl.ds(pl.multiple_of(s * stretch + k * GROUP, GROUP), GROUP)

    @pl.when(step < heads)
    def _():
        cols = pl.ds(pl.multiple_of(step * size, size), size)
        first_ref[...] = dot(mixed_ref[...], w_ref[...], NT) + dot(thr_mixer_ref[...], down_mixer_ref[...])
        for q, at in enumerate(lanes):
            second_ref[:, at] = (dot(conv_ref[:, at].astype(BF16), table_d_ref[q])
                                 + dot(inner_ref[:, :half], lift_ref[:half, at]))
        softrate = soft_ref[...]

        def group(lap, carries):
            k = groups - 1 - lap
            after = []
            for s in range(seqs):
                at = rows_of(s, k)
                restart = restart_ref[at, :] > 0.5
                grown = jnp.exp(-8.0 * softrate / (1.0 + jnp.exp(-second_ref[at, :])))
                decays = jnp.where(restart, 0.0, grown)
                state = local_ref[at, :] + cum_ref[at, :] * carried_ref[s : s + 1, :]
                value, slope = gelu_both(pre_ref[at, :])
                merged = first_ref[at, :]
                branch_grad_ref[at, :] = (merged * state * slope).astype(BF16)
                grads = merged * value
                carry_a, carry_b = carries[s]
                a, b = scan_group(decays, decays * grads, carry_a, carry_b, rows_advanced)
                last = lax.broadcasted_iota(jnp.int32, a.shape, 0) == GROUP - 1
                span_ref[step, at, :] = jnp.where(last, carry_a, pltpu.roll(a, GROUP - 1, 0))
                total_ref[step, at, :] = grads + jnp.where(last, carry_b, pltpu.roll(b, GROUP - 1, 0))
                after.append((a[:1], b[:1]))
            return tuple(after)

        start = (jnp.ones((1, size), F32), jnp.zeros((1, size), F32))
        ends = lax.fori_loop(0, groups, group, (start,) * seqs, unroll=UNROLL)
        for s in range(seqs):
            ends_ref[s : s + 1, cols] = ends[s][0]
            ends_ref[seqs + s : seqs + s + 1, cols] = ends[s][1]
        one_ref[:, :ranks] += dot(branch_grad_ref[...], lift_branch_ref[...], NT)

    @pl.when(step == heads - 1)
    def _():
        for one in exchange:
            one.start()

    @pl.when(step == heads)
    def _():
        for one in exchange:
            one.wait_recv()
        incoming = jnp.zeros(incoming_ref.shape, F32)
        for g in (3, 2, 1):
            longer = all_ends_ref[g, :seqs, :] * incoming + all_ends_ref[g, seqs : 2 * seqs, :]
            incoming = jnp.where(group < g, longer, incoming)
        incoming_ref[...] = incoming

    @pl.when((step >= heads) & (step < 2 * heads))
    def _():
        head = step - heads
        cols = pl.ds(pl.multiple_of(head * size, size), size)
        for q, at in enumerate(lanes):
            rounded = conv_ref[:, at].astype(BF16)
            first_ref[:, at] = dot(rounded, table_d_ref[q]) + dot(inner_ref[:, :half], lift_ref[:half, at])
            second_ref[:, at] = dot(rounded, table_a_ref[q]) + dot(inner_ref[:, half:], lift_ref[half:, at])
        softrate = soft_ref[...]
        rate = -8.0 * softrate

        def group(k, carries):
            after = []
            for s in range(seqs):
                at = rows_of(s, k)
                conv = conv_ref[at, :]
                restart = restart_ref[at, :] > 0.5
                decay_gate, admit, grown, scale = gate_steps(
                    first_ref[at, :], second_ref[at, :], softrate, restart)
                state = local_ref[at, :] + cum_ref[at, :] * carried_ref[s : s + 1, :]
                place = lax.broadcasted_iota(jnp.int32, state.shape, 0)
                before = jnp.where(place >= 1, pltpu.roll(state, 1, 0), carries[s])
                grads = total_ref[head, at, :] + span_ref[head, at, :] * incoming_ref[s : s + 1, cols]
                driven = grads * jnp.where(restart, 1.0, scale)
                admitted = conv * admit
                grad_log = jnp.where(restart, 0.0, grads * (before * grown - admitted * grown * grown / scale))
                low_d_ref[at, :] = (rate * grad_log * decay_gate * (1.0 - decay_gate)).astype(BF16)
                low_a_ref[at, :] = (driven * admitted * (1.0 - admit)).astype(BF16)
                total_ref[head, at, :] = driven * admit
                after.append(state[GROUP - 1 :])
            return tuple(after)

        lax.fori_loop(0, groups, group, tuple(carried_ref[s : s + 1, :] for s in range(seqs)), unroll=UNROLL)
        low_d, low_a = low_d_ref[...], low_a_ref[...]
        for q, at in enumerate(lanes):
            total_ref[head, :, at] += dot(low_d[:, at], table_d_ref[q], NT) + dot(low_a[:, at], table_a_ref[q], NT)
        gates_ref[:, :half] += dot(low_d, lift_ref[:half, :], NT)
        gates_ref[:, half:] += dot(low_a, lift_ref[half:, :], NT)
        lift_grad_ref[:half, :] = dot(inner_ref[:, :half], low_d, TN)
        lift_grad_ref[half:, :] = dot(inner_ref[:, half:], low_a, TN)

    @pl.when(step == 2 * heads)
    def _():
        through_gates_ref[...] = (gates_ref[...] * sequence_mask(rows, 2 * half, seqs)).astype(BF16)
        tops = []
        for s in range(seqs):
            top = slice(s * stretch, s * stretch + 8)
            direct = jnp.concatenate([total_ref[h, top, :] for h in range(heads)], 1)
            tops.append(direct + dot(through_gates_ref[top, :], down_gates_ref[...]))
        halo_ref[...] = jnp.concatenate(tops, 0).astype(BF16)
        downward.start()
        downward.wait_recv()

    @pl.when(step >= 2 * heads)
    def _():
        head = step - 2 * heads
        cols = pl.ds(pl.multiple_of(head * size, size), size)
        grads = total_ref[head] + dot(through_gates_ref[...], down_gates_ref[:, cols])
        for s in range(seqs):
            longer_ref[s, :stretch, :] = grads[s * stretch : (s + 1) * stretch, :]
            longer_ref[s, stretch:, :] = below_ref[s * 8 : (s + 1) * 8, cols].astype(F32)

        def group(k, _):
            for s in range(seqs):
                at = rows_of(s, k)
                ahead = longer_ref[s, pl.ds(pl.multiple_of(k * GROUP, GROUP), GROUP + 8), :]
                total = taps_ref[0:1, :] * agree_ref[at, 0:1] * ahead[:GROUP]
                for j in range(1, taps_ref.shape[0]):
                    moved = pltpu.roll(ahead, GROUP + 8 - j, 0)[:GROUP]
                    total += taps_ref[j : j + 1, :] * agree_ref[at, j : j + 1] * moved
                fed_grad_ref[at, :] = total.astype(BF16)
            return 0

        lax.fori_loop(0, groups, group, 0, unroll=UNROLL)
        one_ref[:, ranks:] += dot(fed_grad_ref[...], lift_input_ref[...], NT)

    @pl.when(step == 3 * heads - 1)
    def _():
        through_one_ref[...] = (one_ref[...] * sequence_mask(rows, 2 * ranks, seqs)).astype(BF16)
        for one in exchange:
            one.wait_send()
        downward.wait_send()
        total_early.clear()
        for chain in chains:
            chain.end()


def mixer_back(seqs, mixed, w_mixer, lift_mixer, down_mixer, conv, inner, lift, table_d, table_a, softrate, restart,
               cum, local, carried, pre, lift_branch, lift_input, down_gates, taps, agree, early, wide):
    rows, width = conv.shape
    count, early_cols = lax.axis_size("replica"), width // 4
    heads, each = table_d.shape[:2]
    per = 2 if heads % 2 == 0 else 1
    heads, size = heads // per, per * each
    first = lambda i: jnp.minimum(i, heads - 1)
    second = lambda i: jnp.clip(i - heads, 0, heads - 1)
    third = lambda i: jnp.maximum(i - 2 * heads, 0)
    either = lambda i: jnp.minimum(i, 2 * heads - 1) % heads
    full = lambda array: pl.BlockSpec(array.shape, lambda i: (0, 0), pipeline_mode=pl.Buffered(1))
    cols = lambda array, at: pl.BlockSpec((array.shape[0], size), lambda i: (0, at(i)))
    table = pl.BlockSpec((per, each, each), lambda i: (either(i), 0, 0))
    middle = inner.shape[1]
    tile = lambda at: pl.BlockSpec((rows, size), lambda i: (0, at(i)))
    whole = lambda count: pl.BlockSpec((rows, count), lambda i: (0, 0))
    return pl.pallas_call(
        functools.partial(mixer_back_kernel, seqs, heads),
        grid=(3 * heads,),
        out_shape=[
            jax.ShapeDtypeStruct((rows, width), BF16),
            jax.ShapeDtypeStruct((rows, 2 * lift_branch.shape[0]), BF16),
            jax.ShapeDtypeStruct((rows, middle), BF16),
            jax.ShapeDtypeStruct(lift.shape, F32),
            jax.ShapeDtypeStruct((rows, width), BF16),
            jax.ShapeDtypeStruct((rows, lift_mixer.shape[0]), BF16),
            jax.ShapeDtypeStruct((count, early.shape[0], early_cols), BF16),
            jax.ShapeDtypeStruct((count,) + wide.shape, BF16),
        ],
        in_specs=[
            full(mixed), pl.BlockSpec((size, width), lambda i: (first(i), 0)), full(lift_mixer), cols(down_mixer, first),
            cols(conv, either), full(inner), cols(lift, either), table, table, cols(softrate, either), full(restart),
            cols(cum, either), cols(local, either), cols(carried, either), cols(pre, first), cols(lift_branch, first),
            cols(lift_input, third), full(down_gates), cols(taps, third), full(agree), ANYWHERE, ANYWHERE,
        ],
        out_specs=[tile(first), whole(2 * lift_branch.shape[0]), whole(middle),
                   pl.BlockSpec((lift.shape[0], size), lambda i: (0, second(i))), tile(third),
                   whole(lift_mixer.shape[0]), ANYWHERE, ANYWHERE],
        scratch_shapes=[
            pltpu.VMEM((heads, rows, size), F32), pltpu.VMEM((heads, rows, size), F32), pltpu.VMEM((8, width), F32),
            pltpu.VMEM((4, 8, width), F32), pltpu.VMEM((seqs, width), F32), pltpu.VMEM((8 * seqs, width), BF16),
            pltpu.VMEM((8 * seqs, width), BF16), pltpu.VMEM((rows, 2 * lift_branch.shape[0]), F32),
            pltpu.VMEM((rows, middle), F32), pltpu.VMEM((rows, size), F32), pltpu.VMEM((rows, size), F32),
            pltpu.VMEM((rows, size), BF16), pltpu.VMEM((rows, size), BF16),
            pltpu.VMEM((seqs, rows // seqs + 8, size), F32), pltpu.SemaphoreType.DMA((4,)),
            pltpu.SemaphoreType.DMA((4,))]
        + GroupSum.shapes(early.shape[0], early_cols) + ReplicaChain.shapes(count) + ReplicaChain.shapes(count),
        compiler_params=pltpu.CompilerParams(
            vmem_limit_bytes=VMEM, collective_id=3, has_side_effects=True),
        cost_estimate=pl.CostEstimate(
            flops=2 * rows * width * width + 20 * rows * width * size + 200 * rows * width,
            bytes_accessed=40 * rows * width + 2 * width * width, transcendentals=12 * rows * width),
    )(mixed, w_mixer, lift_mixer, down_mixer, conv, inner, lift, table_d, table_a, softrate, restart, cum, local,
      carried, pre, lift_branch, lift_input, down_gates, taps, agree, early, wide)


def resident(array):
    return pl.BlockSpec(array.shape, lambda i: (0, 0), pipeline_mode=pl.Buffered(1))


def tile_of(count, tile):
    return tile if count % 128 == 0 and count > tile else count


def grad_hidden_kernel(seqs, gather, steps, *refs):
    if gather:
        cot_ref, wd_ref, lift_out_ref, do_ref, block_ref = refs[:5]
        out_ref, through_ref, all_ref, staged_ref, send, recv, local = refs[-7:]
    else:
        cot_ref, wd_ref, lift_out_ref, do_ref, out_ref, through_ref = refs
    ranks = do_ref.shape[0] // seqs
    step = pl.program_id(0)

    if gather:
        group, replica = lax.axis_index("group"), lax.axis_index("replica")
        beside, above = group + 1 - 2 * (group % 2), (group + 2) % 4
        at_beside, at_above = (beside, replica), (above, replica)
        rows = block_ref.shape[0]
        half = rows // 2

        def place(owner, part):
            return all_ref.at[pl.ds(pl.multiple_of(owner * rows + part * half, half), half), :]

        def own(part):
            return block_ref.at[pl.ds(part * half, half), :]

        def copy(src, dst, slot, partner):
            return pltpu.make_async_remote_copy(
                src_ref=src, dst_ref=dst, send_sem=send.at[slot], recv_sem=recv.at[slot], device_id=partner,
                device_id_type=pl.DeviceIdType.MESH)

        firsts = [copy(own(1), place(group, 1), 0, at_beside), copy(own(0), place(group, 0), 1, at_above),
                  copy(own(0), place(group, 0), 2, at_beside), copy(own(1), place(group, 1), 3, at_above)]
        seconds = [copy(place(beside, 1), place(beside, 1), 4, at_above),
                   copy(place(above, 0), place(above, 0), 5, at_beside)]
        stage = pltpu.make_async_copy(block_ref, staged_ref, local.at[0])
        keep = pltpu.make_async_copy(
            staged_ref, all_ref.at[pl.ds(pl.multiple_of(group * rows, rows), rows), :], local.at[1])

        @pl.when(step == 0)
        def _():
            barrier = pltpu.get_barrier_semaphore()
            for partner in (at_beside, at_above):
                pl.semaphore_signal(barrier, inc=1, device_id=partner, device_id_type=pl.DeviceIdType.MESH)
            pl.semaphore_wait(barrier, 2)
            for one in firsts[:2]:
                one.start()
            stage.start()

    @pl.when(step == 0)
    def _():
        for s in range(seqs):
            through_ref[s] = dot(cot_ref[s], lift_out_ref[s * ranks : (s + 1) * ranks, :], NT).astype(BF16)

    for s in range(seqs):
        out_ref[s] = (dot(cot_ref[s], wd_ref[...], NT)
                      + dot(through_ref[s], do_ref[s * ranks : (s + 1) * ranks, :])).astype(BF16)

    if gather:
        @pl.when(step == 0)
        def _():
            stage.wait()
            keep.start()
            for one in firsts[2:]:
                one.start()

        @pl.when(step == min(1, steps - 1))
        def _():
            for one, then in zip(firsts[:2], seconds):
                one.wait_recv()
                then.start()

        @pl.when(step == steps - 1)
        def _():
            for one in firsts[2:] + seconds:
                one.wait_recv()
            for one in firsts + seconds:
                one.wait_send()
            keep.wait()


def grad_hidden_call(cot, wd, lift_out, do, block, earlier):
    seqs, rows, width = cot.shape
    units, ranks = wd.shape[0], do.shape[0] // seqs
    tile = tile_of(units, 512)
    gather = lax.axis_size("group") == 4
    got = pl.pallas_call(
        functools.partial(grad_hidden_kernel, seqs, gather, pl.cdiv(units, tile)),
        grid=(pl.cdiv(units, tile),),
        out_shape=[jax.ShapeDtypeStruct((seqs, rows, units), BF16), jax.ShapeDtypeStruct((seqs, rows, ranks), BF16)]
        + [jax.ShapeDtypeStruct((rows, width), BF16)] * gather,
        in_specs=[pl.BlockSpec(cot.shape, lambda i: (0, 0, 0), pipeline_mode=pl.Buffered(1)),
                  pl.BlockSpec((tile, width), lambda i: (i, 0)), resident(lift_out),
                  pl.BlockSpec((seqs * ranks, tile), lambda i: (0, i))] + [ANYWHERE] * (gather + gather * len(earlier)),
        out_specs=[pl.BlockSpec((seqs, rows, tile), lambda i: (0, 0, i)),
                   pl.BlockSpec((seqs, rows, ranks), lambda i: (0, 0, 0))] + [ANYWHERE] * gather,
        scratch_shapes=[pltpu.VMEM(block.shape, BF16), pltpu.SemaphoreType.DMA((6,)), pltpu.SemaphoreType.DMA((6,)),
                        pltpu.SemaphoreType.DMA((2,))] if gather else [],
        compiler_params=pltpu.CompilerParams(
            vmem_limit_bytes=VMEM, **(dict(collective_id=1, has_side_effects=True) if gather else {})),
        cost_estimate=pl.CostEstimate(
            flops=2 * seqs * rows * width * units,
            bytes_accessed=2 * width * units + 2 * seqs * rows * (units + width), transcendentals=0),
    )(cot, wd, lift_out, do, *([block, *earlier] if gather else []))
    return got if gather else list(got) + [lax.all_gather(block, "group", axis=0, tiled=True)]


def feed_kernel(steps, tile, units, tok_ref, gh_ref, wg_ref, wu_ref, wg_rows_ref, wu_rows_ref, down_ref, lg_ref,
                lu_ref, through_out_ref, lg_full_ref, lu_full_ref, down_cols_ref, *refs):
    hidden_ref, back_ref, wide_ref, through_ref, inner_ref, gg_ref, gu_ref = refs[-7:]
    ranks = lg_ref.shape[0]
    step = pl.program_id(0)

    @pl.when(step == 0)
    def _():
        inner_ref[...] = dot(tok_ref[...], down_ref[...], NT).astype(BF16)

    @pl.when(step < steps)
    def _():
        tokens, inner = tok_ref[...], inner_ref[...]
        gate = dot(tokens, wg_ref[...]) + dot(inner[:, :ranks], lg_ref[...])
        upper = dot(tokens, wu_ref[...]) + dot(inner[:, ranks:], lu_ref[...])
        grad_hidden = gh_ref[...].astype(F32)
        value, slope = gelu_both(gate)
        hidden = (value * upper).astype(BF16)
        grad_gate = (grad_hidden * upper * slope).astype(BF16)
        grad_upper = (grad_hidden * value).astype(BF16)
        hidden_ref[...] = hidden
        cols = pl.ds(pl.multiple_of(step * tile, tile), tile) if steps > 1 else slice(0, tile)
        gg_ref[:, cols] = grad_gate
        gu_ref[:, cols] = grad_upper
        wide_ref[:ranks, :] = dot(inner[:, :ranks], grad_gate, TN).astype(BF16)
        wide_ref[ranks : 2 * ranks, :] = dot(inner[:, ranks:], grad_upper, TN).astype(BF16)
        wide_ref[2 * ranks :, :] = dot(through_out_ref[...], hidden, TN).astype(BF16)

    @pl.when(step == steps)
    def _():
        through_ref[:, :ranks] = dot(gg_ref[:, :units], lg_full_ref[...], NT).astype(BF16)
        through_ref[:, ranks:] = dot(gu_ref[:, :units], lu_full_ref[...], NT).astype(BF16)

    @pl.when(step >= steps)
    def _():
        back_ref[...] = (dot(gg_ref[:, :units], wg_rows_ref[...], NT) + dot(gu_ref[:, :units], wu_rows_ref[...], NT)
                         + dot(through_ref[...], down_cols_ref[...])).astype(BF16)


def feed_call(s, tok, gh, wg, wu, down, lg, lu, through_out):
    rows, width = tok.shape
    units, ranks = wg.shape[1], lg.shape[0]
    tile, span = tile_of(units, 512), tile_of(width, 512)
    steps, laps = pl.cdiv(units, tile), pl.cdiv(width, span)
    first = lambda i: jnp.minimum(i, steps - 1)
    second = lambda i: jnp.maximum(i - steps, 0)
    cols = pl.BlockSpec((width, tile), lambda i: (0, first(i)))
    across = pl.BlockSpec((span, units), lambda i: (second(i), 0))
    rank = pl.BlockSpec((ranks, tile), lambda i: (0, first(i)))
    out = pl.BlockSpec((rows, tile), lambda i: (0, first(i)))
    return pl.pallas_call(
        functools.partial(feed_kernel, steps, tile, units),
        grid=(steps + laps,),
        out_shape=[jax.ShapeDtypeStruct((rows, units), BF16), jax.ShapeDtypeStruct((rows, width), BF16),
                   jax.ShapeDtypeStruct((3 * ranks, units), BF16), jax.ShapeDtypeStruct((rows, 2 * ranks), BF16)],
        in_specs=[resident(tok), pl.BlockSpec((None, rows, tile), lambda i: (s, 0, first(i))), cols, cols, across,
                  across, resident(down), rank, rank, pl.BlockSpec((None, rows, ranks), lambda i: (s, 0, 0)),
                  resident(lg), resident(lu), pl.BlockSpec((2 * ranks, span), lambda i: (0, second(i)))],
        out_specs=[out, pl.BlockSpec((rows, span), lambda i: (0, second(i))),
                   pl.BlockSpec((3 * ranks, tile), lambda i: (0, first(i))),
                   pl.BlockSpec((rows, 2 * ranks), lambda i: (0, 0))],
        scratch_shapes=[pltpu.VMEM((rows, 2 * ranks), BF16), pltpu.VMEM((rows, steps * tile), BF16),
                        pltpu.VMEM((rows, steps * tile), BF16)],
        compiler_params=pltpu.CompilerParams(vmem_limit_bytes=VMEM),
        cost_estimate=pl.CostEstimate(
            flops=8 * rows * width * units, bytes_accessed=8 * width * units + 6 * rows * units,
            transcendentals=rows * units),
    )(tok, gh, wg, wu, wg, wu, down, lg, lu, through_out, lg, lu, down)


def outward_kernel(seqs, reduce, steps, *refs):
    hiddens, tokens, throughs, (cot_ref, resid_ref), refs = (
        refs[:seqs], refs[seqs : 2 * seqs], refs[2 * seqs : 3 * seqs], refs[3 * seqs : 3 * seqs + 2],
        refs[3 * seqs + 2 :])
    if reduce:
        wd_ref, do_ref, lift_out_ref, back_ref, out_ref, inner_ref, early_ref, sum_ref = refs[:8]
        first_a, first_b, second_a, second_b, pass_a, pass_b, own_ref, send, recv, local = refs[8:]
    else:
        wd_ref, do_ref, lift_out_ref, out_ref, inner_ref, early_ref = refs
    ranks = do_ref.shape[0] // seqs
    step = pl.program_id(0)

    if reduce:
        group, replica = lax.axis_index("group"), lax.axis_index("replica")
        beside, above, across = group + 1 - 2 * (group % 2), (group + 2) % 4, 3 - group
        at_beside, at_above = (beside, replica), (above, replica)
        rows, width = own_ref.shape
        half = width // 2

        def part(owner, side):
            return back_ref.at[pl.ds(pl.multiple_of(owner * rows, rows), rows), pl.ds(side * half, half)]

        def copy(src, dst, slot, partner):
            return pltpu.make_async_remote_copy(
                src_ref=src, dst_ref=dst, send_sem=send.at[slot], recv_sem=recv.at[slot], device_id=partner,
                device_id_type=pl.DeviceIdType.MESH)

        firsts = [copy(part(across, 0), first_a.at[1], 0, at_beside), copy(part(across, 1), first_b.at[1], 1, at_above),
                  copy(part(beside, 0), first_a.at[0], 2, at_beside), copy(part(above, 1), first_b.at[0], 3, at_above)]
        seconds = [copy(pass_a, second_a, 4, at_above), copy(pass_b, second_b, 5, at_beside)]
        loads = [pltpu.make_async_copy(part(above, 0), pass_a, local.at[0]),
                 pltpu.make_async_copy(part(beside, 1), pass_b, local.at[1]),
                 pltpu.make_async_copy(
                     back_ref.at[pl.ds(pl.multiple_of(group * rows, rows), rows), :], own_ref, local.at[2])]

        @pl.when(step == 0)
        def _():
            barrier = pltpu.get_barrier_semaphore()
            for partner in (at_beside, at_above):
                pl.semaphore_signal(barrier, inc=1, device_id=partner, device_id_type=pl.DeviceIdType.MESH)
            pl.semaphore_wait(barrier, 2)
            for one in firsts:
                one.start()
            for one in loads:
                one.start()

    @pl.when(step == 0)
    def _():
        for s, hidden_ref in enumerate(hiddens):
            inner_ref[s] = dot(hidden_ref[...], do_ref[s * ranks : (s + 1) * ranks, :], NT).astype(BF16)

    for s, hidden_ref in enumerate(hiddens):
        out_ref[s] = (dot(hidden_ref[...], wd_ref[...])
                      + dot(inner_ref[s], lift_out_ref[s * ranks : (s + 1) * ranks, :])).astype(BF16)
        own = resid_ref.shape[0] // seqs
        mine = pl.ds(pl.multiple_of(lax.axis_index("group") * own, own), own)
        out_ref[s, mine, :] = (out_ref[s, mine, :].astype(F32) + resid_ref[s * own : (s + 1) * own, :]).astype(BF16)
        both = dot(throughs[s][...], tokens[s][...], TN).astype(BF16)
        for kind, rows_of in enumerate((both[:ranks], both[ranks:], dot(inner_ref[s], cot_ref[s], TN).astype(BF16))):
            row = (kind * seqs + s) * ranks
            early_ref[row : row + ranks, :] = rows_of

    if reduce:
        @pl.when(step == max(steps - 2, 0))
        def _():
            for one in loads:
                one.wait()
            for one in firsts:
                one.wait_recv()
            pass_a[...] = (pass_a[...].astype(F32) + first_a[1].astype(F32)).astype(BF16)
            pass_b[...] = (pass_b[...].astype(F32) + first_b[1].astype(F32)).astype(BF16)
            for one in seconds:
                one.start()

        @pl.when(step == steps - 1)
        def _():
            for one in seconds:
                one.wait_recv()
            sum_ref[:, :half] = (own_ref[:, :half].astype(F32) + first_a[0].astype(F32)
                                 + second_a[...].astype(F32)).astype(BF16)
            sum_ref[:, half:] = (own_ref[:, half:].astype(F32) + first_b[0].astype(F32)
                                 + second_b[...].astype(F32)).astype(BF16)
            for one in firsts + seconds:
                one.wait_send()


def outward_call(hiddens, tokens, throughs, cot, resid, wd, do, lift_out, back):
    rows, units = hiddens[0].shape
    seqs = len(hiddens)
    width, ranks = wd.shape[1], do.shape[0] // seqs
    tile = tile_of(width, 512)
    steps = pl.cdiv(width, tile)
    group = lax.axis_size("group")
    reduce = group == 4 and width % 256 == 0
    own, half = rows // group, width // 2
    scratch = [pltpu.VMEM((2, own, half), BF16)] * 2 + [pltpu.VMEM((own, half), BF16)] * 4 + [
        pltpu.VMEM((own, width), BF16), pltpu.SemaphoreType.DMA((6,)), pltpu.SemaphoreType.DMA((6,)),
        pltpu.SemaphoreType.DMA((3,))]
    got = pl.pallas_call(
        functools.partial(outward_kernel, seqs, reduce, steps),
        grid=(steps,),
        out_shape=[jax.ShapeDtypeStruct((seqs, rows, width), BF16), jax.ShapeDtypeStruct((seqs, rows, ranks), BF16),
                   jax.ShapeDtypeStruct((3 * seqs * ranks, width), BF16)]
        + [jax.ShapeDtypeStruct((own, width), BF16)] * reduce,
        in_specs=[resident(hidden) for hidden in hiddens] + [pl.BlockSpec((rows, tile), lambda i: (0, i))] * seqs
        + [resident(through) for through in throughs] + [pl.BlockSpec((seqs, rows, tile), lambda i: (0, 0, i))]
        + [pl.BlockSpec((resid.shape[0], tile), lambda i: (0, i))]
        + [pl.BlockSpec((units, tile), lambda i: (0, i)), resident(do),
           pl.BlockSpec((seqs * ranks, tile), lambda i: (0, i))] + [ANYWHERE] * reduce,
        out_specs=[pl.BlockSpec((seqs, rows, tile), lambda i: (0, 0, i)),
                   pl.BlockSpec((seqs, rows, ranks), lambda i: (0, 0, 0)),
                   pl.BlockSpec((3 * seqs * ranks, tile), lambda i: (0, i))]
        + [pl.BlockSpec((own, width), lambda i: (0, 0))] * reduce,
        scratch_shapes=scratch if reduce else [],
        compiler_params=pltpu.CompilerParams(
            vmem_limit_bytes=VMEM, **(dict(collective_id=2, has_side_effects=True) if reduce else {})),
        cost_estimate=pl.CostEstimate(
            flops=2 * seqs * rows * width * units,
            bytes_accessed=2 * width * units + 2 * seqs * rows * (units + width), transcendentals=0),
    )(*hiddens, *tokens, *throughs, cot, resid, wd, do, lift_out, *([back] if reduce else []))
    return got if reduce else list(got) + [lax.psum_scatter(back, "group", scatter_dimension=0, tiled=True)]


def pick_kernel(counts, ids_ref, *refs):
    tables, (stack_ref, wide_ref) = refs[: sum(counts)], refs[sum(counts) :]
    for i, table in enumerate(tables):
        if i < counts[0]:
            stack_ref[i, 0] = table[0]
        else:
            wide_ref[i - counts[0], 0] = table[0]


def pick(ids, narrow, wide):
    seqs, ranks = ids.shape[0], narrow[0].shape[1]
    counts = (len(narrow), len(wide))
    widths = (narrow[0].shape[2], wide[0].shape[2])
    tables = [pl.BlockSpec((1, ranks, table.shape[2]), lambda s, ids: (ids[s], 0, 0)) for table in narrow + wide]
    picked = pl.pallas_call(
        functools.partial(pick_kernel, counts),
        out_shape=[jax.ShapeDtypeStruct((count, seqs, ranks, width), BF16) for count, width in zip(counts, widths)],
        grid_spec=pltpu.PrefetchScalarGridSpec(
            num_scalar_prefetch=1,
            grid=(seqs,),
            in_specs=tables,
            out_specs=[pl.BlockSpec((count, 1, ranks, width), lambda s, ids: (0, s, 0, 0))
                       for count, width in zip(counts, widths)],
        ),
    )(ids, *narrow, *wide)
    return [part.reshape(-1, part.shape[-1]) for part in picked]


def gather_kernel(units, counts, seqs, *refs):
    refs = list(refs)
    take = lambda count: [refs.pop(0) for _ in range(count)]
    weights, (passed, values, gain_ref, ids_ref), tables = take(3), take(4), take(sum(counts))
    wholes, (handed_out, normed_ref, own_ref) = take(4), take(3)
    staged, (handed, values_ref), loaded, (send, recv, local, table_sems) = take(4), take(2), take(sum(counts)), refs
    weights = weights + [staged[3]]
    group, replica = lax.axis_index("group"), lax.axis_index("replica")
    beside, above, across = group + 1 - 2 * (group % 2), (group + 2) % 4, 3 - group
    core, level = replica % 2, (replica // 2) % 2
    at_beside, at_above = (beside, replica), (above, replica)
    at_core, at_level = (group, replica + 1 - 2 * core), (group, replica + 2 - 4 * level)
    partners = (at_beside, at_above, at_core, at_level)
    mine, other = 2 * core + level, 2 * core + 1 - level

    barrier = pltpu.get_barrier_semaphore()
    for partner in partners:
        pl.semaphore_signal(barrier, inc=1, device_id=partner, device_id_type=pl.DeviceIdType.MESH)
    pl.semaphore_wait(barrier, 4)

    kept = [pltpu.make_async_copy(weight, stage, local.at[m])
            for m, (weight, stage) in enumerate(zip(weights[:3], staged))] + [None]

    def keep(m):
        whole = wholes[m]
        rows, cols = weights[m].shape
        if m == 2:
            into = whole.at[pl.ds(pl.multiple_of(group * rows, rows), rows), :]
        else:
            into = whole.at[:, pl.ds(pl.multiple_of(group * cols, cols), cols)]
        if kept[m] is not None:
            kept[m].wait()
        kept[m] = pltpu.make_async_copy(staged[m], into, local.at[m])
        kept[m].start()

    def own(m, part, quarter):
        weight = weights[m]
        size = wholes[m].shape[0] // 4
        step = size // units
        if m < 2:
            return weight.at[pl.ds(pl.multiple_of(quarter * size + part * step, step), step), :]
        return weight.at[pl.ds(part * step, step), pl.ds(pl.multiple_of(quarter * size, size), size)]

    def piece(m, part, shard, quarter):
        whole = wholes[m]
        size = whole.shape[0] // 4
        step = size // units
        down, along = (quarter, shard) if m < 2 else (shard, quarter)
        return whole.at[pl.ds(pl.multiple_of(down * size + part * step, step), step),
                        pl.ds(pl.multiple_of(along * size, size), size)]

    def copy(src, dst, k, slot, partner):
        made = pltpu.make_async_remote_copy(
            src_ref=src, dst_ref=dst, send_sem=send.at[k, slot], recv_sem=recv.at[k, slot], device_id=partner,
            device_id_type=pl.DeviceIdType.MESH)
        made.start()
        return made

    def forward(m, part, shard, quarter, k, slot, partner):
        where = piece(m, part, shard, quarter)
        return copy(where, where, k, slot, partner)

    ranks, cols = weights[3].shape
    last = 3 * units

    def stack_piece(first, count, shard):
        return wholes[3].at[pl.ds(first, count), pl.ds(pl.multiple_of(shard * cols, cols), cols)]

    steps = [(m, part) for m in range(3) for part in range(units)]
    made = {}

    def begin(k):
        m, part = steps[k]
        made[k, 0] = copy(own(m, part, mine), piece(m, part, group, mine), k, 0, at_above)
        made[k, 2] = copy(own(m, part, mine), piece(m, part, group, mine), k, 2, at_beside)
        made[k, 1] = copy(own(m, part, other), piece(m, part, group, other), k, 1, at_above)

    begin(0)
    begin(1)
    onward = pltpu.make_async_copy(passed, handed, local.at[4])
    fetch = [pltpu.make_async_copy(values, values_ref, local.at[5])] + [
        pltpu.make_async_copy(table, place, table_sems.at[i]) for i, (table, place) in enumerate(zip(tables, loaded))]
    for one in kept[:3] + [onward] + fetch:
        one.start()
    for m in range(3):
        keep(m)

    def pick_sets():
        for one in fetch[1:]:
            one.wait()
        depth = loaded[0].shape[1]
        for i, table in enumerate(loaded):
            out, first = (staged[3], i) if i < counts[0] else (own_ref, i - counts[0])
            for s in range(seqs):
                row = (first * seqs + s) * depth
                out[row : row + depth, :] = table[ids_ref[s]]
        keep(3)

    def norm_values():
        fetch[0].wait()
        count = values_ref.shape[0]
        step = 64 if count % 64 == 0 else count

        def some_rows(i, _):
            at = pl.ds(pl.multiple_of(i * step, step), step)
            normed_ref[at, :] = norm_rows(values_ref[at, :].astype(F32), gain_ref[...])[0].astype(BF16)
            return 0

        lax.fori_loop(0, count // step, some_rows, 0)

    for t in range(len(steps) + 2):
        if t < len(steps):
            m, part = steps[t]
            made[t, 0].wait_recv()
            made[t, 4] = forward(m, part, above, mine, t, 4, at_beside)
            made[t, 6] = forward(m, part, above, mine, t, 6, at_core)
            made[t, 2].wait_recv()
            made[t, 3] = forward(m, part, beside, mine, t, 3, at_level)
            made[t, 8] = forward(m, part, beside, mine, t, 8, at_core)
            if t + 2 < len(steps):
                begin(t + 2)
            if t == len(steps) // 3:
                pick_sets()
            if t == len(steps) // 2:
                norm_values()
            if t + 3 == len(steps):
                stack_beside = copy(weights[3], stack_piece(0, ranks, group), last, 0, at_beside)
                stack_above = copy(weights[3], stack_piece(0, ranks, group), last, 1, at_above)
            made[t, 1].wait_recv()
            made[t, 7] = forward(m, part, above, other, t, 7, at_core)
        if 1 <= t <= len(steps):
            m, part = steps[t - 1]
            made[t - 1, 4].wait_recv()
            made[t - 1, 5] = forward(m, part, across, mine, t - 1, 5, at_level)
            made[t - 1, 10] = forward(m, part, across, mine, t - 1, 10, at_core)
            made[t - 1, 3].wait_recv()
            made[t - 1, 9] = forward(m, part, beside, other, t - 1, 9, at_core)
        if 2 <= t:
            m, part = steps[t - 2]
            made[t - 2, 5].wait_recv()
            made[t - 2, 11] = forward(m, part, across, other, t - 2, 11, at_core)
        if t == len(steps):
            stack_beside.wait_recv()
            stack_above.wait_recv()
            half = ranks // 2
            lower = stack_piece(0, half, above)
            upper = stack_piece(half, half, beside)
            stack_lower = copy(lower, lower, last, 2, at_beside)
            stack_upper = copy(upper, upper, last, 3, at_above)
    onward.wait()
    onward = pltpu.make_async_copy(handed, handed_out, local.at[4])
    onward.start()
    for k in range(len(steps)):
        for slot in range(6, 12):
            made[k, slot].wait_recv()
    for k in range(len(steps)):
        for slot in range(12):
            made[k, slot].wait_send()
    for one in (stack_lower, stack_upper):
        one.wait_recv()
    for one in (stack_beside, stack_above, stack_lower, stack_upper):
        one.wait_send()
    for one in kept + [onward]:
        one.wait()


def gather_weights(w_branch, w_input, w_mixer, passed, values, gain, ids, narrow, wide):
    width, (rows, _), seqs = w_branch.shape[0], values.shape, ids.shape[0]
    if lax.axis_size("group") != 4 or lax.axis_size("replica") % 4 != 0:
        stack, own = pick(ids, narrow, wide)
        return (lax.all_gather(w_branch, "group", axis=1, tiled=True),
                lax.all_gather(w_input, "group", axis=1, tiled=True),
                lax.all_gather(w_mixer, "group", axis=0, tiled=True),
                lax.all_gather(stack, "group", axis=1, tiled=True), passed,
                norm_rows(values.astype(F32), gain)[0].astype(BF16), own)
    units = 4
    counts = (len(narrow), len(wide))
    ranks = narrow[0].shape[1]
    vmem = pl.BlockSpec(memory_space=pltpu.VMEM)
    stack = jax.ShapeDtypeStruct((counts[0] * seqs * ranks, narrow[0].shape[2]), BF16)
    dma = pltpu.SemaphoreType.DMA
    return pl.pallas_call(
        functools.partial(gather_kernel, units, counts, seqs),
        out_shape=[jax.ShapeDtypeStruct((width, width), BF16)] * 3
        + [jax.ShapeDtypeStruct((stack.shape[0], width), BF16), jax.ShapeDtypeStruct(passed.shape, passed.dtype),
           jax.ShapeDtypeStruct(values.shape, BF16),
           jax.ShapeDtypeStruct((counts[1] * seqs * ranks, wide[0].shape[2]), BF16)],
        in_specs=[ANYWHERE] * 5 + [vmem, pl.BlockSpec(memory_space=pltpu.SMEM)] + [ANYWHERE] * sum(counts),
        out_specs=[ANYWHERE] * 5 + [vmem] * 2,
        scratch_shapes=[pltpu.VMEM(part.shape, BF16)
                        for part in (w_branch, w_input, w_mixer, stack, passed, values, *narrow, *wide)]
        + [dma((3 * units + 1, 12)), dma((3 * units + 1, 12)), dma((6,)), dma((sum(counts),))],
        compiler_params=pltpu.CompilerParams(collective_id=0, has_side_effects=True, vmem_limit_bytes=VMEM),
        cost_estimate=pl.CostEstimate(flops=0, bytes_accessed=400 * 2**20, transcendentals=0),
    )(w_branch, w_input, w_mixer, passed, values, gain, ids, *narrow, *wide)


def ordered_kernel(*refs):
    del refs


def ordered(value, *earlier):
    return pl.pallas_call(
        ordered_kernel,
        out_shape=jax.ShapeDtypeStruct(value.shape, value.dtype),
        in_specs=[ANYWHERE] * (1 + len(earlier)),
        out_specs=ANYWHERE,
        input_output_aliases={0: 0},
    )(value, *earlier)


def row_tiles(rows, width, count):
    step = min(rows, 128)
    return (rows // step,), [pl.BlockSpec((step, width), lambda i: (i, 0))] * count


def by_groups(count, action):
    size = GROUP if count % GROUP == 0 else count

    def one(k, _):
        action(pl.ds(pl.multiple_of(k * size, size), size))
        return 0

    lax.fori_loop(0, count // size, one, 0, unroll=2 if count % (2 * size) == 0 else 1)


def resid_grad_kernel(per, resid_ref, cot_ref, gain_ref, *refs):
    pieces, (full_ref, low_ref) = refs[:-2], refs[-2:]

    def some_rows(at):
        values = resid_ref[at, :]
        rate = lax.rsqrt(jnp.mean(values * values, axis=-1, keepdims=True) + EPS)
        grads = pieces[0][at, :]
        for s, piece in enumerate(pieces[1:], 1):
            grads = jnp.where(pl.program_id(0) >= s * per, piece[at, :], grads)
        grads = cot_ref[at, :].astype(F32) + norm_back(values, gain_ref[...], rate, grads.astype(F32))
        full_ref[at, :] = grads
        low_ref[at, :] = grads.astype(BF16)

    by_groups(resid_ref.shape[0], some_rows)


def resid_grad(resid, cot, gain, pieces):
    rows, width = resid.shape
    step = min(pieces[0].shape[0], 128)
    per = pieces[0].shape[0] // step
    tile = pl.BlockSpec((step, width), lambda i: (i, 0))
    return pl.pallas_call(
        functools.partial(resid_grad_kernel, per),
        grid=(rows // step,),
        out_shape=[jax.ShapeDtypeStruct((rows, width), F32), jax.ShapeDtypeStruct((rows, width), BF16)],
        in_specs=[tile, tile, pl.BlockSpec((1, width), lambda i: (0, 0))] + [
            pl.BlockSpec((step, width), lambda i, s=s: (jnp.clip(i - s * per, 0, per - 1), 0))
            for s in range(len(pieces))],
        out_specs=[tile, tile],
        compiler_params=pltpu.CompilerParams(vmem_limit_bytes=VMEM),
        cost_estimate=pl.CostEstimate(
            flops=20 * rows * width, bytes_accessed=14 * rows * width, transcendentals=rows),
    )(resid, cot, gain, *pieces)


def finish_kernel(grad_resid_ref, inputs_ref, gain_ref, grads_ref, out_ref):
    def some_rows(at):
        values = inputs_ref[at, :].astype(F32)
        rate = lax.rsqrt(jnp.mean(values * values, axis=-1, keepdims=True) + EPS)
        out_ref[at, :] = grad_resid_ref[at, :] + norm_back(values, gain_ref[...], rate, grads_ref[at, :])

    by_groups(inputs_ref.shape[0], some_rows)


def finish(grad_resid, inputs, gain, grads):
    rows, width = inputs.shape
    step = min(rows, 128)
    tile = pl.BlockSpec((step, width), lambda i: (i, 0))
    return pl.pallas_call(
        finish_kernel,
        grid=(rows // step,),
        out_shape=jax.ShapeDtypeStruct((rows, width), F32),
        in_specs=[tile, tile, pl.BlockSpec((1, width), lambda i: (0, 0)), tile],
        out_specs=tile,
        compiler_params=pltpu.CompilerParams(vmem_limit_bytes=VMEM),
        cost_estimate=pl.CostEstimate(
            flops=21 * rows * width, bytes_accessed=14 * rows * width, transcendentals=rows),
    )(grad_resid, inputs, gain, grads)


def tail_kernel(
    steps, branch_grad_ref, fed_grad_ref, w_branch_ref, w_input_ref, through_ref, down_ref, partial_ref,
    out_ref, got_ref, *scratch,
):
    step = pl.program_id(0)
    levels = got_ref.shape[0] // 2
    group, replica = lax.axis_index("group"), lax.axis_index("replica")
    ranks = got_ref.shape[1]
    half = ranks // 2
    total = GroupSum(lambda owner, side: partial_ref.at[owner, pl.ds(side * half, half), :], scratch[:10])
    chain = ReplicaChain(scratch[6], got_ref, scratch[10:])

    @pl.when(step == 0)
    def _():
        greet_all(levels, [(group + 1 - 2 * (group % 2), replica), ((group + 2) % 4, replica)])
        total.begin()

    out_ref[...] = (dot(branch_grad_ref[...], w_branch_ref[...], NT) + dot(fed_grad_ref[...], w_input_ref[...], NT)
                    + dot(through_ref[...], down_ref[...]))

    @pl.when(step == max(steps - 2, 0))
    def _():
        total.middle()

    @pl.when(step == steps - 1)
    def _():
        total.end()
        chain.begin()
        for d in range(1, levels):
            chain.hop(d)
        chain.end()
        total.clear()


def tail_call(branch_grad, fed_grad, w_branch, w_input, through, down, partial):
    rows, width = branch_grad.shape
    ranks, cols = partial.shape[1:]
    count = lax.axis_size("replica")
    tile = tile_of(width, 512)
    steps = pl.cdiv(width, tile)
    weight = pl.BlockSpec((tile, width), lambda i: (i, 0))
    return pl.pallas_call(
        functools.partial(tail_kernel, steps),
        grid=(steps,),
        out_shape=[jax.ShapeDtypeStruct((rows, width), F32), jax.ShapeDtypeStruct((count, ranks, cols), BF16)],
        in_specs=[resident(branch_grad), resident(fed_grad), weight, weight, resident(through),
                  pl.BlockSpec((down.shape[0], tile), lambda i: (0, i)), ANYWHERE],
        out_specs=[pl.BlockSpec((rows, tile), lambda i: (0, i)), ANYWHERE],
        scratch_shapes=GroupSum.shapes(ranks, cols) + ReplicaChain.shapes(count),
        compiler_params=pltpu.CompilerParams(
            vmem_limit_bytes=VMEM, collective_id=4, has_side_effects=True),
        cost_estimate=pl.CostEstimate(
            flops=4 * rows * width * width, bytes_accessed=4 * width * width + 8 * rows * width, transcendentals=0),
    )(branch_grad, fed_grad, w_branch, w_input, through, down, partial)


def spread_kernel(counts, ids_ref, *refs):
    gots, outs = refs[: len(counts)], refs[len(counts) :]
    ranks = outs[0].shape[1]
    replicas = gots[0].shape[0]
    seqs = ids_ref.shape[0] // replicas
    for out_ref in outs:
        out_ref[...] = jnp.zeros_like(out_ref)
    for replica in range(replicas):
        for s in range(seqs):
            place = ids_ref[replica * seqs + s]
            table = 0
            for count, got_ref in zip(counts, gots):
                for at in range(count):
                    rows = pl.ds((at * seqs + s) * ranks, ranks)
                    outs[table][place] += got_ref[replica, rows, :].astype(F32)
                    table += 1


def spread(ids, gots, counts, sets, ranks):
    vmem = pl.BlockSpec(memory_space=pltpu.VMEM)
    return pl.pallas_call(
        functools.partial(spread_kernel, counts),
        out_shape=[jax.ShapeDtypeStruct((sets, ranks, got.shape[2]), F32)
                   for got, count in zip(gots, counts) for _ in range(count)],
        in_specs=[pl.BlockSpec(memory_space=pltpu.SMEM)] + [vmem] * len(gots),
        out_specs=[vmem] * sum(counts),
        compiler_params=pltpu.CompilerParams(vmem_limit_bytes=VMEM),
        cost_estimate=pl.CostEstimate(
            flops=sum(got.size for got in gots), bytes_accessed=4 * sum(got.size for got in gots), transcendentals=0),
    )(ids, *gots)


def products_kernel(plan, *refs):
    out_ref, row = refs[-1], 0
    for place, (kind, first, last) in plan:
        if kind == "product":
            result = dot(refs[place][:, first:last], refs[place + 1][...], TN)
        else:
            result = refs[place][...]
        count = last - first
        out_ref[row : row + count, :] = result.astype(BF16)
        row += count


def products(items, earlier=(), blocks=1):
    operands, specs, plan, total = [], [], [], 0
    width = items[0][3].shape[-1]
    tile = width // blocks if blocks > 1 and width % (128 * blocks) == 0 else tile_of(width, 512)
    for item in items:
        if len(item) == 1:
            plan.append((len(operands), ("rows", 0, item[0].shape[0])))
            operands.append(item[0])
            specs.append(pl.BlockSpec((item[0].shape[0], tile), lambda i: (0, i)))
        else:
            lhs, first, last, rhs = item
            plan.append((len(operands), ("product", first, last)))
            if isinstance(rhs, tuple):
                rhs, s = rhs
                block = pl.BlockSpec((None, rhs.shape[1], tile), lambda i, s=s: (s, 0, i))
            else:
                block = pl.BlockSpec((rhs.shape[0], tile), lambda i: (0, i))
            operands += [lhs, rhs]
            specs += [resident(lhs), block]
        total += plan[-1][1][2] - plan[-1][1][1]
    cells = sum(operand.size for operand in operands)
    direct = blocks > 1 and tile * blocks == width
    result = pl.pallas_call(
        functools.partial(products_kernel, plan),
        grid=(pl.cdiv(width, tile),),
        out_shape=jax.ShapeDtypeStruct((blocks, total, tile) if direct else (total, width), BF16),
        in_specs=specs + [ANYWHERE] * len(earlier),
        out_specs=(pl.BlockSpec((None, total, tile), lambda i: (i, 0, 0)) if direct
                   else pl.BlockSpec((total, tile), lambda i: (0, i))),
        compiler_params=pltpu.CompilerParams(vmem_limit_bytes=VMEM),
        cost_estimate=pl.CostEstimate(flops=64 * cells, bytes_accessed=2 * cells, transcendentals=0),
    )(*operands, *earlier)
    if blocks > 1 and not direct:
        result = jnp.swapaxes(result.reshape(total, blocks, width // blocks), 0, 1)
    return result


def passed_along(block, axis, distance):
    devices = range(lax.axis_size(axis))
    route = [(i - distance, i) for i in devices if i - distance in devices]
    return lax.ppermute(block, axis, route)


def body(
    inputs, segment_ids, adapter_ids, gain_mix, gain_mlp, w_branch, w_input, conv_taps, decay_heads, admit_heads,
    decay_param, w_mixer, w_gate, w_upper, w_down, down_branch, lift_branch, down_input, lift_input, down_decay,
    lift_decay, down_admit, lift_admit, down_mixer, lift_mixer, down_gate, lift_gate, down_upper, lift_upper,
    down_outward, lift_outward, out_grad,
):
    seqs, stretch, width = inputs.shape
    rows = seqs * stretch
    taps = conv_taps.shape[0]
    sets, _, ranks = down_branch.shape
    group, place = lax.axis_size("group"), lax.axis_index("group")
    mask_cols = seqs * ranks

    turned = lambda table: jnp.swapaxes(table, 1, 2)
    full_branch, full_input, full_mixer, stack, late_grad, normed, own_tables = gather_weights(
        w_branch, w_input, w_mixer, out_grad, inputs.reshape(rows, width), gain_mix.reshape(1, width), adapter_ids,
        [turned(down_branch), turned(down_input), turned(down_decay), turned(down_admit), turned(down_mixer),
         turned(down_gate), turned(down_upper), lift_branch, lift_input, lift_decay, lift_admit, lift_mixer,
         lift_outward],
        [lift_gate, lift_upper, turned(down_outward)])
    (p_down_branch, p_down_input, p_down_decay, p_down_admit, p_down_mixer, p_down_gate, p_down_upper,
     p_lift_branch, p_lift_input, p_lift_decay, p_lift_admit, p_lift_mixer, p_lift_outward) = [
        stack[i * mask_cols : (i + 1) * mask_cols] for i in range(13)]
    own_lift_gate, own_lift_upper, own_down_outward = [
        own_tables[i * mask_cols : (i + 1) * mask_cols] for i in range(3)]
    cotangents = lax.all_gather(late_grad, "group", axis=1, tiled=True)

    row_seq = lax.broadcasted_iota(jnp.int32, (rows, mask_cols), 0) // stretch
    col_seq = lax.broadcasted_iota(jnp.int32, (rows, mask_cols), 1) // ranks
    own = (row_seq == col_seq).astype(F32)
    own_two = jnp.concatenate([own, own], 1)

    begin = place * stretch
    padded_ids = jnp.pad(segment_ids, ((0, 0), (taps - 1, taps - 1)), constant_values=-1)
    window = lax.dynamic_slice_in_dim(padded_ids, begin, stretch + 2 * (taps - 1), 1)
    current = window[:, taps - 1 : taps - 1 + stretch + taps - 1]
    agree = [
        ((current == window[:, taps - 1 - j : taps - 1 - j + stretch + taps - 1]) & (current >= 0)).astype(F32)
        for j in range(taps)
    ]
    restart = (1.0 - agree[1][:, :stretch]).reshape(rows, 1)

    x_float = inputs.reshape(rows, width).astype(F32)
    inner_one = (dot(normed, stack[: 2 * mask_cols], NT) * own_two).astype(BF16)
    inner_branch, inner_input = inner_one[:, :mask_cols], inner_one[:, mask_cols:]
    branch_pre = dot(normed, full_branch) + dot(inner_branch, p_lift_branch)
    fed = (dot(normed, full_input) + dot(inner_input, p_lift_input)).astype(BF16)
    fed = fed.reshape(seqs, stretch, width)
    halo = passed_along(fed[:, stretch - (taps - 1) :], "group", 1)
    extended = jnp.concatenate([halo, fed], axis=1).astype(F32)
    convolved = sum(
        conv_taps[j] * agree[j][:, :stretch, None] * extended[:, taps - 1 - j : taps - 1 - j + stretch]
        for j in range(taps)
    ).reshape(rows, width)
    rounded = convolved.astype(BF16)
    softrate = jax.nn.softplus(decay_param).reshape(1, width)
    inner_gates = (dot(rounded, stack[2 * mask_cols : 4 * mask_cols], NT) * own_two).astype(BF16)
    lift_gates = stack[9 * mask_cols : 11 * mask_cols]
    cum, local = forward_gates(seqs, convolved, inner_gates, lift_gates, decay_heads, admit_heads, softrate, restart)
    ends = jnp.concatenate(
        [cum.reshape(seqs, stretch, width)[:, -1], local.reshape(seqs, stretch, width)[:, -1]], 0)
    all_ends = lax.all_gather(ends, "group")
    carried = jnp.zeros((seqs, width), F32)
    for g in range(group - 1):
        longer = all_ends[g, :seqs] * carried + all_ends[g, seqs:]
        carried = jnp.where(g < place, longer, carried)
    carried_rows = jnp.repeat(carried, stretch, axis=0)
    state = local + cum * carried_rows
    merged = (state * gelu(branch_pre)).astype(BF16)
    inner_mixer = (dot(merged, p_down_mixer, NT) * own).astype(BF16)
    mixed = dot(merged, full_mixer) + dot(inner_mixer, p_lift_mixer)
    resid = x_float + mixed
    normed_two_f, _ = norm_rows(resid, gain_mlp)
    normed_two = normed_two_f.astype(BF16).reshape(seqs, stretch, width)

    spans = [slice(s * ranks, (s + 1) * ranks) for s in range(seqs)]
    named = jnp.broadcast_to(jnp.pad(adapter_ids, (0, -seqs % 16)).astype(BF16)[:, None], (-(-seqs // 16) * 16,
                                                                                   w_gate.shape[1]))
    gain_one, gain_two = gain_mix.reshape(1, width), gain_mlp.reshape(1, width)
    agree_cols = jnp.stack([agree[j][:, j : j + stretch].reshape(rows) for j in range(taps)], 1)
    grad_hiddens, through_out, first_tokens = grad_hidden_call(
        cotangents, w_down, p_lift_outward, own_down_outward, normed_two[0], (gain_two, gain_one, agree_cols, named))
    all_tokens = [first_tokens] + [
        lax.all_gather(ordered(normed_two[s], first_tokens), "group", axis=0, tiled=True) for s in range(1, seqs)]
    backs, hiddens, throughs, wides = [], [], [], []
    for s, at in enumerate(spans):
        two_downs = jnp.concatenate([p_down_gate[at], p_down_upper[at]], 0)
        hidden, back, wide, through = feed_call(
            s, all_tokens[s], grad_hiddens, w_gate, w_upper, two_downs, own_lift_gate[at], own_lift_upper[at],
            through_out)
        if s < seqs - 1:
            backs.append(lax.psum_scatter(back, "group", scatter_dimension=0, tiled=True))
        hiddens.append(hidden)
        throughs.append(through)
        wides.append(wide)
    outward, _, early, reduced = outward_call(
        hiddens, all_tokens, throughs, cotangents, resid, w_down, own_down_outward, p_lift_outward, back)
    backs.append(reduced)
    wide = jnp.concatenate(
        [wides[s][i * ranks : (i + 1) * ranks] for i in range(3) for s in range(seqs)] + [named], 0)
    grad_resid, grad_mixed = resid_grad(
        resid, out_grad.reshape(rows, width), gain_two, backs)
    block_out = lax.psum_scatter(outward, "group", scatter_dimension=1, tiled=True)

    kernels = (group == 4 and lax.axis_size("replica") % 2 == 0 and 2 * seqs <= 8 and stretch % GROUP == 0
               and width % 512 == 0 and seqs % 2 == 0)
    if kernels:
        grad_branch_pre, through_one, through_gates, grad_lift_gates, grad_fed, through_mixer, got_early, got_wide = mixer_back(
            seqs, grad_mixed, full_mixer, p_lift_mixer, p_down_mixer, convolved, inner_gates, lift_gates, decay_heads,
            admit_heads, softrate, restart, cum, local, carried, branch_pre, p_lift_branch, p_lift_input,
            stack[2 * mask_cols : 4 * mask_cols], conv_taps, agree_cols, early, wide)
    else:
        through_mixer = (dot(grad_mixed, p_lift_mixer, NT) * own).astype(BF16)
        grad_merged = dot(grad_mixed, full_mixer, NT) + dot(through_mixer, p_down_mixer)
        span, total, firsts, grad_branch_pre = backward_scan(
            seqs, convolved, inner_gates, lift_gates, decay_heads, softrate, restart, cum, local, carried, branch_pre,
            grad_merged)
        all_firsts = lax.all_gather(firsts, "group")
        incoming = jnp.zeros((seqs, width), F32)
        for lap in range(group - 1):
            g = group - 1 - lap
            longer = all_firsts[g, :seqs] * incoming + all_firsts[g, seqs:]
            incoming = jnp.where(g > place, longer, incoming)
        grad_direct, through_gates, grad_lift_gates = backward_gates(
            seqs, convolved, inner_gates, lift_gates, decay_heads, admit_heads, softrate, restart, cum, local, carried,
            span, total, incoming)
        through_gates = (through_gates * own_two).astype(BF16)
        grad_convolved = grad_direct + dot(through_gates, stack[2 * mask_cols : 4 * mask_cols])
        grad_convolved = grad_convolved.reshape(seqs, stretch, width)
        below = passed_along(grad_convolved[:, : taps - 1].astype(BF16), "group", -1).astype(F32)
        grad_extended = jnp.concatenate([grad_convolved, below], axis=1)
        grad_fed = sum(
            conv_taps[j] * agree[j][:, j : j + stretch, None] * grad_extended[:, j : j + stretch] for j in range(taps)
        ).astype(BF16).reshape(rows, width)
        through_branch = (dot(grad_branch_pre, p_lift_branch, NT) * own).astype(BF16)
        through_input = (dot(grad_fed, p_lift_input, NT) * own).astype(BF16)
        through_one = jnp.concatenate([through_branch, through_input], 1)
    both = 2 * mask_cols
    late = products(
        [(through_one, 0, both, normed), (through_gates, 0, both, rounded), (through_mixer, 0, mask_cols, merged),
         (inner_branch, 0, mask_cols, grad_branch_pre), (inner_input, 0, mask_cols, grad_fed), (grad_lift_gates,),
         (inner_mixer, 0, mask_cols, grad_mixed)], (), group)
    if kernels:
        grad_normed, got_late = tail_call(
            grad_branch_pre, grad_fed, full_branch, full_input, through_one, stack[:both], late)
    else:
        grad_normed = (dot(grad_branch_pre, full_branch, NT) + dot(grad_fed, full_input, NT)
                       + dot(through_one, stack[:both]))
        got_late = lax.all_gather(lax.psum_scatter(late, "group", scatter_dimension=0, tiled=False), "replica")
        got_early = lax.all_gather(lax.psum_scatter(early, "group", scatter_dimension=1, tiled=True), "replica")
        got_wide = lax.all_gather(wide, "replica")
    grad_inputs = finish(grad_resid, inputs.reshape(rows, width), gain_one, grad_normed)
    all_ids = got_wide[:, 3 * mask_cols : 3 * mask_cols + seqs, 0].astype(jnp.int32).reshape(-1)
    totals = spread(all_ids, [got_late, got_early, got_wide], (10, 3, 3), sets, ranks)
    (t_down_branch, t_down_input, t_down_decay, t_down_admit, t_down_mixer, t_lift_branch, t_lift_input, t_lift_decay,
     t_lift_admit, t_lift_mixer, t_down_gate, t_down_upper, t_lift_outward, *wides) = totals
    return (
        block_out, grad_inputs.reshape(seqs, stretch, width),
        turned(t_down_branch), t_lift_branch, turned(t_down_input), t_lift_input, turned(t_down_decay), t_lift_decay,
        turned(t_down_admit), t_lift_admit, turned(t_down_mixer), t_lift_mixer, turned(t_down_gate), wides[0],
        turned(t_down_upper), wides[1], turned(wides[2]), t_lift_outward,
    )


def solution(mesh):
    tokens = P("replica", "group", None)
    down, lift = P(None, "group", None), P(None, None, "group")
    cols, split = P(None, "group"), P("group", None)
    in_specs = (
        tokens, P("replica", None), P("replica"), P(), P(), cols, cols, P(), P(), P(), P(), split, cols, cols, split,
    ) + (down, lift) * 8 + (tokens,)
    out_specs = (tokens, tokens) + (down, lift) * 8
    return jax.shard_map(body, mesh=mesh, in_specs=in_specs, out_specs=out_specs, check_vma=False)
```

```python
import functools

import jax
import jax.numpy as jnp
from jax import lax
from jax.experimental import pallas as pl
from jax.experimental.pallas import tpu as pltpu
from jax.sharding import PartitionSpec as P

EPS = 1e-06
F32 = jnp.float32
BF16 = jnp.bfloat16
GELU_C = 0.7978845608028654
GELU_A = 0.044715
NT = (((1,), (1,)), ((), ()))
NN = (((1,), (0,)), ((), ()))
TN = (((0,), (0,)), ((), ()))
ANYWHERE = pl.BlockSpec(memory_space=pl.ANY)
VMEM = 62 * 2**20


def dot(a, b, dims=NN):
    return lax.dot_general(a, b, dims, preferred_element_type=F32)


def gelu(v):
    return 0.5 * v * (1.0 + jnp.tanh(GELU_C * (v + GELU_A * v * v * v)))


def gelu_both(v):
    square = v * v
    half = 0.5 + 0.5 * jnp.tanh(v * (GELU_C + GELU_C * GELU_A * square))
    value = v * half
    return value, half + (value - value * half) * (2.0 * GELU_C + 6.0 * GELU_C * GELU_A * square)


def norm_rows(values, gain):
    rate = lax.rsqrt(jnp.mean(values * values, axis=-1, keepdims=True) + EPS)
    return values * rate * gain, rate


def norm_back(values, gain, rate, grads):
    scaled = grads * gain
    along = jnp.mean(scaled * values, axis=-1, keepdims=True)
    return rate * scaled - values * (rate * rate * rate * along)


def rows_shifted(values, by, fill):
    rows, width = values.shape
    if by % 8 == 0:
        return jnp.concatenate([jnp.full((by, width), fill, values.dtype), values[: rows - by]], 0)
    place = lax.broadcasted_iota(jnp.int32, values.shape, 0)
    return jnp.where(place >= by, pltpu.roll(values, by, 0), fill)


def rows_advanced(values, by, fill):
    rows, width = values.shape
    if by % 8 == 0:
        return jnp.concatenate([values[by:], jnp.full((by, width), fill, values.dtype)], 0)
    place = lax.broadcasted_iota(jnp.int32, values.shape, 0)
    return jnp.where(place < rows - by, pltpu.roll(values, rows - by, 0), fill)


def scan_rows(a, b, moved):
    by = 1
    while by < a.shape[0]:
        b = a * moved(b, by, 0.0) + b
        a = a * moved(a, by, 1.0)
        by *= 2
    return a, b


def gate_steps(pre_d, pre_a, softrate, restart):
    decay_gate = 1.0 / (1.0 + jnp.exp(-pre_d))
    admit_gate = 1.0 / (1.0 + jnp.exp(-pre_a))
    safe = jnp.where(restart, -1.0, -8.0 * decay_gate * softrate)
    grown = jnp.exp(safe)
    scale = jnp.sqrt(jnp.tanh(-safe) * (1.0 + grown * grown))
    return decay_gate, admit_gate, grown, scale


def gate_values(conv, inner, lift, table_d, table_a, softrate, restart):
    rounded = conv.astype(BF16)
    half = lift.shape[0] // 2
    pre_d = dot(rounded, table_d) + dot(inner[:, :half], lift[:half])
    pre_a = dot(rounded, table_a) + dot(inner[:, half:], lift[half:])
    return gate_steps(pre_d, pre_a, softrate, restart)


GROUP = 16
UNROLL = 16


def scan_group(a, b, carry_a, carry_b, moved):
    by = 1
    while by < a.shape[0]:
        b = a * moved(b, by, 0.0) + b
        a = a * moved(a, by, 1.0)
        by *= 2
    return a * carry_a, a * carry_b + b


def forward_gates_kernel(seqs, conv_ref, inner_ref, lift_ref, table_d_ref, table_a_ref, soft_ref, restart_ref,
                         cum_ref, local_ref, pre_d_ref, pre_a_ref):
    rows, size = conv_ref.shape
    stretch = rows // seqs
    half = lift_ref.shape[0] // 2
    rounded = conv_ref[...].astype(BF16)
    pre_d_ref[...] = dot(rounded, table_d_ref[0]) + dot(inner_ref[:, :half], lift_ref[:half, :])
    pre_a_ref[...] = dot(rounded, table_a_ref[0]) + dot(inner_ref[:, half:], lift_ref[half:, :])
    softrate = soft_ref[...]

    def group(k, carries):
        after = []
        for s in range(seqs):
            at = pl.ds(pl.multiple_of(s * stretch + k * GROUP, GROUP), GROUP)
            restart = restart_ref[at, :] > 0.5
            _, admit, grown, scale = gate_steps(pre_d_ref[at, :], pre_a_ref[at, :], softrate, restart)
            decays = jnp.where(restart, 0.0, grown)
            drive = conv_ref[at, :] * admit * jnp.where(restart, 1.0, scale)
            cum, local = scan_group(decays, drive, *carries[s], rows_shifted)
            cum_ref[at, :] = cum
            local_ref[at, :] = local
            after.append((cum[GROUP - 1 :], local[GROUP - 1 :]))
        return tuple(after)

    start = (jnp.ones((1, size), F32), jnp.zeros((1, size), F32))
    lax.fori_loop(0, stretch // GROUP, group, (start,) * seqs, unroll=UNROLL)


def forward_gates(seqs, conv, inner, lift, table_d, table_a, softrate, restart):
    rows, width = conv.shape
    heads, size = table_d.shape[:2]
    tile = pl.BlockSpec((rows, size), lambda h: (0, h))
    table = pl.BlockSpec((1, size, size), lambda h: (h, 0, 0))
    out = jax.ShapeDtypeStruct((rows, width), F32)
    return pl.pallas_call(
        functools.partial(forward_gates_kernel, seqs),
        out_shape=(out, out),
        grid=(heads,),
        in_specs=[
            tile,
            pl.BlockSpec(inner.shape, lambda h: (0, 0)),
            pl.BlockSpec((lift.shape[0], size), lambda h: (0, h)),
            table,
            table,
            pl.BlockSpec((1, size), lambda h: (0, h)),
            pl.BlockSpec(restart.shape, lambda h: (0, 0)),
        ],
        out_specs=(tile, tile),
        scratch_shapes=[pltpu.VMEM((rows, size), F32)] * 2,
        compiler_params=pltpu.CompilerParams(vmem_limit_bytes=40 * 2**20),
        cost_estimate=pl.CostEstimate(
            flops=4 * rows * width * size + 60 * rows * width,
            bytes_accessed=12 * rows * width,
            transcendentals=6 * rows * width),
    )(conv, inner, lift, table_d, table_a, softrate, restart)


def backward_scan_kernel(seqs, conv_ref, inner_ref, lift_ref, table_d_ref, soft_ref, restart_ref, cum_ref, local_ref,
                         carried_ref, pre_ref, grad_ref, span_ref, total_ref, first_ref, branch_grad_ref):
    stretch = conv_ref.shape[0] // seqs
    half = lift_ref.shape[0] // 2
    for s in range(seqs):
        rows = pl.ds(s * stretch, stretch)
        restart = restart_ref[rows, :] > 0.5
        rounded = conv_ref[rows, :].astype(BF16)
        pre_d = dot(rounded, table_d_ref[0]) + dot(inner_ref[rows, :half], lift_ref[:half, :])
        grown = jnp.exp(-8.0 * soft_ref[...] / (1.0 + jnp.exp(-pre_d)))
        decays = jnp.where(restart, 0.0, grown)
        state = local_ref[rows, :] + cum_ref[rows, :] * carried_ref[s : s + 1, :]
        value, slope = gelu_both(pre_ref[rows, :])
        grads = grad_ref[rows, :]
        branch_grad_ref[rows, :] = (grads * state * slope).astype(BF16)
        span, total = scan_rows(rows_advanced(decays, 1, 1.0), grads * value, rows_advanced)
        span_ref[rows, :] = span
        total_ref[rows, :] = total
        first_ref[s : s + 1, :] = decays[:1] * span[:1]
        first_ref[seqs + s : seqs + s + 1, :] = decays[:1] * total[:1]


def backward_scan(seqs, conv, inner, lift, table_d, softrate, restart, cum, local, carried, pre, grads):
    rows, width = conv.shape
    heads, size = table_d.shape[:2]
    tile = pl.BlockSpec((rows, size), lambda h: (0, h))
    table = pl.BlockSpec((1, size, size), lambda h: (h, 0, 0))
    out = jax.ShapeDtypeStruct((rows, width), F32)
    return pl.pallas_call(
        functools.partial(backward_scan_kernel, seqs),
        out_shape=(out, out, jax.ShapeDtypeStruct((2 * seqs, width), F32), jax.ShapeDtypeStruct((rows, width), BF16)),
        grid=(heads,),
        in_specs=[
            tile,
            pl.BlockSpec(inner.shape, lambda h: (0, 0)),
            pl.BlockSpec((lift.shape[0], size), lambda h: (0, h)),
            table,
            pl.BlockSpec((1, size), lambda h: (0, h)),
            pl.BlockSpec(restart.shape, lambda h: (0, 0)),
            tile,
            tile,
            pl.BlockSpec((seqs, size), lambda h: (0, h)),
            tile,
            tile,
        ],
        out_specs=(tile, tile, pl.BlockSpec((2 * seqs, size), lambda h: (0, h)), tile),
        compiler_params=pltpu.CompilerParams(vmem_limit_bytes=48 * 2**20),
        cost_estimate=pl.CostEstimate(
            flops=2 * rows * width * size + 80 * rows * width,
            bytes_accessed=30 * rows * width,
            transcendentals=4 * rows * width),
    )(conv, inner, lift, table_d, softrate, restart, cum, local, carried, pre, grads)


def backward_gates_kernel(seqs, conv_ref, inner_ref, lift_ref, table_d_ref, table_a_ref, soft_ref, restart_ref,
                          cum_ref, local_ref, carried_ref, span_ref, total_ref, incoming_ref,
                          conv_grad_ref, through_ref, lift_grad_ref):
    stretch = conv_ref.shape[0] // seqs
    half = lift_ref.shape[0] // 2

    @pl.when(pl.program_id(0) == 0)
    def _():
        through_ref[...] = jnp.zeros_like(through_ref)

    for s in range(seqs):
        rows = pl.ds(s * stretch, stretch)
        conv = conv_ref[rows, :]
        inner = inner_ref[rows, :]
        restart = restart_ref[rows, :] > 0.5
        softrate = soft_ref[...]
        decay_gate, admit, grown, scale = gate_values(
            conv, inner, lift_ref[...], table_d_ref[0], table_a_ref[0], softrate, restart)
        carried = carried_ref[s : s + 1, :]
        state = local_ref[rows, :] + cum_ref[rows, :] * carried
        place = lax.broadcasted_iota(jnp.int32, state.shape, 0)
        before = jnp.where(place >= 1, pltpu.roll(state, 1, 0), carried)
        grads = total_ref[rows, :] + span_ref[rows, :] * incoming_ref[s : s + 1, :]
        driven = grads * jnp.where(restart, 1.0, scale)
        grad_log = jnp.where(
            restart, 0.0, grads * (before * grown - conv * admit * grown * grown / scale))
        grad_d = (-8.0 * softrate) * grad_log * decay_gate * (1.0 - decay_gate)
        grad_a = driven * conv * admit * (1.0 - admit)
        low_d, low_a = grad_d.astype(BF16), grad_a.astype(BF16)
        conv_grad_ref[rows, :] = driven * admit + dot(low_d, table_d_ref[0], NT) + dot(low_a, table_a_ref[0], NT)
        through_ref[rows, :half] += dot(low_d, lift_ref[:half, :], NT)
        through_ref[rows, half:] += dot(low_a, lift_ref[half:, :], NT)
        first = dot(inner[:, :half], low_d, TN)
        second = dot(inner[:, half:], low_a, TN)
        if s == 0:
            lift_grad_ref[:half, :] = first
            lift_grad_ref[half:, :] = second
        else:
            lift_grad_ref[:half, :] += first
            lift_grad_ref[half:, :] += second


def backward_gates(seqs, conv, inner, lift, table_d, table_a, softrate, restart, cum, local, carried, span, total,
                   incoming):
    rows, width = conv.shape
    heads, size = table_d.shape[:2]
    tile = pl.BlockSpec((rows, size), lambda h: (0, h))
    table = pl.BlockSpec((1, size, size), lambda h: (h, 0, 0))
    edge = pl.BlockSpec((seqs, size), lambda h: (0, h))
    ranks = pl.BlockSpec((lift.shape[0], size), lambda h: (0, h))
    return pl.pallas_call(
        functools.partial(backward_gates_kernel, seqs),
        out_shape=(
            jax.ShapeDtypeStruct((rows, width), F32),
            jax.ShapeDtypeStruct(inner.shape, F32),
            jax.ShapeDtypeStruct(lift.shape, F32),
        ),
        grid=(heads,),
        in_specs=[
            tile,
            pl.BlockSpec(inner.shape, lambda h: (0, 0)),
            ranks,
            table,
            table,
            pl.BlockSpec((1, size), lambda h: (0, h)),
            pl.BlockSpec(restart.shape, lambda h: (0, 0)),
            tile,
            tile,
            edge,
            tile,
            tile,
            edge,
        ],
        out_specs=(tile, pl.BlockSpec(inner.shape, lambda h: (0, 0)), ranks),
        compiler_params=pltpu.CompilerParams(vmem_limit_bytes=48 * 2**20),
        cost_estimate=pl.CostEstimate(
            flops=8 * rows * width * size + 80 * rows * width,
            bytes_accessed=24 * rows * width,
            transcendentals=6 * rows * width),
    )(conv, inner, lift, table_d, table_a, softrate, restart, cum, local, carried, span, total, incoming)


def remote(src, dst, send_sem, recv_sem, partner):
    return pltpu.make_async_remote_copy(
        src_ref=src, dst_ref=dst, send_sem=send_sem, recv_sem=recv_sem, device_id=partner,
        device_id_type=pl.DeviceIdType.MESH)


class GroupSum:
    def __init__(self, block, scratch):
        first_a, first_b, second_a, second_b, pass_a, pass_b, own, send, recv, local = scratch
        group, replica = lax.axis_index("group"), lax.axis_index("replica")
        beside, above, across = group + 1 - 2 * (group % 2), (group + 2) % 4, 3 - group
        at_beside, at_above = (beside, replica), (above, replica)
        self.scratch, self.half = scratch, own.shape[0] // 2
        pairs = [(block(across, 0), first_a.at[1], at_beside), (block(across, 1), first_b.at[1], at_above),
                 (block(beside, 0), first_a.at[0], at_beside), (block(above, 1), first_b.at[0], at_above),
                 (pass_a, second_a, at_above), (pass_b, second_b, at_beside)]
        moves = [remote(src, dst, send.at[slot], recv.at[slot], partner)
                 for slot, (src, dst, partner) in enumerate(pairs)]
        self.firsts, self.seconds = moves[:4], moves[4:]
        pieces = [(block(above, 0), pass_a), (block(beside, 1), pass_b), (block(group, 0), own.at[pl.ds(0, self.half)]),
                  (block(group, 1), own.at[pl.ds(self.half, self.half)])]
        self.loads = [pltpu.make_async_copy(src, dst, local.at[i]) for i, (src, dst) in enumerate(pieces)]

    def begin(self):
        for one in self.firsts + self.loads:
            one.start()

    def middle(self):
        first_a, first_b, _, _, pass_a, pass_b = self.scratch[:6]
        for one in self.loads:
            one.wait()
        for one in self.firsts:
            one.wait_recv()
        pass_a[...] = (pass_a[...].astype(F32) + first_a[1].astype(F32)).astype(BF16)
        pass_b[...] = (pass_b[...].astype(F32) + first_b[1].astype(F32)).astype(BF16)
        for one in self.seconds:
            one.start()

    def end(self):
        first_a, first_b, second_a, second_b, _, _, own = self.scratch[:7]
        half = self.half
        for one in self.seconds:
            one.wait_recv()
        own[:half] = (own[:half].astype(F32) + first_a[0].astype(F32) + second_a[...].astype(F32)).astype(BF16)
        own[half:] = (own[half:].astype(F32) + first_b[0].astype(F32) + second_b[...].astype(F32)).astype(BF16)

    def clear(self):
        for one in self.firsts + self.seconds:
            one.wait_send()

    @staticmethod
    def shapes(ranks, cols):
        half = ranks // 2
        return [pltpu.VMEM((2, half, cols), BF16)] * 2 + [pltpu.VMEM((half, cols), BF16)] * 4 + [
            pltpu.VMEM((ranks, cols), BF16), pltpu.SemaphoreType.DMA((6,)), pltpu.SemaphoreType.DMA((6,)),
            pltpu.SemaphoreType.DMA((4,))]


class ReplicaChain:
    def __init__(self, own, got, sems):
        up_send, low_recv, down_send, high_recv, core_send, core_recv, local = sems
        group, replica = lax.axis_index("group"), lax.axis_index("replica")
        count = got.shape[0]
        self.levels, self.level = count // 2, replica // 2
        at_core = (group, replica + 1 - 2 * (replica % 2))
        at_up, at_down = (group, (replica + 2) % count), (group, (replica + count - 2) % count)
        self.has_up, self.has_down = self.level < self.levels - 1, self.level > 0
        piece = lambda source: got.at[(source + count) % count]
        self.to_up = [remote(own, piece(replica), up_send.at[0], low_recv.at[0], at_up)]
        self.to_down = [remote(own, piece(replica), down_send.at[0], high_recv.at[0], at_down)]
        self.to_core = [remote(own, piece(replica), core_send.at[0], core_recv.at[0], at_core)]
        self.keep = pltpu.make_async_copy(own, piece(replica), local.at[0])
        for d in range(1, self.levels):
            low, high = piece(replica - 2 * d), piece(replica + 2 * d)
            self.to_up.append(remote(low, low, up_send.at[d], low_recv.at[d], at_up))
            self.to_down.append(remote(high, high, down_send.at[d], high_recv.at[d], at_down))
            self.to_core += [remote(low, low, core_send.at[2 * d - 1], core_recv.at[2 * d - 1], at_core),
                             remote(high, high, core_send.at[2 * d], core_recv.at[2 * d], at_core)]

    def begin(self):
        self.keep.start()
        pl.when(self.has_up)(self.to_up[0].start)
        pl.when(self.has_down)(self.to_down[0].start)
        self.to_core[0].start()

    def hop(self, d):
        @pl.when(self.level >= d)
        def _():
            self.to_up[d - 1].wait_recv()
            pl.when(self.has_up)(self.to_up[d].start)
            self.to_core[2 * d - 1].start()

        @pl.when(self.level + d < self.levels)
        def _():
            self.to_down[d - 1].wait_recv()
            pl.when(self.has_down)(self.to_down[d].start)
            self.to_core[2 * d].start()

    def end(self):
        self.to_core[0].wait()
        pl.when(self.has_up)(self.to_up[0].wait_send)
        pl.when(self.has_down)(self.to_down[0].wait_send)
        for d in range(1, self.levels):
            from_low, from_high = self.level >= d, self.level + d < self.levels
            pl.when(from_low)(self.to_core[2 * d - 1].wait)
            pl.when(from_high)(self.to_core[2 * d].wait)
            pl.when(from_low & self.has_up)(self.to_up[d].wait_send)
            pl.when(from_high & self.has_down)(self.to_down[d].wait_send)
        self.keep.wait()

    @staticmethod
    def shapes(count):
        return [pltpu.SemaphoreType.DMA((count // 2,))] * 4 + [pltpu.SemaphoreType.DMA((count,))] * 2 + [
            pltpu.SemaphoreType.DMA((1,))]


def greet_all(levels, group_partners):
    group, replica = lax.axis_index("group"), lax.axis_index("replica")
    level = replica // 2
    barrier = pltpu.get_barrier_semaphore()

    def greet(partner):
        pl.semaphore_signal(barrier, inc=1, device_id=partner, device_id_type=pl.DeviceIdType.MESH)

    for partner in group_partners + [(group, replica + 1 - 2 * (replica % 2))]:
        greet(partner)

    @pl.when(level > 0)
    def _():
        greet((group, (replica + 2 * levels - 2) % (2 * levels)))

    @pl.when(level < levels - 1)
    def _():
        greet((group, (replica + 2) % (2 * levels)))

    ends = (level + levels - 1) // levels + (2 * levels - 2 - level) // levels
    pl.semaphore_wait(barrier, len(group_partners) + 1 + ends)


def sequence_mask(rows, cols, seqs):
    row = lax.broadcasted_iota(jnp.int32, (rows, cols), 0) // (rows // seqs)
    col = lax.broadcasted_iota(jnp.int32, (rows, cols), 1) % (cols // 2) // (cols // 2 // seqs)
    return (row == col).astype(F32)


def mixer_back_kernel(
    seqs, heads, mixed_ref, w_ref, lift_mixer_ref, down_mixer_ref, conv_ref, inner_ref, lift_ref, table_d_ref,
    table_a_ref, soft_ref, restart_ref, cum_ref, local_ref, carried_ref, pre_ref, lift_branch_ref, lift_input_ref,
    down_gates_ref, taps_ref, agree_ref, early_ref, wide_ref,
    branch_grad_ref, through_one_ref, through_gates_ref, lift_grad_ref, fed_grad_ref, thr_mixer_ref,
    got_early_ref, got_wide_ref, span_ref, total_ref, ends_ref, all_ends_ref, incoming_ref, halo_ref, below_ref, one_ref, gates_ref, first_ref,
    second_ref, low_d_ref, low_a_ref, longer_ref, send, recv, *scratch,
):
    rows, size = conv_ref.shape
    stretch = rows // seqs
    half = lift_ref.shape[0] // 2
    ranks = lift_branch_ref.shape[0]
    each = table_d_ref.shape[1]
    lanes = [slice(q * each, (q + 1) * each) for q in range(size // each)]
    step = pl.program_id(0)
    group, replica = lax.axis_index("group"), lax.axis_index("replica")
    partners = [(group + 1 - 2 * (group % 2), replica), ((group + 2) % 4, replica), (3 - group, replica)]

    def copy(src, dst, slot, partner):
        return pltpu.make_async_remote_copy(
            src_ref=src, dst_ref=dst, send_sem=send.at[slot], recv_sem=recv.at[slot], device_id=partner,
            device_id_type=pl.DeviceIdType.MESH)

    early_rows, early_cols = got_early_ref.shape[1:]
    early_half = early_rows // 2
    total_early = GroupSum(
        lambda owner, side: early_ref.at[
            pl.ds(side * early_half, early_half), pl.ds(pl.multiple_of(owner * early_cols, early_cols), early_cols)],
        scratch[:10])
    levels = got_early_ref.shape[0] // 2
    chains = [ReplicaChain(scratch[6], got_early_ref, scratch[10:17]),
              ReplicaChain(wide_ref, got_wide_ref, scratch[17:])]

    exchange = [copy(ends_ref, all_ends_ref.at[group], slot, partner) for slot, partner in enumerate(partners)]
    downward = copy(halo_ref, below_ref, 3, ((group + 3) % 4, replica))

    @pl.when(step == 0)
    def _():
        greet_all(levels, partners)
        total_early.begin()
        chains[1].begin()
        one_ref[...] = jnp.zeros_like(one_ref)
        gates_ref[...] = jnp.zeros_like(gates_ref)
        ends_ref[...] = jnp.zeros_like(ends_ref)
        row = lax.broadcasted_iota(jnp.int32, thr_mixer_ref.shape, 0) // stretch
        col = lax.broadcasted_iota(jnp.int32, thr_mixer_ref.shape, 1) // (thr_mixer_ref.shape[1] // seqs)
        through = dot(mixed_ref[...], lift_mixer_ref[...], NT)
        thr_mixer_ref[...] = jnp.where(row == col, through, 0.0).astype(BF16)

    stops = 3 * heads / (levels + 2)

    @pl.when(step == int(stops / 2))
    def _():
        total_early.middle()

    @pl.when(step == int(stops))
    def _():
        total_early.end()
        chains[0].begin()

    for d in range(1, levels):
        @pl.when(step == int((d + 1) * stops))
        def _(d=d):
            for chain in chains:
                chain.hop(d)

    groups = stretch // GROUP

    def rows_of(s, k):
        return pl.ds(pl.multiple_of(s * stretch + k * GROUP, GROUP), GROUP)

    @pl.when(step < heads)
    def _():
        cols = pl.ds(pl.multiple_of(step * size, size), size)
        first_ref[...] = dot(mixed_ref[...], w_ref[...], NT) + dot(thr_mixer_ref[...], down_mixer_ref[...])
        for q, at in enumerate(lanes):
            second_ref[:, at] = (dot(conv_ref[:, at].astype(BF16), table_d_ref[q])
                                 + dot(inner_ref[:, :half], lift_ref[:half, at]))
        softrate = soft_ref[...]

        def group(lap, carries):
            k = groups - 1 - lap
            after = []
            for s in range(seqs):
                at = rows_of(s, k)
                restart = restart_ref[at, :] > 0.5
                grown = jnp.exp(-8.0 * softrate / (1.0 + jnp.exp(-second_ref[at, :])))
                decays = jnp.where(restart, 0.0, grown)
                state = local_ref[at, :] + cum_ref[at, :] * carried_ref[s : s + 1, :]
                value, slope = gelu_both(pre_ref[at, :])
                merged = first_ref[at, :]
                branch_grad_ref[at, :] = (merged * state * slope).astype(BF16)
                grads = merged * value
                carry_a, carry_b = carries[s]
                a, b = scan_group(decays, decays * grads, carry_a, carry_b, rows_advanced)
                last = lax.broadcasted_iota(jnp.int32, a.shape, 0) == GROUP - 1
                span_ref[step, at, :] = jnp.where(last, carry_a, pltpu.roll(a, GROUP - 1, 0))
                total_ref[step, at, :] = grads + jnp.where(last, carry_b, pltpu.roll(b, GROUP - 1, 0))
                after.append((a[:1], b[:1]))
            return tuple(after)

        start = (jnp.ones((1, size), F32), jnp.zeros((1, size), F32))
        ends = lax.fori_loop(0, groups, group, (start,) * seqs, unroll=UNROLL)
        for s in range(seqs):
            ends_ref[s : s + 1, cols] = ends[s][0]
            ends_ref[seqs + s : seqs + s + 1, cols] = ends[s][1]
        one_ref[:, :ranks] += dot(branch_grad_ref[...], lift_branch_ref[...], NT)

    @pl.when(step == heads - 1)
    def _():
        for one in exchange:
            one.start()

    @pl.when(step == heads)
    def _():
        for one in exchange:
            one.wait_recv()
        incoming = jnp.zeros(incoming_ref.shape, F32)
        for g in (3, 2, 1):
            longer = all_ends_ref[g, :seqs, :] * incoming + all_ends_ref[g, seqs : 2 * seqs, :]
            incoming = jnp.where(group < g, longer, incoming)
        incoming_ref[...] = incoming

    @pl.when((step >= heads) & (step < 2 * heads))
    def _():
        head = step - heads
        cols = pl.ds(pl.multiple_of(head * size, size), size)
        for q, at in enumerate(lanes):
            rounded = conv_ref[:, at].astype(BF16)
            first_ref[:, at] = dot(rounded, table_d_ref[q]) + dot(inner_ref[:, :half], lift_ref[:half, at])
            second_ref[:, at] = dot(rounded, table_a_ref[q]) + dot(inner_ref[:, half:], lift_ref[half:, at])
        softrate = soft_ref[...]
        rate = -8.0 * softrate

        def group(k, carries):
            after = []
            for s in range(seqs):
                at = rows_of(s, k)
                conv = conv_ref[at, :]
                restart = restart_ref[at, :] > 0.5
                decay_gate, admit, grown, scale = gate_steps(
                    first_ref[at, :], second_ref[at, :], softrate, restart)
                state = local_ref[at, :] + cum_ref[at, :] * carried_ref[s : s + 1, :]
                place = lax.broadcasted_iota(jnp.int32, state.shape, 0)
                before = jnp.where(place >= 1, pltpu.roll(state, 1, 0), carries[s])
                grads = total_ref[head, at, :] + span_ref[head, at, :] * incoming_ref[s : s + 1, cols]
                driven = grads * jnp.where(restart, 1.0, scale)
                admitted = conv * admit
                grad_log = jnp.where(restart, 0.0, grads * (before * grown - admitted * grown * grown / scale))
                low_d_ref[at, :] = (rate * grad_log * decay_gate * (1.0 - decay_gate)).astype(BF16)
                low_a_ref[at, :] = (driven * admitted * (1.0 - admit)).astype(BF16)
                total_ref[head, at, :] = driven * admit
                after.append(state[GROUP - 1 :])
            return tuple(after)

        lax.fori_loop(0, groups, group, tuple(carried_ref[s : s + 1, :] for s in range(seqs)), unroll=UNROLL)
        low_d, low_a = low_d_ref[...], low_a_ref[...]
        for q, at in enumerate(lanes):
            total_ref[head, :, at] += dot(low_d[:, at], table_d_ref[q], NT) + dot(low_a[:, at], table_a_ref[q], NT)
        gates_ref[:, :half] += dot(low_d, lift_ref[:half, :], NT)
        gates_ref[:, half:] += dot(low_a, lift_ref[half:, :], NT)
        lift_grad_ref[:half, :] = dot(inner_ref[:, :half], low_d, TN)
        lift_grad_ref[half:, :] = dot(inner_ref[:, half:], low_a, TN)

    @pl.when(step == 2 * heads)
    def _():
        through_gates_ref[...] = (gates_ref[...] * sequence_mask(rows, 2 * half, seqs)).astype(BF16)
        tops = []
        for s in range(seqs):
            top = slice(s * stretch, s * stretch + GROUP)
            direct = jnp.concatenate([total_ref[h, top, :] for h in range(heads)], 1)
            tops.append((direct + dot(through_gates_ref[top, :], down_gates_ref[...]))[:8])
        halo_ref[...] = jnp.concatenate(tops, 0).astype(BF16).astype(F32)
        downward.start()
        downward.wait_recv()

    @pl.when(step >= 2 * heads)
    def _():
        head = step - 2 * heads
        cols = pl.ds(pl.multiple_of(head * size, size), size)
        grads = total_ref[head] + dot(through_gates_ref[...], down_gates_ref[:, cols])
        for s in range(seqs):
            longer_ref[s, :stretch, :] = grads[s * stretch : (s + 1) * stretch, :]
            longer_ref[s, stretch:, :] = below_ref[s * 8 : (s + 1) * 8, cols]

        def group(k, _):
            for s in range(seqs):
                at = rows_of(s, k)
                ahead = longer_ref[s, pl.ds(pl.multiple_of(k * GROUP, GROUP), GROUP + 8), :]
                total = taps_ref[0:1, :] * agree_ref[at, 0:1] * ahead[:GROUP]
                for j in range(1, taps_ref.shape[0]):
                    moved = pltpu.roll(ahead, GROUP + 8 - j, 0)[:GROUP]
                    total += taps_ref[j : j + 1, :] * agree_ref[at, j : j + 1] * moved
                fed_grad_ref[at, :] = total.astype(BF16)
            return 0

        lax.fori_loop(0, groups, group, 0, unroll=UNROLL)
        one_ref[:, ranks:] += dot(fed_grad_ref[...], lift_input_ref[...], NT)

    @pl.when(step == 3 * heads - 1)
    def _():
        through_one_ref[...] = (one_ref[...] * sequence_mask(rows, 2 * ranks, seqs)).astype(BF16)
        for one in exchange:
            one.wait_send()
        downward.wait_send()
        total_early.clear()
        for chain in chains:
            chain.end()


def mixer_back(seqs, mixed, w_mixer, lift_mixer, down_mixer, conv, inner, lift, table_d, table_a, softrate, restart,
               cum, local, carried, pre, lift_branch, lift_input, down_gates, taps, agree, early, wide):
    rows, width = conv.shape
    count, early_cols = lax.axis_size("replica"), width // 4
    heads, each = table_d.shape[:2]
    per = 2 if heads % 2 == 0 else 1
    heads, size = heads // per, per * each
    first = lambda i: jnp.minimum(i, heads - 1)
    second = lambda i: jnp.clip(i - heads, 0, heads - 1)
    third = lambda i: jnp.maximum(i - 2 * heads, 0)
    either = lambda i: jnp.minimum(i, 2 * heads - 1) % heads
    full = lambda array: pl.BlockSpec(array.shape, lambda i: (0, 0), pipeline_mode=pl.Buffered(1))
    cols = lambda array, at: pl.BlockSpec((array.shape[0], size), lambda i: (0, at(i)))
    table = pl.BlockSpec((per, each, each), lambda i: (either(i), 0, 0))
    middle = inner.shape[1]
    tile = lambda at: pl.BlockSpec((rows, size), lambda i: (0, at(i)))
    whole = lambda count: pl.BlockSpec((rows, count), lambda i: (0, 0))
    return pl.pallas_call(
        functools.partial(mixer_back_kernel, seqs, heads),
        grid=(3 * heads,),
        out_shape=[
            jax.ShapeDtypeStruct((rows, width), BF16),
            jax.ShapeDtypeStruct((rows, 2 * lift_branch.shape[0]), BF16),
            jax.ShapeDtypeStruct((rows, middle), BF16),
            jax.ShapeDtypeStruct(lift.shape, F32),
            jax.ShapeDtypeStruct((rows, width), BF16),
            jax.ShapeDtypeStruct((rows, lift_mixer.shape[0]), BF16),
            jax.ShapeDtypeStruct((count, early.shape[0], early_cols), BF16),
            jax.ShapeDtypeStruct((count,) + wide.shape, BF16),
        ],
        in_specs=[
            full(mixed), pl.BlockSpec((size, width), lambda i: (first(i), 0)), full(lift_mixer), cols(down_mixer, first),
            cols(conv, either), full(inner), cols(lift, either), table, table, cols(softrate, either), full(restart),
            cols(cum, either), cols(local, either), cols(carried, either), cols(pre, first), cols(lift_branch, first),
            cols(lift_input, third), full(down_gates), cols(taps, third), full(agree), ANYWHERE, ANYWHERE,
        ],
        out_specs=[tile(first), whole(2 * lift_branch.shape[0]), whole(middle),
                   pl.BlockSpec((lift.shape[0], size), lambda i: (0, second(i))), tile(third),
                   whole(lift_mixer.shape[0]), ANYWHERE, ANYWHERE],
        scratch_shapes=[
            pltpu.VMEM((heads, rows, size), F32), pltpu.VMEM((heads, rows, size), F32), pltpu.VMEM((8, width), F32),
            pltpu.VMEM((4, 8, width), F32), pltpu.VMEM((seqs, width), F32), pltpu.VMEM((8 * seqs, width), F32),
            pltpu.VMEM((8 * seqs, width), F32), pltpu.VMEM((rows, 2 * lift_branch.shape[0]), F32),
            pltpu.VMEM((rows, middle), F32), pltpu.VMEM((rows, size), F32), pltpu.VMEM((rows, size), F32),
            pltpu.VMEM((rows, size), BF16), pltpu.VMEM((rows, size), BF16),
            pltpu.VMEM((seqs, rows // seqs + 8, size), F32), pltpu.SemaphoreType.DMA((4,)),
            pltpu.SemaphoreType.DMA((4,))]
        + GroupSum.shapes(early.shape[0], early_cols) + ReplicaChain.shapes(count) + ReplicaChain.shapes(count),
        compiler_params=pltpu.CompilerParams(
            vmem_limit_bytes=VMEM, collective_id=3, has_side_effects=True),
        cost_estimate=pl.CostEstimate(
            flops=2 * rows * width * width + 20 * rows * width * size + 200 * rows * width,
            bytes_accessed=40 * rows * width + 2 * width * width, transcendentals=12 * rows * width),
    )(mixed, w_mixer, lift_mixer, down_mixer, conv, inner, lift, table_d, table_a, softrate, restart, cum, local,
      carried, pre, lift_branch, lift_input, down_gates, taps, agree, early, wide)


def resident(array):
    return pl.BlockSpec(array.shape, lambda i: (0, 0), pipeline_mode=pl.Buffered(1))


def tile_of(count, tile):
    return tile if count % 128 == 0 and count > tile else count


def grad_hidden_kernel(seqs, gather, steps, *refs):
    if gather:
        cot_ref, wd_ref, lift_out_ref, do_ref, block_ref = refs[:5]
        out_ref, through_ref, all_ref, staged_ref, send, recv, local = refs[-7:]
    else:
        cot_ref, wd_ref, lift_out_ref, do_ref, out_ref, through_ref = refs
    ranks = do_ref.shape[0] // seqs
    step = pl.program_id(0)

    if gather:
        group, replica = lax.axis_index("group"), lax.axis_index("replica")
        beside, above = group + 1 - 2 * (group % 2), (group + 2) % 4
        at_beside, at_above = (beside, replica), (above, replica)
        rows = block_ref.shape[0]
        half = rows // 2

        def place(owner, part):
            return all_ref.at[pl.ds(pl.multiple_of(owner * rows + part * half, half), half), :]

        def own(part):
            return block_ref.at[pl.ds(part * half, half), :]

        def copy(src, dst, slot, partner):
            return pltpu.make_async_remote_copy(
                src_ref=src, dst_ref=dst, send_sem=send.at[slot], recv_sem=recv.at[slot], device_id=partner,
                device_id_type=pl.DeviceIdType.MESH)

        firsts = [copy(own(1), place(group, 1), 0, at_beside), copy(own(0), place(group, 0), 1, at_above),
                  copy(own(0), place(group, 0), 2, at_beside), copy(own(1), place(group, 1), 3, at_above)]
        seconds = [copy(place(beside, 1), place(beside, 1), 4, at_above),
                   copy(place(above, 0), place(above, 0), 5, at_beside)]
        stage = pltpu.make_async_copy(block_ref, staged_ref, local.at[0])
        keep = pltpu.make_async_copy(
            staged_ref, all_ref.at[pl.ds(pl.multiple_of(group * rows, rows), rows), :], local.at[1])

        @pl.when(step == 0)
        def _():
            barrier = pltpu.get_barrier_semaphore()
            for partner in (at_beside, at_above):
                pl.semaphore_signal(barrier, inc=1, device_id=partner, device_id_type=pl.DeviceIdType.MESH)
            pl.semaphore_wait(barrier, 2)
            for one in firsts[:2]:
                one.start()
            stage.start()

    @pl.when(step == 0)
    def _():
        for s in range(seqs):
            through_ref[s] = dot(cot_ref[s], lift_out_ref[s * ranks : (s + 1) * ranks, :], NT).astype(BF16)

    for s in range(seqs):
        out_ref[s] = (dot(cot_ref[s], wd_ref[...], NT)
                      + dot(through_ref[s], do_ref[s * ranks : (s + 1) * ranks, :])).astype(BF16)

    if gather:
        @pl.when(step == 0)
        def _():
            stage.wait()
            keep.start()
            for one in firsts[2:]:
                one.start()

        @pl.when(step == min(1, steps - 1))
        def _():
            for one, then in zip(firsts[:2], seconds):
                one.wait_recv()
                then.start()

        @pl.when(step == steps - 1)
        def _():
            for one in firsts[2:] + seconds:
                one.wait_recv()
            for one in firsts + seconds:
                one.wait_send()
            keep.wait()


def grad_hidden_call(cot, wd, lift_out, do, block, earlier):
    seqs, rows, width = cot.shape
    units, ranks = wd.shape[0], do.shape[0] // seqs
    tile = tile_of(units, 512)
    gather = lax.axis_size("group") == 4
    got = pl.pallas_call(
        functools.partial(grad_hidden_kernel, seqs, gather, pl.cdiv(units, tile)),
        grid=(pl.cdiv(units, tile),),
        out_shape=[jax.ShapeDtypeStruct((seqs, rows, units), BF16), jax.ShapeDtypeStruct((seqs, rows, ranks), BF16)]
        + [jax.ShapeDtypeStruct((rows, width), BF16)] * gather,
        in_specs=[pl.BlockSpec(cot.shape, lambda i: (0, 0, 0), pipeline_mode=pl.Buffered(1)),
                  pl.BlockSpec((tile, width), lambda i: (i, 0)), resident(lift_out),
                  pl.BlockSpec((seqs * ranks, tile), lambda i: (0, i))] + [ANYWHERE] * (gather + gather * len(earlier)),
        out_specs=[pl.BlockSpec((seqs, rows, tile), lambda i: (0, 0, i)),
                   pl.BlockSpec((seqs, rows, ranks), lambda i: (0, 0, 0))] + [ANYWHERE] * gather,
        scratch_shapes=[pltpu.VMEM(block.shape, BF16), pltpu.SemaphoreType.DMA((6,)), pltpu.SemaphoreType.DMA((6,)),
                        pltpu.SemaphoreType.DMA((2,))] if gather else [],
        compiler_params=pltpu.CompilerParams(
            vmem_limit_bytes=VMEM, **(dict(collective_id=1, has_side_effects=True) if gather else {})),
        cost_estimate=pl.CostEstimate(
            flops=2 * seqs * rows * width * units,
            bytes_accessed=2 * width * units + 2 * seqs * rows * (units + width), transcendentals=0),
    )(cot, wd, lift_out, do, *([block, *earlier] if gather else []))
    return got if gather else list(got) + [lax.all_gather(block, "group", axis=0, tiled=True)]


def feed_kernel(steps, tile, units, tok_ref, gh_ref, wg_ref, wu_ref, wg_rows_ref, wu_rows_ref, down_ref, lg_ref,
                lu_ref, through_out_ref, lg_full_ref, lu_full_ref, down_cols_ref, *refs):
    hidden_ref, back_ref, wide_ref, through_ref, inner_ref, gg_ref, gu_ref = refs[-7:]
    ranks = lg_ref.shape[0]
    step = pl.program_id(0)

    @pl.when(step == 0)
    def _():
        inner_ref[...] = dot(tok_ref[...], down_ref[...], NT).astype(BF16)

    @pl.when(step < steps)
    def _():
        tokens, inner = tok_ref[...], inner_ref[...]
        gate = dot(tokens, wg_ref[...]) + dot(inner[:, :ranks], lg_ref[...])
        upper = dot(tokens, wu_ref[...]) + dot(inner[:, ranks:], lu_ref[...])
        grad_hidden = gh_ref[...].astype(F32)
        value, slope = gelu_both(gate)
        hidden = (value * upper).astype(BF16)
        grad_gate = (grad_hidden * upper * slope).astype(BF16)
        grad_upper = (grad_hidden * value).astype(BF16)
        hidden_ref[...] = hidden
        cols = pl.ds(pl.multiple_of(step * tile, tile), tile) if steps > 1 else slice(0, tile)
        gg_ref[:, cols] = grad_gate
        gu_ref[:, cols] = grad_upper
        wide_ref[:ranks, :] = dot(inner[:, :ranks], grad_gate, TN).astype(BF16)
        wide_ref[ranks : 2 * ranks, :] = dot(inner[:, ranks:], grad_upper, TN).astype(BF16)
        wide_ref[2 * ranks :, :] = dot(through_out_ref[...], hidden, TN).astype(BF16)

    @pl.when(step == steps)
    def _():
        through_ref[:, :ranks] = dot(gg_ref[:, :units], lg_full_ref[...], NT).astype(BF16)
        through_ref[:, ranks:] = dot(gu_ref[:, :units], lu_full_ref[...], NT).astype(BF16)

    @pl.when(step >= steps)
    def _():
        back_ref[...] = (dot(gg_ref[:, :units], wg_rows_ref[...], NT) + dot(gu_ref[:, :units], wu_rows_ref[...], NT)
                         + dot(through_ref[...], down_cols_ref[...])).astype(BF16)


def feed_call(s, tok, gh, wg, wu, down, lg, lu, through_out):
    rows, width = tok.shape
    units, ranks = wg.shape[1], lg.shape[0]
    tile, span = tile_of(units, 512), tile_of(width, 512)
    steps, laps = pl.cdiv(units, tile), pl.cdiv(width, span)
    first = lambda i: jnp.minimum(i, steps - 1)
    second = lambda i: jnp.maximum(i - steps, 0)
    cols = pl.BlockSpec((width, tile), lambda i: (0, first(i)))
    across = pl.BlockSpec((span, units), lambda i: (second(i), 0))
    rank = pl.BlockSpec((ranks, tile), lambda i: (0, first(i)))
    out = pl.BlockSpec((rows, tile), lambda i: (0, first(i)))
    return pl.pallas_call(
        functools.partial(feed_kernel, steps, tile, units),
        grid=(steps + laps,),
        out_shape=[jax.ShapeDtypeStruct((rows, units), BF16), jax.ShapeDtypeStruct((rows, width), BF16),
                   jax.ShapeDtypeStruct((3 * ranks, units), BF16), jax.ShapeDtypeStruct((rows, 2 * ranks), BF16)],
        in_specs=[resident(tok), pl.BlockSpec((None, rows, tile), lambda i: (s, 0, first(i))), cols, cols, across,
                  across, resident(down), rank, rank, pl.BlockSpec((None, rows, ranks), lambda i: (s, 0, 0)),
                  resident(lg), resident(lu), pl.BlockSpec((2 * ranks, span), lambda i: (0, second(i)))],
        out_specs=[out, pl.BlockSpec((rows, span), lambda i: (0, second(i))),
                   pl.BlockSpec((3 * ranks, tile), lambda i: (0, first(i))),
                   pl.BlockSpec((rows, 2 * ranks), lambda i: (0, 0))],
        scratch_shapes=[pltpu.VMEM((rows, 2 * ranks), BF16), pltpu.VMEM((rows, steps * tile), BF16),
                        pltpu.VMEM((rows, steps * tile), BF16)],
        compiler_params=pltpu.CompilerParams(vmem_limit_bytes=VMEM),
        cost_estimate=pl.CostEstimate(
            flops=8 * rows * width * units, bytes_accessed=8 * width * units + 6 * rows * units,
            transcendentals=rows * units),
    )(tok, gh, wg, wu, wg, wu, down, lg, lu, through_out, lg, lu, down)


def outward_kernel(seqs, reduce, steps, *refs):
    hiddens, tokens, throughs, (cot_ref, resid_ref), refs = (
        refs[:seqs], refs[seqs : 2 * seqs], refs[2 * seqs : 3 * seqs], refs[3 * seqs : 3 * seqs + 2],
        refs[3 * seqs + 2 :])
    if reduce:
        wd_ref, do_ref, lift_out_ref, back_ref, out_ref, inner_ref, early_ref, sum_ref = refs[:8]
        first_a, first_b, second_a, second_b, pass_a, pass_b, own_ref, send, recv, local = refs[8:]
    else:
        wd_ref, do_ref, lift_out_ref, out_ref, inner_ref, early_ref = refs
    ranks = do_ref.shape[0] // seqs
    step = pl.program_id(0)

    if reduce:
        group, replica = lax.axis_index("group"), lax.axis_index("replica")
        beside, above, across = group + 1 - 2 * (group % 2), (group + 2) % 4, 3 - group
        at_beside, at_above = (beside, replica), (above, replica)
        rows, width = own_ref.shape
        half = width // 2

        def part(owner, side):
            return back_ref.at[pl.ds(pl.multiple_of(owner * rows, rows), rows), pl.ds(side * half, half)]

        def copy(src, dst, slot, partner):
            return pltpu.make_async_remote_copy(
                src_ref=src, dst_ref=dst, send_sem=send.at[slot], recv_sem=recv.at[slot], device_id=partner,
                device_id_type=pl.DeviceIdType.MESH)

        firsts = [copy(part(across, 0), first_a.at[1], 0, at_beside), copy(part(across, 1), first_b.at[1], 1, at_above),
                  copy(part(beside, 0), first_a.at[0], 2, at_beside), copy(part(above, 1), first_b.at[0], 3, at_above)]
        seconds = [copy(pass_a, second_a, 4, at_above), copy(pass_b, second_b, 5, at_beside)]
        loads = [pltpu.make_async_copy(part(above, 0), pass_a, local.at[0]),
                 pltpu.make_async_copy(part(beside, 1), pass_b, local.at[1]),
                 pltpu.make_async_copy(
                     back_ref.at[pl.ds(pl.multiple_of(group * rows, rows), rows), :], own_ref, local.at[2])]

        @pl.when(step == 0)
        def _():
            barrier = pltpu.get_barrier_semaphore()
            for partner in (at_beside, at_above):
                pl.semaphore_signal(barrier, inc=1, device_id=partner, device_id_type=pl.DeviceIdType.MESH)
            pl.semaphore_wait(barrier, 2)
            for one in firsts:
                one.start()
            for one in loads:
                one.start()

    @pl.when(step == 0)
    def _():
        for s, hidden_ref in enumerate(hiddens):
            inner_ref[s] = dot(hidden_ref[...], do_ref[s * ranks : (s + 1) * ranks, :], NT).astype(BF16)

    for s, hidden_ref in enumerate(hiddens):
        out_ref[s] = (dot(hidden_ref[...], wd_ref[...])
                      + dot(inner_ref[s], lift_out_ref[s * ranks : (s + 1) * ranks, :])).astype(BF16)
        own = resid_ref.shape[0] // seqs
        mine = pl.ds(pl.multiple_of(lax.axis_index("group") * own, own), own)
        out_ref[s, mine, :] = (out_ref[s, mine, :].astype(F32) + resid_ref[s * own : (s + 1) * own, :]).astype(BF16)
        both = dot(throughs[s][...], tokens[s][...], TN).astype(BF16)
        for kind, rows_of in enumerate((both[:ranks], both[ranks:], dot(inner_ref[s], cot_ref[s], TN).astype(BF16))):
            row = (kind * seqs + s) * ranks
            early_ref[row : row + ranks, :] = rows_of

    if reduce:
        @pl.when(step == max(steps - 2, 0))
        def _():
            for one in loads:
                one.wait()
            for one in firsts:
                one.wait_recv()
            pass_a[...] = (pass_a[...].astype(F32) + first_a[1].astype(F32)).astype(BF16)
            pass_b[...] = (pass_b[...].astype(F32) + first_b[1].astype(F32)).astype(BF16)
            for one in seconds:
                one.start()

        @pl.when(step == steps - 1)
        def _():
            for one in seconds:
                one.wait_recv()
            sum_ref[:, :half] = (own_ref[:, :half].astype(F32) + first_a[0].astype(F32)
                                 + second_a[...].astype(F32)).astype(BF16)
            sum_ref[:, half:] = (own_ref[:, half:].astype(F32) + first_b[0].astype(F32)
                                 + second_b[...].astype(F32)).astype(BF16)
            for one in firsts + seconds:
                one.wait_send()


def outward_call(hiddens, tokens, throughs, cot, resid, wd, do, lift_out, back):
    rows, units = hiddens[0].shape
    seqs = len(hiddens)
    width, ranks = wd.shape[1], do.shape[0] // seqs
    tile = tile_of(width, 512)
    steps = pl.cdiv(width, tile)
    group = lax.axis_size("group")
    reduce = group == 4 and width % 256 == 0
    own, half = rows // group, width // 2
    scratch = [pltpu.VMEM((2, own, half), BF16)] * 2 + [pltpu.VMEM((own, half), BF16)] * 4 + [
        pltpu.VMEM((own, width), BF16), pltpu.SemaphoreType.DMA((6,)), pltpu.SemaphoreType.DMA((6,)),
        pltpu.SemaphoreType.DMA((3,))]
    got = pl.pallas_call(
        functools.partial(outward_kernel, seqs, reduce, steps),
        grid=(steps,),
        out_shape=[jax.ShapeDtypeStruct((seqs, rows, width), BF16), jax.ShapeDtypeStruct((seqs, rows, ranks), BF16),
                   jax.ShapeDtypeStruct((3 * seqs * ranks, width), BF16)]
        + [jax.ShapeDtypeStruct((own, width), BF16)] * reduce,
        in_specs=[resident(hidden) for hidden in hiddens] + [pl.BlockSpec((rows, tile), lambda i: (0, i))] * seqs
        + [resident(through) for through in throughs] + [pl.BlockSpec((seqs, rows, tile), lambda i: (0, 0, i))]
        + [pl.BlockSpec((resid.shape[0], tile), lambda i: (0, i))]
        + [pl.BlockSpec((units, tile), lambda i: (0, i)), resident(do),
           pl.BlockSpec((seqs * ranks, tile), lambda i: (0, i))] + [ANYWHERE] * reduce,
        out_specs=[pl.BlockSpec((seqs, rows, tile), lambda i: (0, 0, i)),
                   pl.BlockSpec((seqs, rows, ranks), lambda i: (0, 0, 0)),
                   pl.BlockSpec((3 * seqs * ranks, tile), lambda i: (0, i))]
        + [pl.BlockSpec((own, width), lambda i: (0, 0))] * reduce,
        scratch_shapes=scratch if reduce else [],
        compiler_params=pltpu.CompilerParams(
            vmem_limit_bytes=VMEM, **(dict(collective_id=2, has_side_effects=True) if reduce else {})),
        cost_estimate=pl.CostEstimate(
            flops=2 * seqs * rows * width * units,
            bytes_accessed=2 * width * units + 2 * seqs * rows * (units + width), transcendentals=0),
    )(*hiddens, *tokens, *throughs, cot, resid, wd, do, lift_out, *([back] if reduce else []))
    return got if reduce else list(got) + [lax.psum_scatter(back, "group", scatter_dimension=0, tiled=True)]


def pick_kernel(counts, ids_ref, *refs):
    tables, (stack_ref, wide_ref) = refs[: sum(counts)], refs[sum(counts) :]
    for i, table in enumerate(tables):
        if i < counts[0]:
            stack_ref[i, 0] = table[0]
        else:
            wide_ref[i - counts[0], 0] = table[0]


def pick(ids, narrow, wide):
    seqs, ranks = ids.shape[0], narrow[0].shape[1]
    counts = (len(narrow), len(wide))
    widths = (narrow[0].shape[2], wide[0].shape[2])
    tables = [pl.BlockSpec((1, ranks, table.shape[2]), lambda s, ids: (ids[s], 0, 0)) for table in narrow + wide]
    picked = pl.pallas_call(
        functools.partial(pick_kernel, counts),
        out_shape=[jax.ShapeDtypeStruct((count, seqs, ranks, width), BF16) for count, width in zip(counts, widths)],
        grid_spec=pltpu.PrefetchScalarGridSpec(
            num_scalar_prefetch=1,
            grid=(seqs,),
            in_specs=tables,
            out_specs=[pl.BlockSpec((count, 1, ranks, width), lambda s, ids: (0, s, 0, 0))
                       for count, width in zip(counts, widths)],
        ),
    )(ids, *narrow, *wide)
    return [part.reshape(-1, part.shape[-1]) for part in picked]


def gather_kernel(units, counts, seqs, *refs):
    refs = list(refs)
    take = lambda count: [refs.pop(0) for _ in range(count)]
    weights, (passed, values, gain_ref, ids_ref), tables = take(3), take(4), take(sum(counts))
    wholes, (handed_out, normed_ref, own_ref) = take(4), take(3)
    staged, (handed, values_ref), loaded, (send, recv, local, table_sems) = take(4), take(2), take(sum(counts)), refs
    weights = weights + [staged[3]]
    group, replica = lax.axis_index("group"), lax.axis_index("replica")
    beside, above, across = group + 1 - 2 * (group % 2), (group + 2) % 4, 3 - group
    core, level = replica % 2, (replica // 2) % 2
    at_beside, at_above = (beside, replica), (above, replica)
    at_core, at_level = (group, replica + 1 - 2 * core), (group, replica + 2 - 4 * level)
    partners = (at_beside, at_above, at_core, at_level)
    mine, other = 2 * core + level, 2 * core + 1 - level

    barrier = pltpu.get_barrier_semaphore()
    for partner in partners:
        pl.semaphore_signal(barrier, inc=1, device_id=partner, device_id_type=pl.DeviceIdType.MESH)
    pl.semaphore_wait(barrier, 4)

    kept = [pltpu.make_async_copy(weight, stage, local.at[m])
            for m, (weight, stage) in enumerate(zip(weights[:3], staged))] + [None]

    def keep(m):
        whole = wholes[m]
        rows, cols = weights[m].shape
        if m == 2:
            into = whole.at[pl.ds(pl.multiple_of(group * rows, rows), rows), :]
        else:
            into = whole.at[:, pl.ds(pl.multiple_of(group * cols, cols), cols)]
        if kept[m] is not None:
            kept[m].wait()
        kept[m] = pltpu.make_async_copy(staged[m], into, local.at[m])
        kept[m].start()

    def own(m, part, quarter):
        weight = weights[m]
        size = wholes[m].shape[0] // 4
        step = size // units
        if m < 2:
            return weight.at[pl.ds(pl.multiple_of(quarter * size + part * step, step), step), :]
        return weight.at[pl.ds(part * step, step), pl.ds(pl.multiple_of(quarter * size, size), size)]

    def piece(m, part, shard, quarter):
        whole = wholes[m]
        size = whole.shape[0] // 4
        step = size // units
        down, along = (quarter, shard) if m < 2 else (shard, quarter)
        return whole.at[pl.ds(pl.multiple_of(down * size + part * step, step), step),
                        pl.ds(pl.multiple_of(along * size, size), size)]

    def copy(src, dst, k, slot, partner):
        made = pltpu.make_async_remote_copy(
            src_ref=src, dst_ref=dst, send_sem=send.at[k, slot], recv_sem=recv.at[k, slot], device_id=partner,
            device_id_type=pl.DeviceIdType.MESH)
        made.start()
        return made

    def forward(m, part, shard, quarter, k, slot, partner):
        where = piece(m, part, shard, quarter)
        return copy(where, where, k, slot, partner)

    ranks, cols = weights[3].shape
    last = 3 * units

    def stack_piece(first, count, shard):
        return wholes[3].at[pl.ds(first, count), pl.ds(pl.multiple_of(shard * cols, cols), cols)]

    steps = [(m, part) for m in range(3) for part in range(units)]
    made = {}

    def begin(k):
        m, part = steps[k]
        made[k, 0] = copy(own(m, part, mine), piece(m, part, group, mine), k, 0, at_above)
        made[k, 2] = copy(own(m, part, mine), piece(m, part, group, mine), k, 2, at_beside)
        made[k, 1] = copy(own(m, part, other), piece(m, part, group, other), k, 1, at_above)

    begin(0)
    begin(1)
    onward = pltpu.make_async_copy(passed, handed, local.at[4])
    fetch = [pltpu.make_async_copy(values, values_ref, local.at[5])] + [
        pltpu.make_async_copy(table, place, table_sems.at[i]) for i, (table, place) in enumerate(zip(tables, loaded))]
    for one in kept[:3] + [onward] + fetch:
        one.start()
    for m in range(3):
        keep(m)

    def pick_sets():
        for one in fetch[1:]:
            one.wait()
        depth = loaded[0].shape[1]
        for i, table in enumerate(loaded):
            out, first = (staged[3], i) if i < counts[0] else (own_ref, i - counts[0])
            for s in range(seqs):
                row = (first * seqs + s) * depth
                out[row : row + depth, :] = table[ids_ref[s]]
        keep(3)

    def norm_values():
        fetch[0].wait()
        count = values_ref.shape[0]
        step = 64 if count % 64 == 0 else count

        def some_rows(i, _):
            at = pl.ds(pl.multiple_of(i * step, step), step)
            normed_ref[at, :] = norm_rows(values_ref[at, :].astype(F32), gain_ref[...])[0].astype(BF16)
            return 0

        lax.fori_loop(0, count // step, some_rows, 0)

    for t in range(len(steps) + 2):
        if t < len(steps):
            m, part = steps[t]
            made[t, 0].wait_recv()
            made[t, 4] = forward(m, part, above, mine, t, 4, at_beside)
            made[t, 6] = forward(m, part, above, mine, t, 6, at_core)
            made[t, 2].wait_recv()
            made[t, 3] = forward(m, part, beside, mine, t, 3, at_level)
            made[t, 8] = forward(m, part, beside, mine, t, 8, at_core)
            if t + 2 < len(steps):
                begin(t + 2)
            if t == len(steps) // 3:
                pick_sets()
            if t == len(steps) // 2:
                norm_values()
            if t + 3 == len(steps):
                stack_beside = copy(weights[3], stack_piece(0, ranks, group), last, 0, at_beside)
                stack_above = copy(weights[3], stack_piece(0, ranks, group), last, 1, at_above)
            made[t, 1].wait_recv()
            made[t, 7] = forward(m, part, above, other, t, 7, at_core)
        if 1 <= t <= len(steps):
            m, part = steps[t - 1]
            made[t - 1, 4].wait_recv()
            made[t - 1, 5] = forward(m, part, across, mine, t - 1, 5, at_level)
            made[t - 1, 10] = forward(m, part, across, mine, t - 1, 10, at_core)
            made[t - 1, 3].wait_recv()
            made[t - 1, 9] = forward(m, part, beside, other, t - 1, 9, at_core)
        if 2 <= t:
            m, part = steps[t - 2]
            made[t - 2, 5].wait_recv()
            made[t - 2, 11] = forward(m, part, across, other, t - 2, 11, at_core)
        if t == len(steps):
            stack_beside.wait_recv()
            stack_above.wait_recv()
            half = ranks // 2
            lower = stack_piece(0, half, above)
            upper = stack_piece(half, half, beside)
            stack_lower = copy(lower, lower, last, 2, at_beside)
            stack_upper = copy(upper, upper, last, 3, at_above)
    onward.wait()
    onward = pltpu.make_async_copy(handed, handed_out, local.at[4])
    onward.start()
    for k in range(len(steps)):
        for slot in range(6, 12):
            made[k, slot].wait_recv()
    for k in range(len(steps)):
        for slot in range(12):
            made[k, slot].wait_send()
    for one in (stack_lower, stack_upper):
        one.wait_recv()
    for one in (stack_beside, stack_above, stack_lower, stack_upper):
        one.wait_send()
    for one in kept + [onward]:
        one.wait()


def gather_weights(w_branch, w_input, w_mixer, passed, values, gain, ids, narrow, wide):
    width, (rows, _), seqs = w_branch.shape[0], values.shape, ids.shape[0]
    if lax.axis_size("group") != 4 or lax.axis_size("replica") % 4 != 0:
        stack, own = pick(ids, narrow, wide)
        return (lax.all_gather(w_branch, "group", axis=1, tiled=True),
                lax.all_gather(w_input, "group", axis=1, tiled=True),
                lax.all_gather(w_mixer, "group", axis=0, tiled=True),
                lax.all_gather(stack, "group", axis=1, tiled=True), passed,
                norm_rows(values.astype(F32), gain)[0].astype(BF16), own)
    units = 4
    counts = (len(narrow), len(wide))
    ranks = narrow[0].shape[1]
    vmem = pl.BlockSpec(memory_space=pltpu.VMEM)
    stack = jax.ShapeDtypeStruct((counts[0] * seqs * ranks, narrow[0].shape[2]), BF16)
    dma = pltpu.SemaphoreType.DMA
    return pl.pallas_call(
        functools.partial(gather_kernel, units, counts, seqs),
        out_shape=[jax.ShapeDtypeStruct((width, width), BF16)] * 3
        + [jax.ShapeDtypeStruct((stack.shape[0], width), BF16), jax.ShapeDtypeStruct(passed.shape, passed.dtype),
           jax.ShapeDtypeStruct(values.shape, BF16),
           jax.ShapeDtypeStruct((counts[1] * seqs * ranks, wide[0].shape[2]), BF16)],
        in_specs=[ANYWHERE] * 5 + [vmem, pl.BlockSpec(memory_space=pltpu.SMEM)] + [ANYWHERE] * sum(counts),
        out_specs=[ANYWHERE] * 5 + [vmem] * 2,
        scratch_shapes=[pltpu.VMEM(part.shape, BF16)
                        for part in (w_branch, w_input, w_mixer, stack, passed, values, *narrow, *wide)]
        + [dma((3 * units + 1, 12)), dma((3 * units + 1, 12)), dma((6,)), dma((sum(counts),))],
        compiler_params=pltpu.CompilerParams(collective_id=0, has_side_effects=True, vmem_limit_bytes=VMEM),
        cost_estimate=pl.CostEstimate(flops=0, bytes_accessed=400 * 2**20, transcendentals=0),
    )(w_branch, w_input, w_mixer, passed, values, gain, ids, *narrow, *wide)


def ordered_kernel(*refs):
    del refs


def ordered(value, *earlier):
    return pl.pallas_call(
        ordered_kernel,
        out_shape=jax.ShapeDtypeStruct(value.shape, value.dtype),
        in_specs=[ANYWHERE] * (1 + len(earlier)),
        out_specs=ANYWHERE,
        input_output_aliases={0: 0},
    )(value, *earlier)


def row_tiles(rows, width, count):
    step = min(rows, 128)
    return (rows // step,), [pl.BlockSpec((step, width), lambda i: (i, 0))] * count


def by_groups(count, action):
    size = GROUP if count % GROUP == 0 else count

    def one(k, _):
        action(pl.ds(pl.multiple_of(k * size, size), size))
        return 0

    lax.fori_loop(0, count // size, one, 0, unroll=2 if count % (2 * size) == 0 else 1)


def resid_grad_kernel(per, resid_ref, cot_ref, gain_ref, *refs):
    pieces, (full_ref, low_ref) = refs[:-2], refs[-2:]

    def some_rows(at):
        values = resid_ref[at, :]
        rate = lax.rsqrt(jnp.mean(values * values, axis=-1, keepdims=True) + EPS)
        grads = pieces[0][at, :]
        for s, piece in enumerate(pieces[1:], 1):
            grads = jnp.where(pl.program_id(0) >= s * per, piece[at, :], grads)
        grads = cot_ref[at, :].astype(F32) + norm_back(values, gain_ref[...], rate, grads.astype(F32))
        full_ref[at, :] = grads
        low_ref[at, :] = grads.astype(BF16)

    by_groups(resid_ref.shape[0], some_rows)


def resid_grad(resid, cot, gain, pieces):
    rows, width = resid.shape
    step = min(pieces[0].shape[0], 128)
    per = pieces[0].shape[0] // step
    tile = pl.BlockSpec((step, width), lambda i: (i, 0))
    return pl.pallas_call(
        functools.partial(resid_grad_kernel, per),
        grid=(rows // step,),
        out_shape=[jax.ShapeDtypeStruct((rows, width), F32), jax.ShapeDtypeStruct((rows, width), BF16)],
        in_specs=[tile, tile, pl.BlockSpec((1, width), lambda i: (0, 0))] + [
            pl.BlockSpec((step, width), lambda i, s=s: (jnp.clip(i - s * per, 0, per - 1), 0))
            for s in range(len(pieces))],
        out_specs=[tile, tile],
        compiler_params=pltpu.CompilerParams(vmem_limit_bytes=VMEM),
        cost_estimate=pl.CostEstimate(
            flops=20 * rows * width, bytes_accessed=14 * rows * width, transcendentals=rows),
    )(resid, cot, gain, *pieces)


def finish_kernel(grad_resid_ref, inputs_ref, gain_ref, grads_ref, out_ref):
    def some_rows(at):
        values = inputs_ref[at, :].astype(F32)
        rate = lax.rsqrt(jnp.mean(values * values, axis=-1, keepdims=True) + EPS)
        out_ref[at, :] = grad_resid_ref[at, :] + norm_back(values, gain_ref[...], rate, grads_ref[at, :])

    by_groups(inputs_ref.shape[0], some_rows)


def finish(grad_resid, inputs, gain, grads):
    rows, width = inputs.shape
    step = min(rows, 128)
    tile = pl.BlockSpec((step, width), lambda i: (i, 0))
    return pl.pallas_call(
        finish_kernel,
        grid=(rows // step,),
        out_shape=jax.ShapeDtypeStruct((rows, width), F32),
        in_specs=[tile, tile, pl.BlockSpec((1, width), lambda i: (0, 0)), tile],
        out_specs=tile,
        compiler_params=pltpu.CompilerParams(vmem_limit_bytes=VMEM),
        cost_estimate=pl.CostEstimate(
            flops=21 * rows * width, bytes_accessed=14 * rows * width, transcendentals=rows),
    )(grad_resid, inputs, gain, grads)


def tail_kernel(
    steps, branch_grad_ref, fed_grad_ref, w_branch_ref, w_input_ref, through_ref, down_ref, partial_ref,
    out_ref, got_ref, *scratch,
):
    step = pl.program_id(0)
    levels = got_ref.shape[0] // 2
    group, replica = lax.axis_index("group"), lax.axis_index("replica")
    ranks = got_ref.shape[1]
    half = ranks // 2
    total = GroupSum(lambda owner, side: partial_ref.at[owner, pl.ds(side * half, half), :], scratch[:10])
    chain = ReplicaChain(scratch[6], got_ref, scratch[10:])

    @pl.when(step == 0)
    def _():
        greet_all(levels, [(group + 1 - 2 * (group % 2), replica), ((group + 2) % 4, replica)])
        total.begin()

    out_ref[...] = (dot(branch_grad_ref[...], w_branch_ref[...], NT) + dot(fed_grad_ref[...], w_input_ref[...], NT)
                    + dot(through_ref[...], down_ref[...]))

    @pl.when(step == max(steps - 2, 0))
    def _():
        total.middle()

    @pl.when(step == steps - 1)
    def _():
        total.end()
        chain.begin()
        for d in range(1, levels):
            chain.hop(d)
        chain.end()
        total.clear()


def tail_call(branch_grad, fed_grad, w_branch, w_input, through, down, partial):
    rows, width = branch_grad.shape
    ranks, cols = partial.shape[1:]
    count = lax.axis_size("replica")
    tile = tile_of(width, 512)
    steps = pl.cdiv(width, tile)
    weight = pl.BlockSpec((tile, width), lambda i: (i, 0))
    return pl.pallas_call(
        functools.partial(tail_kernel, steps),
        grid=(steps,),
        out_shape=[jax.ShapeDtypeStruct((rows, width), F32), jax.ShapeDtypeStruct((count, ranks, cols), BF16)],
        in_specs=[resident(branch_grad), resident(fed_grad), weight, weight, resident(through),
                  pl.BlockSpec((down.shape[0], tile), lambda i: (0, i)), ANYWHERE],
        out_specs=[pl.BlockSpec((rows, tile), lambda i: (0, i)), ANYWHERE],
        scratch_shapes=GroupSum.shapes(ranks, cols) + ReplicaChain.shapes(count),
        compiler_params=pltpu.CompilerParams(
            vmem_limit_bytes=VMEM, collective_id=4, has_side_effects=True),
        cost_estimate=pl.CostEstimate(
            flops=4 * rows * width * width, bytes_accessed=4 * width * width + 8 * rows * width, transcendentals=0),
    )(branch_grad, fed_grad, w_branch, w_input, through, down, partial)


def spread_kernel(counts, ids_ref, *refs):
    gots, outs = refs[: len(counts)], refs[len(counts) :]
    ranks = outs[0].shape[1]
    replicas = gots[0].shape[0]
    seqs = ids_ref.shape[0] // replicas
    for out_ref in outs:
        out_ref[...] = jnp.zeros_like(out_ref)
    for replica in range(replicas):
        for s in range(seqs):
            place = ids_ref[replica * seqs + s]
            table = 0
            for count, got_ref in zip(counts, gots):
                for at in range(count):
                    rows = pl.ds((at * seqs + s) * ranks, ranks)
                    outs[table][place] += got_ref[replica, rows, :].astype(F32)
                    table += 1


def spread(ids, gots, counts, sets, ranks):
    vmem = pl.BlockSpec(memory_space=pltpu.VMEM)
    return pl.pallas_call(
        functools.partial(spread_kernel, counts),
        out_shape=[jax.ShapeDtypeStruct((sets, ranks, got.shape[2]), F32)
                   for got, count in zip(gots, counts) for _ in range(count)],
        in_specs=[pl.BlockSpec(memory_space=pltpu.SMEM)] + [vmem] * len(gots),
        out_specs=[vmem] * sum(counts),
        compiler_params=pltpu.CompilerParams(vmem_limit_bytes=VMEM),
        cost_estimate=pl.CostEstimate(
            flops=sum(got.size for got in gots), bytes_accessed=4 * sum(got.size for got in gots), transcendentals=0),
    )(ids, *gots)


def products_kernel(plan, *refs):
    out_ref, row = refs[-1], 0
    for place, (kind, first, last) in plan:
        if kind == "product":
            result = dot(refs[place][:, first:last], refs[place + 1][...], TN)
        else:
            result = refs[place][...]
        count = last - first
        out_ref[row : row + count, :] = result.astype(BF16)
        row += count


def products(items, earlier=(), blocks=1):
    operands, specs, plan, total = [], [], [], 0
    width = items[0][3].shape[-1]
    tile = width // blocks if blocks > 1 and width % (128 * blocks) == 0 else tile_of(width, 512)
    for item in items:
        if len(item) == 1:
            plan.append((len(operands), ("rows", 0, item[0].shape[0])))
            operands.append(item[0])
            specs.append(pl.BlockSpec((item[0].shape[0], tile), lambda i: (0, i)))
        else:
            lhs, first, last, rhs = item
            plan.append((len(operands), ("product", first, last)))
            if isinstance(rhs, tuple):
                rhs, s = rhs
                block = pl.BlockSpec((None, rhs.shape[1], tile), lambda i, s=s: (s, 0, i))
            else:
                block = pl.BlockSpec((rhs.shape[0], tile), lambda i: (0, i))
            operands += [lhs, rhs]
            specs += [resident(lhs), block]
        total += plan[-1][1][2] - plan[-1][1][1]
    cells = sum(operand.size for operand in operands)
    direct = blocks > 1 and tile * blocks == width
    result = pl.pallas_call(
        functools.partial(products_kernel, plan),
        grid=(pl.cdiv(width, tile),),
        out_shape=jax.ShapeDtypeStruct((blocks, total, tile) if direct else (total, width), BF16),
        in_specs=specs + [ANYWHERE] * len(earlier),
        out_specs=(pl.BlockSpec((None, total, tile), lambda i: (i, 0, 0)) if direct
                   else pl.BlockSpec((total, tile), lambda i: (0, i))),
        compiler_params=pltpu.CompilerParams(vmem_limit_bytes=VMEM),
        cost_estimate=pl.CostEstimate(flops=64 * cells, bytes_accessed=2 * cells, transcendentals=0),
    )(*operands, *earlier)
    if blocks > 1 and not direct:
        result = jnp.swapaxes(result.reshape(total, blocks, width // blocks), 0, 1)
    return result


def passed_along(block, axis, distance):
    devices = range(lax.axis_size(axis))
    route = [(i - distance, i) for i in devices if i - distance in devices]
    return lax.ppermute(block, axis, route)


def body(
    inputs, segment_ids, adapter_ids, gain_mix, gain_mlp, w_branch, w_input, conv_taps, decay_heads, admit_heads,
    decay_param, w_mixer, w_gate, w_upper, w_down, down_branch, lift_branch, down_input, lift_input, down_decay,
    lift_decay, down_admit, lift_admit, down_mixer, lift_mixer, down_gate, lift_gate, down_upper, lift_upper,
    down_outward, lift_outward, out_grad,
):
    seqs, stretch, width = inputs.shape
    rows = seqs * stretch
    taps = conv_taps.shape[0]
    sets, _, ranks = down_branch.shape
    group, place = lax.axis_size("group"), lax.axis_index("group")
    mask_cols = seqs * ranks

    turned = lambda table: jnp.swapaxes(table, 1, 2)
    full_branch, full_input, full_mixer, stack, late_grad, normed, own_tables = gather_weights(
        w_branch, w_input, w_mixer, out_grad, inputs.reshape(rows, width), gain_mix.reshape(1, width), adapter_ids,
        [turned(down_branch), turned(down_input), turned(down_decay), turned(down_admit), turned(down_mixer),
         turned(down_gate), turned(down_upper), lift_branch, lift_input, lift_decay, lift_admit, lift_mixer,
         lift_outward],
        [lift_gate, lift_upper, turned(down_outward)])
    (p_down_branch, p_down_input, p_down_decay, p_down_admit, p_down_mixer, p_down_gate, p_down_upper,
     p_lift_branch, p_lift_input, p_lift_decay, p_lift_admit, p_lift_mixer, p_lift_outward) = [
        stack[i * mask_cols : (i + 1) * mask_cols] for i in range(13)]
    own_lift_gate, own_lift_upper, own_down_outward = [
        own_tables[i * mask_cols : (i + 1) * mask_cols] for i in range(3)]
    cotangents = lax.all_gather(late_grad, "group", axis=1, tiled=True)

    row_seq = lax.broadcasted_iota(jnp.int32, (rows, mask_cols), 0) // stretch
    col_seq = lax.broadcasted_iota(jnp.int32, (rows, mask_cols), 1) // ranks
    own = (row_seq == col_seq).astype(F32)
    own_two = jnp.concatenate([own, own], 1)

    begin = place * stretch
    padded_ids = jnp.pad(segment_ids, ((0, 0), (taps - 1, taps - 1)), constant_values=-1)
    window = lax.dynamic_slice_in_dim(padded_ids, begin, stretch + 2 * (taps - 1), 1)
    current = window[:, taps - 1 : taps - 1 + stretch + taps - 1]
    agree = [
        ((current == window[:, taps - 1 - j : taps - 1 - j + stretch + taps - 1]) & (current >= 0)).astype(F32)
        for j in range(taps)
    ]
    restart = (1.0 - agree[1][:, :stretch]).reshape(rows, 1)

    x_float = inputs.reshape(rows, width).astype(F32)
    inner_one = (dot(normed, stack[: 2 * mask_cols], NT) * own_two).astype(BF16)
    inner_branch, inner_input = inner_one[:, :mask_cols], inner_one[:, mask_cols:]
    branch_pre = dot(normed, full_branch) + dot(inner_branch, p_lift_branch)
    fed = (dot(normed, full_input) + dot(inner_input, p_lift_input)).astype(BF16)
    fed = fed.reshape(seqs, stretch, width)
    halo = passed_along(fed[:, stretch - (taps - 1) :], "group", 1)
    extended = jnp.concatenate([halo, fed], axis=1).astype(F32)
    convolved = sum(
        conv_taps[j] * agree[j][:, :stretch, None] * extended[:, taps - 1 - j : taps - 1 - j + stretch]
        for j in range(taps)
    ).reshape(rows, width)
    rounded = convolved.astype(BF16)
    softrate = jax.nn.softplus(decay_param).reshape(1, width)
    inner_gates = (dot(rounded, stack[2 * mask_cols : 4 * mask_cols], NT) * own_two).astype(BF16)
    lift_gates = stack[9 * mask_cols : 11 * mask_cols]
    cum, local = forward_gates(seqs, convolved, inner_gates, lift_gates, decay_heads, admit_heads, softrate, restart)
    ends = jnp.concatenate(
        [cum.reshape(seqs, stretch, width)[:, -1], local.reshape(seqs, stretch, width)[:, -1]], 0)
    all_ends = lax.all_gather(ends, "group")
    carried = jnp.zeros((seqs, width), F32)
    for g in range(group - 1):
        longer = all_ends[g, :seqs] * carried + all_ends[g, seqs:]
        carried = jnp.where(g < place, longer, carried)
    carried_rows = jnp.repeat(carried, stretch, axis=0)
    state = local + cum * carried_rows
    merged = (state * gelu(branch_pre)).astype(BF16)
    inner_mixer = (dot(merged, p_down_mixer, NT) * own).astype(BF16)
    mixed = dot(merged, full_mixer) + dot(inner_mixer, p_lift_mixer)
    resid = x_float + mixed
    normed_two_f, _ = norm_rows(resid, gain_mlp)
    normed_two = normed_two_f.astype(BF16).reshape(seqs, stretch, width)

    spans = [slice(s * ranks, (s + 1) * ranks) for s in range(seqs)]
    named = jnp.broadcast_to(jnp.pad(adapter_ids, (0, -seqs % 16)).astype(BF16)[:, None], (-(-seqs // 16) * 16,
                                                                                   w_gate.shape[1]))
    gain_one, gain_two = gain_mix.reshape(1, width), gain_mlp.reshape(1, width)
    agree_cols = jnp.stack([agree[j][:, j : j + stretch].reshape(rows) for j in range(taps)], 1)
    grad_hiddens, through_out, first_tokens = grad_hidden_call(
        cotangents, w_down, p_lift_outward, own_down_outward, normed_two[0], (gain_two, gain_one, agree_cols, named))
    all_tokens = [first_tokens] + [
        lax.all_gather(ordered(normed_two[s], first_tokens), "group", axis=0, tiled=True) for s in range(1, seqs)]
    backs, hiddens, throughs, wides = [], [], [], []
    for s, at in enumerate(spans):
        two_downs = jnp.concatenate([p_down_gate[at], p_down_upper[at]], 0)
        hidden, back, wide, through = feed_call(
            s, all_tokens[s], grad_hiddens, w_gate, w_upper, two_downs, own_lift_gate[at], own_lift_upper[at],
            through_out)
        if s < seqs - 1:
            backs.append(lax.psum_scatter(back, "group", scatter_dimension=0, tiled=True))
        hiddens.append(hidden)
        throughs.append(through)
        wides.append(wide)
    outward, _, early, reduced = outward_call(
        hiddens, all_tokens, throughs, cotangents, resid, w_down, own_down_outward, p_lift_outward, back)
    backs.append(reduced)
    wide = jnp.concatenate(
        [wides[s][i * ranks : (i + 1) * ranks] for i in range(3) for s in range(seqs)] + [named], 0)
    grad_resid, grad_mixed = resid_grad(
        resid, out_grad.reshape(rows, width), gain_two, backs)
    block_out = lax.psum_scatter(outward, "group", scatter_dimension=1, tiled=True)

    kernels = (group == 4 and lax.axis_size("replica") % 2 == 0 and 2 * seqs <= 8 and stretch % GROUP == 0
               and width % 512 == 0 and seqs % 2 == 0)
    if kernels:
        grad_branch_pre, through_one, through_gates, grad_lift_gates, grad_fed, through_mixer, got_early, got_wide = mixer_back(
            seqs, grad_mixed, full_mixer, p_lift_mixer, p_down_mixer, convolved, inner_gates, lift_gates, decay_heads,
            admit_heads, softrate, restart, cum, local, carried, branch_pre, p_lift_branch, p_lift_input,
            stack[2 * mask_cols : 4 * mask_cols], conv_taps, agree_cols, early, wide)
    else:
        through_mixer = (dot(grad_mixed, p_lift_mixer, NT) * own).astype(BF16)
        grad_merged = dot(grad_mixed, full_mixer, NT) + dot(through_mixer, p_down_mixer)
        span, total, firsts, grad_branch_pre = backward_scan(
            seqs, convolved, inner_gates, lift_gates, decay_heads, softrate, restart, cum, local, carried, branch_pre,
            grad_merged)
        all_firsts = lax.all_gather(firsts, "group")
        incoming = jnp.zeros((seqs, width), F32)
        for lap in range(group - 1):
            g = group - 1 - lap
            longer = all_firsts[g, :seqs] * incoming + all_firsts[g, seqs:]
            incoming = jnp.where(g > place, longer, incoming)
        grad_direct, through_gates, grad_lift_gates = backward_gates(
            seqs, convolved, inner_gates, lift_gates, decay_heads, admit_heads, softrate, restart, cum, local, carried,
            span, total, incoming)
        through_gates = (through_gates * own_two).astype(BF16)
        grad_convolved = grad_direct + dot(through_gates, stack[2 * mask_cols : 4 * mask_cols])
        grad_convolved = grad_convolved.reshape(seqs, stretch, width)
        below = passed_along(grad_convolved[:, : taps - 1].astype(BF16), "group", -1).astype(F32)
        grad_extended = jnp.concatenate([grad_convolved, below], axis=1)
        grad_fed = sum(
            conv_taps[j] * agree[j][:, j : j + stretch, None] * grad_extended[:, j : j + stretch] for j in range(taps)
        ).astype(BF16).reshape(rows, width)
        through_branch = (dot(grad_branch_pre, p_lift_branch, NT) * own).astype(BF16)
        through_input = (dot(grad_fed, p_lift_input, NT) * own).astype(BF16)
        through_one = jnp.concatenate([through_branch, through_input], 1)
    both = 2 * mask_cols
    late = products(
        [(through_one, 0, both, normed), (through_gates, 0, both, rounded), (through_mixer, 0, mask_cols, merged),
         (inner_branch, 0, mask_cols, grad_branch_pre), (inner_input, 0, mask_cols, grad_fed), (grad_lift_gates,),
         (inner_mixer, 0, mask_cols, grad_mixed)], (), group)
    if kernels:
        grad_normed, got_late = tail_call(
            grad_branch_pre, grad_fed, full_branch, full_input, through_one, stack[:both], late)
    else:
        grad_normed = (dot(grad_branch_pre, full_branch, NT) + dot(grad_fed, full_input, NT)
                       + dot(through_one, stack[:both]))
        got_late = lax.all_gather(lax.psum_scatter(late, "group", scatter_dimension=0, tiled=False), "replica")
        got_early = lax.all_gather(lax.psum_scatter(early, "group", scatter_dimension=1, tiled=True), "replica")
        got_wide = lax.all_gather(wide, "replica")
    grad_inputs = finish(grad_resid, inputs.reshape(rows, width), gain_one, grad_normed)
    all_ids = got_wide[:, 3 * mask_cols : 3 * mask_cols + seqs, 0].astype(jnp.int32).reshape(-1)
    totals = spread(all_ids, [got_late, got_early, got_wide], (10, 3, 3), sets, ranks)
    (t_down_branch, t_down_input, t_down_decay, t_down_admit, t_down_mixer, t_lift_branch, t_lift_input, t_lift_decay,
     t_lift_admit, t_lift_mixer, t_down_gate, t_down_upper, t_lift_outward, *wides) = totals
    return (
        block_out, grad_inputs.reshape(seqs, stretch, width),
        turned(t_down_branch), t_lift_branch, turned(t_down_input), t_lift_input, turned(t_down_decay), t_lift_decay,
        turned(t_down_admit), t_lift_admit, turned(t_down_mixer), t_lift_mixer, turned(t_down_gate), wides[0],
        turned(t_down_upper), wides[1], turned(wides[2]), t_lift_outward,
    )


def solution(mesh):
    tokens = P("replica", "group", None)
    down, lift = P(None, "group", None), P(None, None, "group")
    cols, split = P(None, "group"), P("group", None)
    in_specs = (
        tokens, P("replica", None), P("replica"), P(), P(), cols, cols, P(), P(), P(), P(), split, cols, cols, split,
    ) + (down, lift) * 8 + (tokens,)
    out_specs = (tokens, tokens) + (down, lift) * 8
    return jax.shard_map(body, mesh=mesh, in_specs=in_specs, out_specs=out_specs, check_vma=False)
```
